32 devices in a mesh: rows: 4 (over z), seq: 8 (over y, x, core).
Axes of the slice: x: 2, y: 2, z: 4, core: 2. Of those that a mesh axis runs over, the one named last changes fastest.
Arguments:
- tokens: bfloat16 [4, 2048, 2048], P('rows', 'seq'), may hold values from -6 to 6
- segments: int32 [4, 2048], P('rows', 'seq'), may hold values from 0 to 4, as said below
- positions: int32 [4, 2048], P('rows', 'seq'), may hold values from 0 to 4095, as said below
- cotangent: bfloat16 [4, 2048, 2048], P('rows', 'seq'), may hold values from -6 to 6
- gain_attn: bfloat16 [2048], P(('rows', 'seq')), may hold values from 0.099609375 to 1.8984375
- query_key_value_weight: bfloat16 [2048, 2304], P(('rows', 'seq')), may hold values from -0.1875 to 0.1875
- gain_q: bfloat16 [64], replicated, may hold values from 0.099609375 to 1.8984375
- gain_k: bfloat16 [64], replicated, may hold values from 0.099609375 to 1.8984375
- w_out: bfloat16 [1536, 2048], P(None, ('rows', 'seq')), may hold values from -2 to 2
- gain_ffn: bfloat16 [2048], P(('rows', 'seq')), may hold values from 0.099609375 to 1.8984375
- w_gate: bfloat16 [2048, 4096], P('rows', 'seq'), may hold values from -0.125 to 0.125
- w_up: bfloat16 [2048, 4096], P('rows', 'seq'), may hold values from -0.125 to 0.125
- w_down: bfloat16 [4096, 2048], P('seq', 'rows'), may hold values from -0.09375 to 0.09375
Outputs:
- layer_out: bfloat16 [4, 2048, 2048], P('rows', 'seq')
- grad_tokens: float32 [4, 2048, 2048], P('rows', 'seq')
- grad_gain_attn: float32 [2048], P(('rows', 'seq'))
- grad_w_qkv: float32 [2048, 2304], P(('rows', 'seq'))
- grad_gain_q: float32 [64], replicated
- grad_gain_k: float32 [64], replicated
- grad_w_out: float32 [1536, 2048], P(None, ('rows', 'seq'))
- grad_gain_ffn: float32 [2048], P(('rows', 'seq'))
- grad_w_gate: float32 [2048, 4096], P('rows', 'seq')
- grad_w_up: float32 [2048, 4096], P('rows', 'seq')
- grad_w_down: float32 [4096, 2048], P('seq', 'rows')
The draws below stay inside these ranges and needn't reach their ends.
Inputs may be any that keep to these rules, and one draw needn't show every extreme that they name: `segments`: along a row segment numbers never fall, and every row holds all of them. Within a document positions rise by one from token to token; every row's first document starts at 0.
All inputs are finite; a program needn't handle non-finite values.
Results may differ from the reference program's by a relative error of at most 0.023.
Values may be sent and summed in bfloat16 or wider, within the bound.
A program may use at most 320 MiB of HBM per device.

```python
import math
import jax
import jax.numpy as jnp
from jax import lax

MODEL_WIDTH = 2048
QUERY_HEADS = 24
KEY_VALUE_HEADS = 6
HEAD_SIZE = 64
FF = 4096
TOK_DEV = 256
LENGTH = 2048
ROWS = 4


def row_layout(key):
    split_keys = jax.random.split(key, 5)
    start_long = jax.random.randint(split_keys[0], (ROWS,), 2, TOK_DEV)
    early_cut = jax.random.randint(split_keys[1], (ROWS,), 1, start_long)
    end_long = LENGTH - jax.random.randint(split_keys[2], (ROWS,), 2, TOK_DEV)
    late_cut = jax.random.randint(split_keys[3], (ROWS,), end_long + 1, LENGTH)
    offsets = jax.random.randint(split_keys[4], (ROWS, 5), 0, 2048)
    long_top = LENGTH + 2047 - (end_long - 1 - start_long)
    offsets = offsets.at[:, 0].set(0)
    offsets = offsets.at[:, 2].set(long_top.astype(jnp.int32))
    token_position_index = jnp.arange(LENGTH, dtype=jnp.int32)[None, :]
    bounds = jnp.stack([jnp.zeros_like(early_cut), early_cut, start_long, end_long, late_cut], axis=1)
    segment = jnp.zeros((ROWS, LENGTH), jnp.int32)
    for number in range(1, 5):
        segment = segment + (token_position_index >= bounds[:, number:number + 1]).astype(jnp.int32)
    doc_start = jnp.zeros((ROWS, LENGTH), jnp.int32)
    doc_offset = jnp.zeros((ROWS, LENGTH), jnp.int32)
    for number in range(5):
        inside = segment == number
        doc_start = doc_start + jnp.where(inside, bounds[:, number:number + 1], 0)
        doc_offset = doc_offset + jnp.where(inside, offsets[:, number:number + 1], 0)
    position = token_position_index - doc_start + doc_offset
    return (segment.astype(jnp.int32), position.astype(jnp.int32))


def draw_segments(key, part):
    shared = row_layout(key)
    return shared[0]


def draw_positions(key, part):
    shared = row_layout(key)
    return shared[1]


def levels(own_key, shape, cuts, least, top_value):
    def one(axis_at, parts):
        draws = jax.random.uniform(jax.random.fold_in(jax.random.fold_in(own_key, 6), axis_at), (parts,), jnp.float32, least / len(cuts), top_value / len(cuts))
        return jnp.repeat(jnp.exp(draws), shape[axis_at] // parts).reshape((-1,) + (1,) * (len(shape) - axis_at - 1))

    factor_of = one(*cuts[0])
    for cut in cuts[1:]:
        factor_of = factor_of * one(*cut)
    return factor_of


def noise(own_key, dims, scale, bound, shards=(), kind=jnp.bfloat16):
    values = jax.random.normal(own_key, dims, jnp.float32) * scale
    if len(shards) > 0:
        values = levels(own_key, dims, shards, -0.22, 0.18) * values
    return jnp.clip(values, min=-bound, max=bound).astype(kind)


def setup_inputs(seed: int = 0) -> dict:
    streams_of = jax.random.split(jax.random.key(seed), 14)
    tokens = noise(streams_of[0], (ROWS, LENGTH, MODEL_WIDTH), 1.0, 6.0, ((0, 4), (1, 8)))
    segments = draw_segments(jax.random.fold_in(streams_of[13], 71), 0)
    positions = draw_positions(jax.random.fold_in(streams_of[13], 71), 0)
    cotangent = noise(streams_of[3], (ROWS, LENGTH, MODEL_WIDTH), 1.0, 6.0, ((0, 4), (1, 8)))
    gain_attn = jnp.clip(1.0 + 0.18 * jax.random.normal(streams_of[4], (MODEL_WIDTH,), jnp.float32), 0.099609375, 1.8984375).astype(jnp.bfloat16)
    query_key_value_weight = noise(streams_of[5], (MODEL_WIDTH, (QUERY_HEADS + 2 * KEY_VALUE_HEADS) * HEAD_SIZE), (MODEL_WIDTH // 2) ** -0.5, 0.1875, ((0, 32),))
    gain_q = jnp.clip(1.0 + 0.18 * jax.random.normal(streams_of[6], (HEAD_SIZE,), jnp.float32), 0.099609375, 1.8984375).astype(jnp.bfloat16)
    gain_k = jnp.clip(1.0 + 0.18 * jax.random.normal(streams_of[7], (HEAD_SIZE,), jnp.float32), 0.099609375, 1.8984375).astype(jnp.bfloat16)
    w_out = noise(streams_of[8], (QUERY_HEADS * HEAD_SIZE, MODEL_WIDTH), 8 ** -0.5, 2.0, ((1, 32),))
    gain_ffn = jnp.clip(1.0 + 0.18 * jax.random.normal(streams_of[9], (MODEL_WIDTH,), jnp.float32), 0.099609375, 1.8984375).astype(jnp.bfloat16)
    w_gate = noise(streams_of[10], (MODEL_WIDTH, FF), MODEL_WIDTH ** -0.5, 0.125, ((0, 4), (1, 8)))
    w_up = noise(streams_of[11], (MODEL_WIDTH, FF), MODEL_WIDTH ** -0.5, 0.125, ((0, 4), (1, 8)))
    w_down = noise(streams_of[12], (FF, MODEL_WIDTH), FF ** -0.5, 0.09375, ((0, 8), (1, 4)))
    return {"tokens": tokens, "segments": segments, "positions": positions, "cotangent": cotangent, "gain_attn": gain_attn, "query_key_value_weight": query_key_value_weight, "gain_q": gain_q, "gain_k": gain_k, "w_out": w_out, "gain_ffn": gain_ffn, "w_gate": w_gate, "w_up": w_up, "w_down": w_down}


EPSILON = 1e-06
THETA = 10000.0

@jax.custom_vjp
def reduced_input(v):
    return lax.optimization_barrier(v.astype(jnp.bfloat16)).astype(jnp.float32)

@jax.custom_vjp
def low_back(v):
    return v

def low_keep(v):
    return (reduced_input(v), None)

def low_pass(kept, grad):
    return (grad,)

def back_keep(v):
    return (v, None)

def back_low(kept, grad):
    return (reduced_input(grad),)
reduced_input.defvjp(low_keep, low_pass)
low_back.defvjp(back_keep, back_low)

def matmul(left, right):
    return jnp.dot(left, right, precision=lax.Precision.HIGHEST, preferred_element_type=jnp.float32)

def rotary_tables(positions):
    half_size = HEAD_SIZE // 2
    inverse = jnp.exp(-math.log(THETA) * jnp.arange(half_size, dtype=jnp.float32) * 2.0 / HEAD_SIZE)
    angles = positions.astype(jnp.float32)[:, None] * inverse[None, :]
    angles = jnp.concatenate([angles, angles], axis=1)
    return (jnp.cos(angles)[:, None, :], jnp.sin(angles)[:, None, :])

def rotate_half(vector):
    first_half = vector[..., :HEAD_SIZE // 2]
    second_half = vector[..., HEAD_SIZE // 2:]
    return jnp.concatenate([-second_half, first_half], axis=-1)

def root_mean_square_norm(inputs, gain):
    return inputs * lax.rsqrt(lax.optimization_barrier(jnp.mean(inputs * inputs, axis=-1, keepdims=True)) + EPSILON) * gain

def attend(query_block, query_index, query_segment, keys_all, values_all, key_index, key_segment):
    scores = low_back(jnp.einsum('tgmd,ngd->tgmn', query_block, keys_all, precision=lax.Precision.HIGHEST))
    allowed = (key_index[None, None, None, :] <= query_index[:, None, None, None]) & (key_segment[None, None, None, :] == query_segment[:, None, None, None])
    masked = jnp.where(allowed, scores, -1e+30)
    largest = lax.optimization_barrier(jnp.max(masked, axis=-1, keepdims=True))
    weights = jnp.where(allowed, jnp.exp(masked - largest), 0.0)
    probabilities = reduced_input(weights / lax.optimization_barrier(jnp.sum(weights, axis=-1, keepdims=True)))
    return jnp.einsum('tgmn,ngd->tgmd', probabilities, values_all, precision=lax.Precision.HIGHEST)

def layer_row(row_input, row_document_ids, row_positions, params):
    gain_one, qkv_weight, query_gain, key_norm_weight, out_weight, gain_two, gate_weight, up_weight, down_weight = params
    sequence_length = row_input.shape[0]
    query_group_count = QUERY_HEADS // KEY_VALUE_HEADS
    query_total_width = QUERY_HEADS * HEAD_SIZE
    key_total_width = KEY_VALUE_HEADS * HEAD_SIZE
    normed = reduced_input(root_mean_square_norm(row_input, gain_one))
    projection_output = low_back(matmul(normed, qkv_weight))
    query_rows = root_mean_square_norm(projection_output[:, :query_total_width].reshape(sequence_length, QUERY_HEADS, HEAD_SIZE), query_gain)
    unnormed_keys = root_mean_square_norm(projection_output[:, query_total_width:query_total_width + key_total_width].reshape(sequence_length, KEY_VALUE_HEADS, HEAD_SIZE), key_norm_weight)
    projected_values = projection_output[:, query_total_width + key_total_width:].reshape(sequence_length, KEY_VALUE_HEADS, HEAD_SIZE)
    cosine_lookup, sine_lookup = rotary_tables(row_positions)
    query_rows = query_rows * cosine_lookup + rotate_half(query_rows) * sine_lookup
    keys_rot = unnormed_keys * cosine_lookup + rotate_half(unnormed_keys) * sine_lookup
    query_reduced_precision = reduced_input(query_rows * HEAD_SIZE ** (-0.5)).reshape(sequence_length, KEY_VALUE_HEADS, query_group_count, HEAD_SIZE)
    key_reduced_precision = reduced_input(keys_rot)
    value_reduced_precision = reduced_input(projected_values)
    rows_per_block = math.gcd(sequence_length, 512)
    count_of_blocks = sequence_length // rows_per_block
    token_position_index = jnp.arange(sequence_length, dtype=jnp.int32)
    step_function = jax.checkpoint(attend)
    attention_output = lax.map(lambda input_blocks: step_function(input_blocks[0], input_blocks[1], input_blocks[2], key_reduced_precision, value_reduced_precision, token_position_index, row_document_ids), (query_reduced_precision.reshape(count_of_blocks, rows_per_block, KEY_VALUE_HEADS, query_group_count, HEAD_SIZE), token_position_index.reshape(count_of_blocks, rows_per_block), row_document_ids.reshape(count_of_blocks, rows_per_block)))
    merged = reduced_input(low_back(attention_output.reshape(sequence_length, query_total_width)))
    residual = row_input + low_back(matmul(merged, out_weight))
    normed_two = reduced_input(root_mean_square_norm(residual, gain_two))
    gate_act = low_back(matmul(normed_two, gate_weight))
    up_act = low_back(matmul(normed_two, up_weight))
    hidden = reduced_input(jax.nn.silu(gate_act) * up_act)
    return residual + low_back(matmul(hidden, down_weight))

def reference(tokens, segments, positions, cotangent, gain_attn, query_key_value_weight, gain_q, gain_k, w_out, gain_ffn, w_gate, w_up, w_down):
    params = tuple((weight.astype(jnp.float32) for weight in (gain_attn, query_key_value_weight, gain_q, gain_k, w_out, gain_ffn, w_gate, w_up, w_down)))
    inputs = tokens.astype(jnp.float32)

    def whole_layer(layer_inputs, layer_params):
        return lax.map(lambda row_args: layer_row(row_args[0], row_args[1], row_args[2], layer_params), (layer_inputs, segments, positions))
    outputs, pullback = jax.vjp(whole_layer, inputs, params)
    input_grad, param_grads = pullback(cotangent.astype(jnp.float32))
    return (outputs.astype(jnp.bfloat16), input_grad, param_grads[0], param_grads[1], param_grads[2], param_grads[3], param_grads[4], param_grads[5], param_grads[6], param_grads[7], param_grads[8])
```

```python
import functools
import math

import jax
import jax.numpy as jnp
from jax import lax
from jax.experimental import pallas as pl
from jax.experimental.pallas import tpu as pltpu
from jax.sharding import PartitionSpec as P

QUERY_HEADS = 24
KEY_VALUE_HEADS = 6
GROUP = QUERY_HEADS // KEY_VALUE_HEADS
D = 64
HALF = D // 2
EPSILON = 1e-06
THETA = 10000.0
PENALTY = -10000.0
SEGMENT_KINDS = 8
BLOCK = 512
F32 = jnp.float32
BF16 = jnp.bfloat16
VMEM_LIMIT = 56 * 1024 * 1024


def dot(a, b):
    return jnp.dot(a, b, preferred_element_type=F32)


def dot_nt(a, b):
    return lax.dot_general(a, b, (((1,), (1,)), ((), ())), preferred_element_type=F32)


def dot_tn(a, b):
    return lax.dot_general(a, b, (((0,), (0,)), ((), ())), preferred_element_type=F32)


def rotary_table(positions, segments):
    inverse = jnp.exp(-math.log(THETA) * jnp.arange(HALF, dtype=F32) * 2.0 / D)
    angles = inverse[:, None] * positions.astype(F32)[None, :]
    hot = jnp.arange(SEGMENT_KINDS, dtype=jnp.int32)[:, None] == segments[None, :]
    return jnp.concatenate([jnp.cos(angles), jnp.sin(angles), hot.astype(F32)], axis=0)


def split3(x):
    high = x.astype(BF16).astype(F32)
    mid = (x - high).astype(BF16).astype(F32)
    return high, mid, x - high - mid


def attention_forward_kernel(heads, proj_ref, table_ref, gq_ref, gk_ref,
                             merged_ref, o_ref, qa_ref, ka_ref, kt_ref, vt_ref, inv_ref):
    blocks, _, tok = table_ref.shape
    length = blocks * tok
    width = heads * D
    gq = gq_ref[...]
    gk = gk_ref[...]
    ones8 = jnp.ones((8, tok), F32)
    row8 = lax.broadcasted_iota(jnp.int32, (16, tok), 0)
    one_row = jnp.where(row8 == 0, 1.0, 0.0).astype(F32)

    def prepare(b, _):
        lanes = pl.ds(pl.multiple_of(b * tok, tok), tok)
        cos = table_ref[b, 0:HALF, :]
        sin = table_ref[b, HALF:D, :]
        hot = table_ref[b, D:D + 8, :]
        pen = (1.0 - hot) * PENALTY
        for h in range(heads):
            rawq = proj_ref[h * D:(h + 1) * D, lanes]
            rawk = proj_ref[width + h * D:width + (h + 1) * D, lanes]
            rawv = proj_ref[2 * width + h * D:2 * width + (h + 1) * D, lanes]

            def rotated(raw, gain):
                inv = lax.rsqrt(jnp.mean(raw * raw, axis=0, keepdims=True) + EPSILON)
                n = raw * inv * gain
                a, c = n[:HALF], n[HALF:]
                return inv, jnp.concatenate([a * cos - c * sin, c * cos + a * sin], axis=0)

            iq, q = rotated(rawq, gq)
            ik, k = rotated(rawk, gk)
            inv_ref[2 * h:2 * h + 1, lanes] = iq
            inv_ref[2 * h + 1:2 * h + 2, lanes] = ik
            q = (q * (D ** -0.5)).astype(BF16)
            kt_ref[h, :, lanes] = k.astype(BF16)
            extra = jnp.concatenate([pen, jnp.zeros((8, tok), F32)], axis=0).astype(BF16)
            qa_ref[h, :, lanes] = jnp.concatenate([q, extra], axis=0)
            full = jnp.concatenate([k, hot, ones8, jnp.zeros((48, tok), F32)], axis=0)
            ka_ref[h, lanes, :] = jnp.transpose(full).astype(BF16)
            vt_ref[h, :, lanes] = jnp.concatenate([rawv, one_row], axis=0).astype(BF16)
        return 0

    lax.fori_loop(0, blocks, prepare, 0)

    causal = (lax.broadcasted_iota(jnp.int32, (BLOCK, BLOCK), 0)
              <= lax.broadcasted_iota(jnp.int32, (BLOCK, BLOCK), 1))

    def query_block(i, _):
        cols = pl.ds(pl.multiple_of(i * BLOCK, BLOCK), BLOCK)

        def step(j, accs, diagonal):
            rows = pl.ds(pl.multiple_of(j * BLOCK, BLOCK), BLOCK)
            new = []
            for h in range(heads):
                s = dot(ka_ref[h, rows, 0:80], qa_ref[h, :, cols])
                p = jnp.exp(s)
                if diagonal:
                    p = jnp.where(causal, p, 0.0)
                new.append(accs[h] + dot(vt_ref[h, :, rows], p.astype(BF16)))
            return tuple(new)

        accs = tuple(jnp.zeros((80, BLOCK), F32) for _ in range(heads))
        accs = lax.fori_loop(0, i, lambda j, c: step(j, c, False), accs)
        accs = step(i, accs, True)
        outs = []
        for h in range(heads):
            total = accs[h][D:D + 1]
            o = accs[h][:D] * (1.0 / total)
            o_ref[h, :, cols] = o
            outs.append(o)
            pieces = split3(-jnp.log(total))
            old = qa_ref[h, 64:80, cols].astype(F32)
            row = lax.broadcasted_iota(jnp.int32, (16, BLOCK), 0)
            extra = jnp.where(row == 8, pieces[0],
                              jnp.where(row == 9, pieces[1], jnp.where(row == 10, pieces[2], old)))
            qa_ref[h, 64:80, cols] = extra.astype(BF16)
        merged_ref[cols, :] = jnp.transpose(jnp.concatenate(outs, axis=0)).astype(BF16)
        return 0

    lax.fori_loop(0, length // BLOCK, query_block, 0)


def attention_backward_kernel(heads, proj_ref, table_ref, gq_ref, gk_ref, dm_ref,
                              o_ref, qa_ref, ka_ref, kt_ref, vt_ref, inv_ref,
                              pg_ref, gains_ref, doa_ref, q_ref, va_ref, dq_ref, dk_ref, dv_ref):
    blocks, _, tok = table_ref.shape
    length = blocks * tok
    width = heads * D
    gq = gq_ref[...]
    gk = gk_ref[...]

    def prepare(b, _):
        lanes = pl.ds(pl.multiple_of(b * tok, tok), tok)
        dmt = jnp.transpose(dm_ref[lanes, :].astype(F32))
        row = lax.broadcasted_iota(jnp.int32, (16, tok), 0)
        for h in range(heads):
            do = dmt[h * D:(h + 1) * D]
            delta = jnp.sum(do * o_ref[h, :, lanes], axis=0, keepdims=True)
            pieces = split3(-delta)
            extra = jnp.where(row == 0, pieces[0],
                              jnp.where(row == 1, pieces[1], jnp.where(row == 2, pieces[2], 0.0)))
            doa_ref[h, :, lanes] = jnp.concatenate([do, extra], axis=0).astype(BF16)
            qk = jnp.concatenate([qa_ref[h, 0:D, lanes].astype(F32), vt_ref[h, 0:D, lanes].astype(F32)], axis=0)
            back = jnp.transpose(qk)
            q_ref[h, lanes, :] = back[:, :D].astype(BF16)
            va_ref[h, lanes, :] = jnp.concatenate(
                [back[:, D:], jnp.ones((tok, 16), F32)], axis=1).astype(BF16)
            dq_ref[h, :, lanes] = jnp.zeros((D, tok), F32)
        return 0

    lax.fori_loop(0, blocks, prepare, 0)

    causal = (lax.broadcasted_iota(jnp.int32, (BLOCK, BLOCK), 0)
              <= lax.broadcasted_iota(jnp.int32, (BLOCK, BLOCK), 1))
    count = length // BLOCK

    def key_block(j, _):
        rows = pl.ds(pl.multiple_of(j * BLOCK, BLOCK), BLOCK)

        def step(i, accs, diagonal):
            cols = pl.ds(pl.multiple_of(i * BLOCK, BLOCK), BLOCK)
            new = []
            for h in range(heads):
                p = jnp.exp(dot(ka_ref[h, rows, 0:80], qa_ref[h, :, cols]))
                if diagonal:
                    p = jnp.where(causal, p, 0.0)
                dp = dot(va_ref[h, rows, :], doa_ref[h, :, cols])
                ds = (p * dp).astype(BF16)
                do = dm_ref[cols, h * D:(h + 1) * D]
                dv = accs[2 * h] + dot(p.astype(BF16), do)
                dk = accs[2 * h + 1] + dot(ds, q_ref[h, cols, :])
                dq_ref[h, :, cols] += dot(kt_ref[h, :, rows], ds)
                new += [dv, dk]
            return tuple(new)

        accs = tuple(jnp.zeros((BLOCK, D), F32) for _ in range(2 * heads))
        accs = step(j, accs, True)
        accs = lax.fori_loop(j + 1, count, lambda i, c: step(i, c, False), accs)
        for h in range(heads):
            both = jnp.transpose(jnp.concatenate([accs[2 * h], accs[2 * h + 1]], axis=1))
            dv_ref[h, :, rows] = both[:D]
            dk_ref[h, :, rows] = both[D:]
        return 0

    lax.fori_loop(0, count, key_block, 0)

    def finish(b, sums):
        lanes = pl.ds(pl.multiple_of(b * tok, tok), tok)
        cos = table_ref[b, 0:HALF, :]
        sin = table_ref[b, HALF:D, :]

        def back(grad, raw, inv, gain):
            a, c = grad[:HALF], grad[HALF:]
            n = jnp.concatenate([a * cos + c * sin, c * cos - a * sin], axis=0)
            v = n * gain
            out = inv * v - raw * (inv * inv * inv) * jnp.mean(v * raw, axis=0, keepdims=True)
            return out, n * raw * inv

        sum_q, sum_k = sums
        for h in range(heads):
            rawq = proj_ref[h * D:(h + 1) * D, lanes]
            rawk = proj_ref[width + h * D:width + (h + 1) * D, lanes]
            out_q, part_q = back(dq_ref[h, :, lanes] * (D ** -0.5), rawq, inv_ref[2 * h:2 * h + 1, lanes], gq)
            out_k, part_k = back(dk_ref[h, :, lanes], rawk, inv_ref[2 * h + 1:2 * h + 2, lanes], gk)
            pg_ref[h * D:(h + 1) * D, lanes] = out_q.astype(BF16)
            pg_ref[width + h * D:width + (h + 1) * D, lanes] = out_k.astype(BF16)
            pg_ref[2 * width + h * D:2 * width + (h + 1) * D, lanes] = dv_ref[h, :, lanes].astype(BF16)
            sum_q = sum_q + part_q
            sum_k = sum_k + part_k
        return sum_q, sum_k

    zero = jnp.zeros((D, tok), F32)
    sum_q, sum_k = lax.fori_loop(0, blocks, finish, (zero, zero))
    total = jnp.concatenate([jnp.sum(sum_q, axis=1, keepdims=True), jnp.sum(sum_k, axis=1, keepdims=True)], axis=0)
    gains_ref[...] = jnp.broadcast_to(total, gains_ref.shape)


def attention_forward(heads, proj, table, gq, gk):
    length = proj.shape[1]
    return pl.pallas_call(
        functools.partial(attention_forward_kernel, heads),
        out_shape=(
            jax.ShapeDtypeStruct((length, heads * D), BF16),
            jax.ShapeDtypeStruct((heads, D, length), F32),
            jax.ShapeDtypeStruct((heads, 80, length), BF16),
            jax.ShapeDtypeStruct((heads, length, 128), BF16),
            jax.ShapeDtypeStruct((heads, D, length), BF16),
            jax.ShapeDtypeStruct((heads, 80, length), BF16),
            jax.ShapeDtypeStruct((8, length), F32),
        ),
        compiler_params=pltpu.CompilerParams(vmem_limit_bytes=VMEM_LIMIT),
        cost_estimate=pl.CostEstimate(flops=4 * heads * 64 * length * length, bytes_accessed=16 << 20, transcendentals=heads * length * length // 2),
    )(proj, table, gq, gk)


def attention_backward(heads, proj, table, gq, gk, dm, kept):
    length = proj.shape[1]
    return pl.pallas_call(
        functools.partial(attention_backward_kernel, heads),
        out_shape=(
            jax.ShapeDtypeStruct((3 * heads * D, length), BF16),
            jax.ShapeDtypeStruct((2 * D, 128), F32),
        ),
        scratch_shapes=[
            pltpu.VMEM((heads, 80, length), BF16),
            pltpu.VMEM((heads, length, D), BF16),
            pltpu.VMEM((heads, length, 80), BF16),
            pltpu.VMEM((heads, D, length), F32),
            pltpu.VMEM((heads, D, length), F32),
            pltpu.VMEM((heads, D, length), F32),
        ],
        compiler_params=pltpu.CompilerParams(vmem_limit_bytes=VMEM_LIMIT),
        cost_estimate=pl.CostEstimate(flops=10 * heads * 64 * length * length, bytes_accessed=16 << 20, transcendentals=heads * length * length // 2),
    )(proj, table, gq, gk, dm, *kept)


def norm_inverse(x):
    return lax.rsqrt(jnp.mean(x * x, axis=-1, keepdims=True) + EPSILON)


def norm_back(grad_normed, values_in, inv_rms, gain):
    scaled = grad_normed * gain
    gain_grad = jnp.sum(grad_normed * values_in * inv_rms, axis=0)
    input_grad = inv_rms * scaled - values_in * inv_rms**3 * jnp.mean(scaled * values_in, axis=-1, keepdims=True)
    return input_grad, gain_grad


def body(tokens, segments, positions, cotangent, gain_attn, w_qkv, gain_q, gain_k, w_out, gain_ffn, w_gate, w_up, w_down):
    seq = lax.axis_size("seq")
    rows = lax.axis_size("rows")
    heads = -(-QUERY_HEADS // seq)
    padded = seq * heads
    depth = w_qkv.shape[0]
    width = heads * D
    tok = tokens.shape[1]

    def spread(columns):
        return jnp.repeat(columns.reshape(depth, KEY_VALUE_HEADS, D), GROUP, axis=1)

    def slabs(columns):
        columns = columns.reshape(depth, QUERY_HEADS, D)
        columns = jnp.pad(columns, ((0, 0), (0, padded - QUERY_HEADS), (0, 0)))
        return columns.reshape(depth, seq, width)

    qw, kw = QUERY_HEADS * D, KEY_VALUE_HEADS * D
    local = jnp.concatenate([
        slabs(w_qkv[:, :qw]),
        slabs(spread(w_qkv[:, qw:qw + kw])),
        slabs(spread(w_qkv[:, qw + kw:])),
        slabs(w_out.T),
    ], axis=2).transpose(1, 0, 2)
    mine = lax.all_to_all(local, "seq", 0, 0, tiled=False)
    attn_w = lax.all_gather(mine.reshape(seq * depth, 4 * width), "rows", axis=0, tiled=True)
    qkv_slab, out_slab = attn_w[:, :3 * width], attn_w[:, 3 * width:]

    gains = lax.all_gather(jnp.stack([gain_attn, gain_ffn])[:, None], ("rows", "seq"), axis=1, tiled=True)
    gain_one = gains[0].reshape(1, -1).astype(F32)
    gain_two = gains[1].reshape(1, -1).astype(F32)
    gate_slab = lax.all_gather(w_gate, "rows", axis=0, tiled=True)
    up_slab = lax.all_gather(w_up, "rows", axis=0, tiled=True)
    down_slab = lax.all_gather(w_down, "rows", axis=1, tiled=True)
    gq = gain_q.astype(F32)[:, None]
    gk = gain_k.astype(F32)[:, None]

    x = tokens[0].astype(F32)
    inv_one = norm_inverse(x)
    normed = (x * inv_one * gain_one).astype(BF16)
    table = lax.all_gather(rotary_table(positions[0], segments[0]), "seq", axis=0, tiled=False)
    normed_all = lax.all_gather(normed, "seq", axis=0, tiled=True)
    proj = lax.dot_general(qkv_slab, normed_all, (((0,), (1,)), ((), ())), preferred_element_type=F32)
    merged, *kept = attention_forward(heads, proj, table, gq, gk)
    out_part = dot_nt(merged, out_slab).astype(BF16)
    residual = x + lax.psum_scatter(out_part, "seq", scatter_dimension=0, tiled=True).astype(F32)
    inv_two = norm_inverse(residual)
    normed_two = (residual * inv_two * gain_two).astype(BF16)
    two_all = lax.all_gather(normed_two, "seq", axis=0, tiled=True)
    g_all = lax.all_gather(cotangent[0], "seq", axis=0, tiled=True)

    gate_act = dot(two_all, gate_slab)
    up_act = dot(two_all, up_slab)
    s = jax.nn.sigmoid(gate_act)
    hidden = (gate_act * s * up_act).astype(BF16)
    hidden_grad = dot_nt(g_all, down_slab)
    gate_grad = (hidden_grad * up_act * s * (1.0 + gate_act * (1.0 - s))).astype(BF16)
    up_grad = (hidden_grad * gate_act * s).astype(BF16)
    two_grad_part = (dot_nt(gate_grad, gate_slab) + dot_nt(up_grad, up_slab)).astype(BF16)
    two_grad = lax.psum_scatter(two_grad_part, "seq", scatter_dimension=0, tiled=True).astype(F32)
    branch_part = dot(hidden, down_slab).astype(BF16)
    branch = lax.psum_scatter(branch_part, "seq", scatter_dimension=0, tiled=True).astype(F32)
    layer_out = (residual + branch).astype(BF16)
    grad_gate = lax.psum_scatter(dot_tn(two_all, gate_grad).astype(BF16), "rows", scatter_dimension=0, tiled=True).astype(F32)
    grad_up = lax.psum_scatter(dot_tn(two_all, up_grad).astype(BF16), "rows", scatter_dimension=0, tiled=True).astype(F32)
    grad_down = lax.psum_scatter(dot_tn(hidden, g_all).astype(BF16), "rows", scatter_dimension=1, tiled=True).astype(F32)

    norm_grad, gain_two_grad = norm_back(two_grad, residual, inv_two, gain_two)
    residual_grad = cotangent[0].astype(F32) + norm_grad
    branch_all = lax.all_gather(residual_grad.astype(BF16), "seq", axis=0, tiled=True)
    dm = dot(branch_all, out_slab).astype(BF16)
    pg, head_gains = attention_backward(heads, proj, table, gq, gk, dm, kept)
    normed_part = lax.dot_general(pg, qkv_slab, (((0,), (1,)), ((), ())), preferred_element_type=F32).astype(BF16)
    normed_grad = lax.psum_scatter(normed_part, "seq", scatter_dimension=0, tiled=True).astype(F32)
    input_norm_grad, gain_one_grad = norm_back(normed_grad, x, inv_one, gain_one)
    grad_tokens = residual_grad + input_norm_grad

    qkv_wgrad = lax.dot_general(normed_all, pg, (((0,), (1,)), ((), ())), preferred_element_type=F32)
    out_wgrad = dot_tn(branch_all, merged)
    attn_grad = jnp.concatenate([qkv_wgrad, out_wgrad], axis=1).astype(BF16)
    attn_grad = lax.psum_scatter(attn_grad, "rows", scatter_dimension=0, tiled=True)
    attn_grad = lax.all_to_all(attn_grad.reshape(seq, depth, 4 * width), "seq", 0, 0, tiled=False).astype(F32)

    def unslab(part):
        part = attn_grad[:, :, part * width:(part + 1) * width].transpose(1, 0, 2)
        return part.reshape(depth, padded, D)[:, :QUERY_HEADS]

    def unspread(part):
        return jnp.sum(unslab(part).reshape(depth, KEY_VALUE_HEADS, GROUP, D), axis=2).reshape(depth, kw)

    grad_qkv = jnp.concatenate([unslab(0).reshape(depth, qw), unspread(1), unspread(2)], axis=1)
    grad_out = unslab(3).reshape(depth, qw).T

    small = lax.psum(jnp.concatenate([gain_one_grad, gain_two_grad, head_gains[:, 0]]), ("rows", "seq"))
    model = gain_one_grad.shape[0]
    start = (lax.axis_index("rows") * seq + lax.axis_index("seq")) * depth
    return (
        layer_out[None],
        grad_tokens[None],
        lax.dynamic_slice_in_dim(small, start, depth),
        grad_qkv,
        small[2 * model:2 * model + D],
        small[2 * model + D:],
        grad_out,
        lax.dynamic_slice_in_dim(small, model + start, depth),
        grad_gate,
        grad_up,
        grad_down,
    )


def solution(mesh):
    both = ("rows", "seq")
    return jax.shard_map(
        body,
        mesh=mesh,
        in_specs=(
            P("rows", "seq", None), P("rows", "seq"), P("rows", "seq"), P("rows", "seq", None),
            P(both), P(both, None), P(), P(), P(None, both), P(both),
            P("rows", "seq"), P("rows", "seq"), P("seq", "rows"),
        ),
        out_specs=(
            P("rows", "seq", None), P("rows", "seq", None), P(both), P(both, None), P(), P(),
            P(None, both), P(both), P("rows", "seq"), P("rows", "seq"), P("seq", "rows"),
        ),
        check_vma=False,
    )
```

```python
import functools
import math

import jax
import jax.numpy as jnp
from jax import lax
from jax.experimental import pallas as pl
from jax.experimental.pallas import tpu as pltpu
from jax.sharding import PartitionSpec as P

QUERY_HEADS = 24
KEY_VALUE_HEADS = 6
GROUP = QUERY_HEADS // KEY_VALUE_HEADS
D = 64
HALF = D // 2
EPSILON = 1e-06
THETA = 10000.0
PENALTY = -10000.0
SEGMENT_KINDS = 8
BLOCK = 512
F32 = jnp.float32
BF16 = jnp.bfloat16
VMEM_LIMIT = 56 * 1024 * 1024


def dot(a, b):
    return jnp.dot(a, b, preferred_element_type=F32)


def dot_nt(a, b):
    return lax.dot_general(a, b, (((1,), (1,)), ((), ())), preferred_element_type=F32)


def dot_tn(a, b):
    return lax.dot_general(a, b, (((0,), (0,)), ((), ())), preferred_element_type=F32)


def rotary_table(positions, segments):
    inverse = jnp.exp(-math.log(THETA) * jnp.arange(HALF, dtype=F32) * 2.0 / D)
    angles = inverse[:, None] * positions.astype(F32)[None, :]
    hot = jnp.arange(SEGMENT_KINDS, dtype=jnp.int32)[:, None] == segments[None, :]
    return jnp.concatenate([jnp.cos(angles), jnp.sin(angles), hot.astype(F32)], axis=0)


def split3(x):
    high = x.astype(BF16).astype(F32)
    mid = (x - high).astype(BF16).astype(F32)
    return high, mid, x - high - mid


def attention_forward_kernel(heads, proj_ref, table_ref, gq_ref, gk_ref,
                             merged_ref, o_ref, qa_ref, ka_ref, kt_ref, vt_ref, inv_ref):
    blocks, _, tok = table_ref.shape
    length = blocks * tok
    width = heads * D
    gq = gq_ref[...]
    gk = gk_ref[...]
    ones8 = jnp.ones((8, tok), F32)
    row8 = lax.broadcasted_iota(jnp.int32, (16, tok), 0)
    one_row = jnp.where(row8 == 0, 1.0, 0.0).astype(F32)

    def prepare(b, _):
        lanes = pl.ds(pl.multiple_of(b * tok, tok), tok)
        cos = table_ref[b, 0:HALF, :]
        sin = table_ref[b, HALF:D, :]
        hot = table_ref[b, D:D + 8, :]
        pen = (1.0 - hot) * PENALTY
        for h in range(heads):
            rawq = proj_ref[h * D:(h + 1) * D, lanes]
            rawk = proj_ref[width + h * D:width + (h + 1) * D, lanes]
            rawv = proj_ref[2 * width + h * D:2 * width + (h + 1) * D, lanes]

            def rotated(raw, gain):
                inv = lax.rsqrt(jnp.mean(raw * raw, axis=0, keepdims=True) + EPSILON)
                n = raw * inv * gain
                a, c = n[:HALF], n[HALF:]
                return inv, jnp.concatenate([a * cos - c * sin, c * cos + a * sin], axis=0)

            iq, q = rotated(rawq, gq)
            ik, k = rotated(rawk, gk)
            inv_ref[2 * h:2 * h + 1, lanes] = iq
            inv_ref[2 * h + 1:2 * h + 2, lanes] = ik
            q = (q * (D ** -0.5)).astype(BF16)
            kt_ref[h, :, lanes] = k.astype(BF16)
            extra = jnp.concatenate([pen, jnp.zeros((8, tok), F32)], axis=0).astype(BF16)
            qa_ref[h, :, lanes] = jnp.concatenate([q, extra], axis=0)
            full = jnp.concatenate([k, hot, ones8, jnp.zeros((48, tok), F32)], axis=0)
            ka_ref[h, lanes, :] = jnp.transpose(full).astype(BF16)
            vt_ref[h, :, lanes] = jnp.concatenate([rawv, one_row], axis=0).astype(BF16)
        return 0

    lax.fori_loop(0, blocks, prepare, 0)

    causal = (lax.broadcasted_iota(jnp.int32, (BLOCK, BLOCK), 0)
              <= lax.broadcasted_iota(jnp.int32, (BLOCK, BLOCK), 1))

    def query_block(i, _):
        cols = pl.ds(pl.multiple_of(i * BLOCK, BLOCK), BLOCK)

        def step(j, accs, diagonal):
            rows = pl.ds(pl.multiple_of(j * BLOCK, BLOCK), BLOCK)
            new = []
            for h in range(heads):
                s = dot(ka_ref[h, rows, 0:80], qa_ref[h, :, cols])
                p = jnp.exp(s)
                if diagonal:
                    p = jnp.where(causal, p, 0.0)
                new.append(accs[h] + dot(vt_ref[h, :, rows], p.astype(BF16)))
            return tuple(new)

        accs = tuple(jnp.zeros((80, BLOCK), F32) for _ in range(heads))
        accs = lax.fori_loop(0, i, lambda j, c: step(j, c, False), accs)
        accs = step(i, accs, True)
        outs = []
        for h in range(heads):
            total = accs[h][D:D + 1]
            o = accs[h][:D] * (1.0 / total)
            o_ref[h, :, cols] = o
            outs.append(o)
            pieces = split3(-jnp.log(total))
            old = qa_ref[h, 64:80, cols].astype(F32)
            row = lax.broadcasted_iota(jnp.int32, (16, BLOCK), 0)
            extra = jnp.where(row == 8, pieces[0],
                              jnp.where(row == 9, pieces[1], jnp.where(row == 10, pieces[2], old)))
            qa_ref[h, 64:80, cols] = extra.astype(BF16)
        merged_ref[cols, :] = jnp.transpose(jnp.concatenate(outs, axis=0)).astype(BF16)
        return 0

    lax.fori_loop(0, length // BLOCK, query_block, 0)


def attention_backward_kernel(heads, proj_ref, table_ref, gq_ref, gk_ref, dm_ref,
                              o_ref, qa_ref, ka_ref, kt_ref, vt_ref, inv_ref,
                              pg_ref, gains_ref, doa_ref, q_ref, va_ref, dq_ref, dk_ref, dv_ref):
    blocks, _, tok = table_ref.shape
    length = blocks * tok
    width = heads * D
    gq = gq_ref[...]
    gk = gk_ref[...]

    def prepare(b, _):
        lanes = pl.ds(pl.multiple_of(b * tok, tok), tok)
        dmt = jnp.transpose(dm_ref[lanes, :].astype(F32))
        row = lax.broadcasted_iota(jnp.int32, (16, tok), 0)
        for h in range(heads):
            do = dmt[h * D:(h + 1) * D]
            delta = jnp.sum(do * o_ref[h, :, lanes], axis=0, keepdims=True)
            pieces = split3(-delta)
            extra = jnp.where(row == 0, pieces[0],
                              jnp.where(row == 1, pieces[1], jnp.where(row == 2, pieces[2], 0.0)))
            doa_ref[h, :, lanes] = jnp.concatenate([do, extra], axis=0).astype(BF16)
            qk = jnp.concatenate([qa_ref[h, 0:D, lanes].astype(F32), vt_ref[h, 0:D, lanes].astype(F32)], axis=0)
            back = jnp.transpose(qk)
            q_ref[h, lanes, :] = back[:, :D].astype(BF16)
            va_ref[h, lanes, :] = jnp.concatenate(
                [back[:, D:], jnp.ones((tok, 16), F32)], axis=1).astype(BF16)
            dq_ref[h, :, lanes] = jnp.zeros((D, tok), F32)
        return 0

    lax.fori_loop(0, blocks, prepare, 0)

    causal = (lax.broadcasted_iota(jnp.int32, (BLOCK, BLOCK), 0)
              <= lax.broadcasted_iota(jnp.int32, (BLOCK, BLOCK), 1))
    count = length // BLOCK

    def key_block(j, _):
        rows = pl.ds(pl.multiple_of(j * BLOCK, BLOCK), BLOCK)

        def step(i, accs, diagonal):
            cols = pl.ds(pl.multiple_of(i * BLOCK, BLOCK), BLOCK)
            new = []
            for h in range(heads):
                p = jnp.exp(dot(ka_ref[h, rows, 0:80], qa_ref[h, :, cols]))
                if diagonal:
                    p = jnp.where(causal, p, 0.0)
                dp = dot(va_ref[h, rows, :], doa_ref[h, :, cols])
                ds = (p * dp).astype(BF16)
                do = dm_ref[cols, h * D:(h + 1) * D]
                dv = accs[2 * h] + dot(p.astype(BF16), do)
                dk = accs[2 * h + 1] + dot(ds, q_ref[h, cols, :])
                dq_ref[h, :, cols] += dot(kt_ref[h, :, rows], ds)
                new += [dv, dk]
            return tuple(new)

        accs = tuple(jnp.zeros((BLOCK, D), F32) for _ in range(2 * heads))
        accs = step(j, accs, True)
        accs = lax.fori_loop(j + 1, count, lambda i, c: step(i, c, False), accs)
        for h in range(heads):
            both = jnp.transpose(jnp.concatenate([accs[2 * h], accs[2 * h + 1]], axis=1))
            dv_ref[h, :, rows] = both[:D]
            dk_ref[h, :, rows] = both[D:]
        return 0

    lax.fori_loop(0, count, key_block, 0)

    def finish(b, sums):
        lanes = pl.ds(pl.multiple_of(b * tok, tok), tok)
        cos = table_ref[b, 0:HALF, :]
        sin = table_ref[b, HALF:D, :]

        def back(grad, raw, inv, gain):
            a, c = grad[:HALF], grad[HALF:]
            n = jnp.concatenate([a * cos + c * sin, c * cos - a * sin], axis=0)
            v = n * gain
            out = inv * v - raw * (inv * inv * inv) * jnp.mean(v * raw, axis=0, keepdims=True)
            return out, n * raw * inv

        sum_q, sum_k = sums
        for h in range(heads):
            rawq = proj_ref[h * D:(h + 1) * D, lanes]
            rawk = proj_ref[width + h * D:width + (h + 1) * D, lanes]
            out_q, part_q = back(dq_ref[h, :, lanes] * (D ** -0.5), rawq, inv_ref[2 * h:2 * h + 1, lanes], gq)
            out_k, part_k = back(dk_ref[h, :, lanes], rawk, inv_ref[2 * h + 1:2 * h + 2, lanes], gk)
            pg_ref[h * D:(h + 1) * D, lanes] = out_q.astype(BF16)
            pg_ref[width + h * D:width + (h + 1) * D, lanes] = out_k.astype(BF16)
            pg_ref[2 * width + h * D:2 * width + (h + 1) * D, lanes] = dv_ref[h, :, lanes].astype(BF16)
            sum_q = sum_q + part_q
            sum_k = sum_k + part_k
        return sum_q, sum_k

    zero = jnp.zeros((D, tok), F32)
    sum_q, sum_k = lax.fori_loop(0, blocks, finish, (zero, zero))
    total = jnp.concatenate([jnp.sum(sum_q, axis=1, keepdims=True), jnp.sum(sum_k, axis=1, keepdims=True)], axis=0)
    gains_ref[...] = jnp.broadcast_to(total, gains_ref.shape)


def attention_forward(heads, proj, table, gq, gk):
    length = proj.shape[1]
    return pl.pallas_call(
        functools.partial(attention_forward_kernel, heads),
        out_shape=(
            jax.ShapeDtypeStruct((length, heads * D), BF16),
            jax.ShapeDtypeStruct((heads, D, length), F32),
            jax.ShapeDtypeStruct((heads, 80, length), BF16),
            jax.ShapeDtypeStruct((heads, length, 128), BF16),
            jax.ShapeDtypeStruct((heads, D, length), BF16),
            jax.ShapeDtypeStruct((heads, 80, length), BF16),
            jax.ShapeDtypeStruct((8, length), F32),
        ),
        compiler_params=pltpu.CompilerParams(vmem_limit_bytes=VMEM_LIMIT),
        cost_estimate=pl.CostEstimate(flops=4 * heads * 64 * length * length, bytes_accessed=16 << 20, transcendentals=heads * length * length // 2),
    )(proj, table, gq, gk)


def attention_backward(heads, proj, table, gq, gk, dm, kept):
    length = proj.shape[1]
    return pl.pallas_call(
        functools.partial(attention_backward_kernel, heads),
        out_shape=(
            jax.ShapeDtypeStruct((3 * heads * D, length), BF16),
            jax.ShapeDtypeStruct((2 * D, 128), F32),
        ),
        scratch_shapes=[
            pltpu.VMEM((heads, 80, length), BF16),
            pltpu.VMEM((heads, length, D), BF16),
            pltpu.VMEM((heads, length, 80), BF16),
            pltpu.VMEM((heads, D, length), F32),
            pltpu.VMEM((heads, D, length), F32),
            pltpu.VMEM((heads, D, length), F32),
        ],
        compiler_params=pltpu.CompilerParams(vmem_limit_bytes=VMEM_LIMIT),
        cost_estimate=pl.CostEstimate(flops=10 * heads * 64 * length * length, bytes_accessed=16 << 20, transcendentals=heads * length * length // 2),
    )(proj, table, gq, gk, dm, *kept)


MESH = pl.DeviceIdType.MESH


class Place:
    def __init__(self):
        self.row = lax.axis_index("rows")
        self.me = lax.axis_index("seq")
        self.core = lax.rem(self.me, 2)
        self.chip = self.me // 2
        self.sib = self.me + 1 - 2 * self.core
        chip = self.chip
        self.chips = (chip, chip + 1 - 2 * lax.rem(chip, 2), lax.rem(chip + 2, 4), 3 - chip)
        self.same = tuple(2 * q + self.core for q in self.chips)

    def greet(self):
        barrier = pltpu.get_barrier_semaphore()
        for other in (self.sib, self.same[1], self.same[2]):
            pl.semaphore_signal(barrier, inc=1, device_id=(self.row, other), device_id_type=MESH)
        pl.semaphore_wait(barrier, 3)

    def send(self, src, dst, send_sem, recv_sem, slot, target):
        return pltpu.make_async_remote_copy(
            src_ref=src, dst_ref=dst, send_sem=send_sem.at[slot], recv_sem=recv_sem.at[slot],
            device_id=(self.row, target), device_id_type=MESH)


GATHER_SLOTS = 10


class Gather:
    def __init__(self, place, every, send_sem, recv_sem):
        half = every.shape[1] // 2
        low = lambda b: every.at[b, 0:half]
        high = lambda b: every.at[b, half:2 * half]
        whole = lambda b: every.at[b]
        send = lambda part, b, slot, target: place.send(part(b), part(b), send_sem, recv_sem, slot, target)
        me, (_, s1, s2, s3), sib = place.me, place.same, place.sib
        self.copies = (
            send(whole, me, 0, sib),
            send(low, me, 1, s1), send(high, me, 2, s1),
            send(high, me, 3, s2), send(low, me, 4, s2),
            send(low, s1, 5, s2), send(high, s2, 6, s1),
            send(whole, s1, 7, sib), send(whole, s2, 8, sib), send(whole, s3, 9, sib),
        )

    def start(self):
        for slot in (1, 3, 2, 4, 0):
            self.copies[slot].start()

    def own_chip(self):
        self.copies[0].wait_recv()

    def neighbours(self):
        c = self.copies
        c[1].wait_recv()
        c[5].start()
        c[3].wait_recv()
        c[6].start()
        c[2].wait_recv()
        c[7].start()
        c[4].wait_recv()
        c[8].start()

    def chip1(self):
        self.copies[7].wait_recv()

    def chip2(self):
        self.copies[8].wait_recv()

    def diagonal(self):
        c = self.copies
        c[5].wait_recv()
        c[6].wait_recv()
        c[9].start()

    def chip3(self):
        self.copies[9].wait_recv()

    def close(self):
        for copy in self.copies:
            copy.wait_send()


SCATTER_SLOTS = 10


class Scatter:
    def __init__(self, place, part, sibling, passing, final, send_sem, recv_sem):
        self.place, self.part, self.sibling, self.passing, self.final = place, part, sibling, passing, final
        half = part.shape[2] // 2
        self.half = half
        core, other = place.core, 1 - place.core
        _, s1, s2, _ = place.same
        send = lambda src, dst, slot, target: place.send(src, dst, send_sem, recv_sem, slot, target)
        low, high = slice(0, half), slice(half, 2 * half)
        self.exchange = tuple(send(part.at[k, other], sibling.at[k], k, place.sib) for k in range(4))
        self.pass1 = send(part.at[3, core, low], passing.at[0], 4, s1)
        self.pass2 = send(part.at[3, core, high], passing.at[1], 5, s2)
        self.first1 = send(part.at[1, core, low], final.at[0, low], 6, s1)
        self.second1 = send(part.at[1, core, high], final.at[0, high], 7, s1)
        self.first2 = send(part.at[2, core, high], final.at[1, high], 8, s2)
        self.second2 = send(part.at[2, core, low], final.at[1, low], 9, s2)

    def add(self, k, start, size, term, offset):
        core, step = self.place.core, 64

        def one(i, _):
            rows = pl.ds(pl.multiple_of(start + i * step, step), step)
            from_rows = pl.ds(pl.multiple_of(offset + i * step, step), step)
            total = self.part[k, core, rows, :].astype(F32) + term[from_rows, :].astype(F32)
            self.part[k, core, rows, :] = total.astype(BF16)
            return 0

        lax.fori_loop(0, size // step, one, 0)

    def combine(self, k):
        self.exchange[k].wait_recv()
        self.add(k, 0, 2 * self.half, self.sibling.at[k], 0)

    def finish_two(self):
        self.pass1.wait_recv()
        self.add(2, 0, self.half, self.passing.at[0], 0)
        self.second2.start()
        self.pass2.wait_recv()
        self.add(1, self.half, self.half, self.passing.at[1], 0)
        self.second1.start()

    def arrive(self):
        for copy in (self.first1, self.second1, self.first2, self.second2):
            copy.wait_recv()

    def total(self, rows):
        return (self.part[0, self.place.core, rows, :].astype(F32) + self.final[0, rows, :].astype(F32)
                + self.final[1, rows, :].astype(F32))

    def close(self):
        for copy in self.exchange + (self.pass1, self.pass2, self.first1, self.second1, self.first2, self.second2):
            copy.wait_send()


def scatter_scratch(tok, width):
    return [
        pltpu.VMEM((4, 2, tok, width), BF16),
        pltpu.VMEM((4, tok, width), BF16),
        pltpu.VMEM((2, tok // 2, width), BF16),
        pltpu.VMEM((2, tok, width), BF16),
        pltpu.SemaphoreType.DMA((SCATTER_SLOTS,)),
        pltpu.SemaphoreType.DMA((SCATTER_SLOTS,)),
    ]


def ffn_kernel(res_ref, gain_ref, g_hbm, gate_hbm, up_hbm, down_hbm,
               out_hbm, rgrad_ref, branch_ref, gain_grad_ref, gate_grad_hbm, up_grad_hbm, down_grad_hbm,
               two_ref, g_ref, gate_ref, up_ref, down_ref, hid_ref, gu_ref, stage_ref, wstage_ref,
               part_ref, sibling_ref, passing_ref, final_ref, rs_send, rs_recv,
               ag_send, ag_recv, load_sem, stage_sem, wstage_sem):
    place = Place()
    _, tok, model = g_ref.shape
    ff = gate_ref.shape[1]
    tile = 256
    loads = [pltpu.make_async_copy(src, dst, load_sem.at[i]) for i, (src, dst) in enumerate(
        ((gate_hbm, gate_ref), (up_hbm, up_ref), (g_hbm, g_ref), (down_hbm, down_ref)))]
    for copy in loads:
        copy.start()

    def norm_rows(i, _):
        rows = pl.ds(pl.multiple_of(i * 32, 32), 32)
        res = res_ref[rows, :]
        inv = lax.rsqrt(jnp.mean(res * res, axis=-1, keepdims=True) + EPSILON)
        two_ref[place.me, rows, :] = (res * inv * gain_ref[...]).astype(BF16)
        return 0

    lax.fori_loop(0, tok // 32, norm_rows, 0)
    place.greet()
    gather = Gather(place, two_ref, ag_send, ag_recv)
    scatter = Scatter(place, part_ref, sibling_ref, passing_ref, final_ref, rs_send, rs_recv)
    gather.start()
    for copy in loads:
        copy.wait()

    def stage_copy(k):
        m = place.chips[k]
        return pltpu.make_async_copy(stage_ref.at[k % 2], out_hbm.at[pl.ds(2 * m, 2)], stage_sem.at[k % 2])

    def compute(k):
        m = place.chips[k]
        pair = pl.ds(2 * m, 2)

        def hidden_tile(h, _):
            cols = pl.ds(pl.multiple_of(h * tile, tile), tile)
            cols2 = pl.ds(pl.multiple_of(ff + h * tile, tile), tile)
            x = two_ref[pair].reshape(2 * tok, model)
            gate = dot(x, gate_ref[:, cols])
            up = dot(x, up_ref[:, cols])
            back = dot_nt(g_ref[pair].reshape(2 * tok, model), down_ref[cols, :])
            s = 1.0 / (1.0 + jnp.exp(-gate))
            act = gate * s
            hid_ref[pair, :, cols] = (act * up).astype(BF16).reshape(2, tok, tile)
            gu_ref[pair, :, cols] = (back * up * s * (1.0 + gate * (1.0 - s))).astype(BF16).reshape(2, tok, tile)
            gu_ref[pair, :, cols2] = (back * act).astype(BF16).reshape(2, tok, tile)
            return 0

        lax.fori_loop(0, ff // tile, hidden_tile, 0)
        if k >= 2:
            stage_copy(k - 2).wait()

        def model_tile(n, _):
            cols = pl.ds(pl.multiple_of(n * tile, tile), tile)
            gg = gu_ref[pair, :, 0:ff].reshape(2 * tok, ff)
            ug = gu_ref[pair, :, ff:2 * ff].reshape(2 * tok, ff)
            back = dot_nt(gg, gate_ref[cols, :]) + dot_nt(ug, up_ref[cols, :])
            part_ref[k, :, :, cols] = back.astype(BF16).reshape(2, tok, tile)
            return 0

        lax.fori_loop(0, model // tile, model_tile, 0)
        scatter.exchange[k].start()

        def out_tile(n, _):
            cols = pl.ds(pl.multiple_of(n * tile, tile), tile)
            hid = hid_ref[pair].reshape(2 * tok, ff)
            out = dot(hid, down_ref[:, cols])
            stage_ref[k % 2, :, :, cols] = out.astype(BF16).reshape(2, tok, tile)
            return 0

        lax.fori_loop(0, model // tile, out_tile, 0)
        stage_copy(k).start()

    gather.own_chip()
    compute(0)
    gather.neighbours()
    gather.chip1()
    compute(1)
    gather.chip2()
    scatter.combine(1)
    scatter.first1.start()
    compute(2)
    gather.diagonal()
    scatter.combine(2)
    scatter.first2.start()
    gather.chip3()
    compute(3)
    scatter.combine(3)
    scatter.pass1.start()
    scatter.pass2.start()
    scatter.combine(0)

    blocks = two_ref.shape[0]

    def wstage_copies(i, slot):
        rows = pl.ds(pl.multiple_of(i * tile, tile), tile)
        return (pltpu.make_async_copy(wstage_ref.at[slot, :, 0:ff], gate_grad_hbm.at[rows], wstage_sem.at[slot, 0]),
                pltpu.make_async_copy(wstage_ref.at[slot, :, ff:2 * ff], up_grad_hbm.at[rows], wstage_sem.at[slot, 1]))

    def gate_up_rows(i, _):
        cols = pl.ds(pl.multiple_of(i * tile, tile), tile)
        slot = lax.rem(i, 2)

        @pl.when(i >= 2)
        def _():
            for copy in wstage_copies(i - 2, slot):
                copy.wait()

        x = two_ref[:, :, cols].reshape(blocks * tok, tile)
        wstage_ref[slot] = dot_tn(x, gu_ref[...].reshape(blocks * tok, 2 * ff)).astype(BF16)
        for copy in wstage_copies(i, slot):
            copy.start()
        return 0

    count = model // tile
    lax.fori_loop(0, count // 2, gate_up_rows, 0)
    scatter.finish_two()
    lax.fori_loop(count // 2, count, gate_up_rows, 0)
    for i in (count - 2, count - 1):
        for copy in wstage_copies(i, i % 2):
            copy.wait()

    stage_copy(2).wait()
    stage_copy(3).wait()

    def down_rows(i, _):
        rows = pl.ds(pl.multiple_of(i * tile, tile), tile)
        h = hid_ref[:, :, rows].reshape(blocks * tok, tile)

        def down_cols(n, _):
            cols = pl.ds(pl.multiple_of(n * 512, 512), 512)
            g = g_ref[:, :, cols].reshape(blocks * tok, 512)
            stage_ref[0, i, :, cols] = dot_tn(h, g).astype(BF16)
            return 0

        lax.fori_loop(0, model // 512, down_cols, 0)
        return 0

    lax.fori_loop(0, ff // tile, down_rows, 0)
    down_out = [pltpu.make_async_copy(stage_ref.at[0, i], down_grad_hbm.at[pl.ds(i * tile, tile)], stage_sem.at[i])
                for i in range(ff // tile)]
    for copy in down_out:
        copy.start()

    scatter.arrive()

    def finish(i, sums):
        rows = pl.ds(pl.multiple_of(i * 32, 32), 32)
        res = res_ref[rows, :]
        inv = lax.rsqrt(jnp.mean(res * res, axis=-1, keepdims=True) + EPSILON)
        grad = scatter.total(rows)
        v = grad * gain_ref[...]
        mean = jnp.mean(v * res, axis=-1, keepdims=True)
        out = g_ref[place.me, rows, :].astype(F32) + inv * v - res * (inv * inv * inv * mean)
        rgrad_ref[rows, :] = out
        branch_ref[rows, :] = out.astype(BF16)
        return sums + jnp.sum(grad * res * inv, axis=0, keepdims=True)

    gain_grad_ref[...] = lax.fori_loop(0, tok // 32, finish, jnp.zeros((1, model), F32))
    for copy in down_out:
        copy.wait()
    gather.close()
    scatter.close()


def feed_forward(res, gain, g_all, gate, up, down):
    tok, model = res.shape
    ff = gate.shape[1]
    blocks = g_all.shape[0]
    any_spec = pl.BlockSpec(memory_space=pl.ANY)
    vmem = pl.BlockSpec(memory_space=pltpu.VMEM)
    return pl.pallas_call(
        ffn_kernel,
        out_shape=(
            jax.ShapeDtypeStruct((blocks, tok, model), BF16),
            jax.ShapeDtypeStruct((tok, model), F32),
            jax.ShapeDtypeStruct((tok, model), BF16),
            jax.ShapeDtypeStruct((1, model), F32),
            jax.ShapeDtypeStruct((model, ff), BF16),
            jax.ShapeDtypeStruct((model, ff), BF16),
            jax.ShapeDtypeStruct((ff, model), BF16),
        ),
        in_specs=[vmem, vmem] + [any_spec] * 4,
        out_specs=(any_spec, vmem, vmem, vmem, any_spec, any_spec, any_spec),
        scratch_shapes=[
            pltpu.VMEM((blocks, tok, model), BF16),
            pltpu.VMEM((blocks, tok, model), BF16),
            pltpu.VMEM((model, ff), BF16),
            pltpu.VMEM((model, ff), BF16),
            pltpu.VMEM((ff, model), BF16),
            pltpu.VMEM((blocks, tok, ff), BF16),
            pltpu.VMEM((blocks, tok, 2 * ff), BF16),
            pltpu.VMEM((2, 2, tok, model), BF16),
            pltpu.VMEM((2, 256, 2 * ff), BF16),
            *scatter_scratch(tok, model),
            pltpu.SemaphoreType.DMA((GATHER_SLOTS,)),
            pltpu.SemaphoreType.DMA((GATHER_SLOTS,)),
            pltpu.SemaphoreType.DMA((4,)),
            pltpu.SemaphoreType.DMA((2,)),
            pltpu.SemaphoreType.DMA((2, 2)),
        ],
        compiler_params=pltpu.CompilerParams(collective_id=3, has_side_effects=True, vmem_limit_bytes=60 * 1024 * 1024),
        cost_estimate=pl.CostEstimate(flops=18 * blocks * tok * model * ff, bytes_accessed=64 << 20, transcendentals=0),
    )(res, gain, g_all, gate, up, down)


def norm_inverse(x):
    return lax.rsqrt(jnp.mean(x * x, axis=-1, keepdims=True) + EPSILON)


def norm_back(grad_normed, values_in, inv_rms, gain):
    scaled = grad_normed * gain
    gain_grad = jnp.sum(grad_normed * values_in * inv_rms, axis=0)
    input_grad = inv_rms * scaled - values_in * inv_rms**3 * jnp.mean(scaled * values_in, axis=-1, keepdims=True)
    return input_grad, gain_grad


def feed_forward_wide(res, gain, g_blocks, gate_slab, up_slab, down_slab):
    blocks, tok, model = g_blocks.shape
    inv = norm_inverse(res)
    two_all = lax.all_gather((res * inv * gain).astype(BF16), "seq", axis=0, tiled=True)
    g_all = g_blocks.reshape(blocks * tok, model)
    gate_act = dot(two_all, gate_slab)
    up_act = dot(two_all, up_slab)
    s = jax.nn.sigmoid(gate_act)
    hidden = (gate_act * s * up_act).astype(BF16)
    hidden_grad = dot_nt(g_all, down_slab)
    gate_grad = (hidden_grad * up_act * s * (1.0 + gate_act * (1.0 - s))).astype(BF16)
    up_grad = (hidden_grad * gate_act * s).astype(BF16)
    part = (dot_nt(gate_grad, gate_slab) + dot_nt(up_grad, up_slab)).astype(BF16)
    two_grad = lax.psum_scatter(part, "seq", scatter_dimension=0, tiled=True).astype(F32)
    branch_part = dot(hidden, down_slab).astype(BF16).reshape(blocks, tok, model)
    norm_grad, gain_grad = norm_back(two_grad, res, inv, gain)
    g = lax.dynamic_index_in_dim(g_blocks, lax.axis_index("seq"), 0, keepdims=False)
    residual_grad = g.astype(F32) + norm_grad
    return (branch_part, residual_grad, residual_grad.astype(BF16), gain_grad[None],
            dot_tn(two_all, gate_grad).astype(BF16), dot_tn(two_all, up_grad).astype(BF16),
            dot_tn(hidden, g_all).astype(BF16))


def body(tokens, segments, positions, cotangent, gain_attn, w_qkv, gain_q, gain_k, w_out, gain_ffn, w_gate, w_up, w_down):
    seq = lax.axis_size("seq")
    rows = lax.axis_size("rows")
    heads = -(-QUERY_HEADS // seq)
    padded = seq * heads
    depth = w_qkv.shape[0]
    width = heads * D
    tok = tokens.shape[1]

    def spread(columns):
        return jnp.repeat(columns.reshape(depth, KEY_VALUE_HEADS, D), GROUP, axis=1)

    def slabs(columns):
        columns = columns.reshape(depth, QUERY_HEADS, D)
        columns = jnp.pad(columns, ((0, 0), (0, padded - QUERY_HEADS), (0, 0)))
        return columns.reshape(depth, seq, width)

    qw, kw = QUERY_HEADS * D, KEY_VALUE_HEADS * D
    local = jnp.concatenate([
        slabs(w_qkv[:, :qw]),
        slabs(spread(w_qkv[:, qw:qw + kw])),
        slabs(spread(w_qkv[:, qw + kw:])),
        slabs(w_out.T),
    ], axis=2).transpose(1, 0, 2)
    mine = lax.all_to_all(local, "seq", 0, 0, tiled=False)
    attn_w = lax.all_gather(mine.reshape(seq * depth, 4 * width), "rows", axis=0, tiled=True)
    qkv_slab, out_slab = attn_w[:, :3 * width], attn_w[:, 3 * width:]

    gains = lax.all_gather(jnp.stack([gain_attn, gain_ffn])[:, None], ("rows", "seq"), axis=1, tiled=True)
    gain_one = gains[0].reshape(1, -1).astype(F32)
    gain_two = gains[1].reshape(1, -1).astype(F32)
    gate_slab = lax.all_gather(w_gate, "rows", axis=0, tiled=True)
    up_slab = lax.all_gather(w_up, "rows", axis=0, tiled=True)
    down_slab = lax.all_gather(w_down, "rows", axis=1, tiled=True)
    gq = gain_q.astype(F32)[:, None]
    gk = gain_k.astype(F32)[:, None]

    x = tokens[0].astype(F32)
    inv_one = norm_inverse(x)
    normed = (x * inv_one * gain_one).astype(BF16)
    table = lax.all_gather(rotary_table(positions[0], segments[0]), "seq", axis=0, tiled=False)
    normed_all = lax.all_gather(normed, "seq", axis=0, tiled=True)
    proj = lax.dot_general(qkv_slab, normed_all, (((0,), (1,)), ((), ())), preferred_element_type=F32)
    merged, *kept = attention_forward(heads, proj, table, gq, gk)
    out_part = dot_nt(merged, out_slab).astype(BF16)
    residual = x + lax.psum_scatter(out_part, "seq", scatter_dimension=0, tiled=True).astype(F32)
    g_all = lax.all_gather(cotangent[0], "seq", axis=0, tiled=False)
    phase = feed_forward if seq == 8 else feed_forward_wide
    branch_part, residual_grad, branch_grad, gain_two_grad, gate_wgrad, up_wgrad, down_wgrad = phase(
        residual, gain_two, g_all, gate_slab, up_slab, down_slab)
    gain_two_grad = gain_two_grad[0]
    branch = lax.psum_scatter(branch_part.reshape(seq * tok, -1), "seq", scatter_dimension=0, tiled=True).astype(F32)
    layer_out = (residual + branch).astype(BF16)
    grad_gate = lax.psum_scatter(gate_wgrad, "rows", scatter_dimension=0, tiled=True).astype(F32)
    grad_up = lax.psum_scatter(up_wgrad, "rows", scatter_dimension=0, tiled=True).astype(F32)
    grad_down = lax.psum_scatter(down_wgrad, "rows", scatter_dimension=1, tiled=True).astype(F32)
    branch_all = lax.all_gather(branch_grad, "seq", axis=0, tiled=True)
    dm = dot(branch_all, out_slab).astype(BF16)
    pg, head_gains = attention_backward(heads, proj, table, gq, gk, dm, kept)
    normed_part = lax.dot_general(pg, qkv_slab, (((0,), (1,)), ((), ())), preferred_element_type=F32).astype(BF16)
    normed_grad = lax.psum_scatter(normed_part, "seq", scatter_dimension=0, tiled=True).astype(F32)
    input_norm_grad, gain_one_grad = norm_back(normed_grad, x, inv_one, gain_one)
    grad_tokens = residual_grad + input_norm_grad

    qkv_wgrad = lax.dot_general(normed_all, pg, (((0,), (1,)), ((), ())), preferred_element_type=F32)
    out_wgrad = dot_tn(branch_all, merged)
    attn_grad = jnp.concatenate([qkv_wgrad, out_wgrad], axis=1).astype(BF16)
    attn_grad = lax.psum_scatter(attn_grad, "rows", scatter_dimension=0, tiled=True)
    attn_grad = lax.all_to_all(attn_grad.reshape(seq, depth, 4 * width), "seq", 0, 0, tiled=False).astype(F32)

    def unslab(part):
        part = attn_grad[:, :, part * width:(part + 1) * width].transpose(1, 0, 2)
        return part.reshape(depth, padded, D)[:, :QUERY_HEADS]

    def unspread(part):
        return jnp.sum(unslab(part).reshape(depth, KEY_VALUE_HEADS, GROUP, D), axis=2).reshape(depth, kw)

    grad_qkv = jnp.concatenate([unslab(0).reshape(depth, qw), unspread(1), unspread(2)], axis=1)
    grad_out = unslab(3).reshape(depth, qw).T

    small = lax.psum(jnp.concatenate([gain_one_grad, gain_two_grad, head_gains[:, 0]]), ("rows", "seq"))
    model = gain_one_grad.shape[0]
    start = (lax.axis_index("rows") * seq + lax.axis_index("seq")) * depth
    return (
        layer_out[None],
        grad_tokens[None],
        lax.dynamic_slice_in_dim(small, start, depth),
        grad_qkv,
        small[2 * model:2 * model + D],
        small[2 * model + D:],
        grad_out,
        lax.dynamic_slice_in_dim(small, model + start, depth),
        grad_gate,
        grad_up,
        grad_down,
    )


def solution(mesh):
    both = ("rows", "seq")
    return jax.shard_map(
        body,
        mesh=mesh,
        in_specs=(
            P("rows", "seq", None), P("rows", "seq"), P("rows", "seq"), P("rows", "seq", None),
            P(both), P(both, None), P(), P(), P(None, both), P(both),
            P("rows", "seq"), P("rows", "seq"), P("seq", "rows"),
        ),
        out_specs=(
            P("rows", "seq", None), P("rows", "seq", None), P(both), P(both, None), P(), P(),
            P(None, both), P(both), P("rows", "seq"), P("rows", "seq"), P("seq", "rows"),
        ),
        check_vma=False,
    )
```

```python
import functools
import math

import jax
import jax.numpy as jnp
from jax import lax
from jax.experimental import pallas as pl
from jax.experimental.pallas import tpu as pltpu
from jax.sharding import PartitionSpec as P

QUERY_HEADS = 24
KEY_VALUE_HEADS = 6
GROUP = QUERY_HEADS // KEY_VALUE_HEADS
D = 64
HALF = D // 2
EPSILON = 1e-06
THETA = 10000.0
PENALTY = -10000.0
SEGMENT_KINDS = 8
TABLE_ROWS = 80
BLOCK = 512
PLANE = 8
F32 = jnp.float32
BF16 = jnp.bfloat16
VMEM_LIMIT = 60 * 1024 * 1024
MESH = pl.DeviceIdType.MESH
ANY_SPEC = pl.BlockSpec(memory_space=pl.ANY)
VMEM_SPEC = pl.BlockSpec(memory_space=pltpu.VMEM)


def dot(a, b):
    return jnp.dot(a, b, preferred_element_type=F32)


def dot_nt(a, b):
    return lax.dot_general(a, b, (((1,), (1,)), ((), ())), preferred_element_type=F32)


def dot_tn(a, b):
    return lax.dot_general(a, b, (((0,), (0,)), ((), ())), preferred_element_type=F32)


def norm_inverse(x):
    return lax.rsqrt(jnp.mean(x * x, axis=-1, keepdims=True) + EPSILON)


def split3(x):
    high = x.astype(BF16).astype(F32)
    mid = (x - high).astype(BF16).astype(F32)
    return high, mid, x - high - mid


def span(start, size):
    return pl.ds(pl.multiple_of(start, size), size)


class Heads:
    def __init__(self, seq):
        self.seq = seq
        self.queries = -(-QUERY_HEADS // seq)
        last = [min((s + 1) * self.queries, QUERY_HEADS) - 1 for s in range(seq)]
        self.pairs = max(last[s] // GROUP - self.first(s) + 1 for s in range(seq) if last[s] >= s * self.queries)
        self.wide = self.queries * D
        self.narrow = self.pairs * D
        self.qkv = self.wide + 2 * self.narrow
        self.columns = self.qkv + self.wide

    def first(self, s):
        return (s * self.queries) // GROUP

    def slot(self, s, h):
        return (s * self.queries + h) // GROUP - (s * self.queries) // GROUP


class Place:
    def __init__(self):
        self.row = lax.axis_index("rows")
        self.me = lax.axis_index("seq")
        self.core = lax.rem(self.me, 2)
        self.chip = self.me // 2
        self.sib = self.me + 1 - 2 * self.core
        chip = self.chip
        self.chips = (chip, chip + 1 - 2 * lax.rem(chip, 2), lax.rem(chip + 2, 4), 3 - chip)
        self.same = tuple(2 * q + self.core for q in self.chips)

    def greet(self):
        barrier = pltpu.get_barrier_semaphore()
        for other in (self.sib, self.same[1], self.same[2]):
            pl.semaphore_signal(barrier, inc=1, device_id=(self.row, other), device_id_type=MESH)
        pl.semaphore_wait(barrier, 3)

    def greet_all(self, rows):
        barrier = pltpu.get_barrier_semaphore()
        for j in range(1, PLANE):
            other = lax.rem(self.me + j, PLANE)
            pl.semaphore_signal(barrier, inc=1, device_id=(self.row, other), device_id_type=MESH)
        for j in range(1, rows):
            other = lax.rem(self.row + j, rows)
            pl.semaphore_signal(barrier, inc=1, device_id=(other, self.me), device_id_type=MESH)
        pl.semaphore_wait(barrier, PLANE - 1 + rows - 1)

    def send(self, src, dst, send_sem, recv_sem, slot, target):
        return pltpu.make_async_remote_copy(
            src_ref=src, dst_ref=dst, send_sem=send_sem.at[slot], recv_sem=recv_sem.at[slot],
            device_id=(self.row, target), device_id_type=MESH)


GATHER_SLOTS = 10


class Gather:
    def __init__(self, place, own, every, send_sem, recv_sem):
        half = every.shape[1] // 2
        low, high, whole = slice(0, half), slice(half, 2 * half), slice(0, 2 * half)

        def send(part, b, slot, target, src=None):
            src = every.at[b, part] if src is None else src.at[part]
            return place.send(src, every.at[b, part], send_sem, recv_sem, slot, target)

        me, (_, s1, s2, s3), sib = place.me, place.same, place.sib
        self.copies = (
            send(whole, me, 0, sib, own),
            send(low, me, 1, s1, own), send(high, me, 2, s1, own),
            send(high, me, 3, s2, own), send(low, me, 4, s2, own),
            send(low, s1, 5, s2), send(high, s2, 6, s1),
            send(whole, s1, 7, sib), send(whole, s2, 8, sib), send(whole, s3, 9, sib),
        )

    def start(self):
        for slot in (1, 3, 2, 4, 0):
            self.copies[slot].start()

    def own_chip(self):
        self.copies[0].wait_recv()

    def neighbours(self):
        c = self.copies
        c[1].wait_recv()
        c[5].start()
        c[3].wait_recv()
        c[6].start()
        c[2].wait_recv()
        c[7].start()
        c[4].wait_recv()
        c[8].start()

    def chip1(self):
        self.copies[7].wait_recv()

    def chip2(self):
        self.copies[8].wait_recv()

    def diagonal(self):
        c = self.copies
        c[5].wait_recv()
        c[6].wait_recv()
        c[9].start()

    def chip3(self):
        self.copies[9].wait_recv()

    def close(self):
        for copy in self.copies:
            copy.wait_send()


SCATTER_SLOTS = 10


class Scatter:
    def __init__(self, place, part, sibling, passing, final, send_sem, recv_sem):
        self.place, self.part, self.sibling, self.passing, self.final = place, part, sibling, passing, final
        half = part.shape[2] // 2
        self.half = half
        core, other = place.core, 1 - place.core
        _, s1, s2, _ = place.same
        send = lambda src, dst, slot, target: place.send(src, dst, send_sem, recv_sem, slot, target)
        low, high = slice(0, half), slice(half, 2 * half)
        self.exchange = tuple(send(part.at[k, other], sibling.at[k], k, place.sib) for k in range(4))
        self.pass1 = send(part.at[3, core, low], passing.at[0], 4, s1)
        self.pass2 = send(part.at[3, core, high], passing.at[1], 5, s2)
        self.first1 = send(part.at[1, core, low], final.at[0, low], 6, s1)
        self.second1 = send(part.at[1, core, high], final.at[0, high], 7, s1)
        self.first2 = send(part.at[2, core, high], final.at[1, high], 8, s2)
        self.second2 = send(part.at[2, core, low], final.at[1, low], 9, s2)

    def add(self, k, start, size, term, offset):
        core, step = self.place.core, 64

        def one(i, _):
            rows = pl.ds(pl.multiple_of(start + i * step, step), step)
            from_rows = pl.ds(pl.multiple_of(offset + i * step, step), step)
            total = self.part[k, core, rows, :].astype(F32) + term[from_rows, :].astype(F32)
            self.part[k, core, rows, :] = total.astype(BF16)
            return 0

        lax.fori_loop(0, size // step, one, 0)

    def combine(self, k):
        self.exchange[k].wait_recv()
        self.add(k, 0, 2 * self.half, self.sibling.at[k], 0)

    def finish_two(self):
        self.pass1.wait_recv()
        self.add(2, 0, self.half, self.passing.at[0], 0)
        self.second2.start()
        self.pass2.wait_recv()
        self.add(1, self.half, self.half, self.passing.at[1], 0)
        self.second1.start()

    def arrive(self):
        for copy in (self.first1, self.second1, self.first2, self.second2):
            copy.wait_recv()

    def total(self, rows):
        return (self.part[0, self.place.core, rows, :].astype(F32) + self.final[0, rows, :].astype(F32)
                + self.final[1, rows, :].astype(F32))

    def close(self):
        for copy in self.exchange + (self.pass1, self.pass2, self.first1, self.second1, self.first2, self.second2):
            copy.wait_send()


def scatter_scratch(tok, width):
    return [
        pltpu.VMEM((4, 2, tok, width), BF16),
        pltpu.VMEM((4, tok, width), BF16),
        pltpu.VMEM((2, tok // 2, width), BF16),
        pltpu.VMEM((2, tok, width), BF16),
        pltpu.SemaphoreType.DMA((SCATTER_SLOTS,)),
        pltpu.SemaphoreType.DMA((SCATTER_SLOTS,)),
    ]


def start_kernel(x_hbm, table_hbm, pieces_hbm, gain_hbm, x_all, table_all, w_all, gain_all,
                 x_send, x_recv, t_send, t_recv, p_send, p_recv, g_send, g_recv, z_send, z_recv, local_sem):
    place = Place()
    rows = w_all.shape[0]
    me, row = place.me, place.row
    local = [pltpu.make_async_copy(src, dst, local_sem.at[i]) for i, (src, dst) in enumerate((
        (pieces_hbm.at[me], w_all.at[row, me]), (gain_hbm, gain_all.at[row, me]),
        (x_hbm, x_all.at[me]), (table_hbm, table_all.at[me])))]
    for copy in local:
        copy.start()
    place.greet_all(rows)
    exchange = []
    for j in range(1, PLANE):
        other = lax.rem(me + j, PLANE)
        exchange.append(place.send(pieces_hbm.at[other], w_all.at[row, me], p_send, p_recv, j, other))
        exchange.append(place.send(gain_hbm, gain_all.at[row, me], g_send, g_recv, j, other))
    for copy in exchange:
        copy.start()
    gathers = (Gather(place, x_hbm, x_all, x_send, x_recv), Gather(place, table_hbm, table_all, t_send, t_recv))
    gathers[1].start()
    gathers[0].start()
    for copy in local[:2]:
        copy.wait()
    for copy in exchange:
        copy.wait_recv()
    along = []
    for j in range(1, rows):
        other = lax.rem(row + j, rows)
        for i, every in enumerate((w_all, gain_all)):
            along.append(pltpu.make_async_remote_copy(
                src_ref=every.at[row], dst_ref=every.at[row], send_sem=z_send.at[2 * j + i], recv_sem=z_recv.at[2 * j + i],
                device_id=(other, me), device_id_type=MESH))
    for copy in along:
        copy.start()
    for name in ("own_chip", "neighbours", "chip1", "chip2", "diagonal", "chip3"):
        for gather in gathers[::-1]:
            getattr(gather, name)()
    for copy in local[2:]:
        copy.wait()
    for copy in along:
        copy.wait_recv()
    for copy in exchange + along:
        copy.wait_send()
    for gather in gathers:
        gather.close()


def start_phase(rows, x, table, pieces, gain):
    tok, model = x.shape
    dma = pltpu.SemaphoreType.DMA
    return pl.pallas_call(
        start_kernel,
        out_shape=(
            jax.ShapeDtypeStruct((PLANE, tok, model), BF16),
            jax.ShapeDtypeStruct((PLANE,) + table.shape, F32),
            jax.ShapeDtypeStruct((rows,) + pieces.shape, BF16),
            jax.ShapeDtypeStruct((rows, PLANE) + gain.shape, F32),
        ),
        in_specs=[ANY_SPEC] * 4,
        out_specs=(ANY_SPEC,) * 4,
        scratch_shapes=[dma((GATHER_SLOTS,))] * 4 + [dma((PLANE,))] * 4 + [dma((2 * rows,))] * 2 + [dma((4,))],
        compiler_params=pltpu.CompilerParams(collective_id=0, has_side_effects=True),
        cost_estimate=pl.CostEstimate(flops=0, bytes_accessed=160 << 20, transcendentals=0),
    )(x, table, pieces, gain)


class Forward:
    def __init__(self, heads, me, table, gq, gk, raw, merged, o, qa, ka, kt, vt, inv):
        self.heads, self.table, self.gq, self.gk = heads, table, gq[...], gk[...]
        self.raw, self.merged, self.o, self.qa, self.ka, self.kt, self.vt, self.inv = raw, merged, o, qa, ka, kt, vt, inv
        self.slots = [heads.slot(me, h) for h in range(heads.queries)]

    def prepare(self, b, projected):
        heads = self.heads
        tok = self.table.shape[2]
        lanes = span(b * tok, tok)
        cos = self.table[b, 0:HALF, :]
        sin = self.table[b, HALF:D, :]
        hot = self.table[b, D:D + 8, :]
        row = lax.broadcasted_iota(jnp.int32, (16, tok), 0)
        one_row = jnp.where(row == 0, 1.0, 0.0).astype(F32)
        penalty = jnp.concatenate([(1.0 - hot) * PENALTY, jnp.zeros((8, tok), F32)], axis=0).astype(BF16)
        self.raw[:, lanes] = projected[:heads.wide + heads.narrow]

        def rotated(raw, gain):
            inv = lax.rsqrt(jnp.mean(raw * raw, axis=0, keepdims=True) + EPSILON)
            n = raw * inv * gain
            a, c = n[:HALF], n[HALF:]
            return inv, jnp.concatenate([a * cos - c * sin, c * cos + a * sin], axis=0)

        for h in range(heads.queries):
            inv, q = rotated(projected[h * D:(h + 1) * D], self.gq)
            self.inv[h:h + 1, lanes] = inv
            self.qa[h, :, lanes] = jnp.concatenate([(q * (D ** -0.5)).astype(BF16), penalty], axis=0)
        for g in range(heads.pairs):
            start = heads.wide + g * D
            inv, k = rotated(projected[start:start + D], self.gk)
            self.inv[heads.queries + g:heads.queries + g + 1, lanes] = inv
            self.kt[g, :, lanes] = k.astype(BF16)
            full = jnp.concatenate([k, hot, jnp.ones((8, tok), F32), jnp.zeros((48, tok), F32)], axis=0)
            self.ka[g, lanes, :] = jnp.transpose(full).astype(BF16)
            start += heads.narrow
            self.vt[g, :, lanes] = jnp.concatenate([projected[start:start + D], one_row], axis=0).astype(BF16)

    def query_block(self, i):
        heads = self.heads
        cols = span(i * BLOCK, BLOCK)
        causal = (lax.broadcasted_iota(jnp.int32, (BLOCK, BLOCK), 0)
                  <= lax.broadcasted_iota(jnp.int32, (BLOCK, BLOCK), 1))

        def step(j, accs, diagonal):
            rows = span(j * BLOCK, BLOCK)
            new = []
            for h in range(heads.queries):
                slot = self.slots[h]
                p = jnp.exp(dot(self.ka[slot, rows, 0:80], self.qa[h, :, cols]))
                if diagonal:
                    p = jnp.where(causal, p, 0.0)
                new.append(accs[h] + dot(self.vt[slot, :, rows], p.astype(BF16)))
            return tuple(new)

        accs = tuple(jnp.zeros((80, BLOCK), F32) for _ in range(heads.queries))
        accs = lax.fori_loop(0, i, lambda j, c: step(j, c, False), accs)
        accs = step(i, accs, True)
        row = lax.broadcasted_iota(jnp.int32, (16, BLOCK), 0)
        lead = self.merged.shape[1] - heads.wide
        outs = [jnp.zeros((lead, BLOCK), F32)] if lead else []
        for h in range(heads.queries):
            total = accs[h][D:D + 1]
            o = accs[h][:D] * (1.0 / total)
            self.o[h, :, cols] = o
            outs.append(o)
            pieces = split3(-jnp.log(total))
            old = self.qa[h, 64:80, cols].astype(F32)
            extra = jnp.where(row == 8, pieces[0],
                              jnp.where(row == 9, pieces[1], jnp.where(row == 10, pieces[2], old)))
            self.qa[h, 64:80, cols] = extra.astype(BF16)
        merged = jnp.transpose(jnp.concatenate(outs, axis=0)).astype(BF16)
        self.merged[cols, :] = merged
        return merged


class Backward:
    def __init__(self, heads, me, table, gq, gk, raw, o, qa, ka, kt, vt, inv, doa, dopad, qpad, va, dq, acc):
        self.heads, self.table, self.gq, self.gk = heads, table, gq[...], gk[...]
        self.raw, self.o, self.qa, self.ka, self.kt, self.vt, self.inv = raw, o, qa, ka, kt, vt, inv
        self.doa, self.dopad, self.qpad, self.va, self.dq, self.acc = doa, dopad, qpad, va, dq, acc
        self.slots = [heads.slot(me, h) for h in range(heads.queries)]

    def prepare(self, b):
        heads = self.heads
        tok = self.table.shape[2]
        lanes = span(b * tok, tok)
        for h in range(heads.queries):
            q = jnp.concatenate([jnp.zeros((D, tok), F32), self.qa[h, 0:D, lanes].astype(F32)], axis=0)
            self.qpad[h, lanes, :] = jnp.transpose(q).astype(BF16)
            self.acc[h, lanes, :] = jnp.zeros((tok, 2 * D), F32)
        for g in range(heads.pairs):
            v = jnp.concatenate([self.vt[g, 0:D, lanes].astype(F32), jnp.ones((D, tok), F32)], axis=0)
            self.va[g, lanes, :] = jnp.transpose(v).astype(BF16)

    def gradient(self, b, dm):
        heads = self.heads
        tok = self.table.shape[2]
        lanes = span(b * tok, tok)
        row = lax.broadcasted_iota(jnp.int32, (16, tok), 0)
        dmt = jnp.transpose(dm.astype(BF16).astype(F32))
        for h in range(heads.queries):
            do = dmt[h * D:(h + 1) * D]
            delta = jnp.sum(do * self.o[h, :, lanes], axis=0, keepdims=True)
            pieces = split3(-delta)
            extra = jnp.where(row == 0, pieces[0],
                              jnp.where(row == 1, pieces[1], jnp.where(row == 2, pieces[2], 0.0)))
            self.doa[h, :, lanes] = jnp.concatenate([do, extra], axis=0).astype(BF16)
            both = jnp.concatenate([do, jnp.zeros((D, tok), F32)], axis=0)
            self.dopad[h, lanes, :] = jnp.transpose(both).astype(BF16)

    def query_block(self, i):
        heads = self.heads
        cols = span(i * BLOCK, BLOCK)
        causal = (lax.broadcasted_iota(jnp.int32, (BLOCK, BLOCK), 0)
                  <= lax.broadcasted_iota(jnp.int32, (BLOCK, BLOCK), 1))

        def step(j, accs, diagonal):
            rows = span(j * BLOCK, BLOCK)
            new = []
            for h in range(heads.queries):
                slot = self.slots[h]
                p = jnp.exp(dot(self.ka[slot, rows, 0:80], self.qa[h, :, cols]))
                if diagonal:
                    p = jnp.where(causal, p, 0.0)
                dp = dot(self.va[slot, rows, 0:80], self.doa[h, :, cols])
                ds = (p * dp).astype(BF16)
                self.acc[h, rows, :] += dot(p.astype(BF16), self.dopad[h, cols, :]) + dot(ds, self.qpad[h, cols, :])
                new.append(accs[h] + dot(self.kt[slot, :, rows], ds))
            return tuple(new)

        accs = tuple(jnp.zeros((D, BLOCK), F32) for _ in range(heads.queries))
        accs = lax.fori_loop(0, i, lambda j, c: step(j, c, False), accs)
        accs = step(i, accs, True)
        for h in range(heads.queries):
            self.dq[h, :, cols] = accs[h]

    def finish(self, b, sums):
        heads = self.heads
        tok = self.table.shape[2]
        lanes = span(b * tok, tok)
        cos = self.table[b, 0:HALF, :]
        sin = self.table[b, HALF:D, :]
        scale = self.table[b, 72:73, :]

        def back(grad, raw, inv, gain):
            a, c = grad[:HALF], grad[HALF:]
            n = jnp.concatenate([a * cos + c * sin, c * cos - a * sin], axis=0)
            v = n * gain
            out = inv * v - raw * (inv * inv * inv) * jnp.mean(v * raw, axis=0, keepdims=True)
            return out * scale, n * raw * inv

        sum_q, sum_k = sums
        pairs = [jnp.zeros((2 * D, tok), F32) for _ in range(heads.pairs)]
        out = []
        for h in range(heads.queries):
            raw = self.raw[h * D:(h + 1) * D, lanes]
            grad, part = back(self.dq[h, :, lanes] * (D ** -0.5), raw, self.inv[h:h + 1, lanes], self.gq)
            out.append(grad)
            sum_q = sum_q + part
            both = jnp.transpose(self.acc[h, lanes, :])
            for g in range(heads.pairs):
                pairs[g] = pairs[g] + jnp.where(self.slots[h] == g, both, 0.0)
        for g in range(heads.pairs):
            start = heads.wide + g * D
            raw = self.raw[start:start + D, lanes]
            inv = self.inv[heads.queries + g:heads.queries + g + 1, lanes]
            grad, part = back(pairs[g][D:], raw, inv, self.gk)
            out.append(grad)
            sum_k = sum_k + part
        for g in range(heads.pairs):
            out.append(pairs[g][:D] * scale)
        return jnp.concatenate(out, axis=0), (sum_q, sum_k)


def kept_shapes(heads, length, lead):
    return (
        jax.ShapeDtypeStruct((heads.wide + heads.narrow, length), F32),
        jax.ShapeDtypeStruct((length, lead + heads.wide), BF16),
        jax.ShapeDtypeStruct((heads.queries, D, length), F32),
        jax.ShapeDtypeStruct((heads.queries, 80, length), BF16),
        jax.ShapeDtypeStruct((heads.pairs, length, 128), BF16),
        jax.ShapeDtypeStruct((heads.pairs, D, length), BF16),
        jax.ShapeDtypeStruct((heads.pairs, 80, length), BF16),
        jax.ShapeDtypeStruct((8, length), F32),
    )


def backward_scratch(heads, length):
    return [
        pltpu.VMEM((heads.queries, 80, length), BF16),
        pltpu.VMEM((heads.queries, length, 2 * D), BF16),
        pltpu.VMEM((heads.queries, length, 2 * D), BF16),
        pltpu.VMEM((heads.pairs, length, 2 * D), BF16),
        pltpu.VMEM((heads.queries, D, length), F32),
        pltpu.VMEM((heads.queries, length, 2 * D), F32),
    ]


def local_forward_kernel(heads, proj_ref, table_ref, gq_ref, gk_ref, *kept):
    forward = Forward(heads, lax.axis_index("seq"), table_ref, gq_ref, gk_ref, *kept)
    blocks, _, tok = table_ref.shape

    def prepare(b, _):
        rows = span(b * tok, tok)
        forward.prepare(b, jnp.transpose(proj_ref[rows, :]) * table_ref[b, 72:73, :])
        return 0

    def query_block(i, _):
        forward.query_block(i)
        return 0

    lax.fori_loop(0, blocks, prepare, 0)
    lax.fori_loop(0, blocks * tok // BLOCK, query_block, 0)


def local_backward_kernel(heads, dm_ref, table_ref, gq_ref, gk_ref, raw_ref, o_ref, qa_ref, ka_ref, kt_ref, vt_ref, inv_ref,
                          pg_ref, gains_ref, *scratch):
    backward = Backward(heads, lax.axis_index("seq"), table_ref, gq_ref, gk_ref, raw_ref, o_ref, qa_ref, ka_ref, kt_ref,
                        vt_ref, inv_ref, *scratch)
    blocks, _, tok = table_ref.shape

    def prepare(b, _):
        backward.prepare(b)
        backward.gradient(b, dm_ref[span(b * tok, tok), :])
        return 0

    def query_block(i, _):
        backward.query_block(i)
        return 0

    def finish(b, sums):
        grad, sums = backward.finish(b, sums)
        pg_ref[span(b * tok, tok), :] = jnp.transpose(grad).astype(BF16)
        return sums

    lax.fori_loop(0, blocks, prepare, 0)
    lax.fori_loop(0, blocks * tok // BLOCK, query_block, 0)
    zero = jnp.zeros((D, tok), F32)
    sum_q, sum_k = lax.fori_loop(0, blocks, finish, (zero, zero))
    gains_ref[0:D, :] = jnp.broadcast_to(jnp.sum(sum_q, axis=1, keepdims=True), (D, 128))
    gains_ref[D:2 * D, :] = jnp.broadcast_to(jnp.sum(sum_k, axis=1, keepdims=True), (D, 128))


def attention_kernel(heads, x_hbm, g_hbm, w_hbm, table_ref, gq_ref, gk_ref,
                     res_ref, g_all, raw_ref, merged_ref, o_ref, qa_ref, ka_ref, kt_ref, vt_ref, inv_ref,
                     x_ref, w_ref, part_ref, sibling_ref, passing_ref, final_ref, rs_send, rs_recv,
                     ag_send, ag_recv, load_sem):
    place = Place()
    blocks, tok, model = x_ref.shape
    load_w = pltpu.make_async_copy(w_hbm, w_ref, load_sem.at[blocks])
    load_w.start()
    loads = [pltpu.make_async_copy(x_hbm.at[b], x_ref.at[b], load_sem.at[b]) for b in range(blocks)]
    for copy in loads:
        copy.start()
    keep_own = pltpu.make_async_copy(g_hbm, g_all.at[place.me], load_sem.at[blocks + 1])
    keep_own.start()
    place.greet()
    gather = Gather(place, g_hbm, g_all, ag_send, ag_recv)
    scatter = Scatter(place, part_ref, sibling_ref, passing_ref, final_ref, rs_send, rs_recv)
    gather.start()
    forward = Forward(heads, place.me, table_ref, gq_ref, gk_ref, raw_ref, merged_ref, o_ref, qa_ref, ka_ref, kt_ref,
                      vt_ref, inv_ref)
    load_w.wait()
    for copy in loads:
        copy.wait()

    def prepare(b, _):
        proj = dot(x_ref[b], w_ref[:, 0:512])
        forward.prepare(b, jnp.transpose(proj) * table_ref[b, 72:73, :])
        return 0

    lax.fori_loop(0, blocks, prepare, 0)
    tile = 512

    def compute(k):
        merged = forward.query_block(place.chips[k])

        def model_tile(n, _):
            cols = span(n * tile, tile)
            out = dot_nt(merged_ref[span(place.chips[k] * BLOCK, BLOCK), :], w_ref[cols, 384:640])
            part_ref[k, :, :, cols] = out.astype(BF16).reshape(2, tok, tile)
            return 0

        lax.fori_loop(0, model // tile, model_tile, 0)
        scatter.exchange[k].start()

    compute(3)
    gather.own_chip()
    gather.neighbours()
    scatter.combine(3)
    scatter.pass1.start()
    scatter.pass2.start()
    compute(1)
    scatter.combine(1)
    scatter.first1.start()
    gather.chip1()
    gather.chip2()
    compute(2)
    scatter.combine(2)
    scatter.first2.start()
    gather.diagonal()
    compute(0)
    scatter.combine(0)
    scatter.finish_two()
    gather.chip3()
    scatter.arrive()

    def finish(i, _):
        rows = span(i * 32, 32)
        res_ref[rows, :] = x_ref[place.me, rows, :].astype(F32) + scatter.total(rows)
        return 0

    lax.fori_loop(0, tok // 32, finish, 0)
    keep_own.wait()
    gather.close()
    scatter.close()


def attention_phase(heads, x_all, g, w, table, gq, gk):
    blocks, tok, model = x_all.shape
    dma = pltpu.SemaphoreType.DMA
    lead = 256 - heads.wide
    kept = kept_shapes(heads, blocks * tok, lead)
    return pl.pallas_call(
        functools.partial(attention_kernel, heads),
        out_shape=(jax.ShapeDtypeStruct((tok, model), F32), jax.ShapeDtypeStruct((blocks, tok, model), BF16)) + kept,
        in_specs=[ANY_SPEC] * 3 + [VMEM_SPEC] * 3,
        out_specs=(VMEM_SPEC, ANY_SPEC) + (VMEM_SPEC,) * len(kept),
        scratch_shapes=[
            pltpu.VMEM((blocks, tok, model), BF16),
            pltpu.VMEM((model, heads.columns), BF16),
            *scatter_scratch(tok, model),
            dma((GATHER_SLOTS,)), dma((GATHER_SLOTS,)), dma((blocks + 2,)),
        ],
        compiler_params=pltpu.CompilerParams(collective_id=1, has_side_effects=True, vmem_limit_bytes=VMEM_LIMIT),
        cost_estimate=pl.CostEstimate(flops=40 << 30, bytes_accessed=64 << 20, transcendentals=0),
    )(x_all, g, w, table, gq, gk)


def ffn_kernel(res_ref, gain_ref, g_hbm, gate_hbm, up_hbm, down_hbm,
               out_hbm, rgrad_ref, branch_ref, gain_grad_ref, gate_grad_hbm, up_grad_hbm, down_grad_hbm,
               two_ref, g_ref, gate_ref, up_ref, down_ref, hid_ref, gu_ref, stage_ref, wstage_ref,
               part_ref, sibling_ref, passing_ref, final_ref, rs_send, rs_recv,
               ag_send, ag_recv, load_sem, stage_sem, wstage_sem):
    place = Place()
    _, tok, model = g_ref.shape
    ff = gate_ref.shape[1]
    tile = 256
    loads = [pltpu.make_async_copy(src, dst, load_sem.at[i]) for i, (src, dst) in enumerate(
        ((gate_hbm, gate_ref), (up_hbm, up_ref), (g_hbm, g_ref), (down_hbm, down_ref)))]
    for copy in loads:
        copy.start()

    def norm_rows(i, _):
        rows = pl.ds(pl.multiple_of(i * 32, 32), 32)
        res = res_ref[rows, :]
        inv = lax.rsqrt(jnp.mean(res * res, axis=-1, keepdims=True) + EPSILON)
        two_ref[place.me, rows, :] = (res * inv * gain_ref[...]).astype(BF16)
        return 0

    lax.fori_loop(0, tok // 32, norm_rows, 0)
    place.greet()
    gather = Gather(place, two_ref.at[place.me], two_ref, ag_send, ag_recv)
    scatter = Scatter(place, part_ref, sibling_ref, passing_ref, final_ref, rs_send, rs_recv)
    gather.start()
    for copy in loads:
        copy.wait()

    def stage_copy(k):
        return pltpu.make_async_copy(stage_ref.at[k % 2], out_hbm.at[k], stage_sem.at[k % 2])

    def compute(k):
        m = place.chips[k]
        pair = pl.ds(2 * m, 2)

        def hidden_tile(h, _):
            cols = pl.ds(pl.multiple_of(h * tile, tile), tile)
            cols2 = pl.ds(pl.multiple_of(ff + h * tile, tile), tile)
            x = two_ref[pair].reshape(2 * tok, model)
            gate = dot(x, gate_ref[:, cols])
            up = dot(x, up_ref[:, cols])
            back = dot_nt(g_ref[pair].reshape(2 * tok, model), down_ref[cols, :])
            s = 1.0 / (1.0 + jnp.exp(-gate))
            act = gate * s
            hid_ref[pair, :, cols] = (act * up).astype(BF16).reshape(2, tok, tile)
            gu_ref[pair, :, cols] = (back * up * s * (1.0 + gate * (1.0 - s))).astype(BF16).reshape(2, tok, tile)
            gu_ref[pair, :, cols2] = (back * act).astype(BF16).reshape(2, tok, tile)
            return 0

        lax.fori_loop(0, ff // tile, hidden_tile, 0)
        if k >= 2:
            stage_copy(k - 2).wait()

        def model_tile(n, _):
            cols = pl.ds(pl.multiple_of(n * tile, tile), tile)
            gg = gu_ref[pair, :, 0:ff].reshape(2 * tok, ff)
            ug = gu_ref[pair, :, ff:2 * ff].reshape(2 * tok, ff)
            back = dot_nt(gg, gate_ref[cols, :]) + dot_nt(ug, up_ref[cols, :])
            part_ref[k, :, :, cols] = back.astype(BF16).reshape(2, tok, tile)
            return 0

        lax.fori_loop(0, model // tile, model_tile, 0)
        scatter.exchange[k].start()

        def out_tile(n, _):
            cols = pl.ds(pl.multiple_of(n * tile, tile), tile)
            hid = hid_ref[pair].reshape(2 * tok, ff)
            out = dot(hid, down_ref[:, cols])
            stage_ref[k % 2, :, :, cols] = out.astype(BF16).reshape(2, tok, tile)
            return 0

        lax.fori_loop(0, model // tile, out_tile, 0)
        stage_copy(k).start()

    gather.own_chip()
    compute(0)
    gather.neighbours()
    gather.chip1()
    compute(1)
    gather.chip2()
    scatter.combine(1)
    scatter.first1.start()
    compute(2)
    gather.diagonal()
    scatter.combine(2)
    scatter.first2.start()
    gather.chip3()
    compute(3)
    scatter.combine(3)
    scatter.pass1.start()
    scatter.pass2.start()
    scatter.combine(0)

    blocks = two_ref.shape[0]

    def wstage_copies(i, slot):
        rows = pl.ds(pl.multiple_of(i * tile, tile), tile)
        return (pltpu.make_async_copy(wstage_ref.at[slot, :, 0:ff], gate_grad_hbm.at[rows], wstage_sem.at[slot, 0]),
                pltpu.make_async_copy(wstage_ref.at[slot, :, ff:2 * ff], up_grad_hbm.at[rows], wstage_sem.at[slot, 1]))

    def gate_up_rows(i, _):
        cols = pl.ds(pl.multiple_of(i * tile, tile), tile)
        slot = lax.rem(i, 2)

        @pl.when(i >= 2)
        def _():
            for copy in wstage_copies(i - 2, slot):
                copy.wait()

        x = two_ref[:, :, cols].reshape(blocks * tok, tile)
        wstage_ref[slot] = dot_tn(x, gu_ref[...].reshape(blocks * tok, 2 * ff)).astype(BF16)
        for copy in wstage_copies(i, slot):
            copy.start()
        return 0

    count = model // tile
    lax.fori_loop(0, count // 2, gate_up_rows, 0)
    scatter.finish_two()
    lax.fori_loop(count // 2, count, gate_up_rows, 0)
    for i in (count - 2, count - 1):
        for copy in wstage_copies(i, i % 2):
            copy.wait()

    stage_copy(2).wait()
    stage_copy(3).wait()

    def down_rows(i, _):
        rows = pl.ds(pl.multiple_of(i * tile, tile), tile)
        h = hid_ref[:, :, rows].reshape(blocks * tok, tile)

        def down_cols(n, _):
            cols = pl.ds(pl.multiple_of(n * 512, 512), 512)
            g = g_ref[:, :, cols].reshape(blocks * tok, 512)
            stage_ref[0, i, :, cols] = dot_tn(h, g).astype(BF16)
            return 0

        lax.fori_loop(0, model // 512, down_cols, 0)
        return 0

    lax.fori_loop(0, ff // tile, down_rows, 0)
    down_out = [pltpu.make_async_copy(stage_ref.at[0, i], down_grad_hbm.at[pl.ds(i * tile, tile)], stage_sem.at[i])
                for i in range(ff // tile)]
    for copy in down_out:
        copy.start()

    scatter.arrive()

    def finish(i, sums):
        rows = pl.ds(pl.multiple_of(i * 32, 32), 32)
        res = res_ref[rows, :]
        inv = lax.rsqrt(jnp.mean(res * res, axis=-1, keepdims=True) + EPSILON)
        grad = scatter.total(rows)
        v = grad * gain_ref[...]
        mean = jnp.mean(v * res, axis=-1, keepdims=True)
        out = g_ref[place.me, rows, :].astype(F32) + inv * v - res * (inv * inv * inv * mean)
        rgrad_ref[rows, :] = out
        branch_ref[rows, :] = out.astype(BF16)
        return sums + jnp.sum(grad * res * inv, axis=0, keepdims=True)

    gain_grad_ref[...] = lax.fori_loop(0, tok // 32, finish, jnp.zeros((1, model), F32))
    for copy in down_out:
        copy.wait()
    gather.close()
    scatter.close()


def feed_forward(res, gain, g_all, gate, up, down):
    tok, model = res.shape
    ff = gate.shape[1]
    blocks = g_all.shape[0]
    any_spec = pl.BlockSpec(memory_space=pl.ANY)
    vmem = pl.BlockSpec(memory_space=pltpu.VMEM)
    return pl.pallas_call(
        ffn_kernel,
        out_shape=(
            jax.ShapeDtypeStruct((4, 2, tok, model), BF16),
            jax.ShapeDtypeStruct((tok, model), F32),
            jax.ShapeDtypeStruct((tok, model), BF16),
            jax.ShapeDtypeStruct((1, model), F32),
            jax.ShapeDtypeStruct((model, ff), BF16),
            jax.ShapeDtypeStruct((model, ff), BF16),
            jax.ShapeDtypeStruct((ff, model), BF16),
        ),
        in_specs=[vmem, vmem] + [any_spec] * 4,
        out_specs=(any_spec, vmem, vmem, vmem, any_spec, any_spec, any_spec),
        scratch_shapes=[
            pltpu.VMEM((blocks, tok, model), BF16),
            pltpu.VMEM((blocks, tok, model), BF16),
            pltpu.VMEM((model, ff), BF16),
            pltpu.VMEM((model, ff), BF16),
            pltpu.VMEM((ff, model), BF16),
            pltpu.VMEM((blocks, tok, ff), BF16),
            pltpu.VMEM((blocks, tok, 2 * ff), BF16),
            pltpu.VMEM((2, 2, tok, model), BF16),
            pltpu.VMEM((2, 256, 2 * ff), BF16),
            *scatter_scratch(tok, model),
            pltpu.SemaphoreType.DMA((GATHER_SLOTS,)),
            pltpu.SemaphoreType.DMA((GATHER_SLOTS,)),
            pltpu.SemaphoreType.DMA((4,)),
            pltpu.SemaphoreType.DMA((2,)),
            pltpu.SemaphoreType.DMA((2, 2)),
        ],
        compiler_params=pltpu.CompilerParams(collective_id=2, has_side_effects=True, vmem_limit_bytes=60 * 1024 * 1024),
        cost_estimate=pl.CostEstimate(flops=18 * blocks * tok * model * ff, bytes_accessed=64 << 20, transcendentals=0),
    )(res, gain, g_all, gate, up, down)


def backward_kernel(heads, branch_hbm, out_hbm, x_hbm, w_hbm, table_ref, gq_ref, gk_ref, merged_hbm,
                    raw_ref, o_ref, qa_ref, ka_ref, kt_ref, vt_ref, inv_ref,
                    ysum_ref, outsum_ref, grad_hbm, gains_ref,
                    every_ref, w_ref, pg_ref, merged_ref, xt_ref, wstage_ref,
                    doa_ref, dopad_ref, qpad_ref, va_ref, dq_ref, acc_ref,
                    part_ref, sibling_ref, passing_ref, final_ref, rs_send, rs_recv, rs2_send, rs2_recv,
                    ag_send, ag_recv, load_sem, xt_sem, wstage_sem, ready_sem):
    place = Place()
    blocks, tok, model = every_ref.shape
    load_w = pltpu.make_async_copy(w_hbm, w_ref, load_sem.at[0])
    load_out = pltpu.make_async_copy(out_hbm, part_ref, load_sem.at[1])
    load_own = pltpu.make_async_copy(branch_hbm, every_ref.at[place.me], load_sem.at[2])
    load_merged = pltpu.make_async_copy(merged_hbm, merged_ref, load_sem.at[3])
    load_own.start()
    load_w.start()
    load_out.start()
    load_merged.start()
    place.greet()
    gather = Gather(place, branch_hbm, every_ref, ag_send, ag_recv)
    gather.start()
    first = Scatter(place, part_ref, sibling_ref, passing_ref, final_ref, rs_send, rs_recv)
    second = Scatter(place, part_ref, sibling_ref, passing_ref, final_ref, rs2_send, rs2_recv)
    back = Backward(heads, place.me, table_ref, gq_ref, gk_ref, raw_ref, o_ref, qa_ref, ka_ref, kt_ref, vt_ref, inv_ref,
                    doa_ref, dopad_ref, qpad_ref, va_ref, dq_ref, acc_ref)
    lead = 256 - heads.wide

    def prepare(b, _):
        back.prepare(b)
        return 0

    lax.fori_loop(0, blocks, prepare, 0)
    load_out.wait()
    for copy in first.exchange:
        copy.start()
    load_w.wait()
    load_own.wait()

    def compute(k):
        m = place.chips[k]

        def gradient(j, _):
            b = 2 * m + j
            dm = dot(every_ref[b], w_ref[:, 384:640])
            back.gradient(b, dm[:, lead:])
            return 0

        lax.fori_loop(0, 2, gradient, 0)
        back.query_block(m)

    gather.own_chip()
    compute(0)
    gather.neighbours()
    first.combine(3)
    first.pass1.start()
    first.pass2.start()
    gather.chip1()
    compute(1)
    first.combine(1)
    first.first1.start()
    gather.chip2()
    compute(2)
    first.combine(2)
    first.first2.start()
    gather.diagonal()
    first.combine(0)
    gather.chip3()
    compute(3)
    first.finish_two()

    pad = 512 - heads.qkv

    def finish(b, sums):
        grad, sums = back.finish(b, sums)
        grad = jnp.concatenate([grad, jnp.zeros((pad, tok), F32)], axis=0)
        pg_ref[b] = jnp.transpose(grad).astype(BF16)
        return sums

    zero = jnp.zeros((D, tok), F32)
    sum_q, sum_k = lax.fori_loop(0, blocks, finish, (zero, zero))
    gains_ref[0:D, :] = jnp.broadcast_to(jnp.sum(sum_q, axis=1, keepdims=True), (D, 128))
    gains_ref[D:2 * D, :] = jnp.broadcast_to(jnp.sum(sum_k, axis=1, keepdims=True), (D, 128))
    load_merged.wait()

    tile = 256
    count = model // tile

    def x_copy(i, slot):
        return pltpu.make_async_copy(x_hbm.at[:, :, span(i * tile, tile)], xt_ref.at[slot], xt_sem.at[slot])

    def grad_copy(i, slot):
        return pltpu.make_async_copy(wstage_ref.at[slot], grad_hbm.at[span(i * tile, tile)], wstage_sem.at[slot])

    x_copy(0, 0).start()

    def weight_rows(i, _):
        slot = lax.rem(i, 2)
        cols = span(i * tile, tile)

        @pl.when(i + 1 < count)
        def _():
            x_copy(i + 1, 1 - slot).start()

        @pl.when(i >= 2)
        def _():
            grad_copy(i - 2, slot).wait()

        out = dot_tn(every_ref[:, :, cols].reshape(blocks * tok, tile), merged_ref[...])
        x_copy(i, slot).wait()
        x = xt_ref[slot].reshape(blocks * tok, tile)
        qkv = dot_tn(x, pg_ref[...].reshape(blocks * tok, 512))
        wstage_ref[slot, :, 0:heads.qkv] = qkv[:, 0:heads.qkv].astype(BF16)
        wstage_ref[slot, :, heads.qkv:heads.columns] = out[:, lead:].astype(BF16)
        grad_copy(i, slot).start()
        return 0

    lax.fori_loop(0, count, weight_rows, 0)
    first.arrive()

    def take(out_ref, scatter):
        def one(i, _):
            rows = span(i * 32, 32)
            out_ref[rows, :] = scatter.total(rows)
            return 0

        lax.fori_loop(0, tok // 32, one, 0)

    take(outsum_ref, first)
    first.close()
    for other in (place.sib, place.same[1], place.same[2]):
        pl.semaphore_signal(ready_sem, inc=1, device_id=(place.row, other), device_id_type=MESH)
    pl.semaphore_wait(ready_sem, 3)

    def project(k):
        m = place.chips[k]

        def model_tile(n, _):
            cols = span(n * 512, 512)
            out = dot_nt(pg_ref[pl.ds(2 * m, 2)].reshape(2 * tok, 512), w_ref[cols, 0:512])
            part_ref[k, :, :, cols] = out.astype(BF16).reshape(2, tok, 512)
            return 0

        lax.fori_loop(0, model // 512, model_tile, 0)
        second.exchange[k].start()

    project(3)
    project(1)
    second.combine(3)
    second.pass1.start()
    second.pass2.start()
    project(2)
    second.combine(1)
    second.first1.start()
    project(0)
    second.combine(2)
    second.first2.start()
    second.combine(0)
    for i in (count - 2, count - 1):
        grad_copy(i, i % 2).wait()
    second.finish_two()
    second.arrive()
    take(ysum_ref, second)
    gather.close()
    second.close()


def backward_phase(heads, branch, out_part, x_all, w, table, gq, gk, kept):
    blocks, tok, model = x_all.shape
    length = blocks * tok
    dma = pltpu.SemaphoreType.DMA
    raw, merged, *rest = kept
    return pl.pallas_call(
        functools.partial(backward_kernel, heads),
        out_shape=(
            jax.ShapeDtypeStruct((tok, model), F32),
            jax.ShapeDtypeStruct((tok, model), F32),
            jax.ShapeDtypeStruct((model, heads.columns), BF16),
            jax.ShapeDtypeStruct((2 * D, 128), F32),
        ),
        in_specs=[ANY_SPEC] * 4 + [VMEM_SPEC] * 3 + [ANY_SPEC] + [VMEM_SPEC] * (1 + len(rest)),
        out_specs=(VMEM_SPEC, VMEM_SPEC, ANY_SPEC, VMEM_SPEC),
        scratch_shapes=[
            pltpu.VMEM((blocks, tok, model), BF16),
            pltpu.VMEM((model, heads.columns), BF16),
            pltpu.VMEM((blocks, tok, 512), BF16),
            pltpu.VMEM(merged.shape, BF16),
            pltpu.VMEM((2, blocks, tok, 256), BF16),
            pltpu.VMEM((2, 256, heads.columns), BF16),
            *backward_scratch(heads, length),
            *scatter_scratch(tok, model),
            dma((SCATTER_SLOTS,)), dma((SCATTER_SLOTS,)),
            dma((GATHER_SLOTS,)), dma((GATHER_SLOTS,)), dma((4,)), dma((2,)), dma((2,)),
            pltpu.SemaphoreType.REGULAR,
        ],
        compiler_params=pltpu.CompilerParams(collective_id=3, has_side_effects=True, vmem_limit_bytes=62 * 1024 * 1024),
        cost_estimate=pl.CostEstimate(flops=60 << 30, bytes_accessed=64 << 20, transcendentals=0),
    )(branch, out_part, x_all, w, table, gq, gk, merged, raw, *rest)


def norm_back(grad_normed, values_in, inv_rms, gain):
    scaled = grad_normed * gain
    gain_grad = jnp.sum(grad_normed * values_in * inv_rms, axis=0)
    input_grad = inv_rms * scaled - values_in * inv_rms**3 * jnp.mean(scaled * values_in, axis=-1, keepdims=True)
    return input_grad, gain_grad


def start_wide(rows, x, table, pieces, gain):
    return (
        lax.all_gather(x, "seq", axis=0, tiled=False),
        lax.all_gather(table, "seq", axis=0, tiled=False),
        lax.all_gather(lax.all_to_all(pieces, "seq", 0, 0, tiled=False), "rows", axis=0, tiled=False),
        lax.all_gather(lax.all_gather(gain, "seq", axis=0, tiled=False), "rows", axis=0, tiled=False),
    )


def scatter_rows(part, tok):
    return lax.psum_scatter(part.reshape(-1, part.shape[-1]), "seq", scatter_dimension=0, tiled=True).astype(F32)


def attention_wide(heads, x_all, g, w, table, gq, gk):
    blocks, tok, model = x_all.shape
    proj = dot(x_all.reshape(blocks * tok, model), w[:, :heads.qkv])
    kept = pl.pallas_call(
        functools.partial(local_forward_kernel, heads),
        out_shape=kept_shapes(heads, blocks * tok, 0),
        compiler_params=pltpu.CompilerParams(vmem_limit_bytes=VMEM_LIMIT),
    )(proj, table, gq, gk)
    total = scatter_rows(dot_nt(kept[1], w[:, heads.qkv:]).astype(BF16), tok)
    own = lax.dynamic_index_in_dim(x_all, lax.axis_index("seq"), 0, keepdims=False)
    return (own.astype(F32) + total, lax.all_gather(g, "seq", axis=0, tiled=False)) + tuple(kept)


def feed_forward_wide(res, gain, g_blocks, gate_slab, up_slab, down_slab):
    blocks, tok, model = g_blocks.shape
    inv = norm_inverse(res)
    two_all = lax.all_gather((res * inv * gain).astype(BF16), "seq", axis=0, tiled=True)
    g_all = g_blocks.reshape(blocks * tok, model)
    gate_act = dot(two_all, gate_slab)
    up_act = dot(two_all, up_slab)
    s = jax.nn.sigmoid(gate_act)
    hidden = (gate_act * s * up_act).astype(BF16)
    hidden_grad = dot_nt(g_all, down_slab)
    gate_grad = (hidden_grad * up_act * s * (1.0 + gate_act * (1.0 - s))).astype(BF16)
    up_grad = (hidden_grad * gate_act * s).astype(BF16)
    two_grad = scatter_rows((dot_nt(gate_grad, gate_slab) + dot_nt(up_grad, up_slab)).astype(BF16), tok)
    branch_part = dot(hidden, down_slab).astype(BF16).reshape(blocks, tok, model)
    norm_grad, gain_grad = norm_back(two_grad, res, inv, gain)
    g = lax.dynamic_index_in_dim(g_blocks, lax.axis_index("seq"), 0, keepdims=False)
    residual_grad = g.astype(F32) + norm_grad
    return (branch_part, residual_grad, residual_grad.astype(BF16), gain_grad[None],
            dot_tn(two_all, gate_grad).astype(BF16), dot_tn(two_all, up_grad).astype(BF16),
            dot_tn(hidden, g_all).astype(BF16))


def backward_wide(heads, branch, out_part, x_all, w, table, gq, gk, kept):
    blocks, tok, model = x_all.shape
    length = blocks * tok
    raw, merged, *rest = kept
    out_sum = scatter_rows(out_part, tok)
    branch_all = lax.all_gather(branch, "seq", axis=0, tiled=True)
    pg, gains = pl.pallas_call(
        functools.partial(local_backward_kernel, heads),
        out_shape=(jax.ShapeDtypeStruct((length, heads.qkv), BF16), jax.ShapeDtypeStruct((2 * D, 128), F32)),
        scratch_shapes=backward_scratch(heads, length),
        compiler_params=pltpu.CompilerParams(vmem_limit_bytes=VMEM_LIMIT),
    )(dot(branch_all, w[:, heads.qkv:]), table, gq, gk, raw, *rest)
    y_sum = scatter_rows(dot_nt(pg, w[:, :heads.qkv]).astype(BF16), tok)
    grad = jnp.concatenate([dot_tn(x_all.reshape(length, model), pg), dot_tn(branch_all, merged)], axis=1)
    return y_sum, out_sum, grad.astype(BF16), gains


def rotary_table(x, positions, segments):
    inverse = jnp.exp(-math.log(THETA) * jnp.arange(HALF, dtype=F32) * 2.0 / D)
    angles = inverse[:, None] * positions.astype(F32)[None, :]
    hot = jnp.arange(SEGMENT_KINDS, dtype=jnp.int32)[:, None] == segments[None, :]
    root = jnp.pad(norm_inverse(x).T, ((0, 7), (0, 0)))
    return jnp.concatenate([jnp.cos(angles), jnp.sin(angles), hot.astype(F32), root], axis=0)


def attention_pieces(heads, w_qkv, w_out):
    depth = w_qkv.shape[0]
    qw, kw = QUERY_HEADS * D, KEY_VALUE_HEADS * D
    out_t = w_out.T

    def columns(array, start, first, count, most):
        parts = []
        for i in range(count):
            n = first + i
            parts.append(array[:, start + n * D:start + (n + 1) * D] if n < most else jnp.zeros((depth, D), BF16))
        return parts

    pieces = []
    for s in range(heads.seq):
        q, k = s * heads.queries, heads.first(s)
        parts = (columns(w_qkv, 0, q, heads.queries, QUERY_HEADS)
                 + columns(w_qkv, qw, k, heads.pairs, KEY_VALUE_HEADS)
                 + columns(w_qkv, qw + kw, k, heads.pairs, KEY_VALUE_HEADS)
                 + columns(out_t, 0, q, heads.queries, QUERY_HEADS))
        pieces.append(jnp.concatenate(parts, axis=1))
    return jnp.stack(pieces)


def attention_sums(heads, pieces):
    depth = pieces.shape[1]
    cut = lambda s, start, n: pieces[s, :, start + n * D:start + (n + 1) * D]
    queries = [cut(n // heads.queries, 0, n % heads.queries) for n in range(QUERY_HEADS)]
    outs = [cut(n // heads.queries, heads.qkv, n % heads.queries) for n in range(QUERY_HEADS)]

    def pairs(start):
        found = []
        for n in range(KEY_VALUE_HEADS):
            terms = [cut(s, start, n - heads.first(s)) for s in range(heads.seq)
                     if s * heads.queries < QUERY_HEADS and 0 <= n - heads.first(s) < heads.pairs]
            found.append(functools.reduce(jnp.add, terms))
        return found

    qkv = jnp.concatenate(queries + pairs(heads.wide) + pairs(heads.wide + heads.narrow), axis=1)
    return qkv, jnp.concatenate(outs, axis=1)


def body(tokens, segments, positions, cotangent, gain_attn, w_qkv, gain_q, gain_k, w_out, gain_ffn, w_gate, w_up, w_down):
    seq = lax.axis_size("seq")
    rows = lax.axis_size("rows")
    heads = Heads(seq)
    depth = w_qkv.shape[0]
    tok, model = tokens.shape[1:]
    plane = seq == PLANE

    gate_slab = lax.all_gather(w_gate, "rows", axis=0, tiled=True)
    up_slab = lax.all_gather(w_up, "rows", axis=0, tiled=True)
    down_slab = lax.all_gather(w_down, "rows", axis=1, tiled=True)
    gq = gain_q.astype(F32)[:, None]
    gk = gain_k.astype(F32)[:, None]
    x = tokens[0].astype(F32)

    scaled = (w_qkv.astype(F32) * gain_attn.astype(F32)[:, None]).astype(BF16)
    pieces = attention_pieces(heads, scaled, w_out)
    gain = jnp.pad(gain_ffn.astype(F32)[None], ((0, 7), (0, 128 - depth)))
    x_all, table, w, gains = (start_phase if plane else start_wide)(
        rows, tokens[0], rotary_table(x, positions[0], segments[0]), pieces, gain)
    w = w.reshape(model, heads.columns)
    gain_two = gains[:, :, 0, :depth].reshape(1, model)

    residual, g_all, *kept = (attention_phase if plane else attention_wide)(heads, x_all, cotangent[0], w, table, gq, gk)
    out_part, residual_grad, branch, gain_two_grad, gate_wgrad, up_wgrad, down_wgrad = (
        feed_forward if plane else feed_forward_wide)(residual, gain_two, g_all, gate_slab, up_slab, down_slab)
    grad_gate = lax.psum_scatter(gate_wgrad, "rows", scatter_dimension=0, tiled=True).astype(F32)
    grad_up = lax.psum_scatter(up_wgrad, "rows", scatter_dimension=0, tiled=True).astype(F32)
    grad_down = lax.psum_scatter(down_wgrad, "rows", scatter_dimension=1, tiled=True).astype(F32)
    y_sum, out_sum, attn_grad, head_gains = (backward_phase if plane else backward_wide)(
        heads, branch, out_part, x_all, w, table, gq, gk, kept)

    layer_out = (residual + out_sum).astype(BF16)
    inv = norm_inverse(x)
    grad_tokens = residual_grad + y_sum - x * (inv * inv * jnp.mean(y_sum * x, axis=-1, keepdims=True))

    attn_grad = lax.psum_scatter(attn_grad, "rows", scatter_dimension=0, tiled=True)
    attn_grad = lax.all_to_all(attn_grad.reshape(seq, depth, heads.columns), "seq", 0, 0, tiled=False).astype(F32)
    unscaled, grad_out = attention_sums(heads, attn_grad)
    grad_gain_attn = jnp.sum(unscaled * w_qkv.astype(F32), axis=1)
    grad_qkv = unscaled * gain_attn.astype(F32)[:, None]

    small = lax.psum(jnp.concatenate([gain_two_grad[0], head_gains[:, 0]]), ("rows", "seq"))
    start = (lax.axis_index("rows") * seq + lax.axis_index("seq")) * depth
    return (
        layer_out[None],
        grad_tokens[None],
        grad_gain_attn,
        grad_qkv,
        small[model:model + D],
        small[model + D:],
        grad_out.T,
        lax.dynamic_slice_in_dim(small, start, depth),
        grad_gate,
        grad_up,
        grad_down,
    )


def solution(mesh):
    both = ("rows", "seq")
    return jax.shard_map(
        body,
        mesh=mesh,
        in_specs=(
            P("rows", "seq", None), P("rows", "seq"), P("rows", "seq"), P("rows", "seq", None),
            P(both), P(both, None), P(), P(), P(None, both), P(both),
            P("rows", "seq"), P("rows", "seq"), P("seq", "rows"),
        ),
        out_specs=(
            P("rows", "seq", None), P("rows", "seq", None), P(both), P(both, None), P(), P(),
            P(None, both), P(both), P("rows", "seq"), P("rows", "seq"), P("seq", "rows"),
        ),
        check_vma=False,
    )
```

```python
import functools
import math

import jax
import jax.numpy as jnp
from jax import lax
from jax.experimental import pallas as pl
from jax.experimental.pallas import tpu as pltpu
from jax.sharding import PartitionSpec as P

QUERY_HEADS = 24
KEY_VALUE_HEADS = 6
GROUP = QUERY_HEADS // KEY_VALUE_HEADS
D = 64
HALF = D // 2
EPSILON = 1e-06
THETA = 10000.0
PENALTY = -10000.0
SEGMENT_KINDS = 8
TABLE_ROWS = 80
BLOCK = 512
PLANE = 8
F32 = jnp.float32
BF16 = jnp.bfloat16
VMEM_LIMIT = 60 * 1024 * 1024
MESH = pl.DeviceIdType.MESH
ANY_SPEC = pl.BlockSpec(memory_space=pl.ANY)
VMEM_SPEC = pl.BlockSpec(memory_space=pltpu.VMEM)


def dot(a, b):
    return jnp.dot(a, b, preferred_element_type=F32)


def dot_nt(a, b):
    return lax.dot_general(a, b, (((1,), (1,)), ((), ())), preferred_element_type=F32)


def dot_tn(a, b):
    return lax.dot_general(a, b, (((0,), (0,)), ((), ())), preferred_element_type=F32)


def norm_inverse(x):
    return lax.rsqrt(jnp.mean(x * x, axis=-1, keepdims=True) + EPSILON)


def split3(x):
    high = x.astype(BF16).astype(F32)
    mid = (x - high).astype(BF16).astype(F32)
    return high, mid, x - high - mid


def span(start, size):
    return pl.ds(pl.multiple_of(start, size), size)


class Heads:
    def __init__(self, seq):
        self.seq = seq
        self.queries = -(-QUERY_HEADS // seq)
        last = [min((s + 1) * self.queries, QUERY_HEADS) - 1 for s in range(seq)]
        self.pairs = max(last[s] // GROUP - self.first(s) + 1 for s in range(seq) if last[s] >= s * self.queries)
        self.wide = self.queries * D
        self.narrow = self.pairs * D
        self.qkv = self.wide + 2 * self.narrow
        self.columns = self.qkv + self.wide

    def first(self, s):
        return (s * self.queries) // GROUP

    def slot(self, s, h):
        return (s * self.queries + h) // GROUP - (s * self.queries) // GROUP


class Place:
    def __init__(self):
        self.row = lax.axis_index("rows")
        self.me = lax.axis_index("seq")
        self.core = lax.rem(self.me, 2)
        self.chip = self.me // 2
        self.sib = self.me + 1 - 2 * self.core
        chip = self.chip
        self.chips = (chip, chip + 1 - 2 * lax.rem(chip, 2), lax.rem(chip + 2, 4), 3 - chip)
        self.same = tuple(2 * q + self.core for q in self.chips)

    def greet(self, rows=1):
        barrier = pltpu.get_barrier_semaphore()
        for other in (self.sib, self.same[1], self.same[2]):
            pl.semaphore_signal(barrier, inc=1, device_id=(self.row, other), device_id_type=MESH)
        for j in range(1, rows):
            other = lax.rem(self.row + j, rows)
            pl.semaphore_signal(barrier, inc=1, device_id=(other, self.me), device_id_type=MESH)
        pl.semaphore_wait(barrier, 3 + rows - 1)

    def greet_all(self, rows):
        barrier = pltpu.get_barrier_semaphore()
        for j in range(1, PLANE):
            other = lax.rem(self.me + j, PLANE)
            pl.semaphore_signal(barrier, inc=1, device_id=(self.row, other), device_id_type=MESH)
        for j in range(1, rows):
            other = lax.rem(self.row + j, rows)
            pl.semaphore_signal(barrier, inc=1, device_id=(other, self.me), device_id_type=MESH)
        pl.semaphore_wait(barrier, PLANE - 1 + rows - 1)

    def send(self, src, dst, send_sem, recv_sem, slot, target):
        return pltpu.make_async_remote_copy(
            src_ref=src, dst_ref=dst, send_sem=send_sem.at[slot], recv_sem=recv_sem.at[slot],
            device_id=(self.row, target), device_id_type=MESH)


class Line:
    def __init__(self, place):
        self.place = place
        row = place.row
        self.a = row + 1 - 2 * lax.rem(row, 2)
        self.b = 3 - row
        self.c = lax.rem(row + 2, 4)
        self.middle = (row + 1) // 2 == 1

    def send(self, src, dst, send_sem, send_slot, recv_sem, recv_slot, target):
        return pltpu.make_async_remote_copy(
            src_ref=src, dst_ref=dst, send_sem=send_sem.at[send_slot], recv_sem=recv_sem.at[recv_slot],
            device_id=(target, self.place.me), device_id_type=MESH)


ROW_SLOTS = 4


class RowGather:
    def __init__(self, line, own, every, send_sem, recv_sem):
        self.line = line
        mine = every.at[line.place.row]
        passed = every.at[line.c]
        self.to_a = line.send(own, mine, send_sem, 0, recv_sem, 0, line.a)
        self.to_c = line.send(own, mine, send_sem, 1, recv_sem, 1, line.c)
        self.to_b = line.send(own, mine, send_sem, 2, recv_sem, 2, line.b)
        self.on = line.send(passed, passed, send_sem, 3, recv_sem, 2, line.a)

    def start(self):
        self.to_c.start()
        self.to_a.start()

        @pl.when(self.line.middle)
        def _():
            self.to_b.start()

    def forward(self):
        self.to_c.wait_recv()

        @pl.when(self.line.middle)
        def _():
            self.on.start()

    def finish(self):
        self.to_a.wait_recv()
        self.to_b.wait_recv()

    def close(self):
        self.to_a.wait_send()
        self.to_c.wait_send()

        @pl.when(self.line.middle)
        def _():
            self.to_b.wait_send()
            self.on.wait_send()


class RowScatter:
    def __init__(self, line, part, recv, merge, total, send_sem, recv_sem):
        self.line, self.total = line, total
        self.to_a = line.send(part.at[line.a], recv.at[0], send_sem, 0, recv_sem, 0, line.a)
        self.to_b = line.send(part.at[line.b], recv.at[1], send_sem, 1, recv_sem, 1, line.b)
        self.to_c = line.send(part.at[line.c], recv.at[2], send_sem, 2, recv_sem, 2, line.c)
        self.added = line.send(total, recv.at[2], send_sem, 2, recv_sem, 2, line.c)
        self.over = line.send(part.at[line.b], merge, send_sem, 3, recv_sem, 3, line.a)

    def start_over(self):
        @pl.when(jnp.logical_not(self.line.middle))
        def _():
            self.over.start()

    def start(self):
        @pl.when(jnp.logical_not(self.line.middle))
        def _():
            self.to_c.start()

        @pl.when(self.line.middle)
        def _():
            self.to_b.start()

        self.to_a.start()

    def add(self, work):
        @pl.when(self.line.middle)
        def _():
            self.over.wait_recv()
            work()
            self.added.start()

    def finish(self):
        self.to_a.wait_recv()
        self.to_c.wait_recv()

        @pl.when(self.line.middle)
        def _():
            self.to_b.wait_recv()

    def close(self):
        self.to_a.wait_send()
        self.to_c.wait_send()

        @pl.when(self.line.middle)
        def _():
            self.to_b.wait_send()

        @pl.when(jnp.logical_not(self.line.middle))
        def _():
            self.over.wait_send()


GATHER_SLOTS = 10


class Gather:
    def __init__(self, place, own, every, send_sem, recv_sem):
        half = every.shape[1] // 2
        low, high, whole = slice(0, half), slice(half, 2 * half), slice(0, 2 * half)

        def send(part, b, slot, target, src=None):
            src = every.at[b, part] if src is None else src.at[part]
            return place.send(src, every.at[b, part], send_sem, recv_sem, slot, target)

        me, (_, s1, s2, s3), sib = place.me, place.same, place.sib
        self.copies = (
            send(whole, me, 0, sib, own),
            send(low, me, 1, s1, own), send(high, me, 2, s1, own),
            send(high, me, 3, s2, own), send(low, me, 4, s2, own),
            send(low, s1, 5, s2), send(high, s2, 6, s1),
            send(whole, s1, 7, sib), send(whole, s2, 8, sib), send(whole, s3, 9, sib),
        )

    def start(self):
        for slot in (1, 3, 2, 4, 0):
            self.copies[slot].start()

    def own_chip(self):
        self.copies[0].wait_recv()

    def neighbours(self):
        c = self.copies
        c[1].wait_recv()
        c[5].start()
        c[3].wait_recv()
        c[6].start()
        c[2].wait_recv()
        c[7].start()
        c[4].wait_recv()
        c[8].start()

    def chip1(self):
        self.copies[7].wait_recv()

    def chip2(self):
        self.copies[8].wait_recv()

    def diagonal(self):
        c = self.copies
        c[5].wait_recv()
        c[6].wait_recv()
        c[9].start()

    def chip3(self):
        self.copies[9].wait_recv()

    def close(self):
        for copy in self.copies:
            copy.wait_send()


SCATTER_SLOTS = 10


class Scatter:
    def __init__(self, place, part, sibling, passing, final, send_sem, recv_sem):
        self.place, self.part, self.sibling, self.passing, self.final = place, part, sibling, passing, final
        half = part.shape[2] // 2
        self.half = half
        core, other = place.core, 1 - place.core
        _, s1, s2, _ = place.same
        send = lambda src, dst, slot, target: place.send(src, dst, send_sem, recv_sem, slot, target)
        low, high = slice(0, half), slice(half, 2 * half)
        self.exchange = tuple(send(part.at[k, other], sibling.at[k], k, place.sib) for k in range(4))
        self.pass1 = send(part.at[3, core, low], passing.at[0], 4, s1)
        self.pass2 = send(part.at[3, core, high], passing.at[1], 5, s2)
        self.first1 = send(part.at[1, core, low], final.at[0, low], 6, s1)
        self.second1 = send(part.at[1, core, high], final.at[0, high], 7, s1)
        self.first2 = send(part.at[2, core, high], final.at[1, high], 8, s2)
        self.second2 = send(part.at[2, core, low], final.at[1, low], 9, s2)

    def add(self, k, start, size, term, offset):
        core, step = self.place.core, 64

        def one(i, _):
            rows = pl.ds(pl.multiple_of(start + i * step, step), step)
            from_rows = pl.ds(pl.multiple_of(offset + i * step, step), step)
            total = self.part[k, core, rows, :].astype(F32) + term[from_rows, :].astype(F32)
            self.part[k, core, rows, :] = total.astype(BF16)
            return 0

        lax.fori_loop(0, size // step, one, 0)

    def combine(self, k):
        self.exchange[k].wait_recv()
        self.add(k, 0, 2 * self.half, self.sibling.at[k], 0)

    def finish_two(self):
        self.pass1.wait_recv()
        self.add(2, 0, self.half, self.passing.at[0], 0)
        self.second2.start()
        self.pass2.wait_recv()
        self.add(1, self.half, self.half, self.passing.at[1], 0)
        self.second1.start()

    def arrive(self):
        for copy in (self.first1, self.second1, self.first2, self.second2):
            copy.wait_recv()

    def total(self, rows):
        return (self.part[0, self.place.core, rows, :].astype(F32) + self.final[0, rows, :].astype(F32)
                + self.final[1, rows, :].astype(F32))

    def close(self):
        for copy in self.exchange + (self.pass1, self.pass2, self.first1, self.second1, self.first2, self.second2):
            copy.wait_send()


def scatter_scratch(tok, width):
    return [
        pltpu.VMEM((4, 2, tok, width), BF16),
        pltpu.VMEM((4, tok, width), BF16),
        pltpu.VMEM((2, tok // 2, width), BF16),
        pltpu.VMEM((2, tok, width), BF16),
        pltpu.SemaphoreType.DMA((SCATTER_SLOTS,)),
        pltpu.SemaphoreType.DMA((SCATTER_SLOTS,)),
    ]


def start_kernel(x_hbm, table_hbm, pieces_hbm, gain_hbm, x_all, table_all, w_all, gain_all,
                 x_send, x_recv, t_send, t_recv, p_send, p_recv, g_send, g_recv, z_send, z_recv, w_send, w_recv, local_sem):
    place = Place()
    rows = w_all.shape[0]
    me, row = place.me, place.row
    local = [pltpu.make_async_copy(src, dst, local_sem.at[i]) for i, (src, dst) in enumerate((
        (pieces_hbm.at[me], w_all.at[row, me]), (gain_hbm, gain_all.at[row, me]),
        (x_hbm, x_all.at[me]), (table_hbm, table_all.at[me])))]
    for copy in local:
        copy.start()
    place.greet_all(rows)
    exchange = []
    for j in range(1, PLANE):
        other = lax.rem(me + j, PLANE)
        exchange.append(place.send(pieces_hbm.at[other], w_all.at[row, me], p_send, p_recv, j, other))
        exchange.append(place.send(gain_hbm, gain_all.at[row, me], g_send, g_recv, j, other))
    for copy in exchange:
        copy.start()
    gathers = (Gather(place, x_hbm, x_all, x_send, x_recv), Gather(place, table_hbm, table_all, t_send, t_recv))
    gathers[1].start()
    gathers[0].start()
    for copy in local[:2]:
        copy.wait()
    for copy in exchange:
        copy.wait_recv()
    line = Line(place)
    weights = RowGather(line, w_all.at[row], w_all, w_send, w_recv)
    weights.start()
    along = []
    for j in range(1, rows):
        other = lax.rem(row + j, rows)
        along.append(line.send(gain_all.at[row], gain_all.at[row], z_send, j, z_recv, j, other))
    for copy in along:
        copy.start()
    for name in ("own_chip", "neighbours"):
        for gather in gathers[::-1]:
            getattr(gather, name)()
    weights.forward()
    for name in ("chip1", "chip2", "diagonal", "chip3"):
        for gather in gathers[::-1]:
            getattr(gather, name)()
    weights.finish()
    weights.close()
    for copy in local[2:]:
        copy.wait()
    for copy in along:
        copy.wait_recv()
    for copy in exchange + along:
        copy.wait_send()
    for gather in gathers:
        gather.close()


def start_phase(rows, x, table, pieces, gain):
    tok, model = x.shape
    dma = pltpu.SemaphoreType.DMA
    return pl.pallas_call(
        start_kernel,
        out_shape=(
            jax.ShapeDtypeStruct((PLANE, tok, model), BF16),
            jax.ShapeDtypeStruct((PLANE,) + table.shape, F32),
            jax.ShapeDtypeStruct((rows,) + pieces.shape, BF16),
            jax.ShapeDtypeStruct((rows, PLANE) + gain.shape, F32),
        ),
        in_specs=[ANY_SPEC] * 4,
        out_specs=(ANY_SPEC,) * 4,
        scratch_shapes=[dma((GATHER_SLOTS,))] * 4 + [dma((PLANE,))] * 4 + [dma((rows,))] * 2 + [dma((ROW_SLOTS,))] * 2 + [dma((4,))],
        compiler_params=pltpu.CompilerParams(collective_id=0, has_side_effects=True),
        cost_estimate=pl.CostEstimate(flops=0, bytes_accessed=160 << 20, transcendentals=0),
    )(x, table, pieces, gain)


class Forward:
    def __init__(self, heads, me, table, gq, gk, raw, merged, o, qa, ka, kt, vt, inv):
        self.heads, self.table, self.gq, self.gk = heads, table, gq[...], gk[...]
        self.raw, self.merged, self.o, self.qa, self.ka, self.kt, self.vt, self.inv = raw, merged, o, qa, ka, kt, vt, inv
        self.slots = [heads.slot(me, h) for h in range(heads.queries)]

    def prepare(self, b, projected):
        heads = self.heads
        tok = self.table.shape[2]
        lanes = span(b * tok, tok)
        cos = self.table[b, 0:HALF, :]
        sin = self.table[b, HALF:D, :]
        hot = self.table[b, D:D + 8, :]
        row = lax.broadcasted_iota(jnp.int32, (16, tok), 0)
        one_row = jnp.where(row == 0, 1.0, 0.0).astype(F32)
        penalty = jnp.concatenate([(1.0 - hot) * PENALTY, jnp.zeros((8, tok), F32)], axis=0).astype(BF16)
        self.raw[:, lanes] = projected[:heads.wide + heads.narrow]

        def rotated(raw, gain):
            inv = lax.rsqrt(jnp.mean(raw * raw, axis=0, keepdims=True) + EPSILON)
            n = raw * inv * gain
            a, c = n[:HALF], n[HALF:]
            return inv, jnp.concatenate([a * cos - c * sin, c * cos + a * sin], axis=0)

        for h in range(heads.queries):
            inv, q = rotated(projected[h * D:(h + 1) * D], self.gq)
            self.inv[h:h + 1, lanes] = inv
            self.qa[h, :, lanes] = jnp.concatenate([(q * (D ** -0.5)).astype(BF16), penalty], axis=0)
        for g in range(heads.pairs):
            start = heads.wide + g * D
            inv, k = rotated(projected[start:start + D], self.gk)
            self.inv[heads.queries + g:heads.queries + g + 1, lanes] = inv
            self.kt[g, :, lanes] = k.astype(BF16)
            full = jnp.concatenate([k, hot, jnp.ones((8, tok), F32), jnp.zeros((48, tok), F32)], axis=0)
            self.ka[g, lanes, :] = jnp.transpose(full).astype(BF16)
            start += heads.narrow
            self.vt[g, :, lanes] = jnp.concatenate([projected[start:start + D], one_row], axis=0).astype(BF16)

    def query_block(self, i):
        heads = self.heads
        cols = span(i * BLOCK, BLOCK)
        causal = (lax.broadcasted_iota(jnp.int32, (BLOCK, BLOCK), 0)
                  <= lax.broadcasted_iota(jnp.int32, (BLOCK, BLOCK), 1))

        def step(j, accs, diagonal):
            rows = span(j * BLOCK, BLOCK)
            new = []
            for h in range(heads.queries):
                slot = self.slots[h]
                p = jnp.exp(dot(self.ka[slot, rows, 0:80], self.qa[h, :, cols]))
                if diagonal:
                    p = jnp.where(causal, p, 0.0)
                new.append(accs[h] + dot(self.vt[slot, :, rows], p.astype(BF16)))
            return tuple(new)

        accs = tuple(jnp.zeros((80, BLOCK), F32) for _ in range(heads.queries))
        accs = lax.fori_loop(0, i, lambda j, c: step(j, c, False), accs)
        accs = step(i, accs, True)
        row = lax.broadcasted_iota(jnp.int32, (16, BLOCK), 0)
        lead = self.merged.shape[1] - heads.wide
        outs = [jnp.zeros((lead, BLOCK), F32)] if lead else []
        for h in range(heads.queries):
            total = accs[h][D:D + 1]
            o = accs[h][:D] * (1.0 / total)
            self.o[h, :, cols] = o
            outs.append(o)
            pieces = split3(-jnp.log(total))
            old = self.qa[h, 64:80, cols].astype(F32)
            extra = jnp.where(row == 8, pieces[0],
                              jnp.where(row == 9, pieces[1], jnp.where(row == 10, pieces[2], old)))
            self.qa[h, 64:80, cols] = extra.astype(BF16)
        merged = jnp.transpose(jnp.concatenate(outs, axis=0)).astype(BF16)
        self.merged[cols, :] = merged
        return merged


class Backward:
    def __init__(self, heads, me, table, gq, gk, raw, o, qa, ka, kt, vt, inv, doa, dopad, qpad, va, dq, acc):
        self.heads, self.table, self.gq, self.gk = heads, table, gq[...], gk[...]
        self.raw, self.o, self.qa, self.ka, self.kt, self.vt, self.inv = raw, o, qa, ka, kt, vt, inv
        self.doa, self.dopad, self.qpad, self.va, self.dq, self.acc = doa, dopad, qpad, va, dq, acc
        self.slots = [heads.slot(me, h) for h in range(heads.queries)]

    def prepare(self, b):
        heads = self.heads
        tok = self.table.shape[2]
        lanes = span(b * tok, tok)
        for h in range(heads.queries):
            q = jnp.concatenate([jnp.zeros((D, tok), F32), self.qa[h, 0:D, lanes].astype(F32)], axis=0)
            self.qpad[h, lanes, :] = jnp.transpose(q).astype(BF16)
            self.acc[h, lanes, :] = jnp.zeros((tok, 2 * D), F32)
        for g in range(heads.pairs):
            v = jnp.concatenate([self.vt[g, 0:D, lanes].astype(F32), jnp.ones((D, tok), F32)], axis=0)
            self.va[g, lanes, :] = jnp.transpose(v).astype(BF16)

    def gradient(self, b, dm):
        heads = self.heads
        tok = self.table.shape[2]
        lanes = span(b * tok, tok)
        row = lax.broadcasted_iota(jnp.int32, (16, tok), 0)
        dmt = jnp.transpose(dm.astype(BF16).astype(F32))
        for h in range(heads.queries):
            do = dmt[h * D:(h + 1) * D]
            delta = jnp.sum(do * self.o[h, :, lanes], axis=0, keepdims=True)
            pieces = split3(-delta)
            extra = jnp.where(row == 0, pieces[0],
                              jnp.where(row == 1, pieces[1], jnp.where(row == 2, pieces[2], 0.0)))
            self.doa[h, :, lanes] = jnp.concatenate([do, extra], axis=0).astype(BF16)
            both = jnp.concatenate([do, jnp.zeros((D, tok), F32)], axis=0)
            self.dopad[h, lanes, :] = jnp.transpose(both).astype(BF16)

    def query_block(self, i):
        heads = self.heads
        cols = span(i * BLOCK, BLOCK)
        causal = (lax.broadcasted_iota(jnp.int32, (BLOCK, BLOCK), 0)
                  <= lax.broadcasted_iota(jnp.int32, (BLOCK, BLOCK), 1))

        def step(j, accs, diagonal):
            rows = span(j * BLOCK, BLOCK)
            new = []
            for h in range(heads.queries):
                slot = self.slots[h]
                p = jnp.exp(dot(self.ka[slot, rows, 0:80], self.qa[h, :, cols]))
                if diagonal:
                    p = jnp.where(causal, p, 0.0)
                dp = dot(self.va[slot, rows, 0:80], self.doa[h, :, cols])
                ds = (p * dp).astype(BF16)
                self.acc[h, rows, :] += dot(p.astype(BF16), self.dopad[h, cols, :]) + dot(ds, self.qpad[h, cols, :])
                new.append(accs[h] + dot(self.kt[slot, :, rows], ds))
            return tuple(new)

        accs = tuple(jnp.zeros((D, BLOCK), F32) for _ in range(heads.queries))
        accs = lax.fori_loop(0, i, lambda j, c: step(j, c, False), accs)
        accs = step(i, accs, True)
        for h in range(heads.queries):
            self.dq[h, :, cols] = accs[h]

    def finish(self, b, sums):
        heads = self.heads
        tok = self.table.shape[2]
        lanes = span(b * tok, tok)
        cos = self.table[b, 0:HALF, :]
        sin = self.table[b, HALF:D, :]
        scale = self.table[b, 72:73, :]

        def back(grad, raw, inv, gain):
            a, c = grad[:HALF], grad[HALF:]
            n = jnp.concatenate([a * cos + c * sin, c * cos - a * sin], axis=0)
            v = n * gain
            out = inv * v - raw * (inv * inv * inv) * jnp.mean(v * raw, axis=0, keepdims=True)
            return out * scale, n * raw * inv

        sum_q, sum_k = sums
        pairs = [jnp.zeros((2 * D, tok), F32) for _ in range(heads.pairs)]
        out = []
        for h in range(heads.queries):
            raw = self.raw[h * D:(h + 1) * D, lanes]
            grad, part = back(self.dq[h, :, lanes] * (D ** -0.5), raw, self.inv[h:h + 1, lanes], self.gq)
            out.append(grad)
            sum_q = sum_q + part
            both = jnp.transpose(self.acc[h, lanes, :])
            for g in range(heads.pairs):
                pairs[g] = pairs[g] + jnp.where(self.slots[h] == g, both, 0.0)
        for g in range(heads.pairs):
            start = heads.wide + g * D
            raw = self.raw[start:start + D, lanes]
            inv = self.inv[heads.queries + g:heads.queries + g + 1, lanes]
            grad, part = back(pairs[g][D:], raw, inv, self.gk)
            out.append(grad)
            sum_k = sum_k + part
        for g in range(heads.pairs):
            out.append(pairs[g][:D] * scale)
        return jnp.concatenate(out, axis=0), (sum_q, sum_k)


def kept_shapes(heads, length, lead):
    return (
        jax.ShapeDtypeStruct((heads.wide + heads.narrow, length), F32),
        jax.ShapeDtypeStruct((length, lead + heads.wide), BF16),
        jax.ShapeDtypeStruct((heads.queries, D, length), F32),
        jax.ShapeDtypeStruct((heads.queries, 80, length), BF16),
        jax.ShapeDtypeStruct((heads.pairs, length, 128), BF16),
        jax.ShapeDtypeStruct((heads.pairs, D, length), BF16),
        jax.ShapeDtypeStruct((heads.pairs, 80, length), BF16),
        jax.ShapeDtypeStruct((8, length), F32),
    )


def backward_scratch(heads, length):
    return [
        pltpu.VMEM((heads.queries, 80, length), BF16),
        pltpu.VMEM((heads.queries, length, 2 * D), BF16),
        pltpu.VMEM((heads.queries, length, 2 * D), BF16),
        pltpu.VMEM((heads.pairs, length, 2 * D), BF16),
        pltpu.VMEM((heads.queries, D, length), F32),
        pltpu.VMEM((heads.queries, length, 2 * D), F32),
    ]


def local_forward_kernel(heads, proj_ref, table_ref, gq_ref, gk_ref, *kept):
    forward = Forward(heads, lax.axis_index("seq"), table_ref, gq_ref, gk_ref, *kept)
    blocks, _, tok = table_ref.shape

    def prepare(b, _):
        rows = span(b * tok, tok)
        forward.prepare(b, jnp.transpose(proj_ref[rows, :]) * table_ref[b, 72:73, :])
        return 0

    def query_block(i, _):
        forward.query_block(i)
        return 0

    lax.fori_loop(0, blocks, prepare, 0)
    lax.fori_loop(0, blocks * tok // BLOCK, query_block, 0)


def local_backward_kernel(heads, dm_ref, table_ref, gq_ref, gk_ref, raw_ref, o_ref, qa_ref, ka_ref, kt_ref, vt_ref, inv_ref,
                          pg_ref, gains_ref, *scratch):
    backward = Backward(heads, lax.axis_index("seq"), table_ref, gq_ref, gk_ref, raw_ref, o_ref, qa_ref, ka_ref, kt_ref,
                        vt_ref, inv_ref, *scratch)
    blocks, _, tok = table_ref.shape

    def prepare(b, _):
        backward.prepare(b)
        backward.gradient(b, dm_ref[span(b * tok, tok), :])
        return 0

    def query_block(i, _):
        backward.query_block(i)
        return 0

    def finish(b, sums):
        grad, sums = backward.finish(b, sums)
        pg_ref[span(b * tok, tok), :] = jnp.transpose(grad).astype(BF16)
        return sums

    lax.fori_loop(0, blocks, prepare, 0)
    lax.fori_loop(0, blocks * tok // BLOCK, query_block, 0)
    zero = jnp.zeros((D, tok), F32)
    sum_q, sum_k = lax.fori_loop(0, blocks, finish, (zero, zero))
    gains_ref[0:D, :] = jnp.broadcast_to(jnp.sum(sum_q, axis=1, keepdims=True), (D, 128))
    gains_ref[D:2 * D, :] = jnp.broadcast_to(jnp.sum(sum_k, axis=1, keepdims=True), (D, 128))


def attention_kernel(heads, x_hbm, g_hbm, w_hbm, gate_hbm, up_hbm, down_hbm, table_ref, gq_ref, gk_ref,
                     res_ref, g_all, gate_all, up_all, down_all, raw_ref, merged_ref, o_ref, qa_ref, ka_ref, kt_ref, vt_ref, inv_ref,
                     x_ref, w_ref, part_ref, sibling_ref, passing_ref, final_ref, rs_send, rs_recv,
                     ag_send, ag_recv, load_sem, own_sem, z_send, z_recv):
    place = Place()
    blocks, tok, model = x_ref.shape
    slabs = ((gate_hbm, gate_all), (up_hbm, up_all), (down_hbm, down_all))
    keep_slabs = [pltpu.make_async_copy(own, every.at[place.row], own_sem.at[i]) for i, (own, every) in enumerate(slabs)]
    for copy in keep_slabs:
        copy.start()
    load_w = pltpu.make_async_copy(w_hbm, w_ref, load_sem.at[blocks])
    load_w.start()
    loads = [pltpu.make_async_copy(x_hbm.at[b], x_ref.at[b], load_sem.at[b]) for b in range(blocks)]
    for copy in loads:
        copy.start()
    keep_own = pltpu.make_async_copy(g_hbm, g_all.at[place.me], load_sem.at[blocks + 1])
    keep_own.start()
    place.greet(4)
    gather = Gather(place, g_hbm, g_all, ag_send, ag_recv)
    scatter = Scatter(place, part_ref, sibling_ref, passing_ref, final_ref, rs_send, rs_recv)
    line = Line(place)
    weights = [RowGather(line, own, every, z_send.at[i], z_recv.at[i]) for i, (own, every) in enumerate(slabs)]
    for one in weights:
        one.start()
    gather.start()
    forward = Forward(heads, place.me, table_ref, gq_ref, gk_ref, raw_ref, merged_ref, o_ref, qa_ref, ka_ref, kt_ref,
                      vt_ref, inv_ref)
    load_w.wait()
    for copy in loads:
        copy.wait()

    def prepare(b, _):
        proj = dot(x_ref[b], w_ref[:, 0:512])
        forward.prepare(b, jnp.transpose(proj) * table_ref[b, 72:73, :])
        return 0

    lax.fori_loop(0, blocks, prepare, 0)
    tile = 512

    def compute(k):
        merged = forward.query_block(place.chips[k])

        def model_tile(n, _):
            cols = span(n * tile, tile)
            out = dot_nt(merged_ref[span(place.chips[k] * BLOCK, BLOCK), :], w_ref[cols, 384:640])
            part_ref[k, :, :, cols] = out.astype(BF16).reshape(2, tok, tile)
            return 0

        lax.fori_loop(0, model // tile, model_tile, 0)
        scatter.exchange[k].start()

    compute(3)
    gather.own_chip()
    gather.neighbours()
    scatter.combine(3)
    scatter.pass1.start()
    scatter.pass2.start()
    compute(1)
    scatter.combine(1)
    scatter.first1.start()
    gather.chip1()
    gather.chip2()
    weights[0].forward()
    compute(2)
    scatter.combine(2)
    scatter.first2.start()
    gather.diagonal()
    compute(0)
    scatter.combine(0)
    weights[1].forward()
    scatter.finish_two()
    gather.chip3()
    scatter.arrive()

    def finish(i, _):
        rows = span(i * 32, 32)
        res_ref[rows, :] = x_ref[place.me, rows, :].astype(F32) + scatter.total(rows)
        return 0

    lax.fori_loop(0, tok // 32, finish, 0)
    weights[2].forward()
    for one in weights:
        one.finish()
        one.close()
    for copy in keep_slabs:
        copy.wait()
    keep_own.wait()
    gather.close()
    scatter.close()


def attention_phase(heads, x_all, g, w, slabs, table, gq, gk):
    blocks, tok, model = x_all.shape
    dma = pltpu.SemaphoreType.DMA
    lead = 256 - heads.wide
    kept = kept_shapes(heads, blocks * tok, lead)
    return pl.pallas_call(
        functools.partial(attention_kernel, heads),
        out_shape=(jax.ShapeDtypeStruct((tok, model), F32), jax.ShapeDtypeStruct((blocks, tok, model), BF16))
        + tuple(jax.ShapeDtypeStruct((4,) + slab.shape, BF16) for slab in slabs) + kept,
        in_specs=[ANY_SPEC] * 6 + [VMEM_SPEC] * 3,
        out_specs=(VMEM_SPEC,) + (ANY_SPEC,) * 4 + (VMEM_SPEC,) * len(kept),
        scratch_shapes=[
            pltpu.VMEM((blocks, tok, model), BF16),
            pltpu.VMEM((model, heads.columns), BF16),
            *scatter_scratch(tok, model),
            dma((GATHER_SLOTS,)), dma((GATHER_SLOTS,)), dma((blocks + 2,)),
            dma((3,)), dma((3, ROW_SLOTS)), dma((3, ROW_SLOTS)),
        ],
        compiler_params=pltpu.CompilerParams(collective_id=1, has_side_effects=True, vmem_limit_bytes=VMEM_LIMIT),
        cost_estimate=pl.CostEstimate(flops=40 << 30, bytes_accessed=64 << 20, transcendentals=0),
    )(x_all, g, w, *slabs, table, gq, gk)


def ffn_kernel(res_ref, gain_ref, g_hbm, gate_hbm, up_hbm, down_hbm,
               out_hbm, rgrad_ref, branch_ref, gain_grad_ref, gate_grad_hbm, up_grad_hbm, down_grad_hbm,
               two_ref, g_ref, gate_ref, up_ref, down_ref, hid_ref, gu_ref, stage_ref, wstage_ref,
               part_ref, sibling_ref, passing_ref, final_ref, rs_send, rs_recv,
               ag_send, ag_recv, load_sem, stage_sem, wstage_sem, down_sem):
    place = Place()
    _, tok, model = g_ref.shape
    ff = gate_ref.shape[1]
    tile = 256
    share = model // 4
    loads = [pltpu.make_async_copy(src, dst, load_sem.at[i]) for i, (src, dst) in enumerate(
        [(gate_hbm, gate_ref), (up_hbm, up_ref), (g_hbm, g_ref)]
        + [(down_hbm.at[r], down_ref.at[:, r * share:(r + 1) * share]) for r in range(4)])]
    for copy in loads:
        copy.start()

    def norm_rows(i, _):
        rows = pl.ds(pl.multiple_of(i * 32, 32), 32)
        res = res_ref[rows, :]
        inv = lax.rsqrt(jnp.mean(res * res, axis=-1, keepdims=True) + EPSILON)
        two_ref[place.me, rows, :] = (res * inv * gain_ref[...]).astype(BF16)
        return 0

    lax.fori_loop(0, tok // 32, norm_rows, 0)
    place.greet()
    gather = Gather(place, two_ref.at[place.me], two_ref, ag_send, ag_recv)
    scatter = Scatter(place, part_ref, sibling_ref, passing_ref, final_ref, rs_send, rs_recv)
    gather.start()
    for copy in loads:
        copy.wait()

    def stage_copy(k):
        return pltpu.make_async_copy(stage_ref.at[k % 2], out_hbm.at[k], stage_sem.at[k % 2])

    def compute(k):
        m = place.chips[k]
        pair = pl.ds(2 * m, 2)

        def hidden_tile(h, _):
            cols = pl.ds(pl.multiple_of(h * tile, tile), tile)
            cols2 = pl.ds(pl.multiple_of(ff + h * tile, tile), tile)
            x = two_ref[pair].reshape(2 * tok, model)
            gate = dot(x, gate_ref[:, cols])
            up = dot(x, up_ref[:, cols])
            back = dot_nt(g_ref[pair].reshape(2 * tok, model), down_ref[cols, :])
            s = 1.0 / (1.0 + jnp.exp(-gate))
            act = gate * s
            hid_ref[pair, :, cols] = (act * up).astype(BF16).reshape(2, tok, tile)
            gu_ref[pair, :, cols] = (back * up * s * (1.0 + gate * (1.0 - s))).astype(BF16).reshape(2, tok, tile)
            gu_ref[pair, :, cols2] = (back * act).astype(BF16).reshape(2, tok, tile)
            return 0

        lax.fori_loop(0, ff // tile, hidden_tile, 0)
        if k >= 2:
            stage_copy(k - 2).wait()

        def model_tile(n, _):
            cols = pl.ds(pl.multiple_of(n * tile, tile), tile)
            gg = gu_ref[pair, :, 0:ff].reshape(2 * tok, ff)
            ug = gu_ref[pair, :, ff:2 * ff].reshape(2 * tok, ff)
            back = dot_nt(gg, gate_ref[cols, :]) + dot_nt(ug, up_ref[cols, :])
            part_ref[k, :, :, cols] = back.astype(BF16).reshape(2, tok, tile)
            return 0

        lax.fori_loop(0, model // tile, model_tile, 0)
        scatter.exchange[k].start()

        def out_tile(n, _):
            cols = pl.ds(pl.multiple_of(n * tile, tile), tile)
            hid = hid_ref[pair].reshape(2 * tok, ff)
            out = dot(hid, down_ref[:, cols])
            stage_ref[k % 2, :, :, cols] = out.astype(BF16).reshape(2, tok, tile)
            return 0

        lax.fori_loop(0, model // tile, out_tile, 0)
        stage_copy(k).start()

    gather.own_chip()
    compute(0)
    gather.neighbours()
    gather.chip1()
    compute(1)
    gather.chip2()
    scatter.combine(1)
    scatter.first1.start()
    compute(2)
    gather.diagonal()
    scatter.combine(2)
    scatter.first2.start()
    gather.chip3()
    compute(3)
    scatter.combine(3)
    scatter.pass1.start()
    scatter.pass2.start()
    scatter.combine(0)

    blocks = two_ref.shape[0]

    def wstage_copies(i, slot):
        return (pltpu.make_async_copy(wstage_ref.at[slot, :, 0:ff], gate_grad_hbm.at[i], wstage_sem.at[slot, 0]),
                pltpu.make_async_copy(wstage_ref.at[slot, :, ff:2 * ff], up_grad_hbm.at[i], wstage_sem.at[slot, 1]))

    def gate_up_rows(i, _):
        cols = pl.ds(pl.multiple_of(i * tile, tile), tile)
        slot = lax.rem(i, 2)

        @pl.when(i >= 2)
        def _():
            for copy in wstage_copies(i - 2, slot):
                copy.wait()

        x = two_ref[:, :, cols].reshape(blocks * tok, tile)
        wstage_ref[slot] = dot_tn(x, gu_ref[...].reshape(blocks * tok, 2 * ff)).astype(BF16)
        for copy in wstage_copies(i, slot):
            copy.start()
        return 0

    count = model // tile
    lax.fori_loop(0, count // 2, gate_up_rows, 0)
    scatter.finish_two()
    lax.fori_loop(count // 2, count, gate_up_rows, 0)
    for i in (count - 2, count - 1):
        for copy in wstage_copies(i, i % 2):
            copy.wait()

    stage_copy(2).wait()
    stage_copy(3).wait()

    def down_rows(i, _):
        rows = pl.ds(pl.multiple_of(i * tile, tile), tile)
        h = hid_ref[:, :, rows].reshape(blocks * tok, tile)

        def down_cols(n, _):
            cols = pl.ds(pl.multiple_of(n * 512, 512), 512)
            g = g_ref[:, :, cols].reshape(blocks * tok, 512)
            stage_ref[0, i, :, cols] = dot_tn(h, g).astype(BF16)
            return 0

        lax.fori_loop(0, model // 512, down_cols, 0)
        return 0

    lax.fori_loop(0, ff // tile, down_rows, 0)
    down_out = [pltpu.make_async_copy(stage_ref.at[0, i, :, r * share:(r + 1) * share],
                                      down_grad_hbm.at[r, i * tile:(i + 1) * tile], down_sem.at[4 * i + r])
                for i in range(ff // tile) for r in range(4)]
    for copy in down_out:
        copy.start()

    scatter.arrive()

    def finish(i, sums):
        rows = pl.ds(pl.multiple_of(i * 32, 32), 32)
        res = res_ref[rows, :]
        inv = lax.rsqrt(jnp.mean(res * res, axis=-1, keepdims=True) + EPSILON)
        grad = scatter.total(rows)
        v = grad * gain_ref[...]
        mean = jnp.mean(v * res, axis=-1, keepdims=True)
        out = g_ref[place.me, rows, :].astype(F32) + inv * v - res * (inv * inv * inv * mean)
        rgrad_ref[rows, :] = out
        branch_ref[rows, :] = out.astype(BF16)
        return sums + jnp.sum(grad * res * inv, axis=0, keepdims=True)

    gain_grad_ref[...] = lax.fori_loop(0, tok // 32, finish, jnp.zeros((1, model), F32))
    for copy in down_out:
        copy.wait()
    gather.close()
    scatter.close()


def feed_forward(res, gain, g_all, gate, up, down):
    tok, model = res.shape
    ff = gate.shape[1]
    blocks = g_all.shape[0]
    any_spec = pl.BlockSpec(memory_space=pl.ANY)
    vmem = pl.BlockSpec(memory_space=pltpu.VMEM)
    return pl.pallas_call(
        ffn_kernel,
        out_shape=(
            jax.ShapeDtypeStruct((4, 2, tok, model), BF16),
            jax.ShapeDtypeStruct((tok, model), F32),
            jax.ShapeDtypeStruct((tok, model), BF16),
            jax.ShapeDtypeStruct((1, model), F32),
            jax.ShapeDtypeStruct((model // 256, 256, ff), BF16),
            jax.ShapeDtypeStruct((model // 256, 256, ff), BF16),
            jax.ShapeDtypeStruct((4, ff, model // 4), BF16),
        ),
        in_specs=[vmem, vmem] + [any_spec] * 4,
        out_specs=(any_spec, vmem, vmem, vmem, any_spec, any_spec, any_spec),
        scratch_shapes=[
            pltpu.VMEM((blocks, tok, model), BF16),
            pltpu.VMEM((blocks, tok, model), BF16),
            pltpu.VMEM((model, ff), BF16),
            pltpu.VMEM((model, ff), BF16),
            pltpu.VMEM((ff, model), BF16),
            pltpu.VMEM((blocks, tok, ff), BF16),
            pltpu.VMEM((blocks, tok, 2 * ff), BF16),
            pltpu.VMEM((2, 2, tok, model), BF16),
            pltpu.VMEM((2, 256, 2 * ff), BF16),
            *scatter_scratch(tok, model),
            pltpu.SemaphoreType.DMA((GATHER_SLOTS,)),
            pltpu.SemaphoreType.DMA((GATHER_SLOTS,)),
            pltpu.SemaphoreType.DMA((7,)),
            pltpu.SemaphoreType.DMA((2,)),
            pltpu.SemaphoreType.DMA((2, 2)),
            pltpu.SemaphoreType.DMA((8,)),
        ],
        compiler_params=pltpu.CompilerParams(collective_id=2, has_side_effects=True, vmem_limit_bytes=60 * 1024 * 1024),
        cost_estimate=pl.CostEstimate(flops=18 * blocks * tok * model * ff, bytes_accessed=64 << 20, transcendentals=0),
    )(res, gain, g_all, gate, up, down)


def backward_kernel(heads, branch_hbm, out_hbm, x_hbm, w_hbm, gate_grad, up_grad, down_grad,
                    table_ref, gq_ref, gk_ref, small_in, merged_hbm,
                    raw_ref, o_ref, qa_ref, ka_ref, kt_ref, vt_ref, inv_ref,
                    ysum_ref, outsum_ref, grad_hbm, gate_recv, up_recv, down_recv, attn_recv, attn_merge, pieces_out, small_out,
                    every_ref, w_ref, pg_ref, merged_ref, xt_ref, wstage_ref,
                    doa_ref, dopad_ref, qpad_ref, va_ref, dq_ref, acc_ref,
                    part_ref, sibling_ref, passing_ref, final_ref, rs_send, rs_recv, rs2_send, rs2_recv,
                    ag_send, ag_recv, load_sem, xt_sem, wstage_sem, ready_sem,
                    ffn_merge, ffn_own, z_send, z_recv, own_sem, small_ref, small_row, small_mid, small_last,
                    s_send, s_recv, t_send, t_recv, p_send, p_recv):
    place = Place()
    blocks, tok, model = every_ref.shape
    load_w = pltpu.make_async_copy(w_hbm, w_ref, load_sem.at[0])
    load_out = pltpu.make_async_copy(out_hbm, part_ref, load_sem.at[1])
    load_own = pltpu.make_async_copy(branch_hbm, every_ref.at[place.me], load_sem.at[2])
    load_merged = pltpu.make_async_copy(merged_hbm, merged_ref, load_sem.at[3])
    load_own.start()
    load_w.start()
    load_out.start()
    load_merged.start()
    place.greet_all(4)
    gather = Gather(place, branch_hbm, every_ref, ag_send, ag_recv)
    gather.start()
    line = Line(place)
    ffn = [RowScatter(line, part, recv, ffn_merge.at[i], ffn_merge.at[i], z_send.at[i], z_recv.at[i])
           for i, (part, recv) in enumerate(((gate_grad, gate_recv), (up_grad, up_recv), (down_grad, down_recv)))]
    for one in ffn:
        one.start_over()
    for one in ffn:
        one.start()

    def ffn_add(i):
        own = (gate_grad, up_grad, down_grad)[i]

        def work():
            load = pltpu.make_async_copy(own.at[line.c], ffn_own, own_sem.at[0])
            load.start()
            load.wait()

            def add(n, _):
                rows = span(n * 64, 64)
                ffn_merge[i, rows, :] = (ffn_merge[i, rows, :].astype(F32) + ffn_own[rows, :].astype(F32)).astype(BF16)
                return 0

            lax.fori_loop(0, ffn_own.shape[0] // 64, add, 0)

        ffn[i].add(work)

    first = Scatter(place, part_ref, sibling_ref, passing_ref, final_ref, rs_send, rs_recv)
    second = Scatter(place, part_ref, sibling_ref, passing_ref, final_ref, rs2_send, rs2_recv)
    back = Backward(heads, place.me, table_ref, gq_ref, gk_ref, raw_ref, o_ref, qa_ref, ka_ref, kt_ref, vt_ref, inv_ref,
                    doa_ref, dopad_ref, qpad_ref, va_ref, dq_ref, acc_ref)
    lead = 256 - heads.wide

    def prepare(b, _):
        back.prepare(b)
        return 0

    lax.fori_loop(0, blocks, prepare, 0)
    load_out.wait()
    for copy in first.exchange:
        copy.start()
    load_w.wait()
    load_own.wait()

    def compute(k):
        m = place.chips[k]

        def gradient(j, _):
            b = 2 * m + j
            dm = dot(every_ref[b], w_ref[:, 384:640])
            back.gradient(b, dm[:, lead:])
            return 0

        lax.fori_loop(0, 2, gradient, 0)
        back.query_block(m)

    gather.own_chip()
    compute(0)
    gather.neighbours()
    first.combine(3)
    first.pass1.start()
    first.pass2.start()
    ffn_add(0)
    gather.chip1()
    compute(1)
    first.combine(1)
    first.first1.start()
    gather.chip2()
    ffn_add(1)
    compute(2)
    first.combine(2)
    first.first2.start()
    gather.diagonal()
    first.combine(0)
    gather.chip3()
    ffn_add(2)
    compute(3)
    first.finish_two()

    pad = 512 - heads.qkv

    def finish(b, sums):
        grad, sums = back.finish(b, sums)
        grad = jnp.concatenate([grad, jnp.zeros((pad, tok), F32)], axis=0)
        pg_ref[b] = jnp.transpose(grad).astype(BF16)
        return sums

    zero = jnp.zeros((D, tok), F32)
    sum_q, sum_k = lax.fori_loop(0, blocks, finish, (zero, zero))
    head_gains = jnp.sum(jnp.transpose(jnp.concatenate([sum_q, sum_k], axis=0)), axis=0, keepdims=True)
    row8 = lax.broadcasted_iota(jnp.int32, (8, 128), 0)
    for r in range(4):
        for n in range(PLANE):
            small_ref[r, n] = jnp.where(row8 == 1, head_gains, small_in[r, n])
    small_sends = []
    for j in range(1, 4):
        other = lax.rem(place.row + j, 4)
        small_sends.append(line.send(small_ref.at[other], small_row.at[place.row], s_send, j, s_recv, j, other))
    for copy in small_sends:
        copy.start()
    small_row[place.row] = small_ref[place.row]
    load_merged.wait()

    tile = 256
    count = model // tile

    def x_copy(i, slot):
        return pltpu.make_async_copy(x_hbm.at[:, :, span(i * tile, tile)], xt_ref.at[slot], xt_sem.at[slot])

    def grad_copy(i, slot):
        return pltpu.make_async_copy(wstage_ref.at[slot], grad_hbm.at[i // 2, lax.rem(i, 2)], wstage_sem.at[slot])

    x_copy(0, 0).start()

    def weight_rows(i, _):
        slot = lax.rem(i, 2)
        cols = span(i * tile, tile)

        @pl.when(i + 1 < count)
        def _():
            x_copy(i + 1, 1 - slot).start()

        @pl.when(i >= 2)
        def _():
            grad_copy(i - 2, slot).wait()

        out = dot_tn(every_ref[:, :, cols].reshape(blocks * tok, tile), merged_ref[...])
        x_copy(i, slot).wait()
        x = xt_ref[slot].reshape(blocks * tok, tile)
        qkv = dot_tn(x, pg_ref[...].reshape(blocks * tok, 512))
        wstage_ref[slot, :, 0:heads.qkv] = qkv[:, 0:heads.qkv].astype(BF16)
        wstage_ref[slot, :, heads.qkv:heads.columns] = out[:, lead:].astype(BF16)
        grad_copy(i, slot).start()
        return 0

    lax.fori_loop(0, count, weight_rows, 0)
    for i in (count - 2, count - 1):
        grad_copy(i, i % 2).wait()
    columns = heads.columns
    gather.close()
    merged_term = every_ref.at[0:2, :, 0:columns]
    attn = RowScatter(line, grad_hbm, attn_recv, attn_merge, merged_term, z_send.at[3], z_recv.at[3])
    attn.start_over()
    attn.start()
    own_term = pltpu.make_async_copy(grad_hbm.at[place.row], every_ref.at[6:8, :, 0:columns], own_sem.at[1])
    own_term.start()
    first.arrive()

    def take(out_ref, scatter):
        def one(i, _):
            rows = span(i * 32, 32)
            out_ref[rows, :] = scatter.total(rows)
            return 0

        lax.fori_loop(0, tok // 32, one, 0)

    take(outsum_ref, first)
    first.close()
    for other in (place.sib, place.same[1], place.same[2]):
        pl.semaphore_signal(ready_sem, inc=1, device_id=(place.row, other), device_id_type=MESH)
    pl.semaphore_wait(ready_sem, 3)

    def project(k):
        m = place.chips[k]

        def model_tile(n, _):
            cols = span(n * 512, 512)
            out = dot_nt(pg_ref[pl.ds(2 * m, 2)].reshape(2 * tok, 512), w_ref[cols, 0:512])
            part_ref[k, :, :, cols] = out.astype(BF16).reshape(2, tok, 512)
            return 0

        lax.fori_loop(0, model // 512, model_tile, 0)
        second.exchange[k].start()

    def add_blocks(target, source):
        def add(n, _):
            b, rows = n // 4, span(lax.rem(n, 4) * 64, 64)
            every_ref[target + b, rows, 0:columns] = (
                every_ref[target + b, rows, 0:columns].astype(F32) + every_ref[source + b, rows, 0:columns].astype(F32)
            ).astype(BF16)
            return 0

        lax.fori_loop(0, 8, add, 0)

    def attn_work():
        loads = [pltpu.make_async_copy(src, every_ref.at[2 * n:2 * n + 2, :, 0:columns], own_sem.at[2 + n])
                 for n, src in enumerate((attn_merge, grad_hbm.at[line.c]))]
        for copy in loads:
            copy.start()
        for copy in loads:
            copy.wait()
        add_blocks(0, 2)

    project(3)
    project(1)
    second.combine(3)
    second.pass1.start()
    second.pass2.start()
    project(2)
    attn.add(attn_work)
    second.combine(1)
    second.first1.start()
    project(0)
    second.combine(2)
    second.first2.start()
    second.combine(0)
    second.finish_two()
    for copy in small_sends:
        copy.wait_recv()
    small_mid[...] = (small_row[0] + small_row[1]) + (small_row[2] + small_row[3])
    plane_sends = []
    for j in range(1, PLANE):
        other = lax.rem(place.me + j, PLANE)
        plane_sends.append(place.send(small_mid.at[other], small_last.at[place.me], t_send, t_recv, j, other))
    for copy in plane_sends:
        copy.start()
    small_last[place.me] = small_mid[place.me]
    second.arrive()
    take(ysum_ref, second)
    for one in ffn:
        one.finish()
        one.close()
    for copy in plane_sends:
        copy.wait_recv()
    total = small_last[0]
    for n in range(1, PLANE):
        total = total + small_last[n]
    small_out[...] = total
    own_term.wait()
    attn.finish()

    def fold(slot):
        load = pltpu.make_async_copy(attn_recv.at[slot], every_ref.at[4:6, :, 0:columns], own_sem.at[4 + slot])
        load.start()
        load.wait()
        add_blocks(6, 4)

    fold(0)
    fold(2)

    @pl.when(line.middle)
    def _():
        fold(1)

    def piece(n):
        return every_ref.at[6 + n // 4, span(lax.rem(n, 4) * 64, 64), 0:columns]

    keep = pltpu.make_async_copy(piece(place.me), pieces_out.at[place.me], own_sem.at[7])
    keep.start()
    for j in range(1, PLANE):
        other = lax.rem(place.me + j, PLANE)
        copy = place.send(piece(other), pieces_out.at[place.me], p_send, p_recv, j, other)
        copy.start()
        plane_sends.append(copy)
    for copy in plane_sends[PLANE - 1:]:
        copy.wait_recv()
    keep.wait()
    for copy in plane_sends + small_sends:
        copy.wait_send()
    attn.close()
    second.close()


def backward_phase(heads, branch, out_part, x_all, w, weight_grads, table, gq, gk, small, kept):
    blocks, tok, model = x_all.shape
    length = blocks * tok
    dma = pltpu.SemaphoreType.DMA
    raw, merged, *rest = kept
    return pl.pallas_call(
        functools.partial(backward_kernel, heads),
        out_shape=(
            jax.ShapeDtypeStruct((tok, model), F32),
            jax.ShapeDtypeStruct((tok, model), F32),
            jax.ShapeDtypeStruct((4, 2, 256, heads.columns), BF16),
            *(jax.ShapeDtypeStruct((3,) + grad.shape[1:], BF16) for grad in weight_grads),
            jax.ShapeDtypeStruct((3, 2, 256, heads.columns), BF16),
            jax.ShapeDtypeStruct((2, 256, heads.columns), BF16),
            jax.ShapeDtypeStruct((PLANE, 64, heads.columns), BF16),
            jax.ShapeDtypeStruct((8, 128), F32),
        ),
        in_specs=[ANY_SPEC] * 7 + [VMEM_SPEC] * 4 + [ANY_SPEC] + [VMEM_SPEC] * (1 + len(rest)),
        out_specs=(VMEM_SPEC, VMEM_SPEC) + (ANY_SPEC,) * 7 + (VMEM_SPEC,),
        scratch_shapes=[
            pltpu.VMEM((blocks, tok, model), BF16),
            pltpu.VMEM((model, heads.columns), BF16),
            pltpu.VMEM((blocks, tok, 512), BF16),
            pltpu.VMEM(merged.shape, BF16),
            pltpu.VMEM((2, blocks, tok, 256), BF16),
            pltpu.VMEM((2, 256, heads.columns), BF16),
            *backward_scratch(heads, length),
            *scatter_scratch(tok, model),
            dma((SCATTER_SLOTS,)), dma((SCATTER_SLOTS,)),
            dma((GATHER_SLOTS,)), dma((GATHER_SLOTS,)), dma((4,)), dma((2,)), dma((2,)),
            pltpu.SemaphoreType.REGULAR,
            pltpu.VMEM((3,) + weight_grads[0].shape[1:], BF16),
            pltpu.VMEM(weight_grads[0].shape[1:], BF16),
            dma((4, ROW_SLOTS)), dma((4, ROW_SLOTS)), dma((8,)),
            pltpu.VMEM((4, PLANE, 8, 128), F32),
            pltpu.VMEM((4, PLANE, 8, 128), F32),
            pltpu.VMEM((PLANE, 8, 128), F32),
            pltpu.VMEM((PLANE, 8, 128), F32),
            dma((4,)), dma((4,)), dma((PLANE,)), dma((PLANE,)), dma((PLANE,)), dma((PLANE,)),
        ],
        compiler_params=pltpu.CompilerParams(collective_id=3, has_side_effects=True, vmem_limit_bytes=62 * 1024 * 1024),
        cost_estimate=pl.CostEstimate(flops=60 << 30, bytes_accessed=64 << 20, transcendentals=0),
    )(branch, out_part, x_all, w, *weight_grads, table, gq, gk, small, merged, raw, *rest)


def norm_back(grad_normed, values_in, inv_rms, gain):
    scaled = grad_normed * gain
    gain_grad = jnp.sum(grad_normed * values_in * inv_rms, axis=0)
    input_grad = inv_rms * scaled - values_in * inv_rms**3 * jnp.mean(scaled * values_in, axis=-1, keepdims=True)
    return input_grad, gain_grad


def start_wide(rows, x, table, pieces, gain):
    return (
        lax.all_gather(x, "seq", axis=0, tiled=False),
        lax.all_gather(table, "seq", axis=0, tiled=False),
        lax.all_gather(lax.all_to_all(pieces, "seq", 0, 0, tiled=False), "rows", axis=0, tiled=False),
        lax.all_gather(lax.all_gather(gain, "seq", axis=0, tiled=False), "rows", axis=0, tiled=False),
    )


def scatter_rows(part, tok):
    return lax.psum_scatter(part.reshape(-1, part.shape[-1]), "seq", scatter_dimension=0, tiled=True).astype(F32)


def attention_wide(heads, x_all, g, w, table, gq, gk):
    blocks, tok, model = x_all.shape
    proj = dot(x_all.reshape(blocks * tok, model), w[:, :heads.qkv])
    kept = pl.pallas_call(
        functools.partial(local_forward_kernel, heads),
        out_shape=kept_shapes(heads, blocks * tok, 0),
        compiler_params=pltpu.CompilerParams(vmem_limit_bytes=VMEM_LIMIT),
    )(proj, table, gq, gk)
    total = scatter_rows(dot_nt(kept[1], w[:, heads.qkv:]).astype(BF16), tok)
    own = lax.dynamic_index_in_dim(x_all, lax.axis_index("seq"), 0, keepdims=False)
    return (own.astype(F32) + total, lax.all_gather(g, "seq", axis=0, tiled=False)) + tuple(kept)


def feed_forward_wide(res, gain, g_blocks, gate_slab, up_slab, down_slab):
    blocks, tok, model = g_blocks.shape
    inv = norm_inverse(res)
    two_all = lax.all_gather((res * inv * gain).astype(BF16), "seq", axis=0, tiled=True)
    g_all = g_blocks.reshape(blocks * tok, model)
    gate_act = dot(two_all, gate_slab)
    up_act = dot(two_all, up_slab)
    s = jax.nn.sigmoid(gate_act)
    hidden = (gate_act * s * up_act).astype(BF16)
    hidden_grad = dot_nt(g_all, down_slab)
    gate_grad = (hidden_grad * up_act * s * (1.0 + gate_act * (1.0 - s))).astype(BF16)
    up_grad = (hidden_grad * gate_act * s).astype(BF16)
    two_grad = scatter_rows((dot_nt(gate_grad, gate_slab) + dot_nt(up_grad, up_slab)).astype(BF16), tok)
    branch_part = dot(hidden, down_slab).astype(BF16).reshape(blocks, tok, model)
    norm_grad, gain_grad = norm_back(two_grad, res, inv, gain)
    g = lax.dynamic_index_in_dim(g_blocks, lax.axis_index("seq"), 0, keepdims=False)
    residual_grad = g.astype(F32) + norm_grad
    return (branch_part, residual_grad, residual_grad.astype(BF16), gain_grad[None],
            dot_tn(two_all, gate_grad).astype(BF16), dot_tn(two_all, up_grad).astype(BF16),
            dot_tn(hidden, g_all).astype(BF16))


def backward_wide(heads, branch, out_part, x_all, w, table, gq, gk, kept):
    blocks, tok, model = x_all.shape
    length = blocks * tok
    raw, merged, *rest = kept
    out_sum = scatter_rows(out_part, tok)
    branch_all = lax.all_gather(branch, "seq", axis=0, tiled=True)
    pg, gains = pl.pallas_call(
        functools.partial(local_backward_kernel, heads),
        out_shape=(jax.ShapeDtypeStruct((length, heads.qkv), BF16), jax.ShapeDtypeStruct((2 * D, 128), F32)),
        scratch_shapes=backward_scratch(heads, length),
        compiler_params=pltpu.CompilerParams(vmem_limit_bytes=VMEM_LIMIT),
    )(dot(branch_all, w[:, heads.qkv:]), table, gq, gk, raw, *rest)
    y_sum = scatter_rows(dot_nt(pg, w[:, :heads.qkv]).astype(BF16), tok)
    grad = jnp.concatenate([dot_tn(x_all.reshape(length, model), pg), dot_tn(branch_all, merged)], axis=1)
    return y_sum, out_sum, grad.astype(BF16), gains


def rotary_table(x, positions, segments):
    inverse = jnp.exp(-math.log(THETA) * jnp.arange(HALF, dtype=F32) * 2.0 / D)
    angles = inverse[:, None] * positions.astype(F32)[None, :]
    hot = jnp.arange(SEGMENT_KINDS, dtype=jnp.int32)[:, None] == segments[None, :]
    root = jnp.pad(norm_inverse(x).T, ((0, 7), (0, 0)))
    return jnp.concatenate([jnp.cos(angles), jnp.sin(angles), hot.astype(F32), root], axis=0)


def attention_pieces(heads, w_qkv, w_out):
    depth = w_qkv.shape[0]
    qw, kw = QUERY_HEADS * D, KEY_VALUE_HEADS * D
    out_t = w_out.T

    def columns(array, start, first, count, most):
        parts = []
        for i in range(count):
            n = first + i
            parts.append(array[:, start + n * D:start + (n + 1) * D] if n < most else jnp.zeros((depth, D), BF16))
        return parts

    pieces = []
    for s in range(heads.seq):
        q, k = s * heads.queries, heads.first(s)
        parts = (columns(w_qkv, 0, q, heads.queries, QUERY_HEADS)
                 + columns(w_qkv, qw, k, heads.pairs, KEY_VALUE_HEADS)
                 + columns(w_qkv, qw + kw, k, heads.pairs, KEY_VALUE_HEADS)
                 + columns(out_t, 0, q, heads.queries, QUERY_HEADS))
        pieces.append(jnp.concatenate(parts, axis=1))
    return jnp.stack(pieces)


def attention_sums(heads, pieces):
    depth = pieces.shape[1]
    cut = lambda s, start, n: pieces[s, :, start + n * D:start + (n + 1) * D]
    queries = [cut(n // heads.queries, 0, n % heads.queries) for n in range(QUERY_HEADS)]
    outs = [cut(n // heads.queries, heads.qkv, n % heads.queries) for n in range(QUERY_HEADS)]

    def pairs(start):
        found = []
        for n in range(KEY_VALUE_HEADS):
            terms = [cut(s, start, n - heads.first(s)) for s in range(heads.seq)
                     if s * heads.queries < QUERY_HEADS and 0 <= n - heads.first(s) < heads.pairs]
            found.append(functools.reduce(jnp.add, terms))
        return found

    qkv = jnp.concatenate(queries + pairs(heads.wide) + pairs(heads.wide + heads.narrow), axis=1)
    return qkv, jnp.concatenate(outs, axis=1)


def body(tokens, segments, positions, cotangent, gain_attn, w_qkv, gain_q, gain_k, w_out, gain_ffn, w_gate, w_up, w_down):
    seq = lax.axis_size("seq")
    rows = lax.axis_size("rows")
    heads = Heads(seq)
    depth = w_qkv.shape[0]
    tok, model = tokens.shape[1:]
    plane = seq == PLANE and rows == 4
    row = lax.axis_index("rows")

    gq = gain_q.astype(F32)[:, None]
    gk = gain_k.astype(F32)[:, None]
    x = tokens[0].astype(F32)
    scaled = (w_qkv.astype(F32) * gain_attn.astype(F32)[:, None]).astype(BF16)
    pieces = attention_pieces(heads, scaled, w_out)
    gain = jnp.pad(gain_ffn.astype(F32)[None], ((0, 7), (0, 128 - depth)))
    x_all, table, w, gains = (start_phase if plane else start_wide)(
        rows, tokens[0], rotary_table(x, positions[0], segments[0]), pieces, gain)
    w = w.reshape(model, heads.columns)
    gain_two = gains[:, :, 0, :depth].reshape(1, model)
    inv = norm_inverse(x)

    if plane:
        residual, g_all, gate, up, down, *kept = attention_phase(
            heads, x_all, cotangent[0], w, (w_gate, w_up, w_down), table, gq, gk)
        out_part, residual_grad, branch, gain_two_grad, *weight_grads = feed_forward(
            residual, gain_two, g_all, gate.reshape(model, -1), up.reshape(model, -1), down)
        weight_grads = [grad.reshape((4,) + w_gate.shape) for grad in weight_grads]
        small = jnp.pad(gain_two_grad.reshape(rows, seq, 1, depth), ((0, 0), (0, 0), (0, 7), (0, 128 - depth)))
        y_sum, out_sum, _, gate_recv, up_recv, down_recv, _, _, attn_grad, small = backward_phase(
            heads, branch, out_part, x_all, w, weight_grads, table, gq, gk, small, kept)
        middle = (row + 1) // 2 == 1

        def row_total(part, recv):
            own = lax.dynamic_index_in_dim(part, row, 0, keepdims=False).astype(F32)
            return own + recv[0].astype(F32) + recv[2].astype(F32) + jnp.where(middle, recv[1].astype(F32), 0.0)

        grad_gate, grad_up, grad_down = (
            row_total(part, recv) for part, recv in zip(weight_grads, (gate_recv, up_recv, down_recv)))
        grad_gain_ffn, head_gains = small[0, :depth], small[1]
    else:
        gate_slab = lax.all_gather(w_gate, "rows", axis=0, tiled=True)
        up_slab = lax.all_gather(w_up, "rows", axis=0, tiled=True)
        down_slab = lax.all_gather(w_down, "rows", axis=1, tiled=True)
        residual, g_all, *kept = attention_wide(heads, x_all, cotangent[0], w, table, gq, gk)
        out_part, residual_grad, branch, gain_two_grad, gate_wgrad, up_wgrad, down_wgrad = feed_forward_wide(
            residual, gain_two, g_all, gate_slab, up_slab, down_slab)
        grad_gate = lax.psum_scatter(gate_wgrad, "rows", scatter_dimension=0, tiled=True).astype(F32)
        grad_up = lax.psum_scatter(up_wgrad, "rows", scatter_dimension=0, tiled=True).astype(F32)
        grad_down = lax.psum_scatter(down_wgrad, "rows", scatter_dimension=1, tiled=True).astype(F32)
        y_sum, out_sum, attn_grad, head_gains = backward_wide(heads, branch, out_part, x_all, w, table, gq, gk, kept)
        attn_grad = lax.psum_scatter(attn_grad, "rows", scatter_dimension=0, tiled=True)
        attn_grad = lax.all_to_all(attn_grad.reshape(seq, depth, heads.columns), "seq", 0, 0, tiled=False)
        small = lax.psum(jnp.concatenate([gain_two_grad[0], head_gains[:, 0]]), ("rows", "seq"))
        grad_gain_ffn = lax.dynamic_slice_in_dim(small, (row * seq + lax.axis_index("seq")) * depth, depth)
        head_gains = small[model:]

    layer_out = (residual + out_sum).astype(BF16)
    grad_tokens = residual_grad + y_sum - x * (inv * inv * jnp.mean(y_sum * x, axis=-1, keepdims=True))
    unscaled, grad_out = attention_sums(heads, attn_grad.astype(F32))
    grad_gain_attn = jnp.sum(unscaled * w_qkv.astype(F32), axis=1)
    grad_qkv = unscaled * gain_attn.astype(F32)[:, None]
    return (
        layer_out[None],
        grad_tokens[None],
        grad_gain_attn,
        grad_qkv,
        head_gains[:D],
        head_gains[D:],
        grad_out.T,
        grad_gain_ffn,
        grad_gate,
        grad_up,
        grad_down,
    )


def solution(mesh):
    both = ("rows", "seq")
    return jax.shard_map(
        body,
        mesh=mesh,
        in_specs=(
            P("rows", "seq", None), P("rows", "seq"), P("rows", "seq"), P("rows", "seq", None),
            P(both), P(both, None), P(), P(), P(None, both), P(both),
            P("rows", "seq"), P("rows", "seq"), P("seq", "rows"),
        ),
        out_specs=(
            P("rows", "seq", None), P("rows", "seq", None), P(both), P(both, None), P(), P(),
            P(None, both), P(both), P("rows", "seq"), P("rows", "seq"), P("seq", "rows"),
        ),
        check_vma=False,
    )
```

```python
import functools
import math

import jax
import jax.numpy as jnp
from jax import lax
from jax.experimental import pallas as pl
from jax.experimental.pallas import tpu as pltpu
from jax.sharding import PartitionSpec as P

QUERY_HEADS = 24
KEY_VALUE_HEADS = 6
GROUP = QUERY_HEADS // KEY_VALUE_HEADS
D = 64
HALF = D // 2
EPSILON = 1e-06
THETA = 10000.0
PENALTY = -10000.0
SEGMENT_KINDS = 8
TABLE_ROWS = 80
BLOCK = 512
PLANE = 8
F32 = jnp.float32
BF16 = jnp.bfloat16
VMEM_LIMIT = 60 * 1024 * 1024
MESH = pl.DeviceIdType.MESH
ANY_SPEC = pl.BlockSpec(memory_space=pl.ANY)
VMEM_SPEC = pl.BlockSpec(memory_space=pltpu.VMEM)


def dot(a, b):
    return jnp.dot(a, b, preferred_element_type=F32)


def dot_nt(a, b):
    return lax.dot_general(a, b, (((1,), (1,)), ((), ())), preferred_element_type=F32)


def dot_tn(a, b):
    return lax.dot_general(a, b, (((0,), (0,)), ((), ())), preferred_element_type=F32)


def norm_inverse(x):
    return lax.rsqrt(jnp.mean(x * x, axis=-1, keepdims=True) + EPSILON)


def split3(x):
    high = x.astype(BF16).astype(F32)
    mid = (x - high).astype(BF16).astype(F32)
    return high, mid, x - high - mid


def span(start, size):
    return pl.ds(pl.multiple_of(start, size), size)


class Heads:
    def __init__(self, seq):
        self.seq = seq
        self.queries = -(-QUERY_HEADS // seq)
        last = [min((s + 1) * self.queries, QUERY_HEADS) - 1 for s in range(seq)]
        self.pairs = max(last[s] // GROUP - self.first(s) + 1 for s in range(seq) if last[s] >= s * self.queries)
        self.wide = self.queries * D
        self.narrow = self.pairs * D
        self.qkv = self.wide + 2 * self.narrow
        self.columns = self.qkv + self.wide

    def first(self, s):
        return (s * self.queries) // GROUP

    def slot(self, s, h):
        return (s * self.queries + h) // GROUP - (s * self.queries) // GROUP


class Place:
    def __init__(self):
        self.row = lax.axis_index("rows")
        self.me = lax.axis_index("seq")
        self.core = lax.rem(self.me, 2)
        self.chip = self.me // 2
        self.sib = self.me + 1 - 2 * self.core
        chip = self.chip
        self.chips = (chip, chip + 1 - 2 * lax.rem(chip, 2), lax.rem(chip + 2, 4), 3 - chip)
        self.same = tuple(2 * q + self.core for q in self.chips)

    def greet(self, rows=1):
        barrier = pltpu.get_barrier_semaphore()
        for other in (self.sib, self.same[1], self.same[2]):
            pl.semaphore_signal(barrier, inc=1, device_id=(self.row, other), device_id_type=MESH)
        for j in range(1, rows):
            other = lax.rem(self.row + j, rows)
            pl.semaphore_signal(barrier, inc=1, device_id=(other, self.me), device_id_type=MESH)
        pl.semaphore_wait(barrier, 3 + rows - 1)

    def greet_all(self, rows):
        barrier = pltpu.get_barrier_semaphore()
        for j in range(1, PLANE):
            other = lax.rem(self.me + j, PLANE)
            pl.semaphore_signal(barrier, inc=1, device_id=(self.row, other), device_id_type=MESH)
        for j in range(1, rows):
            other = lax.rem(self.row + j, rows)
            pl.semaphore_signal(barrier, inc=1, device_id=(other, self.me), device_id_type=MESH)
        pl.semaphore_wait(barrier, PLANE - 1 + rows - 1)

    def send(self, src, dst, send_sem, recv_sem, slot, target):
        return pltpu.make_async_remote_copy(
            src_ref=src, dst_ref=dst, send_sem=send_sem.at[slot], recv_sem=recv_sem.at[slot],
            device_id=(self.row, target), device_id_type=MESH)


class Line:
    def __init__(self, place):
        self.place = place
        row = place.row
        self.a = row + 1 - 2 * lax.rem(row, 2)
        self.b = 3 - row
        self.c = lax.rem(row + 2, 4)
        self.middle = (row + 1) // 2 == 1

    def send(self, src, dst, send_sem, send_slot, recv_sem, recv_slot, target):
        return pltpu.make_async_remote_copy(
            src_ref=src, dst_ref=dst, send_sem=send_sem.at[send_slot], recv_sem=recv_sem.at[recv_slot],
            device_id=(target, self.place.me), device_id_type=MESH)


ROW_SLOTS = 4


class RowGather:
    def __init__(self, line, own, at, send_sem, recv_sem):
        self.line = line
        mine, passed = at(line.place.row), at(line.c)
        self.to_a = line.send(own, mine, send_sem, 0, recv_sem, 0, line.a)
        self.to_c = line.send(own, mine, send_sem, 1, recv_sem, 1, line.c)
        self.to_b = line.send(own, mine, send_sem, 2, recv_sem, 2, line.b)
        self.on = line.send(passed, passed, send_sem, 3, recv_sem, 2, line.a)

    def start(self):
        self.to_c.start()
        self.to_a.start()

        @pl.when(self.line.middle)
        def _():
            self.to_b.start()

    def forward(self):
        self.to_c.wait_recv()

        @pl.when(self.line.middle)
        def _():
            self.on.start()

    def finish(self):
        self.to_a.wait_recv()
        self.to_b.wait_recv()

    def close(self):
        self.to_a.wait_send()
        self.to_c.wait_send()

        @pl.when(self.line.middle)
        def _():
            self.to_b.wait_send()
            self.on.wait_send()


class RowScatter:
    def __init__(self, line, part, recv, merge, total, send_sem, recv_sem):
        self.line, self.total = line, total
        self.to_a = line.send(part.at[line.a], recv.at[0], send_sem, 0, recv_sem, 0, line.a)
        self.to_b = line.send(part.at[line.b], recv.at[1], send_sem, 1, recv_sem, 1, line.b)
        self.to_c = line.send(part.at[line.c], recv.at[2], send_sem, 2, recv_sem, 2, line.c)
        self.added = line.send(total, recv.at[2], send_sem, 2, recv_sem, 2, line.c)
        self.over = line.send(part.at[line.b], merge, send_sem, 3, recv_sem, 3, line.a)

    def start_over(self):
        @pl.when(jnp.logical_not(self.line.middle))
        def _():
            self.over.start()

    def start(self):
        @pl.when(jnp.logical_not(self.line.middle))
        def _():
            self.to_c.start()

        @pl.when(self.line.middle)
        def _():
            self.to_b.start()

        self.to_a.start()

    def add(self, work):
        @pl.when(self.line.middle)
        def _():
            self.over.wait_recv()
            work()
            self.added.start()

    def finish(self):
        self.to_a.wait_recv()
        self.to_c.wait_recv()

        @pl.when(self.line.middle)
        def _():
            self.to_b.wait_recv()

    def close(self):
        self.to_a.wait_send()
        self.to_c.wait_send()

        @pl.when(self.line.middle)
        def _():
            self.to_b.wait_send()

        @pl.when(jnp.logical_not(self.line.middle))
        def _():
            self.over.wait_send()


GATHER_SLOTS = 10


class Gather:
    def __init__(self, place, own, every, send_sem, recv_sem):
        half = every.shape[1] // 2
        low, high, whole = slice(0, half), slice(half, 2 * half), slice(0, 2 * half)

        def send(part, b, slot, target, src=None):
            src = every.at[b, part] if src is None else src.at[part]
            return place.send(src, every.at[b, part], send_sem, recv_sem, slot, target)

        me, (_, s1, s2, s3), sib = place.me, place.same, place.sib
        self.copies = (
            send(whole, me, 0, sib, own),
            send(low, me, 1, s1, own), send(high, me, 2, s1, own),
            send(high, me, 3, s2, own), send(low, me, 4, s2, own),
            send(low, s1, 5, s2), send(high, s2, 6, s1),
            send(whole, s1, 7, sib), send(whole, s2, 8, sib), send(whole, s3, 9, sib),
        )

    def start(self):
        for slot in (1, 3, 2, 4, 0):
            self.copies[slot].start()

    def own_chip(self):
        self.copies[0].wait_recv()

    def neighbours(self):
        c = self.copies
        c[1].wait_recv()
        c[5].start()
        c[3].wait_recv()
        c[6].start()
        c[2].wait_recv()
        c[7].start()
        c[4].wait_recv()
        c[8].start()

    def chip1(self):
        self.copies[7].wait_recv()

    def chip2(self):
        self.copies[8].wait_recv()

    def diagonal(self):
        c = self.copies
        c[5].wait_recv()
        c[6].wait_recv()
        c[9].start()

    def chip3(self):
        self.copies[9].wait_recv()

    def close(self):
        for copy in self.copies:
            copy.wait_send()


SCATTER_SLOTS = 10


class Scatter:
    def __init__(self, place, part, sibling, passing, final, send_sem, recv_sem):
        self.place, self.part, self.sibling, self.passing, self.final = place, part, sibling, passing, final
        half = part.shape[2] // 2
        self.half = half
        core, other = place.core, 1 - place.core
        _, s1, s2, _ = place.same
        send = lambda src, dst, slot, target: place.send(src, dst, send_sem, recv_sem, slot, target)
        low, high = slice(0, half), slice(half, 2 * half)
        self.exchange = tuple(send(part.at[k, other], sibling.at[k], k, place.sib) for k in range(4))
        self.pass1 = send(part.at[3, core, low], passing.at[0], 4, s1)
        self.pass2 = send(part.at[3, core, high], passing.at[1], 5, s2)
        self.first1 = send(part.at[1, core, low], final.at[0, low], 6, s1)
        self.second1 = send(part.at[1, core, high], final.at[0, high], 7, s1)
        self.first2 = send(part.at[2, core, high], final.at[1, high], 8, s2)
        self.second2 = send(part.at[2, core, low], final.at[1, low], 9, s2)

    def add(self, k, start, size, term, offset):
        core, step = self.place.core, 64

        def one(i, _):
            rows = pl.ds(pl.multiple_of(start + i * step, step), step)
            from_rows = pl.ds(pl.multiple_of(offset + i * step, step), step)
            self.part[k, core, rows, :] = self.part[k, core, rows, :] + term[from_rows, :]
            return 0

        lax.fori_loop(0, size // step, one, 0)

    def combine(self, k):
        self.exchange[k].wait_recv()
        self.add(k, 0, 2 * self.half, self.sibling.at[k], 0)

    def finish_two(self):
        self.pass1.wait_recv()
        self.add(2, 0, self.half, self.passing.at[0], 0)
        self.second2.start()
        self.pass2.wait_recv()
        self.add(1, self.half, self.half, self.passing.at[1], 0)
        self.second1.start()

    def arrive(self):
        for copy in (self.first1, self.second1, self.first2, self.second2):
            copy.wait_recv()

    def total(self, rows):
        return (self.part[0, self.place.core, rows, :].astype(F32) + self.final[0, rows, :].astype(F32)
                + self.final[1, rows, :].astype(F32))

    def close(self):
        for copy in self.exchange + (self.pass1, self.pass2, self.first1, self.second1, self.first2, self.second2):
            copy.wait_send()


def scatter_scratch(tok, width):
    return [
        pltpu.VMEM((4, 2, tok, width), BF16),
        pltpu.VMEM((4, tok, width), BF16),
        pltpu.VMEM((2, tok // 2, width), BF16),
        pltpu.VMEM((2, tok, width), BF16),
        pltpu.SemaphoreType.DMA((SCATTER_SLOTS,)),
        pltpu.SemaphoreType.DMA((SCATTER_SLOTS,)),
    ]


def start_kernel(x_ref, table_ref, pieces_ref, gain_ref, x_all, table_all, w_all, gain_all,
                 x_send, x_recv, t_send, t_recv, p_send, p_recv, g_send, g_recv, z_send, z_recv, w_send, w_recv, local_sem):
    place = Place()
    rows = w_all.shape[0]
    me, row = place.me, place.row
    local = [pltpu.make_async_copy(src, dst, local_sem.at[i]) for i, (src, dst) in enumerate((
        (pieces_ref.at[me], w_all.at[row, me]), (gain_ref, gain_all.at[row, me]),
        (x_ref, x_all.at[me]), (table_ref, table_all.at[me])))]
    for copy in local:
        copy.start()
    place.greet_all(rows)
    exchange = []
    for j in range(1, PLANE):
        other = lax.rem(me + j, PLANE)
        exchange.append(place.send(pieces_ref.at[other], w_all.at[row, me], p_send, p_recv, j, other))
        exchange.append(place.send(gain_ref, gain_all.at[row, me], g_send, g_recv, j, other))
    for copy in exchange:
        copy.start()
    gathers = (Gather(place, x_ref, x_all, x_send, x_recv), Gather(place, table_ref, table_all, t_send, t_recv))
    gathers[1].start()
    gathers[0].start()
    for copy in local[:2]:
        copy.wait()
    for copy in exchange:
        copy.wait_recv()
    line = Line(place)
    weights = RowGather(line, w_all.at[row], lambda r: w_all.at[r], w_send, w_recv)
    weights.start()
    along = []
    for j in range(1, rows):
        other = lax.rem(row + j, rows)
        along.append(line.send(gain_all.at[row], gain_all.at[row], z_send, j, z_recv, j, other))
    for copy in along:
        copy.start()
    for name in ("own_chip", "neighbours"):
        for gather in gathers[::-1]:
            getattr(gather, name)()
    weights.forward()
    for name in ("chip1", "chip2", "diagonal", "chip3"):
        for gather in gathers[::-1]:
            getattr(gather, name)()
    weights.finish()
    weights.close()
    for copy in local[2:]:
        copy.wait()
    for copy in along:
        copy.wait_recv()
    for copy in exchange + along:
        copy.wait_send()
    for gather in gathers:
        gather.close()


def start_phase(rows, x, table, pieces, gain):
    tok, model = x.shape
    dma = pltpu.SemaphoreType.DMA
    return pl.pallas_call(
        start_kernel,
        out_shape=(
            jax.ShapeDtypeStruct((PLANE, tok, model), BF16),
            jax.ShapeDtypeStruct((PLANE,) + table.shape, F32),
            jax.ShapeDtypeStruct((rows,) + pieces.shape, BF16),
            jax.ShapeDtypeStruct((rows, PLANE) + gain.shape, F32),
        ),
        in_specs=[VMEM_SPEC] * 4,
        out_specs=(ANY_SPEC,) * 4,
        scratch_shapes=[dma((GATHER_SLOTS,))] * 4 + [dma((PLANE,))] * 4 + [dma((rows,))] * 2 + [dma((ROW_SLOTS,))] * 2 + [dma((4,))],
        compiler_params=pltpu.CompilerParams(collective_id=0, has_side_effects=True),
        cost_estimate=pl.CostEstimate(flops=0, bytes_accessed=160 << 20, transcendentals=0),
    )(x, table, pieces, gain)


class Forward:
    def __init__(self, heads, me, table, gq, gk, raw, merged, o, qa, ka, kt, vt, inv):
        self.heads, self.table, self.gq, self.gk = heads, table, gq[...], gk[...]
        self.raw, self.merged, self.o, self.qa, self.ka, self.kt, self.vt, self.inv = raw, merged, o, qa, ka, kt, vt, inv
        self.slots = [heads.slot(me, h) for h in range(heads.queries)]

    def prepare(self, b, projected):
        heads = self.heads
        tok = self.table.shape[2]
        lanes = span(b * tok, tok)
        cos = self.table[b, 0:HALF, :]
        sin = self.table[b, HALF:D, :]
        hot = self.table[b, D:D + 8, :]
        row = lax.broadcasted_iota(jnp.int32, (16, tok), 0)
        one_row = jnp.where(row == 0, 1.0, 0.0).astype(F32)
        penalty = jnp.concatenate([(1.0 - hot) * PENALTY, jnp.zeros((8, tok), F32)], axis=0).astype(BF16)
        self.raw[:, lanes] = projected[:heads.wide + heads.narrow]

        def rotated(raw, gain):
            inv = lax.rsqrt(jnp.mean(raw * raw, axis=0, keepdims=True) + EPSILON)
            n = raw * inv * gain
            a, c = n[:HALF], n[HALF:]
            return inv, jnp.concatenate([a * cos - c * sin, c * cos + a * sin], axis=0)

        for h in range(heads.queries):
            inv, q = rotated(projected[h * D:(h + 1) * D], self.gq)
            self.inv[h:h + 1, lanes] = inv
            self.qa[h, :, lanes] = jnp.concatenate([(q * (D ** -0.5)).astype(BF16), penalty], axis=0)
        for g in range(heads.pairs):
            start = heads.wide + g * D
            inv, k = rotated(projected[start:start + D], self.gk)
            self.inv[heads.queries + g:heads.queries + g + 1, lanes] = inv
            self.kt[g, :, lanes] = k.astype(BF16)
            full = jnp.concatenate([k, hot, jnp.ones((8, tok), F32), jnp.zeros((48, tok), F32)], axis=0)
            self.ka[g, lanes, :] = jnp.transpose(full).astype(BF16)
            start += heads.narrow
            self.vt[g, :, lanes] = jnp.concatenate([projected[start:start + D], one_row], axis=0).astype(BF16)

    def query_block(self, i):
        heads = self.heads
        cols = span(i * BLOCK, BLOCK)
        causal = (lax.broadcasted_iota(jnp.int32, (BLOCK, BLOCK), 0)
                  <= lax.broadcasted_iota(jnp.int32, (BLOCK, BLOCK), 1))

        def step(j, accs, diagonal):
            rows = span(j * BLOCK, BLOCK)
            new = []
            for h in range(heads.queries):
                slot = self.slots[h]
                p = jnp.exp(dot(self.ka[slot, rows, 0:80], self.qa[h, :, cols]))
                if diagonal:
                    p = jnp.where(causal, p, 0.0)
                new.append(accs[h] + dot(self.vt[slot, :, rows], p.astype(BF16)))
            return tuple(new)

        accs = tuple(jnp.zeros((80, BLOCK), F32) for _ in range(heads.queries))
        accs = lax.fori_loop(0, i, lambda j, c: step(j, c, False), accs)
        accs = step(i, accs, True)
        row = lax.broadcasted_iota(jnp.int32, (16, BLOCK), 0)
        lead = self.merged.shape[1] - heads.wide
        outs = [jnp.zeros((lead, BLOCK), F32)] if lead else []
        for h in range(heads.queries):
            total = accs[h][D:D + 1]
            o = accs[h][:D] * (1.0 / total)
            self.o[h, :, cols] = o
            outs.append(o)
            pieces = split3(-jnp.log(total))
            old = self.qa[h, 64:80, cols].astype(F32)
            extra = jnp.where(row == 8, pieces[0],
                              jnp.where(row == 9, pieces[1], jnp.where(row == 10, pieces[2], old)))
            self.qa[h, 64:80, cols] = extra.astype(BF16)
        merged = jnp.transpose(jnp.concatenate(outs, axis=0)).astype(BF16)
        self.merged[cols, :] = merged
        return merged


class Backward:
    def __init__(self, heads, me, table, gq, gk, raw, o, qa, ka, kt, vt, inv, doa, dopad, qpad, va, dq, acc):
        self.heads, self.table, self.gq, self.gk = heads, table, gq[...], gk[...]
        self.raw, self.o, self.qa, self.ka, self.kt, self.vt, self.inv = raw, o, qa, ka, kt, vt, inv
        self.doa, self.dopad, self.qpad, self.va, self.dq, self.acc = doa, dopad, qpad, va, dq, acc
        self.slots = [heads.slot(me, h) for h in range(heads.queries)]

    def prepare(self, b):
        heads = self.heads
        tok = self.table.shape[2]
        lanes = span(b * tok, tok)
        for h in range(heads.queries):
            q = jnp.concatenate([jnp.zeros((D, tok), F32), self.qa[h, 0:D, lanes].astype(F32)], axis=0)
            self.qpad[h, lanes, :] = jnp.transpose(q).astype(BF16)
            self.acc[h, lanes, :] = jnp.zeros((tok, 2 * D), F32)
        for g in range(heads.pairs):
            v = jnp.concatenate([self.vt[g, 0:D, lanes].astype(F32), jnp.ones((D, tok), F32)], axis=0)
            self.va[g, lanes, :] = jnp.transpose(v).astype(BF16)

    def gradient(self, b, dm):
        heads = self.heads
        tok = self.table.shape[2]
        lanes = span(b * tok, tok)
        row = lax.broadcasted_iota(jnp.int32, (16, tok), 0)
        dmt = jnp.transpose(dm.astype(BF16).astype(F32))
        for h in range(heads.queries):
            do = dmt[h * D:(h + 1) * D]
            delta = jnp.sum(do * self.o[h, :, lanes], axis=0, keepdims=True)
            pieces = split3(-delta)
            extra = jnp.where(row == 0, pieces[0],
                              jnp.where(row == 1, pieces[1], jnp.where(row == 2, pieces[2], 0.0)))
            self.doa[h, :, lanes] = jnp.concatenate([do, extra], axis=0).astype(BF16)
            both = jnp.concatenate([do, jnp.zeros((D, tok), F32)], axis=0)
            self.dopad[h, lanes, :] = jnp.transpose(both).astype(BF16)

    def query_block(self, i):
        heads = self.heads
        cols = span(i * BLOCK, BLOCK)
        causal = (lax.broadcasted_iota(jnp.int32, (BLOCK, BLOCK), 0)
                  <= lax.broadcasted_iota(jnp.int32, (BLOCK, BLOCK), 1))

        def step(j, accs, diagonal):
            rows = span(j * BLOCK, BLOCK)
            new = []
            for h in range(heads.queries):
                slot = self.slots[h]
                p = jnp.exp(dot(self.ka[slot, rows, 0:80], self.qa[h, :, cols]))
                if diagonal:
                    p = jnp.where(causal, p, 0.0)
                dp = dot(self.va[slot, rows, 0:80], self.doa[h, :, cols])
                ds = (p * dp).astype(BF16)
                self.acc[h, rows, :] += dot(p.astype(BF16), self.dopad[h, cols, :]) + dot(ds, self.qpad[h, cols, :])
                new.append(accs[h] + dot(self.kt[slot, :, rows], ds))
            return tuple(new)

        accs = tuple(jnp.zeros((D, BLOCK), F32) for _ in range(heads.queries))
        accs = lax.fori_loop(0, i, lambda j, c: step(j, c, False), accs)
        accs = step(i, accs, True)
        for h in range(heads.queries):
            self.dq[h, :, cols] = accs[h]

    def finish(self, b, sums):
        heads = self.heads
        tok = self.table.shape[2]
        lanes = span(b * tok, tok)
        cos = self.table[b, 0:HALF, :]
        sin = self.table[b, HALF:D, :]
        scale = self.table[b, 72:73, :]

        def back(grad, raw, inv, gain):
            a, c = grad[:HALF], grad[HALF:]
            n = jnp.concatenate([a * cos + c * sin, c * cos - a * sin], axis=0)
            v = n * gain
            out = inv * v - raw * (inv * inv * inv) * jnp.mean(v * raw, axis=0, keepdims=True)
            return out * scale, n * raw * inv

        sum_q, sum_k = sums
        pairs = [jnp.zeros((2 * D, tok), F32) for _ in range(heads.pairs)]
        out = []
        for h in range(heads.queries):
            raw = self.raw[h * D:(h + 1) * D, lanes]
            grad, part = back(self.dq[h, :, lanes] * (D ** -0.5), raw, self.inv[h:h + 1, lanes], self.gq)
            out.append(grad)
            sum_q = sum_q + part
            both = jnp.transpose(self.acc[h, lanes, :])
            for g in range(heads.pairs):
                pairs[g] = pairs[g] + jnp.where(self.slots[h] == g, both, 0.0)
        for g in range(heads.pairs):
            start = heads.wide + g * D
            raw = self.raw[start:start + D, lanes]
            inv = self.inv[heads.queries + g:heads.queries + g + 1, lanes]
            grad, part = back(pairs[g][D:], raw, inv, self.gk)
            out.append(grad)
            sum_k = sum_k + part
        for g in range(heads.pairs):
            out.append(pairs[g][:D] * scale)
        return jnp.concatenate(out, axis=0), (sum_q, sum_k)


def kept_shapes(heads, length, lead):
    return (
        jax.ShapeDtypeStruct((heads.wide + heads.narrow, length), F32),
        jax.ShapeDtypeStruct((length, lead + heads.wide), BF16),
        jax.ShapeDtypeStruct((heads.queries, D, length), F32),
        jax.ShapeDtypeStruct((heads.queries, 80, length), BF16),
        jax.ShapeDtypeStruct((heads.pairs, length, 128), BF16),
        jax.ShapeDtypeStruct((heads.pairs, D, length), BF16),
        jax.ShapeDtypeStruct((heads.pairs, 80, length), BF16),
        jax.ShapeDtypeStruct((8, length), F32),
    )


def backward_scratch(heads, length):
    return [
        pltpu.VMEM((heads.queries, 80, length), BF16),
        pltpu.VMEM((heads.queries, length, 2 * D), BF16),
        pltpu.VMEM((heads.queries, length, 2 * D), BF16),
        pltpu.VMEM((heads.pairs, length, 2 * D), BF16),
        pltpu.VMEM((heads.queries, D, length), F32),
        pltpu.VMEM((heads.queries, length, 2 * D), F32),
    ]


def local_forward_kernel(heads, proj_ref, table_ref, gq_ref, gk_ref, *kept):
    forward = Forward(heads, lax.axis_index("seq"), table_ref, gq_ref, gk_ref, *kept)
    blocks, _, tok = table_ref.shape

    def prepare(b, _):
        rows = span(b * tok, tok)
        forward.prepare(b, jnp.transpose(proj_ref[rows, :]) * table_ref[b, 72:73, :])
        return 0

    def query_block(i, _):
        forward.query_block(i)
        return 0

    lax.fori_loop(0, blocks, prepare, 0)
    lax.fori_loop(0, blocks * tok // BLOCK, query_block, 0)


def local_backward_kernel(heads, dm_ref, table_ref, gq_ref, gk_ref, raw_ref, o_ref, qa_ref, ka_ref, kt_ref, vt_ref, inv_ref,
                          pg_ref, gains_ref, *scratch):
    backward = Backward(heads, lax.axis_index("seq"), table_ref, gq_ref, gk_ref, raw_ref, o_ref, qa_ref, ka_ref, kt_ref,
                        vt_ref, inv_ref, *scratch)
    blocks, _, tok = table_ref.shape

    def prepare(b, _):
        backward.prepare(b)
        backward.gradient(b, dm_ref[span(b * tok, tok), :])
        return 0

    def query_block(i, _):
        backward.query_block(i)
        return 0

    def finish(b, sums):
        grad, sums = backward.finish(b, sums)
        pg_ref[span(b * tok, tok), :] = jnp.transpose(grad).astype(BF16)
        return sums

    lax.fori_loop(0, blocks, prepare, 0)
    lax.fori_loop(0, blocks * tok // BLOCK, query_block, 0)
    zero = jnp.zeros((D, tok), F32)
    sum_q, sum_k = lax.fori_loop(0, blocks, finish, (zero, zero))
    gains_ref[0:D, :] = jnp.broadcast_to(jnp.sum(sum_q, axis=1, keepdims=True), (D, 128))
    gains_ref[D:2 * D, :] = jnp.broadcast_to(jnp.sum(sum_k, axis=1, keepdims=True), (D, 128))


def attention_kernel(heads, x_hbm, g_hbm, w_hbm, gate_hbm, up_hbm, table_ref, gq_ref, gk_ref, gain_ref,
                     res_ref, two_ref, g_all, gate_all, up_all, raw_hbm, merged_hbm, o_hbm, qa_hbm, ka_hbm, kt_hbm, vt_hbm, inv_hbm,
                     raw_ref, merged_ref, o_ref, qa_ref, ka_ref, kt_ref, vt_ref, inv_ref, kept_sem, x_ref, w_ref, part_ref, sibling_ref, passing_ref, final_ref, rs_send, rs_recv,
                     ag_send, ag_recv, load_sem, z_send, z_recv):
    place = Place()
    blocks, tok, model = x_ref.shape
    slabs = ((gate_hbm, gate_all), (up_hbm, up_all))
    load_w = pltpu.make_async_copy(w_hbm, w_ref, load_sem.at[blocks])
    load_w.start()
    loads = [pltpu.make_async_copy(x_hbm.at[b], x_ref.at[b], load_sem.at[b]) for b in range(blocks)]
    for copy in loads:
        copy.start()
    place.greet(4)
    gather = Gather(place, g_hbm, g_all, ag_send, ag_recv)
    scatter = Scatter(place, part_ref, sibling_ref, passing_ref, final_ref, rs_send, rs_recv)
    line = Line(place)
    weights = [RowGather(line, own, lambda r, every=every: every.at[r], z_send.at[i], z_recv.at[i])
               for i, (own, every) in enumerate(slabs)]
    for one in weights:
        one.start()
    gather.start()
    forward = Forward(heads, place.me, table_ref, gq_ref, gk_ref, raw_ref, merged_ref, o_ref, qa_ref, ka_ref, kt_ref,
                      vt_ref, inv_ref)
    load_w.wait()
    for copy in loads:
        copy.wait()

    def prepare(b, _):
        proj = dot(x_ref[b], w_ref[:, 0:512])
        forward.prepare(b, jnp.transpose(proj) * table_ref[b, 72:73, :])
        return 0

    lax.fori_loop(0, blocks, prepare, 0)
    tile = 512

    def compute(k):
        merged = forward.query_block(place.chips[k])

        def model_tile(n, _):
            cols = span(n * tile, tile)
            out = dot_nt(merged_ref[span(place.chips[k] * BLOCK, BLOCK), :], w_ref[cols, 384:640])
            part_ref[k, :, :, cols] = out.astype(BF16).reshape(2, tok, tile)
            return 0

        lax.fori_loop(0, model // tile, model_tile, 0)
        scatter.exchange[k].start()

    compute(3)
    gather.own_chip()
    gather.neighbours()
    scatter.combine(3)
    scatter.pass1.start()
    scatter.pass2.start()
    compute(1)
    scatter.combine(1)
    scatter.first1.start()
    gather.chip1()
    gather.chip2()
    weights[0].forward()
    compute(2)
    scatter.combine(2)
    scatter.first2.start()
    gather.diagonal()
    compute(0)
    keep = [pltpu.make_async_copy(src, dst, kept_sem.at[i]) for i, (src, dst) in enumerate((
        (raw_ref, raw_hbm), (merged_ref, merged_hbm), (o_ref, o_hbm), (qa_ref, qa_hbm), (ka_ref, ka_hbm),
        (kt_ref, kt_hbm), (vt_ref, vt_hbm), (inv_ref, inv_hbm)))]
    for copy in keep:
        copy.start()
    scatter.combine(0)
    weights[1].forward()
    scatter.finish_two()
    gather.chip3()
    scatter.arrive()

    def finish(i, _):
        rows = span(i * 32, 32)
        res = x_ref[place.me, rows, :].astype(F32) + scatter.total(rows)
        res_ref[rows, :] = res
        two_ref[rows, :] = (res * norm_inverse(res) * gain_ref[...]).astype(BF16)
        return 0

    lax.fori_loop(0, tok // 32, finish, 0)
    for one in weights:
        one.finish()
        one.close()
    for copy in keep:
        copy.wait()
    gather.close()
    scatter.close()


def attention_phase(heads, x_all, g, w, slabs, table, gq, gk, gain):
    blocks, tok, model = x_all.shape
    dma = pltpu.SemaphoreType.DMA
    lead = 256 - heads.wide
    kept = kept_shapes(heads, blocks * tok, lead)
    return pl.pallas_call(
        functools.partial(attention_kernel, heads),
        out_shape=(jax.ShapeDtypeStruct((tok, model), F32), jax.ShapeDtypeStruct((tok, model), BF16),
                   jax.ShapeDtypeStruct((blocks, tok, model), BF16))
        + tuple(jax.ShapeDtypeStruct((4,) + slab.shape, BF16) for slab in slabs) + kept,
        in_specs=[ANY_SPEC] * 5 + [VMEM_SPEC] * 4,
        out_specs=(VMEM_SPEC, VMEM_SPEC) + (ANY_SPEC,) * (3 + len(kept)),
        scratch_shapes=[
            *(pltpu.VMEM(array.shape, array.dtype) for array in kept),
            dma((len(kept),)),
            pltpu.VMEM((blocks, tok, model), BF16),
            pltpu.VMEM((model, heads.columns), BF16),
            *scatter_scratch(tok, model),
            dma((GATHER_SLOTS,)), dma((GATHER_SLOTS,)), dma((blocks + 1,)),
            dma((2, ROW_SLOTS)), dma((2, ROW_SLOTS)),
        ],
        compiler_params=pltpu.CompilerParams(collective_id=1, has_side_effects=True, vmem_limit_bytes=VMEM_LIMIT),
        cost_estimate=pl.CostEstimate(flops=40 << 30, bytes_accessed=64 << 20, transcendentals=0),
    )(x_all, g, w, *slabs, table, gq, gk, gain)


def ffn_kernel(res_ref, gain_ref, two_hbm, g_own, g_hbm, gate_own, gate_hbm, up_own, up_hbm, down_hbm,
               out_hbm, rgrad_ref, branch_ref, gain_grad_ref, gate_grad_hbm, up_grad_hbm,
               gate_grad_own, up_grad_own, down_own, down_recv,
               two_ref, g_ref, weight_ref, down_ref, hid_ref, gu_ref, stage_ref, wstage_ref, dsum_ref, dgrad_ref, merge_ref,
               part_ref, sibling_ref, passing_ref, final_ref, rs_send, rs_recv,
               ag_send, ag_recv, load_sem, g_sem, stage_sem, wstage_sem, own_sem, za_send, za_recv, zr_send, zr_recv):
    place = Place()
    blocks, tok, model = g_ref.shape
    ff = weight_ref.shape[1] // 2
    share = model // 4
    tile = 256
    def down_at(r):
        return down_ref.at[:, span(r * share, share)]

    loads, g_loads = [], []
    for i, (own, every) in enumerate(((gate_own, gate_hbm), (up_own, up_hbm))):
        for j in range(4):
            r = lax.rem(place.row + j, 4)
            loads.append(pltpu.make_async_copy(
                every.at[r] if j else own, weight_ref.at[span(r * share, share), i * ff:(i + 1) * ff], load_sem.at[4 * i + j]))
    for j in range(blocks):
        b = lax.rem(place.me + j, blocks)
        g_loads.append(pltpu.make_async_copy(g_hbm.at[b] if j else g_own, g_ref.at[b], g_sem.at[j]))
    own_loads = [pltpu.make_async_copy(two_hbm, two_ref.at[place.me], load_sem.at[8]),
                 pltpu.make_async_copy(down_hbm, down_at(place.row), load_sem.at[9])]
    for copy in own_loads + loads + g_loads:
        copy.start()
    place.greet(4)
    line = Line(place)
    gather = Gather(place, two_hbm, two_ref, ag_send, ag_recv)
    scatter = Scatter(place, part_ref, sibling_ref, passing_ref, final_ref, rs_send, rs_recv)
    downs = RowGather(line, down_hbm, down_at, za_send, za_recv)
    down_sum = RowScatter(line, dgrad_ref, down_recv, merge_ref, merge_ref, zr_send, zr_recv)
    gather.start()
    downs.start()
    for copy in loads + own_loads:
        copy.wait()

    def forward(k):
        pair = pl.ds(2 * place.chips[k], 2)

        def hidden_tile(h, _):
            cols, cols2 = span(h * tile, tile), span(ff + h * tile, tile)
            x = two_ref[pair].reshape(2 * tok, model)
            gate = dot(x, weight_ref[:, cols])
            up = dot(x, weight_ref[:, cols2])
            s = 1.0 / (1.0 + jnp.exp(-gate))
            act = gate * s
            hid_ref[pair, :, cols] = (act * up).astype(BF16).reshape(2, tok, tile)
            gu_ref[pair, :, cols] = (up * s * (1.0 + gate * (1.0 - s))).astype(BF16).reshape(2, tok, tile)
            gu_ref[pair, :, cols2] = act.astype(BF16).reshape(2, tok, tile)
            return 0

        lax.fori_loop(0, ff // tile, hidden_tile, 0)

    def backward(k):
        pair = pl.ds(2 * place.chips[k], 2)

        def hidden_tile(h, _):
            cols, cols2 = span(h * tile, tile), span(ff + h * tile, tile)
            back = dot_nt(g_ref[pair].reshape(2 * tok, model), down_ref[cols, :])
            for where in (cols, cols2):
                factor = gu_ref[pair, :, where].reshape(2 * tok, tile).astype(F32)
                gu_ref[pair, :, where] = (back * factor).astype(BF16).reshape(2, tok, tile)
            return 0

        lax.fori_loop(0, ff // tile, hidden_tile, 0)

        def model_tile(n, _):
            cols = span(n * tile, tile)
            back = dot_nt(gu_ref[pair].reshape(2 * tok, 2 * ff), weight_ref[cols, :])
            part_ref[k, :, :, cols] = back.astype(BF16).reshape(2, tok, tile)
            return 0

        lax.fori_loop(0, model // tile, model_tile, 0)
        scatter.exchange[k].start()

    def stage_copy(n):
        slot = lax.rem(n, 2)
        return pltpu.make_async_copy(stage_ref.at[slot], out_hbm.at[n // 4, :, :, span(lax.rem(n, 4) * share, share)],
                                     stage_sem.at[slot])

    def out_tile(n, _):
        @pl.when(n >= 2)
        def _():
            stage_copy(n - 2).wait()

        k, r = n // 4, lax.rem(n, 4)
        chip = place.chip
        m = jnp.where(k == 0, chip, jnp.where(k == 1, place.chips[1], jnp.where(k == 2, place.chips[2], place.chips[3])))
        out = dot(hid_ref[pl.ds(2 * m, 2)].reshape(2 * tok, ff), down_ref[:, span(r * share, share)])
        stage_ref[lax.rem(n, 2)] = out.astype(BF16).reshape(2, tok, share)
        stage_copy(n).start()
        return 0

    def down_grad(k):
        pair = pl.ds(2 * place.chips[k], 2)

        def down_rows(n, _):
            rows, r = span(lax.rem(n, ff // tile) * tile, tile), n // (ff // tile)
            h = hid_ref[pair, :, rows].reshape(2 * tok, tile)
            g = g_ref[pair, :, span(r * share, share)].reshape(2 * tok, share)
            term = dot_tn(h, g)
            if k:
                term = dsum_ref[r, rows, :] + term
            if k < 3:
                dsum_ref[r, rows, :] = term
            else:
                dgrad_ref[r, rows, :] = term.astype(BF16)
            return 0

        lax.fori_loop(0, 4 * (ff // tile), down_rows, 0)

    def wstage_copies(i, slot):
        return (pltpu.make_async_copy(wstage_ref.at[slot, :, 0:ff], gate_grad_hbm.at[i], wstage_sem.at[slot, 0]),
                pltpu.make_async_copy(wstage_ref.at[slot, :, ff:2 * ff], up_grad_hbm.at[i], wstage_sem.at[slot, 1]))

    def own_copies(half, slot):
        rows = span(half * tile, tile)
        return (pltpu.make_async_copy(wstage_ref.at[slot, :, 0:ff], gate_grad_own.at[rows], own_sem.at[0]),
                pltpu.make_async_copy(wstage_ref.at[slot, :, ff:2 * ff], up_grad_own.at[rows], own_sem.at[1]))

    def gate_up_rows(i, _):
        cols = span(i * tile, tile)
        slot = lax.rem(i, 2)

        @pl.when(i >= 2)
        def _():
            for copy in wstage_copies(i - 2, slot):
                copy.wait()

        x = two_ref[:, :, cols].reshape(blocks * tok, tile)
        wstage_ref[slot] = dot_tn(x, gu_ref[...].reshape(blocks * tok, 2 * ff)).astype(BF16)
        for copy in wstage_copies(i, slot):
            copy.start()

        @pl.when(i // 2 == place.row)
        def _():
            for copy in own_copies(lax.rem(i, 2), slot):
                copy.start()

        out_tile(2 * i, 0)
        out_tile(2 * i + 1, 0)

        @pl.when(i // 2 == place.row)
        def _():
            for copy in own_copies(lax.rem(i, 2), slot):
                copy.wait()

        return 0

    gather.own_chip()
    forward(0)
    for copy in g_loads:
        copy.wait()
    down_grad(0)
    gather.neighbours()
    downs.forward()
    gather.chip1()
    forward(1)
    down_grad(1)
    gather.chip2()
    forward(2)
    down_grad(2)
    gather.diagonal()
    gather.chip3()
    forward(3)
    downs.finish()
    backward(3)
    down_grad(3)
    down_sum.start_over()
    down_sum.start()
    own_down = pltpu.make_async_copy(dgrad_ref.at[place.row], down_own, load_sem.at[10])
    own_down.start()
    scatter.combine(3)
    scatter.pass1.start()
    scatter.pass2.start()
    backward(1)
    backward(2)
    scatter.combine(1)
    scatter.first1.start()
    scatter.combine(2)
    scatter.first2.start()
    backward(0)
    scatter.finish_two()
    scatter.combine(0)
    count = model // tile
    lax.fori_loop(0, count // 2, gate_up_rows, 0)

    def merge():
        def add(n, _):
            rows = span(n * 64, 64)
            merge_ref[rows, :] = (merge_ref[rows, :].astype(F32) + dgrad_ref[line.c, rows, :].astype(F32)).astype(BF16)
            return 0

        lax.fori_loop(0, ff // 64, add, 0)

    down_sum.add(merge)
    lax.fori_loop(count // 2, count, gate_up_rows, 0)
    scatter.arrive()

    def finish(i, sums):
        rows = span(i * 32, 32)
        res = res_ref[rows, :]
        inv = norm_inverse(res)
        grad = scatter.total(rows)
        v = grad * gain_ref[...]
        mean = jnp.mean(v * res, axis=-1, keepdims=True)
        out = g_ref[place.me, rows, :].astype(F32) + inv * v - res * (inv * inv * inv * mean)
        rgrad_ref[rows, :] = out
        branch_ref[rows, :] = out.astype(BF16)
        return sums + jnp.sum(grad * res * inv, axis=0, keepdims=True)

    gain_grad_ref[...] = lax.fori_loop(0, tok // 32, finish, jnp.zeros((1, model), F32))
    for i in (count - 2, count - 1):
        for copy in wstage_copies(i, i % 2):
            copy.wait()
    for n in (14, 15):
        stage_copy(n).wait()
    own_down.wait()
    down_sum.finish()
    down_sum.close()
    downs.close()
    gather.close()
    scatter.close()


def feed_forward(res, gain, two, g, g_all, slabs):
    tok, model = res.shape
    ff = slabs[0].shape[1]
    blocks = g_all.shape[0]
    dma = pltpu.SemaphoreType.DMA
    return pl.pallas_call(
        ffn_kernel,
        out_shape=(
            jax.ShapeDtypeStruct((4, 2, tok, model), BF16),
            jax.ShapeDtypeStruct((tok, model), F32),
            jax.ShapeDtypeStruct((tok, model), BF16),
            jax.ShapeDtypeStruct((1, model), F32),
            jax.ShapeDtypeStruct((model // 256, 256, ff), BF16),
            jax.ShapeDtypeStruct((model // 256, 256, ff), BF16),
            jax.ShapeDtypeStruct((model // 4, ff), BF16),
            jax.ShapeDtypeStruct((model // 4, ff), BF16),
            jax.ShapeDtypeStruct((ff, model // 4), BF16),
            jax.ShapeDtypeStruct((3, ff, model // 4), BF16),
        ),
        in_specs=[VMEM_SPEC, VMEM_SPEC] + [ANY_SPEC] * 8,
        out_specs=(ANY_SPEC, VMEM_SPEC, VMEM_SPEC, VMEM_SPEC) + (ANY_SPEC,) * 6,
        scratch_shapes=[
            pltpu.VMEM((blocks, tok, model), BF16),
            pltpu.VMEM((blocks, tok, model), BF16),
            pltpu.VMEM((model, 2 * ff), BF16),
            pltpu.VMEM((ff, model), BF16),
            pltpu.VMEM((blocks, tok, ff), BF16),
            pltpu.VMEM((blocks, tok, 2 * ff), BF16),
            pltpu.VMEM((2, 2, tok, model // 4), BF16),
            pltpu.VMEM((2, 256, 2 * ff), BF16),
            pltpu.VMEM((4, ff, model // 4), F32),
            pltpu.VMEM((4, ff, model // 4), BF16),
            pltpu.VMEM((ff, model // 4), BF16),
            *scatter_scratch(tok, model),
            dma((GATHER_SLOTS,)), dma((GATHER_SLOTS,)), dma((11,)), dma((blocks,)), dma((2,)), dma((2, 2)), dma((2,)),
            dma((ROW_SLOTS,)), dma((ROW_SLOTS,)), dma((ROW_SLOTS,)), dma((ROW_SLOTS,)),
        ],
        compiler_params=pltpu.CompilerParams(collective_id=2, has_side_effects=True, vmem_limit_bytes=62 * 1024 * 1024),
        cost_estimate=pl.CostEstimate(flops=18 * blocks * tok * model * ff, bytes_accessed=64 << 20, transcendentals=0),
    )(res, gain, two, g, g_all, *slabs)


def backward_kernel(heads, branch_hbm, out_hbm, x_hbm, w_hbm, gate_grad, up_grad, merged_hbm,
                    table_ref, gq_ref, gk_ref, gain_grad_ref, qkv_ref, gain_ref,
                    raw_hbm, o_hbm, qa_hbm, ka_hbm, kt_hbm, vt_hbm, inv_hbm,
                    ysum_ref, outsum_ref, grad_qkv_ref, grad_out_ref, grad_gain_ref, small_out,
                    grad_hbm, gate_recv, up_recv, attn_recv,
                    raw_ref, o_ref, qa_ref, ka_ref, kt_ref, vt_ref, inv_ref, kept_sem,
                    every_ref, w_ref, pg_ref, merged_ref, xt_ref, wstage_ref, gwo_ref,
                    doa_ref, dopad_ref, qpad_ref, va_ref, dq_ref, acc_ref,
                    part_ref, sibling_ref, passing_ref, final_ref, rs_send, rs_recv, rs2_send, rs2_recv,
                    ag_send, ag_recv, load_sem, xt_sem, wstage_sem, ready_sem,
                    ffn_merge, ffn_own, z_send, z_recv, own_sem, small_ref, small_row, small_mid, small_last, pieces_ref, amerge_ref, aown_ref,
                    s_send, s_recv, t_send, t_recv, p_send, p_recv):
    place = Place()
    blocks, tok, model = every_ref.shape[0] * every_ref.shape[1], every_ref.shape[2], every_ref.shape[3]
    branch_all = every_ref.reshape(blocks, tok, model)
    columns = heads.columns
    lead = 256 - heads.wide
    load_w = pltpu.make_async_copy(w_hbm, w_ref, load_sem.at[0])
    load_out = pltpu.make_async_copy(out_hbm, part_ref, load_sem.at[1])
    load_own = pltpu.make_async_copy(branch_hbm, branch_all.at[place.me], load_sem.at[2])
    load_merged = pltpu.make_async_copy(merged_hbm, merged_ref, load_sem.at[3])
    load_out.start()
    load_own.start()
    load_w.start()
    load_kept = [pltpu.make_async_copy(src, dst, kept_sem.at[i]) for i, (src, dst) in enumerate((
        (qa_hbm, qa_ref), (vt_hbm, vt_ref), (o_hbm, o_ref), (ka_hbm, ka_ref), (kt_hbm, kt_ref), (raw_hbm, raw_ref),
        (inv_hbm, inv_ref)))]
    for copy in load_kept:
        copy.start()
    load_merged.start()
    place.greet_all(4)
    gather = Gather(place, branch_hbm, branch_all, ag_send, ag_recv)
    gather.start()
    line = Line(place)
    ffn = [RowScatter(line, part, recv, ffn_merge.at[i], ffn_merge.at[i], z_send.at[i], z_recv.at[i])
           for i, (part, recv) in enumerate(((gate_grad, gate_recv), (up_grad, up_recv)))]
    for one in ffn:
        one.start_over()
    for one in ffn:
        one.start()
    first = Scatter(place, part_ref, sibling_ref, passing_ref, final_ref, rs_send, rs_recv)
    second = Scatter(place, every_ref, sibling_ref, passing_ref, final_ref, rs2_send, rs2_recv)
    load_out.wait()
    for copy in first.exchange:
        copy.start()

    def ffn_add(i):
        own = (gate_grad, up_grad)[i]

        def work():
            load = pltpu.make_async_copy(own.at[line.c], ffn_own, own_sem.at[0])
            load.start()
            load.wait()

            def add(n, _):
                rows = span(n * 64, 64)
                ffn_merge[i, rows, :] = ffn_merge[i, rows, :] + ffn_own[rows, :]
                return 0

            lax.fori_loop(0, ffn_own.shape[0] // 64, add, 0)

        ffn[i].add(work)

    def tell(n, others):
        for other in others:
            pl.semaphore_signal(ready_sem.at[n], inc=1, device_id=(place.row, other), device_id_type=MESH)

    back = Backward(heads, place.me, table_ref, gq_ref, gk_ref, raw_ref, o_ref, qa_ref, ka_ref, kt_ref, vt_ref, inv_ref,
                    doa_ref, dopad_ref, qpad_ref, va_ref, dq_ref, acc_ref)

    def prepare(b, _):
        back.prepare(b)
        return 0

    for copy in load_kept:
        copy.wait()
    lax.fori_loop(0, blocks, prepare, 0)
    load_w.wait()
    load_own.wait()

    def compute(k):
        m = place.chips[k]

        def gradient(j, _):
            b = 2 * m + j
            dm = dot(branch_all[b], w_ref[:, 384:640])
            back.gradient(b, dm[:, lead:])
            return 0

        lax.fori_loop(0, 2, gradient, 0)
        back.query_block(m)

    gather.own_chip()
    compute(0)
    gather.neighbours()
    first.combine(3)
    first.pass1.start()
    first.pass2.start()
    ffn_add(0)
    gather.chip1()
    compute(1)
    first.combine(1)
    first.first1.start()
    gather.chip2()
    ffn_add(1)
    compute(2)
    first.combine(2)
    first.first2.start()
    gather.diagonal()
    first.combine(0)
    tell(0, (place.sib,))
    gather.chip3()
    compute(3)
    first.finish_two()
    tell(1, place.same[1:3])
    load_merged.wait()
    tile = 256
    count = model // tile

    def x_copy(i, slot):
        return pltpu.make_async_copy(x_hbm.at[:, :, span(i * tile, tile)], xt_ref.at[slot], xt_sem.at[slot])

    x_copy(0, 0).start()

    def out_rows(i, _):
        out = dot_tn(branch_all[:, :, span(i * tile, tile)].reshape(blocks * tok, tile), merged_ref[...])
        gwo_ref[i] = out.astype(BF16)
        return 0

    lax.fori_loop(0, count, out_rows, 0)
    gather.close()
    pad = 512 - heads.qkv

    def finish(b, sums):
        grad, sums = back.finish(b, sums)
        grad = jnp.concatenate([grad, jnp.zeros((pad, tok), F32)], axis=0)
        pg_ref[b] = jnp.transpose(grad).astype(BF16)
        return sums

    zero = jnp.zeros((D, tok), F32)
    sums = lax.fori_loop(0, blocks, finish, (zero, zero))

    def grad_copy(i, slot):
        return pltpu.make_async_copy(wstage_ref.at[slot], grad_hbm.at[i // 2, lax.rem(i, 2)], wstage_sem.at[slot])

    def weight_rows(i, _):
        slot = lax.rem(i, 2)

        @pl.when(i + 1 < count)
        def _():
            x_copy(i + 1, 1 - slot).start()

        @pl.when(i >= 2)
        def _():
            grad_copy(i - 2, slot).wait()

        x_copy(i, slot).wait()
        x = xt_ref[slot].reshape(blocks * tok, tile)
        qkv = dot_tn(x, pg_ref[...].reshape(blocks * tok, 512))
        wstage_ref[slot, :, 0:heads.qkv] = qkv[:, 0:heads.qkv].astype(BF16)
        wstage_ref[slot, :, heads.qkv:columns] = gwo_ref[i, :, lead:]
        grad_copy(i, slot).start()
        return 0

    lax.fori_loop(0, count, weight_rows, 0)
    for i in (count - 2, count - 1):
        grad_copy(i, i % 2).wait()

    def block(n):
        return part_ref.at[n, :, :, 0:columns]

    attn = RowScatter(line, grad_hbm, attn_recv, amerge_ref, amerge_ref, z_send.at[2], z_recv.at[2])
    attn.start_over()
    attn.start()
    load_passed = pltpu.make_async_copy(grad_hbm.at[line.c], aown_ref, own_sem.at[2])
    load_passed.start()

    def attn_work():
        def add(n, _):
            b, rows = n // 4, span(lax.rem(n, 4) * 64, 64)
            amerge_ref[b, rows, :] = amerge_ref[b, rows, :] + aown_ref[b, rows, :]
            return 0

        lax.fori_loop(0, 8, add, 0)

    def project(k):
        m = place.chips[k]

        def model_tile(n, _):
            cols = span(n * 512, 512)
            out = dot_nt(pg_ref[pl.ds(2 * m, 2)].reshape(2 * tok, 512), w_ref[cols, 0:512])
            every_ref[k, :, :, cols] = out.astype(BF16).reshape(2, tok, 512)
            return 0

        lax.fori_loop(0, model // 512, model_tile, 0)
        if k == 3:
            pl.semaphore_wait(ready_sem.at[0], 1)
        second.exchange[k].start()

    project(3)
    project(1)
    second.combine(3)
    pl.semaphore_wait(ready_sem.at[1], 2)
    second.pass1.start()
    second.pass2.start()
    project(2)
    second.combine(1)
    load_passed.wait()
    attn.add(attn_work)
    project(0)
    second.combine(2)

    head_gains = jnp.sum(jnp.transpose(jnp.concatenate(sums, axis=0)), axis=0, keepdims=True)
    row8 = lax.broadcasted_iota(jnp.int32, (8, 128), 0)
    for r in range(4):
        for n in range(PLANE):
            start = (r * PLANE + n) * D
            piece = jnp.concatenate([gain_grad_ref[:, start:start + D], jnp.zeros((1, 128 - D), F32)], axis=1)
            small_ref[r, n] = jnp.where(row8 == 0, piece, jnp.where(row8 == 1, head_gains, 0.0))
    small_sends = []
    for j in range(1, 4):
        other = lax.rem(place.row + j, 4)
        small_sends.append(line.send(small_ref.at[other], small_row.at[place.row], s_send, j, s_recv, j, other))
    for copy in small_sends:
        copy.start()
    small_row[place.row] = small_ref[place.row]

    def take(out_ref, scatter):
        def one(i, _):
            rows = span(i * 32, 32)
            out_ref[rows, :] = scatter.total(rows)
            return 0

        lax.fori_loop(0, tok // 32, one, 0)

    first.arrive()
    take(outsum_ref, first)
    tell(2, place.same[1:3])
    first.close()
    pl.semaphore_wait(ready_sem.at[2], 2)
    second.first1.start()
    second.first2.start()
    second.combine(0)
    own_term = pltpu.make_async_copy(grad_hbm.at[place.row], block(0), own_sem.at[1])
    own_term.start()

    def add_blocks(target, source):
        def add(n, _):
            b, rows = n // 4, span(lax.rem(n, 4) * 64, 64)
            part_ref[target, b, rows, 0:columns] = part_ref[target, b, rows, 0:columns] + part_ref[source, b, rows, 0:columns]
            return 0

        lax.fori_loop(0, 8, add, 0)

    second.finish_two()
    for copy in small_sends:
        copy.wait_recv()
    small_mid[...] = (small_row[0] + small_row[1]) + (small_row[2] + small_row[3])
    plane_sends = []
    for j in range(1, PLANE):
        other = lax.rem(place.me + j, PLANE)
        plane_sends.append(place.send(small_mid.at[other], small_last.at[place.me], t_send, t_recv, j, other))
    for copy in plane_sends:
        copy.start()
    small_last[place.me] = small_mid[place.me]
    second.arrive()
    take(ysum_ref, second)
    for one in ffn:
        one.finish()
        one.close()
    for copy in plane_sends:
        copy.wait_recv()
    total = small_last[0]
    for n in range(1, PLANE):
        total = total + small_last[n]
    small_out[...] = total
    own_term.wait()
    attn.finish()

    def fold(slots):
        loads = [pltpu.make_async_copy(attn_recv.at[slot], block(buffer), own_sem.at[4 + slot]) for slot, buffer in slots]
        for copy in loads:
            copy.start()
        for copy in loads:
            copy.wait()
        for _, buffer in slots:
            add_blocks(0, buffer)

    fold(((0, 1), (2, 3)))

    @pl.when(line.middle)
    def _():
        fold(((1, 1),))

    def piece(n):
        return part_ref.at[0, n // 4, span(lax.rem(n, 4) * 64, 64), 0:columns]

    keep = pltpu.make_async_copy(piece(place.me), pieces_ref.at[place.me], own_sem.at[7])
    keep.start()
    for j in range(1, PLANE):
        other = lax.rem(place.me + j, PLANE)
        copy = place.send(piece(other), pieces_ref.at[place.me], p_send, p_recv, j, other)
        copy.start()
        plane_sends.append(copy)
    for copy in plane_sends[PLANE - 1:]:
        copy.wait_recv()
    keep.wait()
    unscaled, out_t = attention_sums(heads, lambda s: pieces_ref[s].astype(F32))
    grad_gain_ref[...] = jnp.broadcast_to(jnp.sum(unscaled * qkv_ref[...].astype(F32), axis=1, keepdims=True), grad_gain_ref.shape)
    grad_qkv_ref[...] = unscaled * gain_ref[...]
    grad_out_ref[...] = jnp.transpose(out_t)
    for copy in plane_sends + small_sends:
        copy.wait_send()
    attn.close()
    second.close()


def backward_phase(heads, branch, out_part, x_all, w, weight_grads, table, gq, gk, gain_grad, w_qkv, gain_attn, kept):
    blocks, tok, model = x_all.shape
    length = blocks * tok
    depth = w_qkv.shape[0]
    dma = pltpu.SemaphoreType.DMA
    raw, merged, *rest = kept
    return pl.pallas_call(
        functools.partial(backward_kernel, heads),
        out_shape=(
            jax.ShapeDtypeStruct((tok, model), F32),
            jax.ShapeDtypeStruct((tok, model), F32),
            jax.ShapeDtypeStruct(w_qkv.shape, F32),
            jax.ShapeDtypeStruct((QUERY_HEADS * D, depth), F32),
            jax.ShapeDtypeStruct((depth, 128), F32),
            jax.ShapeDtypeStruct((8, 128), F32),
            jax.ShapeDtypeStruct((4, 2, 256, heads.columns), BF16),
            *(jax.ShapeDtypeStruct((3,) + grad.shape[1:], BF16) for grad in weight_grads),
            jax.ShapeDtypeStruct((3, 2, 256, heads.columns), BF16),
        ),
        in_specs=[ANY_SPEC] * 7 + [VMEM_SPEC] * 6 + [ANY_SPEC] * (1 + len(rest)),
        out_specs=(VMEM_SPEC,) * 6 + (ANY_SPEC,) * 4,
        scratch_shapes=[
            *(pltpu.VMEM(array.shape, array.dtype) for array in (raw, *rest)),
            dma((7,)),
            pltpu.VMEM((4, 2, tok, model), BF16),
            pltpu.VMEM((model, heads.columns), BF16),
            pltpu.VMEM((blocks, tok, 512), BF16),
            pltpu.VMEM(merged.shape, BF16),
            pltpu.VMEM((2, blocks, tok, 256), BF16),
            pltpu.VMEM((2, 256, heads.columns), BF16),
            pltpu.VMEM((model // 256, 256, 256), BF16),
            *backward_scratch(heads, length),
            *scatter_scratch(tok, model),
            dma((SCATTER_SLOTS,)), dma((SCATTER_SLOTS,)),
            dma((GATHER_SLOTS,)), dma((GATHER_SLOTS,)), dma((4,)), dma((2,)), dma((2,)),
            pltpu.SemaphoreType.REGULAR((3,)),
            pltpu.VMEM((2,) + weight_grads[0].shape[1:], BF16),
            pltpu.VMEM(weight_grads[0].shape[1:], BF16),
            dma((3, ROW_SLOTS)), dma((3, ROW_SLOTS)), dma((8,)),
            pltpu.VMEM((4, PLANE, 8, 128), F32),
            pltpu.VMEM((4, PLANE, 8, 128), F32),
            pltpu.VMEM((PLANE, 8, 128), F32),
            pltpu.VMEM((PLANE, 8, 128), F32),
            pltpu.VMEM((PLANE, depth, heads.columns), BF16),
            pltpu.VMEM((2, 256, heads.columns), BF16),
            pltpu.VMEM((2, 256, heads.columns), BF16),
            dma((4,)), dma((4,)), dma((PLANE,)), dma((PLANE,)), dma((PLANE,)), dma((PLANE,)),
        ],
        compiler_params=pltpu.CompilerParams(collective_id=3, has_side_effects=True, vmem_limit_bytes=63 * 1024 * 1024),
        cost_estimate=pl.CostEstimate(flops=60 << 30, bytes_accessed=64 << 20, transcendentals=0),
    )(branch, out_part, x_all, w, *weight_grads, merged, table, gq, gk, gain_grad, w_qkv, gain_attn, raw, *rest)


def norm_back(grad_normed, values_in, inv_rms, gain):
    scaled = grad_normed * gain
    gain_grad = jnp.sum(grad_normed * values_in * inv_rms, axis=0)
    input_grad = inv_rms * scaled - values_in * inv_rms**3 * jnp.mean(scaled * values_in, axis=-1, keepdims=True)
    return input_grad, gain_grad


def start_wide(rows, x, table, pieces, gain):
    return (
        lax.all_gather(x, "seq", axis=0, tiled=False),
        lax.all_gather(table, "seq", axis=0, tiled=False),
        lax.all_gather(lax.all_to_all(pieces, "seq", 0, 0, tiled=False), "rows", axis=0, tiled=False),
        lax.all_gather(lax.all_gather(gain, "seq", axis=0, tiled=False), "rows", axis=0, tiled=False),
    )


def scatter_rows(part, tok):
    return lax.psum_scatter(part.reshape(-1, part.shape[-1]), "seq", scatter_dimension=0, tiled=True).astype(F32)


def attention_wide(heads, x_all, g, w, table, gq, gk):
    blocks, tok, model = x_all.shape
    proj = dot(x_all.reshape(blocks * tok, model), w[:, :heads.qkv])
    kept = pl.pallas_call(
        functools.partial(local_forward_kernel, heads),
        out_shape=kept_shapes(heads, blocks * tok, 0),
        compiler_params=pltpu.CompilerParams(vmem_limit_bytes=VMEM_LIMIT),
    )(proj, table, gq, gk)
    total = scatter_rows(dot_nt(kept[1], w[:, heads.qkv:]).astype(BF16), tok)
    own = lax.dynamic_index_in_dim(x_all, lax.axis_index("seq"), 0, keepdims=False)
    return (own.astype(F32) + total, lax.all_gather(g, "seq", axis=0, tiled=False)) + tuple(kept)


def feed_forward_wide(res, gain, g_blocks, gate_slab, up_slab, down_slab):
    blocks, tok, model = g_blocks.shape
    inv = norm_inverse(res)
    two_all = lax.all_gather((res * inv * gain).astype(BF16), "seq", axis=0, tiled=True)
    g_all = g_blocks.reshape(blocks * tok, model)
    gate_act = dot(two_all, gate_slab)
    up_act = dot(two_all, up_slab)
    s = jax.nn.sigmoid(gate_act)
    hidden = (gate_act * s * up_act).astype(BF16)
    hidden_grad = dot_nt(g_all, down_slab)
    gate_grad = (hidden_grad * up_act * s * (1.0 + gate_act * (1.0 - s))).astype(BF16)
    up_grad = (hidden_grad * gate_act * s).astype(BF16)
    two_grad = scatter_rows((dot_nt(gate_grad, gate_slab) + dot_nt(up_grad, up_slab)).astype(BF16), tok)
    branch_part = dot(hidden, down_slab).astype(BF16).reshape(blocks, tok, model)
    norm_grad, gain_grad = norm_back(two_grad, res, inv, gain)
    g = lax.dynamic_index_in_dim(g_blocks, lax.axis_index("seq"), 0, keepdims=False)
    residual_grad = g.astype(F32) + norm_grad
    return (branch_part, residual_grad, residual_grad.astype(BF16), gain_grad[None],
            dot_tn(two_all, gate_grad).astype(BF16), dot_tn(two_all, up_grad).astype(BF16),
            dot_tn(hidden, g_all).astype(BF16))


def backward_wide(heads, branch, out_part, x_all, w, table, gq, gk, kept):
    blocks, tok, model = x_all.shape
    length = blocks * tok
    raw, merged, *rest = kept
    out_sum = scatter_rows(out_part, tok)
    branch_all = lax.all_gather(branch, "seq", axis=0, tiled=True)
    pg, gains = pl.pallas_call(
        functools.partial(local_backward_kernel, heads),
        out_shape=(jax.ShapeDtypeStruct((length, heads.qkv), BF16), jax.ShapeDtypeStruct((2 * D, 128), F32)),
        scratch_shapes=backward_scratch(heads, length),
        compiler_params=pltpu.CompilerParams(vmem_limit_bytes=VMEM_LIMIT),
    )(dot(branch_all, w[:, heads.qkv:]), table, gq, gk, raw, *rest)
    y_sum = scatter_rows(dot_nt(pg, w[:, :heads.qkv]).astype(BF16), tok)
    grad = jnp.concatenate([dot_tn(x_all.reshape(length, model), pg), dot_tn(branch_all, merged)], axis=1)
    return y_sum, out_sum, grad.astype(BF16), gains


def rotary_table(x, positions, segments):
    inverse = jnp.exp(-math.log(THETA) * jnp.arange(HALF, dtype=F32) * 2.0 / D)
    angles = inverse[:, None] * positions.astype(F32)[None, :]
    hot = jnp.arange(SEGMENT_KINDS, dtype=jnp.int32)[:, None] == segments[None, :]
    root = jnp.pad(norm_inverse(x).T, ((0, 7), (0, 0)))
    return jnp.concatenate([jnp.cos(angles), jnp.sin(angles), hot.astype(F32), root], axis=0)


def attention_pieces(heads, w_qkv, w_out):
    depth = w_qkv.shape[0]
    qw, kw = QUERY_HEADS * D, KEY_VALUE_HEADS * D
    out_t = w_out.T

    def columns(array, start, first, count, most):
        parts = []
        for i in range(count):
            n = first + i
            parts.append(array[:, start + n * D:start + (n + 1) * D] if n < most else jnp.zeros((depth, D), BF16))
        return parts

    pieces = []
    for s in range(heads.seq):
        q, k = s * heads.queries, heads.first(s)
        parts = (columns(w_qkv, 0, q, heads.queries, QUERY_HEADS)
                 + columns(w_qkv, qw, k, heads.pairs, KEY_VALUE_HEADS)
                 + columns(w_qkv, qw + kw, k, heads.pairs, KEY_VALUE_HEADS)
                 + columns(out_t, 0, q, heads.queries, QUERY_HEADS))
        pieces.append(jnp.concatenate(parts, axis=1))
    return jnp.stack(pieces)


def attention_sums(heads, piece):
    pieces = [piece(s) for s in range(heads.seq)]
    cut = lambda s, start, n: pieces[s][:, start + n * D:start + (n + 1) * D]
    queries = [cut(n // heads.queries, 0, n % heads.queries) for n in range(QUERY_HEADS)]
    outs = [cut(n // heads.queries, heads.qkv, n % heads.queries) for n in range(QUERY_HEADS)]

    def pairs(start):
        found = []
        for n in range(KEY_VALUE_HEADS):
            terms = [cut(s, start, n - heads.first(s)) for s in range(heads.seq)
                     if s * heads.queries < QUERY_HEADS and 0 <= n - heads.first(s) < heads.pairs]
            found.append(functools.reduce(jnp.add, terms))
        return found

    qkv = jnp.concatenate(queries + pairs(heads.wide) + pairs(heads.wide + heads.narrow), axis=1)
    return qkv, jnp.concatenate(outs, axis=1)


def body(tokens, segments, positions, cotangent, gain_attn, w_qkv, gain_q, gain_k, w_out, gain_ffn, w_gate, w_up, w_down):
    seq = lax.axis_size("seq")
    rows = lax.axis_size("rows")
    heads = Heads(seq)
    depth = w_qkv.shape[0]
    tok, model = tokens.shape[1:]
    plane = seq == PLANE and rows == 4
    row = lax.axis_index("rows")

    gq = gain_q.astype(F32)[:, None]
    gk = gain_k.astype(F32)[:, None]
    x = tokens[0].astype(F32)
    scaled = (w_qkv.astype(F32) * gain_attn.astype(F32)[:, None]).astype(BF16)
    pieces = attention_pieces(heads, scaled, w_out)
    gain = jnp.pad(gain_ffn.astype(F32)[None], ((0, 7), (0, 128 - depth)))
    x_all, table, w, gains = (start_phase if plane else start_wide)(
        rows, tokens[0], rotary_table(x, positions[0], segments[0]), pieces, gain)
    w = w.reshape(model, heads.columns)
    gain_two = gains[:, :, 0, :depth].reshape(1, model)
    inv = norm_inverse(x)

    if plane:
        residual, two, g_all, gate, up, *kept = attention_phase(
            heads, x_all, cotangent[0], w, (w_gate, w_up), table, gq, gk, gain_two)
        out_part, residual_grad, branch, gain_two_grad, *weight_grads, gate_own, up_own, down_own, down_recv = feed_forward(
            residual, gain_two, two, cotangent[0], g_all, (w_gate, gate, w_up, up, w_down))
        weight_grads = [grad.reshape((4,) + w_gate.shape) for grad in weight_grads]
        y_sum, out_sum, grad_qkv, grad_out, grad_gain_attn, small, _, gate_recv, up_recv, _ = backward_phase(
            heads, branch, out_part, x_all, w, weight_grads, table, gq, gk, gain_two_grad, w_qkv,
            gain_attn.astype(F32)[:, None], kept)
        grad_gain_attn = grad_gain_attn[:, 0]
        middle = (row + 1) // 2 == 1

        def row_total(own, recv):
            return own.astype(F32) + recv[0].astype(F32) + recv[2].astype(F32) + jnp.where(middle, recv[1].astype(F32), 0.0)

        grad_gate, grad_up, grad_down = (
            row_total(own, recv) for own, recv in ((gate_own, gate_recv), (up_own, up_recv), (down_own, down_recv)))
        grad_gain_ffn, head_gains = small[0, :depth], small[1]
    else:
        gate_slab = lax.all_gather(w_gate, "rows", axis=0, tiled=True)
        up_slab = lax.all_gather(w_up, "rows", axis=0, tiled=True)
        down_slab = lax.all_gather(w_down, "rows", axis=1, tiled=True)
        residual, g_all, *kept = attention_wide(heads, x_all, cotangent[0], w, table, gq, gk)
        out_part, residual_grad, branch, gain_two_grad, gate_wgrad, up_wgrad, down_wgrad = feed_forward_wide(
            residual, gain_two, g_all, gate_slab, up_slab, down_slab)
        grad_gate = lax.psum_scatter(gate_wgrad, "rows", scatter_dimension=0, tiled=True).astype(F32)
        grad_up = lax.psum_scatter(up_wgrad, "rows", scatter_dimension=0, tiled=True).astype(F32)
        grad_down = lax.psum_scatter(down_wgrad, "rows", scatter_dimension=1, tiled=True).astype(F32)
        y_sum, out_sum, attn_grad, head_gains = backward_wide(heads, branch, out_part, x_all, w, table, gq, gk, kept)
        attn_grad = lax.psum_scatter(attn_grad, "rows", scatter_dimension=0, tiled=True)
        attn_grad = lax.all_to_all(attn_grad.reshape(seq, depth, heads.columns), "seq", 0, 0, tiled=False)
        small = lax.psum(jnp.concatenate([gain_two_grad[0], head_gains[:, 0]]), ("rows", "seq"))
        grad_gain_ffn = lax.dynamic_slice_in_dim(small, (row * seq + lax.axis_index("seq")) * depth, depth)
        head_gains = small[model:]
        attn_grad = attn_grad.astype(F32)
        unscaled, grad_out = attention_sums(heads, lambda s: attn_grad[s])
        grad_out = grad_out.T
        grad_gain_attn = jnp.sum(unscaled * w_qkv.astype(F32), axis=1)
        grad_qkv = unscaled * gain_attn.astype(F32)[:, None]

    layer_out = (residual + out_sum).astype(BF16)
    grad_tokens = residual_grad + y_sum - x * (inv * inv * jnp.mean(y_sum * x, axis=-1, keepdims=True))
    return (
        layer_out[None],
        grad_tokens[None],
        grad_gain_attn,
        grad_qkv,
        head_gains[:D],
        head_gains[D:],
        grad_out,
        grad_gain_ffn,
        grad_gate,
        grad_up,
        grad_down,
    )


def solution(mesh):
    both = ("rows", "seq")
    return jax.shard_map(
        body,
        mesh=mesh,
        in_specs=(
            P("rows", "seq", None), P("rows", "seq"), P("rows", "seq"), P("rows", "seq", None),
            P(both), P(both, None), P(), P(), P(None, both), P(both),
            P("rows", "seq"), P("rows", "seq"), P("seq", "rows"),
        ),
        out_specs=(
            P("rows", "seq", None), P("rows", "seq", None), P(both), P(both, None), P(), P(),
            P(None, both), P(both), P("rows", "seq"), P("rows", "seq"), P("seq", "rows"),
        ),
        check_vma=False,
    )
```

```python
import functools
import math

import jax
import jax.numpy as jnp
from jax import lax
from jax.experimental import pallas as pl
from jax.experimental.pallas import tpu as pltpu
from jax.sharding import PartitionSpec as P

QUERY_HEADS = 24
KEY_VALUE_HEADS = 6
GROUP = QUERY_HEADS // KEY_VALUE_HEADS
D = 64
HALF = D // 2
EPSILON = 1e-06
THETA = 10000.0
PENALTY = -10000.0
SEGMENT_KINDS = 8
TABLE_ROWS = 80
BLOCK = 512
PLANE = 8
F32 = jnp.float32
BF16 = jnp.bfloat16
VMEM_LIMIT = 60 * 1024 * 1024
MESH = pl.DeviceIdType.MESH
ANY_SPEC = pl.BlockSpec(memory_space=pl.ANY)
VMEM_SPEC = pl.BlockSpec(memory_space=pltpu.VMEM)


def dot(a, b):
    return jnp.dot(a, b, preferred_element_type=F32)


def dot_nt(a, b):
    return lax.dot_general(a, b, (((1,), (1,)), ((), ())), preferred_element_type=F32)


def dot_tn(a, b):
    return lax.dot_general(a, b, (((0,), (0,)), ((), ())), preferred_element_type=F32)


def norm_inverse(x):
    return lax.rsqrt(jnp.mean(x * x, axis=-1, keepdims=True) + EPSILON)


def split3(x):
    high = x.astype(BF16).astype(F32)
    mid = (x - high).astype(BF16).astype(F32)
    return high, mid, x - high - mid


def span(start, size):
    return pl.ds(pl.multiple_of(start, size), size)


class Heads:
    def __init__(self, seq):
        self.seq = seq
        self.queries = -(-QUERY_HEADS // seq)
        last = [min((s + 1) * self.queries, QUERY_HEADS) - 1 for s in range(seq)]
        self.pairs = max(last[s] // GROUP - self.first(s) + 1 for s in range(seq) if last[s] >= s * self.queries)
        self.wide = self.queries * D
        self.narrow = self.pairs * D
        self.qkv = self.wide + 2 * self.narrow
        self.columns = self.qkv + self.wide

    def first(self, s):
        return (s // 2 * 2 * self.queries) // GROUP

    def slot(self, s, h):
        return (s * self.queries + h) // GROUP - self.first(s)


class Place:
    def __init__(self):
        self.row = lax.axis_index("rows")
        self.me = lax.axis_index("seq")
        self.core = lax.rem(self.me, 2)
        self.chip = self.me // 2
        self.sib = self.me + 1 - 2 * self.core
        chip = self.chip
        self.chips = (chip, chip + 1 - 2 * lax.rem(chip, 2), lax.rem(chip + 2, 4), 3 - chip)
        self.same = tuple(2 * q + self.core for q in self.chips)

    def greet(self, rows=1):
        barrier = pltpu.get_barrier_semaphore()
        for other in (self.sib, self.same[1], self.same[2]):
            pl.semaphore_signal(barrier, inc=1, device_id=(self.row, other), device_id_type=MESH)
        for j in range(1, rows):
            other = lax.rem(self.row + j, rows)
            pl.semaphore_signal(barrier, inc=1, device_id=(other, self.me), device_id_type=MESH)
        pl.semaphore_wait(barrier, 3 + rows - 1)

    def greet_all(self, rows):
        barrier = pltpu.get_barrier_semaphore()
        for j in range(1, PLANE):
            other = lax.rem(self.me + j, PLANE)
            pl.semaphore_signal(barrier, inc=1, device_id=(self.row, other), device_id_type=MESH)
        for j in range(1, rows):
            other = lax.rem(self.row + j, rows)
            pl.semaphore_signal(barrier, inc=1, device_id=(other, self.me), device_id_type=MESH)
        pl.semaphore_wait(barrier, PLANE - 1 + rows - 1)

    def send(self, src, dst, send_sem, recv_sem, slot, target):
        return pltpu.make_async_remote_copy(
            src_ref=src, dst_ref=dst, send_sem=send_sem.at[slot], recv_sem=recv_sem.at[slot],
            device_id=(self.row, target), device_id_type=MESH)


class Line:
    def __init__(self, place):
        self.place = place
        row = place.row
        self.a = row + 1 - 2 * lax.rem(row, 2)
        self.b = 3 - row
        self.c = lax.rem(row + 2, 4)
        self.middle = (row + 1) // 2 == 1

    def send(self, src, dst, send_sem, send_slot, recv_sem, recv_slot, target):
        return pltpu.make_async_remote_copy(
            src_ref=src, dst_ref=dst, send_sem=send_sem.at[send_slot], recv_sem=recv_sem.at[recv_slot],
            device_id=(target, self.place.me), device_id_type=MESH)


ROW_SLOTS = 4


class RowGather:
    def __init__(self, line, own, at, send_sem, recv_sem):
        self.line = line
        mine, passed = at(line.place.row), at(line.c)
        self.to_a = line.send(own, mine, send_sem, 0, recv_sem, 0, line.a)
        self.to_c = line.send(own, mine, send_sem, 1, recv_sem, 1, line.c)
        self.to_b = line.send(own, mine, send_sem, 2, recv_sem, 2, line.b)
        self.on = line.send(passed, passed, send_sem, 3, recv_sem, 2, line.a)

    def start(self):
        self.to_c.start()
        self.to_a.start()

        @pl.when(self.line.middle)
        def _():
            self.to_b.start()

    def forward(self):
        self.to_c.wait_recv()

        @pl.when(self.line.middle)
        def _():
            self.on.start()

    def finish(self):
        self.to_a.wait_recv()
        self.to_b.wait_recv()

    def close(self):
        self.to_a.wait_send()
        self.to_c.wait_send()

        @pl.when(self.line.middle)
        def _():
            self.to_b.wait_send()
            self.on.wait_send()


class RowScatter:
    def __init__(self, line, part, recv, merge, total, send_sem, recv_sem):
        self.line, self.total = line, total
        self.to_a = line.send(part.at[line.a], recv.at[0], send_sem, 0, recv_sem, 0, line.a)
        self.to_b = line.send(part.at[line.b], recv.at[1], send_sem, 1, recv_sem, 1, line.b)
        self.to_c = line.send(part.at[line.c], recv.at[2], send_sem, 2, recv_sem, 2, line.c)
        self.added = line.send(total, recv.at[2], send_sem, 2, recv_sem, 2, line.c)
        self.over = line.send(part.at[line.b], merge, send_sem, 3, recv_sem, 3, line.a)

    def start_over(self):
        @pl.when(jnp.logical_not(self.line.middle))
        def _():
            self.over.start()

    def start(self):
        @pl.when(jnp.logical_not(self.line.middle))
        def _():
            self.to_c.start()

        @pl.when(self.line.middle)
        def _():
            self.to_b.start()

        self.to_a.start()

    def add(self, work):
        @pl.when(self.line.middle)
        def _():
            self.over.wait_recv()
            work()
            self.added.start()

    def finish(self):
        self.to_a.wait_recv()
        self.to_c.wait_recv()

        @pl.when(self.line.middle)
        def _():
            self.to_b.wait_recv()

    def close(self):
        self.to_a.wait_send()
        self.to_c.wait_send()

        @pl.when(self.line.middle)
        def _():
            self.to_b.wait_send()

        @pl.when(jnp.logical_not(self.line.middle))
        def _():
            self.over.wait_send()


GATHER_SLOTS = 10


class Gather:
    def __init__(self, place, own, every, send_sem, recv_sem):
        half = every.shape[1] // 2
        low, high, whole = slice(0, half), slice(half, 2 * half), slice(0, 2 * half)

        def send(part, b, slot, target, src=None):
            src = every.at[b, part] if src is None else src.at[part]
            return place.send(src, every.at[b, part], send_sem, recv_sem, slot, target)

        me, (_, s1, s2, s3), sib = place.me, place.same, place.sib
        self.copies = (
            send(whole, me, 0, sib, own),
            send(low, me, 1, s1, own), send(high, me, 2, s1, own),
            send(high, me, 3, s2, own), send(low, me, 4, s2, own),
            send(low, s1, 5, s2), send(high, s2, 6, s1),
            send(whole, s1, 7, sib), send(whole, s2, 8, sib), send(whole, s3, 9, sib),
        )

    def start(self):
        for slot in (1, 3, 2, 4, 0):
            self.copies[slot].start()

    def own_chip(self):
        self.copies[0].wait_recv()

    def neighbours(self):
        c = self.copies
        c[1].wait_recv()
        c[5].start()
        c[3].wait_recv()
        c[6].start()
        c[2].wait_recv()
        c[7].start()
        c[4].wait_recv()
        c[8].start()

    def chip1(self):
        self.copies[7].wait_recv()

    def chip2(self):
        self.copies[8].wait_recv()

    def diagonal(self):
        c = self.copies
        c[5].wait_recv()
        c[6].wait_recv()
        c[9].start()

    def chip3(self):
        self.copies[9].wait_recv()

    def close(self):
        for copy in self.copies:
            copy.wait_send()


SCATTER_SLOTS = 10


class Scatter:
    def __init__(self, place, part, sibling, passing, final, send_sem, recv_sem):
        self.place, self.part, self.sibling, self.passing, self.final = place, part, sibling, passing, final
        half = part.shape[2] // 2
        self.half = half
        core, other = place.core, 1 - place.core
        _, s1, s2, _ = place.same
        send = lambda src, dst, slot, target: place.send(src, dst, send_sem, recv_sem, slot, target)
        low, high = slice(0, half), slice(half, 2 * half)
        self.exchange = tuple(send(part.at[k, other], sibling.at[k], k, place.sib) for k in range(4))
        self.pass1 = send(part.at[3, core, low], passing.at[0], 4, s1)
        self.pass2 = send(part.at[3, core, high], passing.at[1], 5, s2)
        self.first1 = send(part.at[1, core, low], final.at[0, low], 6, s1)
        self.second1 = send(part.at[1, core, high], final.at[0, high], 7, s1)
        self.first2 = send(part.at[2, core, high], final.at[1, high], 8, s2)
        self.second2 = send(part.at[2, core, low], final.at[1, low], 9, s2)

    def add(self, k, start, size, term, offset):
        core, step = self.place.core, 64

        def one(i, _):
            rows = pl.ds(pl.multiple_of(start + i * step, step), step)
            from_rows = pl.ds(pl.multiple_of(offset + i * step, step), step)
            self.part[k, core, rows, :] = self.part[k, core, rows, :] + term[from_rows, :]
            return 0

        lax.fori_loop(0, size // step, one, 0)

    def combine(self, k):
        self.exchange[k].wait_recv()
        self.add(k, 0, 2 * self.half, self.sibling.at[k], 0)

    def finish_two(self):
        self.pass1.wait_recv()
        self.add(2, 0, self.half, self.passing.at[0], 0)
        self.second2.start()
        self.pass2.wait_recv()
        self.add(1, self.half, self.half, self.passing.at[1], 0)
        self.second1.start()

    def arrive(self):
        for copy in (self.first1, self.second1, self.first2, self.second2):
            copy.wait_recv()

    def total(self, rows):
        return (self.part[0, self.place.core, rows, :].astype(F32) + self.final[0, rows, :].astype(F32)
                + self.final[1, rows, :].astype(F32))

    def close(self):
        for copy in self.exchange + (self.pass1, self.pass2, self.first1, self.second1, self.first2, self.second2):
            copy.wait_send()


def scatter_scratch(tok, width):
    return [
        pltpu.VMEM((4, 2, tok, width), BF16),
        pltpu.VMEM((4, tok, width), BF16),
        pltpu.VMEM((2, tok // 2, width), BF16),
        pltpu.VMEM((2, tok, width), BF16),
        pltpu.SemaphoreType.DMA((SCATTER_SLOTS,)),
        pltpu.SemaphoreType.DMA((SCATTER_SLOTS,)),
    ]


def start_kernel(x_ref, table_ref, kv_ref, qo_ref, gain_ref, x_all, table_all, kv_all, qo_all, gain_all,
                 x_send, x_recv, t_send, t_recv, k_send, k_recv, p_send, p_recv, g_send, g_recv, z_send, z_recv,
                 w_send, w_recv, pair_send, pair_recv, local_sem):
    place = Place()
    rows = qo_all.shape[0]
    me, row, core = place.me, place.row, place.core
    local = [pltpu.make_async_copy(src, dst, local_sem.at[i]) for i, (src, dst) in enumerate((
        (kv_ref.at[me], kv_all.at[core, row, me]), (qo_ref.at[me], qo_all.at[row, me]), (gain_ref, gain_all.at[row, me]),
        (x_ref, x_all.at[me]), (table_ref, table_all.at[me])))]
    for copy in local:
        copy.start()
    place.greet_all(rows)
    exchange, rest = [], []
    for j in range(1, PLANE):
        other = lax.rem(me + j, PLANE)
        exchange.append(place.send(kv_ref.at[other], kv_all.at[lax.rem(other, 2), row, me], k_send, k_recv, j, other))
        rest.append(place.send(qo_ref.at[other], qo_all.at[row, me], p_send, p_recv, j, other))
        rest.append(place.send(gain_ref, gain_all.at[row, me], g_send, g_recv, j, other))
    for copy in exchange + rest:
        copy.start()
    gathers = (Gather(place, x_ref, x_all, x_send, x_recv), Gather(place, table_ref, table_all, t_send, t_recv))
    gathers[1].start()
    gathers[0].start()
    for copy in local[:3]:
        copy.wait()
    line = Line(place)
    weights = [RowGather(line, at(row), at, w_send.at[i], w_recv.at[i])
               for i, at in enumerate((lambda r: kv_all.at[core, r], lambda r: qo_all.at[r]))]
    for copy in exchange:
        copy.wait_recv()
    weights[0].start()
    for copy in rest:
        copy.wait_recv()
    weights[1].start()
    along = []
    for j in range(1, rows):
        other = lax.rem(row + j, rows)
        along.append(line.send(gain_all.at[row], gain_all.at[row], z_send, j, z_recv, j, other))
    for copy in along:
        copy.start()
    for gather in gathers[::-1]:
        gather.own_chip()
    weights[0].forward()
    for gather in gathers[::-1]:
        gather.neighbours()
    weights[0].finish()
    pair = place.send(kv_all.at[core], kv_all.at[core], pair_send, pair_recv, 0, place.sib)
    pair.start()
    weights[1].forward()
    for name in ("chip1", "chip2", "diagonal", "chip3"):
        for gather in gathers[::-1]:
            getattr(gather, name)()
    for copy in local[3:]:
        copy.wait()
    for copy in along:
        copy.wait_recv()
    for copy in exchange + rest + along:
        copy.wait_send()
    for gather in gathers:
        gather.close()
    weights[1].finish()
    pair.wait_recv()
    pair.wait_send()
    for one in weights:
        one.close()


def start_phase(rows, x, table, kv, qo, gain):
    tok, model = x.shape
    dma = pltpu.SemaphoreType.DMA
    return pl.pallas_call(
        start_kernel,
        out_shape=(
            jax.ShapeDtypeStruct((PLANE, tok, model), BF16),
            jax.ShapeDtypeStruct((PLANE,) + table.shape, F32),
            jax.ShapeDtypeStruct((2, rows) + kv.shape, BF16),
            jax.ShapeDtypeStruct((rows,) + qo.shape, BF16),
            jax.ShapeDtypeStruct((rows, PLANE) + gain.shape, F32),
        ),
        in_specs=[VMEM_SPEC] * 5,
        out_specs=(ANY_SPEC,) * 5,
        scratch_shapes=[dma((GATHER_SLOTS,))] * 4 + [dma((PLANE,))] * 6 + [dma((rows,))] * 2
        + [dma((2, ROW_SLOTS))] * 2 + [dma((1,))] * 2 + [dma((5,))],
        compiler_params=pltpu.CompilerParams(collective_id=0, has_side_effects=True),
        cost_estimate=pl.CostEstimate(flops=0, bytes_accessed=160 << 20, transcendentals=0),
    )(x, table, kv, qo, gain)


def load_slab(kv_hbm, qo_hbm, w_ref, sem):
    parts = ((kv_hbm.at[0], 0, 128), (kv_hbm.at[1], 128, 256), (qo_hbm, 256, 640))
    return [pltpu.make_async_copy(src, w_ref.at[:, a:b], sem.at[i]) for i, (src, a, b) in enumerate(parts)]


class Forward:
    def __init__(self, heads, me, table, gq, gk, raw, merged, o, qa, ka, kt, vt, inv):
        self.heads, self.table, self.gq, self.gk = heads, table, gq[...], gk[...]
        self.raw, self.merged, self.o, self.qa, self.ka, self.kt, self.vt, self.inv = raw, merged, o, qa, ka, kt, vt, inv
        self.slots = [heads.slot(me, h) for h in range(heads.queries)]

    def prepare(self, b, projected):
        heads = self.heads
        tok = self.table.shape[2]
        lanes = span(b * tok, tok)
        cos = self.table[b, 0:HALF, :]
        sin = self.table[b, HALF:D, :]
        hot = self.table[b, D:D + 8, :]
        row = lax.broadcasted_iota(jnp.int32, (16, tok), 0)
        one_row = jnp.where(row == 0, 1.0, 0.0).astype(F32)
        penalty = jnp.concatenate([(1.0 - hot) * PENALTY, jnp.zeros((8, tok), F32)], axis=0).astype(BF16)
        lead = 2 * heads.narrow
        self.raw[0:heads.wide, lanes] = projected[lead:lead + heads.wide]

        def rotated(raw, gain):
            inv = lax.rsqrt(jnp.mean(raw * raw, axis=0, keepdims=True) + EPSILON)
            n = raw * inv * gain
            a, c = n[:HALF], n[HALF:]
            return inv, jnp.concatenate([a * cos - c * sin, c * cos + a * sin], axis=0)

        for h in range(heads.queries):
            inv, q = rotated(projected[lead + h * D:lead + (h + 1) * D], self.gq)
            self.inv[h:h + 1, lanes] = inv
            self.qa[h, :, lanes] = jnp.concatenate([(q * (D ** -0.5)).astype(BF16), penalty], axis=0)
        for g in range(heads.pairs):
            start = 2 * g * D
            self.raw[heads.wide + g * D:heads.wide + (g + 1) * D, lanes] = projected[start:start + D]
            inv, k = rotated(projected[start:start + D], self.gk)
            self.inv[heads.queries + g:heads.queries + g + 1, lanes] = inv
            self.kt[g, :, lanes] = k.astype(BF16)
            full = jnp.concatenate([k, hot, jnp.ones((8, tok), F32), jnp.zeros((48, tok), F32)], axis=0)
            self.ka[g, lanes, :] = jnp.transpose(full).astype(BF16)
            start += D
            self.vt[g, :, lanes] = jnp.concatenate([projected[start:start + D], one_row], axis=0).astype(BF16)

    def query_block(self, i):
        heads = self.heads
        cols = span(i * BLOCK, BLOCK)
        causal = (lax.broadcasted_iota(jnp.int32, (BLOCK, BLOCK), 0)
                  <= lax.broadcasted_iota(jnp.int32, (BLOCK, BLOCK), 1))

        def step(j, accs, diagonal):
            rows = span(j * BLOCK, BLOCK)
            new = []
            for h in range(heads.queries):
                slot = self.slots[h]
                p = jnp.exp(dot(self.ka[slot, rows, 0:80], self.qa[h, :, cols]))
                if diagonal:
                    p = jnp.where(causal, p, 0.0)
                new.append(accs[h] + dot(self.vt[slot, :, rows], p.astype(BF16)))
            return tuple(new)

        accs = tuple(jnp.zeros((80, BLOCK), F32) for _ in range(heads.queries))
        accs = lax.fori_loop(0, i, lambda j, c: step(j, c, False), accs)
        accs = step(i, accs, True)
        row = lax.broadcasted_iota(jnp.int32, (16, BLOCK), 0)
        lead = self.merged.shape[1] - heads.wide
        outs = [jnp.zeros((lead, BLOCK), F32)] if lead else []
        for h in range(heads.queries):
            total = accs[h][D:D + 1]
            o = accs[h][:D] * (1.0 / total)
            self.o[h, :, cols] = o
            outs.append(o)
            pieces = split3(-jnp.log(total))
            old = self.qa[h, 64:80, cols].astype(F32)
            extra = jnp.where(row == 8, pieces[0],
                              jnp.where(row == 9, pieces[1], jnp.where(row == 10, pieces[2], old)))
            self.qa[h, 64:80, cols] = extra.astype(BF16)
        merged = jnp.transpose(jnp.concatenate(outs, axis=0)).astype(BF16)
        self.merged[cols, :] = merged
        return merged


class Backward:
    def __init__(self, heads, me, table, gq, gk, raw, o, qa, ka, kt, vt, inv, doa, dopad, qpad, va, dq, acc):
        self.heads, self.table, self.gq, self.gk = heads, table, gq[...], gk[...]
        self.raw, self.o, self.qa, self.ka, self.kt, self.vt, self.inv = raw, o, qa, ka, kt, vt, inv
        self.doa, self.dopad, self.qpad, self.va, self.dq, self.acc = doa, dopad, qpad, va, dq, acc
        self.slots = [heads.slot(me, h) for h in range(heads.queries)]

    def prepare(self, b):
        heads = self.heads
        tok = self.table.shape[2]
        lanes = span(b * tok, tok)
        for h in range(heads.queries):
            q = jnp.concatenate([jnp.zeros((D, tok), F32), self.qa[h, 0:D, lanes].astype(F32)], axis=0)
            self.qpad[h, lanes, :] = jnp.transpose(q).astype(BF16)
            self.acc[h, lanes, :] = jnp.zeros((tok, 2 * D), F32)
        for g in range(heads.pairs):
            v = jnp.concatenate([self.vt[g, 0:D, lanes].astype(F32), jnp.ones((D, tok), F32)], axis=0)
            self.va[g, lanes, :] = jnp.transpose(v).astype(BF16)

    def gradient(self, b, dm):
        heads = self.heads
        tok = self.table.shape[2]
        lanes = span(b * tok, tok)
        row = lax.broadcasted_iota(jnp.int32, (16, tok), 0)
        dmt = jnp.transpose(dm.astype(BF16).astype(F32))
        for h in range(heads.queries):
            do = dmt[h * D:(h + 1) * D]
            delta = jnp.sum(do * self.o[h, :, lanes], axis=0, keepdims=True)
            pieces = split3(-delta)
            extra = jnp.where(row == 0, pieces[0],
                              jnp.where(row == 1, pieces[1], jnp.where(row == 2, pieces[2], 0.0)))
            self.doa[h, :, lanes] = jnp.concatenate([do, extra], axis=0).astype(BF16)
            both = jnp.concatenate([do, jnp.zeros((D, tok), F32)], axis=0)
            self.dopad[h, lanes, :] = jnp.transpose(both).astype(BF16)

    def query_block(self, i):
        heads = self.heads
        cols = span(i * BLOCK, BLOCK)
        causal = (lax.broadcasted_iota(jnp.int32, (BLOCK, BLOCK), 0)
                  <= lax.broadcasted_iota(jnp.int32, (BLOCK, BLOCK), 1))

        def step(j, accs, diagonal):
            rows = span(j * BLOCK, BLOCK)
            new = []
            for h in range(heads.queries):
                slot = self.slots[h]
                p = jnp.exp(dot(self.ka[slot, rows, 0:80], self.qa[h, :, cols]))
                if diagonal:
                    p = jnp.where(causal, p, 0.0)
                dp = dot(self.va[slot, rows, 0:80], self.doa[h, :, cols])
                ds = (p * dp).astype(BF16)
                self.acc[h, rows, :] += dot(p.astype(BF16), self.dopad[h, cols, :]) + dot(ds, self.qpad[h, cols, :])
                new.append(accs[h] + dot(self.kt[slot, :, rows], ds))
            return tuple(new)

        accs = tuple(jnp.zeros((D, BLOCK), F32) for _ in range(heads.queries))
        accs = lax.fori_loop(0, i, lambda j, c: step(j, c, False), accs)
        accs = step(i, accs, True)
        for h in range(heads.queries):
            self.dq[h, :, cols] = accs[h]

    def finish(self, b, sums):
        heads = self.heads
        tok = self.table.shape[2]
        lanes = span(b * tok, tok)
        cos = self.table[b, 0:HALF, :]
        sin = self.table[b, HALF:D, :]
        scale = self.table[b, 72:73, :]

        def back(grad, raw, inv, gain):
            a, c = grad[:HALF], grad[HALF:]
            n = jnp.concatenate([a * cos + c * sin, c * cos - a * sin], axis=0)
            v = n * gain
            out = inv * v - raw * (inv * inv * inv) * jnp.mean(v * raw, axis=0, keepdims=True)
            return out * scale, n * raw * inv

        sum_q, sum_k = sums
        pairs = [jnp.zeros((2 * D, tok), F32) for _ in range(heads.pairs)]
        out = []
        for h in range(heads.queries):
            raw = self.raw[h * D:(h + 1) * D, lanes]
            grad, part = back(self.dq[h, :, lanes] * (D ** -0.5), raw, self.inv[h:h + 1, lanes], self.gq)
            out.append(grad)
            sum_q = sum_q + part
            both = jnp.transpose(self.acc[h, lanes, :])
            for g in range(heads.pairs):
                pairs[g] = pairs[g] + jnp.where(self.slots[h] == g, both, 0.0)
        both_out = []
        for g in range(heads.pairs):
            start = heads.wide + g * D
            raw = self.raw[start:start + D, lanes]
            inv = self.inv[heads.queries + g:heads.queries + g + 1, lanes]
            grad, part = back(pairs[g][D:], raw, inv, self.gk)
            both_out += [grad, pairs[g][:D] * scale]
            sum_k = sum_k + part
        return jnp.concatenate(both_out + out, axis=0), (sum_q, sum_k)


def kept_shapes(heads, length, lead):
    return (
        jax.ShapeDtypeStruct((heads.wide + heads.narrow, length), F32),
        jax.ShapeDtypeStruct((length, lead + heads.wide), BF16),
        jax.ShapeDtypeStruct((heads.queries, D, length), F32),
        jax.ShapeDtypeStruct((heads.queries, 80, length), BF16),
        jax.ShapeDtypeStruct((heads.pairs, length, 128), BF16),
        jax.ShapeDtypeStruct((heads.pairs, D, length), BF16),
        jax.ShapeDtypeStruct((heads.pairs, 80, length), BF16),
        jax.ShapeDtypeStruct((8, length), F32),
    )


def backward_scratch(heads, length):
    return [
        pltpu.VMEM((heads.queries, 80, length), BF16),
        pltpu.VMEM((heads.queries, length, 2 * D), BF16),
        pltpu.VMEM((heads.queries, length, 2 * D), BF16),
        pltpu.VMEM((heads.pairs, length, 2 * D), BF16),
        pltpu.VMEM((heads.queries, D, length), F32),
        pltpu.VMEM((heads.queries, length, 2 * D), F32),
    ]


def local_forward_kernel(heads, proj_ref, table_ref, gq_ref, gk_ref, *kept):
    forward = Forward(heads, lax.axis_index("seq"), table_ref, gq_ref, gk_ref, *kept)
    blocks, _, tok = table_ref.shape

    def prepare(b, _):
        rows = span(b * tok, tok)
        forward.prepare(b, jnp.transpose(proj_ref[rows, :]) * table_ref[b, 72:73, :])
        return 0

    def query_block(i, _):
        forward.query_block(i)
        return 0

    lax.fori_loop(0, blocks, prepare, 0)
    lax.fori_loop(0, blocks * tok // BLOCK, query_block, 0)


def local_backward_kernel(heads, dm_ref, table_ref, gq_ref, gk_ref, raw_ref, o_ref, qa_ref, ka_ref, kt_ref, vt_ref, inv_ref,
                          pg_ref, gains_ref, *scratch):
    backward = Backward(heads, lax.axis_index("seq"), table_ref, gq_ref, gk_ref, raw_ref, o_ref, qa_ref, ka_ref, kt_ref,
                        vt_ref, inv_ref, *scratch)
    blocks, _, tok = table_ref.shape

    def prepare(b, _):
        backward.prepare(b)
        backward.gradient(b, dm_ref[span(b * tok, tok), :])
        return 0

    def query_block(i, _):
        backward.query_block(i)
        return 0

    def finish(b, sums):
        grad, sums = backward.finish(b, sums)
        pg_ref[span(b * tok, tok), :] = jnp.transpose(grad).astype(BF16)
        return sums

    lax.fori_loop(0, blocks, prepare, 0)
    lax.fori_loop(0, blocks * tok // BLOCK, query_block, 0)
    zero = jnp.zeros((D, tok), F32)
    sum_q, sum_k = lax.fori_loop(0, blocks, finish, (zero, zero))
    gains_ref[0:D, :] = jnp.broadcast_to(jnp.sum(sum_q, axis=1, keepdims=True), (D, 128))
    gains_ref[D:2 * D, :] = jnp.broadcast_to(jnp.sum(sum_k, axis=1, keepdims=True), (D, 128))


def attention_kernel(heads, x_hbm, g_hbm, kv_hbm, qo_hbm, gate_hbm, up_hbm, table_ref, gq_ref, gk_ref, gain_ref,
                     res_ref, two_ref, g_all, gate_all, up_all, raw_hbm, merged_hbm, o_hbm, qa_hbm, ka_hbm, kt_hbm, vt_hbm, inv_hbm,
                     raw_ref, merged_ref, o_ref, qa_ref, ka_ref, kt_ref, vt_ref, inv_ref, kept_sem, x_ref, w_ref, part_ref, sibling_ref, passing_ref, final_ref, rs_send, rs_recv,
                     ag_send, ag_recv, load_sem, slab_sem, z_send, z_recv):
    place = Place()
    blocks, tok, model = x_ref.shape
    slabs = ((gate_hbm, gate_all), (up_hbm, up_all))
    load_w = load_slab(kv_hbm, qo_hbm, w_ref, slab_sem)
    for copy in load_w:
        copy.start()
    loads = [pltpu.make_async_copy(x_hbm.at[b], x_ref.at[b], load_sem.at[b]) for b in range(blocks)]
    for copy in loads:
        copy.start()
    place.greet(4)
    gather = Gather(place, g_hbm, g_all, ag_send, ag_recv)
    scatter = Scatter(place, part_ref, sibling_ref, passing_ref, final_ref, rs_send, rs_recv)
    line = Line(place)
    weights = [RowGather(line, own, lambda r, every=every: every.at[r], z_send.at[i], z_recv.at[i])
               for i, (own, every) in enumerate(slabs)]
    for one in weights:
        one.start()
    gather.start()
    forward = Forward(heads, place.me, table_ref, gq_ref, gk_ref, raw_ref, merged_ref, o_ref, qa_ref, ka_ref, kt_ref,
                      vt_ref, inv_ref)
    for copy in load_w + loads:
        copy.wait()

    def prepare(b, _):
        proj = dot(x_ref[b], w_ref[:, 0:512])
        forward.prepare(b, jnp.transpose(proj) * table_ref[b, 72:73, :])
        return 0

    lax.fori_loop(0, blocks, prepare, 0, unroll=2)
    tile = 512

    def compute(k):
        merged = forward.query_block(place.chips[k])

        def model_tile(n, _):
            cols = span(n * tile, tile)
            out = dot_nt(merged_ref[span(place.chips[k] * BLOCK, BLOCK), :], w_ref[cols, 384:640])
            part_ref[k, :, :, cols] = out.astype(BF16).reshape(2, tok, tile)
            return 0

        lax.fori_loop(0, model // tile, model_tile, 0, unroll=True)
        scatter.exchange[k].start()

    compute(3)
    gather.own_chip()
    gather.neighbours()
    scatter.combine(3)
    scatter.pass1.start()
    scatter.pass2.start()
    compute(1)
    scatter.combine(1)
    scatter.first1.start()
    gather.chip1()
    gather.chip2()
    weights[0].forward()
    compute(2)
    scatter.combine(2)
    scatter.first2.start()
    gather.diagonal()
    compute(0)
    keep = [pltpu.make_async_copy(src, dst, kept_sem.at[i]) for i, (src, dst) in enumerate((
        (raw_ref, raw_hbm), (merged_ref, merged_hbm), (o_ref, o_hbm), (qa_ref, qa_hbm), (ka_ref, ka_hbm),
        (kt_ref, kt_hbm), (vt_ref, vt_hbm), (inv_ref, inv_hbm)))]
    for copy in keep:
        copy.start()
    scatter.combine(0)
    weights[1].forward()
    scatter.finish_two()
    gather.chip3()
    scatter.arrive()

    def finish(i, _):
        rows = span(i * 32, 32)
        res = x_ref[place.me, rows, :].astype(F32) + scatter.total(rows)
        res_ref[rows, :] = res
        two_ref[rows, :] = (res * norm_inverse(res) * gain_ref[...]).astype(BF16)
        return 0

    lax.fori_loop(0, tok // 32, finish, 0)
    for one in weights:
        one.finish()
        one.close()
    for copy in keep:
        copy.wait()
    gather.close()
    scatter.close()


def attention_phase(heads, x_all, g, kv, qo, slabs, table, gq, gk, gain):
    blocks, tok, model = x_all.shape
    dma = pltpu.SemaphoreType.DMA
    lead = 256 - heads.wide
    kept = kept_shapes(heads, blocks * tok, lead)
    return pl.pallas_call(
        functools.partial(attention_kernel, heads),
        out_shape=(jax.ShapeDtypeStruct((tok, model), F32), jax.ShapeDtypeStruct((tok, model), BF16),
                   jax.ShapeDtypeStruct((blocks, tok, model), BF16))
        + tuple(jax.ShapeDtypeStruct((4,) + slab.shape, BF16) for slab in slabs) + kept,
        in_specs=[ANY_SPEC] * 6 + [VMEM_SPEC] * 4,
        out_specs=(VMEM_SPEC, VMEM_SPEC) + (ANY_SPEC,) * (3 + len(kept)),
        scratch_shapes=[
            *(pltpu.VMEM(array.shape, array.dtype) for array in kept),
            dma((len(kept),)),
            pltpu.VMEM((blocks, tok, model), BF16),
            pltpu.VMEM((model, heads.columns), BF16),
            *scatter_scratch(tok, model),
            dma((GATHER_SLOTS,)), dma((GATHER_SLOTS,)), dma((blocks,)), dma((3,)),
            dma((2, ROW_SLOTS)), dma((2, ROW_SLOTS)),
        ],
        compiler_params=pltpu.CompilerParams(collective_id=1, has_side_effects=True, vmem_limit_bytes=VMEM_LIMIT),
        cost_estimate=pl.CostEstimate(flops=40 << 30, bytes_accessed=64 << 20, transcendentals=0),
    )(x_all, g, kv, qo, *slabs, table, gq, gk, gain)


def ffn_kernel(res_ref, gain_ref, two_hbm, g_own, g_hbm, gate_own, gate_hbm, up_own, up_hbm, down_hbm,
               out_hbm, rgrad_ref, branch_ref, gain_grad_ref, gate_grad_hbm, up_grad_hbm,
               gate_grad_own, up_grad_own, down_own, down_recv,
               two_ref, g_ref, weight_ref, down_ref, hid_ref, gu_ref, stage_ref, wstage_ref, dsum_ref, dgrad_ref, merge_ref,
               part_ref, sibling_ref, passing_ref, final_ref, rs_send, rs_recv,
               ag_send, ag_recv, load_sem, g_sem, stage_sem, wstage_sem, own_sem, za_send, za_recv, zr_send, zr_recv):
    place = Place()
    blocks, tok, model = g_ref.shape
    ff = weight_ref.shape[1] // 2
    share = model // 4
    tile = 256
    def down_at(r):
        return down_ref.at[:, span(r * share, share)]

    loads, g_loads = [], []
    for i, (own, every) in enumerate(((gate_own, gate_hbm), (up_own, up_hbm))):
        for j in range(4):
            r = lax.rem(place.row + j, 4)
            loads.append(pltpu.make_async_copy(
                every.at[r] if j else own, weight_ref.at[span(r * share, share), i * ff:(i + 1) * ff], load_sem.at[4 * i + j]))
    for j in range(blocks):
        b = lax.rem(place.me + j, blocks)
        g_loads.append(pltpu.make_async_copy(g_hbm.at[b] if j else g_own, g_ref.at[b], g_sem.at[j]))
    own_loads = [pltpu.make_async_copy(two_hbm, two_ref.at[place.me], load_sem.at[8]),
                 pltpu.make_async_copy(down_hbm, down_at(place.row), load_sem.at[9])]
    for copy in own_loads + loads + g_loads:
        copy.start()
    place.greet(4)
    line = Line(place)
    gather = Gather(place, two_hbm, two_ref, ag_send, ag_recv)
    scatter = Scatter(place, part_ref, sibling_ref, passing_ref, final_ref, rs_send, rs_recv)
    downs = RowGather(line, down_hbm, down_at, za_send, za_recv)
    down_sum = RowScatter(line, dgrad_ref, down_recv, merge_ref, merge_ref, zr_send, zr_recv)
    gather.start()
    downs.start()
    for copy in loads + own_loads:
        copy.wait()

    def forward(k):
        pair = pl.ds(2 * place.chips[k], 2)

        def hidden_tile(h, _):
            cols, cols2 = span(h * tile, tile), span(ff + h * tile, tile)
            x = two_ref[pair].reshape(2 * tok, model)
            gate = dot(x, weight_ref[:, cols])
            up = dot(x, weight_ref[:, cols2])
            s = 1.0 / (1.0 + jnp.exp(-gate))
            act = gate * s
            hid_ref[pair, :, cols] = (act * up).astype(BF16).reshape(2, tok, tile)
            gu_ref[pair, :, cols] = (up * s * (1.0 + gate * (1.0 - s))).astype(BF16).reshape(2, tok, tile)
            gu_ref[pair, :, cols2] = act.astype(BF16).reshape(2, tok, tile)
            return 0

        lax.fori_loop(0, ff // tile, hidden_tile, 0, unroll=True)

    def backward(k):
        pair = pl.ds(2 * place.chips[k], 2)

        def hidden_tile(h, _):
            cols, cols2 = span(h * tile, tile), span(ff + h * tile, tile)
            back = dot_nt(g_ref[pair].reshape(2 * tok, model), down_ref[cols, :])
            for where in (cols, cols2):
                factor = gu_ref[pair, :, where].reshape(2 * tok, tile).astype(F32)
                gu_ref[pair, :, where] = (back * factor).astype(BF16).reshape(2, tok, tile)
            return 0

        lax.fori_loop(0, ff // tile, hidden_tile, 0, unroll=True)

        def model_tile(n, _):
            cols = span(n * tile, tile)
            back = dot_nt(gu_ref[pair].reshape(2 * tok, 2 * ff), weight_ref[cols, :])
            part_ref[k, :, :, cols] = back.astype(BF16).reshape(2, tok, tile)
            return 0

        lax.fori_loop(0, model // tile, model_tile, 0, unroll=True)
        scatter.exchange[k].start()

    def stage_copy(n):
        slot = lax.rem(n, 2)
        return pltpu.make_async_copy(stage_ref.at[slot], out_hbm.at[n // 4, :, :, span(lax.rem(n, 4) * share, share)],
                                     stage_sem.at[slot])

    def out_tile(n, _):
        @pl.when(n >= 2)
        def _():
            stage_copy(n - 2).wait()

        k, r = n // 4, lax.rem(n, 4)
        chip = place.chip
        m = jnp.where(k == 0, chip, jnp.where(k == 1, place.chips[1], jnp.where(k == 2, place.chips[2], place.chips[3])))
        out = dot(hid_ref[pl.ds(2 * m, 2)].reshape(2 * tok, ff), down_ref[:, span(r * share, share)])
        stage_ref[lax.rem(n, 2)] = out.astype(BF16).reshape(2, tok, share)
        stage_copy(n).start()
        return 0

    def down_grad(k):
        pair = pl.ds(2 * place.chips[k], 2)

        def down_rows(n, _):
            rows, r = span(lax.rem(n, ff // tile) * tile, tile), n // (ff // tile)
            h = hid_ref[pair, :, rows].reshape(2 * tok, tile)
            g = g_ref[pair, :, span(r * share, share)].reshape(2 * tok, share)
            term = dot_tn(h, g)
            if k:
                term = dsum_ref[r, rows, :] + term
            if k < 3:
                dsum_ref[r, rows, :] = term
            else:
                dgrad_ref[r, rows, :] = term.astype(BF16)
            return 0

        lax.fori_loop(0, 4 * (ff // tile), down_rows, 0, unroll=4)

    def wstage_copies(i, slot):
        return (pltpu.make_async_copy(wstage_ref.at[slot, :, 0:ff], gate_grad_hbm.at[i], wstage_sem.at[slot, 0]),
                pltpu.make_async_copy(wstage_ref.at[slot, :, ff:2 * ff], up_grad_hbm.at[i], wstage_sem.at[slot, 1]))

    def own_copies(half, slot):
        rows = span(half * tile, tile)
        return (pltpu.make_async_copy(wstage_ref.at[slot, :, 0:ff], gate_grad_own.at[rows], own_sem.at[0]),
                pltpu.make_async_copy(wstage_ref.at[slot, :, ff:2 * ff], up_grad_own.at[rows], own_sem.at[1]))

    def gate_up_rows(i, _):
        cols = span(i * tile, tile)
        slot = lax.rem(i, 2)

        @pl.when(i >= 2)
        def _():
            for copy in wstage_copies(i - 2, slot):
                copy.wait()

        x = two_ref[:, :, cols].reshape(blocks * tok, tile)
        wstage_ref[slot] = dot_tn(x, gu_ref[...].reshape(blocks * tok, 2 * ff)).astype(BF16)
        for copy in wstage_copies(i, slot):
            copy.start()

        @pl.when(i // 2 == place.row)
        def _():
            for copy in own_copies(lax.rem(i, 2), slot):
                copy.start()

        out_tile(2 * i, 0)
        out_tile(2 * i + 1, 0)

        @pl.when(i // 2 == place.row)
        def _():
            for copy in own_copies(lax.rem(i, 2), slot):
                copy.wait()

        return 0

    gather.own_chip()
    forward(0)
    for copy in g_loads:
        copy.wait()
    down_grad(0)
    gather.neighbours()
    downs.forward()
    gather.chip1()
    forward(1)
    down_grad(1)
    gather.chip2()
    forward(2)
    down_grad(2)
    gather.diagonal()
    gather.chip3()
    forward(3)
    downs.finish()
    backward(3)
    down_grad(3)
    down_sum.start_over()
    down_sum.start()
    own_down = pltpu.make_async_copy(dgrad_ref.at[place.row], down_own, load_sem.at[10])
    own_down.start()
    scatter.combine(3)
    scatter.pass1.start()
    scatter.pass2.start()
    backward(1)
    backward(2)
    scatter.combine(1)
    scatter.first1.start()
    scatter.combine(2)
    scatter.first2.start()
    backward(0)
    scatter.finish_two()
    scatter.combine(0)
    count = model // tile
    lax.fori_loop(0, count // 2, gate_up_rows, 0)

    def merge():
        def add(n, _):
            rows = span(n * 64, 64)
            merge_ref[rows, :] = (merge_ref[rows, :].astype(F32) + dgrad_ref[line.c, rows, :].astype(F32)).astype(BF16)
            return 0

        lax.fori_loop(0, ff // 64, add, 0)

    down_sum.add(merge)
    lax.fori_loop(count // 2, count, gate_up_rows, 0)
    scatter.arrive()

    def finish(i, sums):
        rows = span(i * 32, 32)
        res = res_ref[rows, :]
        inv = norm_inverse(res)
        grad = scatter.total(rows)
        v = grad * gain_ref[...]
        mean = jnp.mean(v * res, axis=-1, keepdims=True)
        out = g_ref[place.me, rows, :].astype(F32) + inv * v - res * (inv * inv * inv * mean)
        rgrad_ref[rows, :] = out
        branch_ref[rows, :] = out.astype(BF16)
        return sums + jnp.sum(grad * res * inv, axis=0, keepdims=True)

    gain_grad_ref[...] = lax.fori_loop(0, tok // 32, finish, jnp.zeros((1, model), F32), unroll=2)
    for i in (count - 2, count - 1):
        for copy in wstage_copies(i, i % 2):
            copy.wait()
    for n in (14, 15):
        stage_copy(n).wait()
    own_down.wait()
    down_sum.finish()
    down_sum.close()
    downs.close()
    gather.close()
    scatter.close()


def feed_forward(res, gain, two, g, g_all, slabs):
    tok, model = res.shape
    ff = slabs[0].shape[1]
    blocks = g_all.shape[0]
    dma = pltpu.SemaphoreType.DMA
    return pl.pallas_call(
        ffn_kernel,
        out_shape=(
            jax.ShapeDtypeStruct((4, 2, tok, model), BF16),
            jax.ShapeDtypeStruct((tok, model), F32),
            jax.ShapeDtypeStruct((tok, model), BF16),
            jax.ShapeDtypeStruct((1, model), F32),
            jax.ShapeDtypeStruct((model // 256, 256, ff), BF16),
            jax.ShapeDtypeStruct((model // 256, 256, ff), BF16),
            jax.ShapeDtypeStruct((model // 4, ff), BF16),
            jax.ShapeDtypeStruct((model // 4, ff), BF16),
            jax.ShapeDtypeStruct((ff, model // 4), BF16),
            jax.ShapeDtypeStruct((3, ff, model // 4), BF16),
        ),
        in_specs=[VMEM_SPEC, VMEM_SPEC] + [ANY_SPEC] * 8,
        out_specs=(ANY_SPEC, VMEM_SPEC, VMEM_SPEC, VMEM_SPEC) + (ANY_SPEC,) * 6,
        scratch_shapes=[
            pltpu.VMEM((blocks, tok, model), BF16),
            pltpu.VMEM((blocks, tok, model), BF16),
            pltpu.VMEM((model, 2 * ff), BF16),
            pltpu.VMEM((ff, model), BF16),
            pltpu.VMEM((blocks, tok, ff), BF16),
            pltpu.VMEM((blocks, tok, 2 * ff), BF16),
            pltpu.VMEM((2, 2, tok, model // 4), BF16),
            pltpu.VMEM((2, 256, 2 * ff), BF16),
            pltpu.VMEM((4, ff, model // 4), F32),
            pltpu.VMEM((4, ff, model // 4), BF16),
            pltpu.VMEM((ff, model // 4), BF16),
            *scatter_scratch(tok, model),
            dma((GATHER_SLOTS,)), dma((GATHER_SLOTS,)), dma((11,)), dma((blocks,)), dma((2,)), dma((2, 2)), dma((2,)),
            dma((ROW_SLOTS,)), dma((ROW_SLOTS,)), dma((ROW_SLOTS,)), dma((ROW_SLOTS,)),
        ],
        compiler_params=pltpu.CompilerParams(collective_id=2, has_side_effects=True, vmem_limit_bytes=62 * 1024 * 1024),
        cost_estimate=pl.CostEstimate(flops=18 * blocks * tok * model * ff, bytes_accessed=64 << 20, transcendentals=0),
    )(res, gain, two, g, g_all, *slabs)


def backward_kernel(heads, branch_hbm, out_hbm, x_hbm, kv_hbm, qo_hbm, gate_grad, up_grad, merged_hbm,
                    table_ref, gq_ref, gk_ref, gain_grad_ref, qkv_ref, gain_ref,
                    raw_hbm, o_hbm, qa_hbm, ka_hbm, kt_hbm, vt_hbm, inv_hbm,
                    ysum_ref, outsum_ref, grad_qkv_ref, grad_out_ref, grad_gain_ref, small_out,
                    grad_hbm, gate_recv, up_recv, qo_recv, kv_recv,
                    raw_ref, o_ref, qa_ref, ka_ref, kt_ref, vt_ref, inv_ref, kept_sem,
                    every_ref, w_ref, pg_ref, merged_ref, xt_ref, wstage_ref, gwo_ref,
                    doa_ref, dopad_ref, qpad_ref, va_ref, dq_ref, acc_ref,
                    part_ref, sibling_ref, passing_ref, final_ref, rs_send, rs_recv, rs2_send, rs2_recv,
                    ag_send, ag_recv, load_sem, xt_sem, wstage_sem, ready_sem,
                    ffn_merge, ffn_own, z_send, z_recv, own_sem, small_ref, small_row, small_mid, small_last, pieces_ref, amerge_ref, aown_ref,
                    kv_own, kv_in, kmerge_ref, slab_sem, pair_send, pair_recv,
                    s_send, s_recv, t_send, t_recv, p_send, p_recv):
    place = Place()
    blocks, tok, model = every_ref.shape[0] * every_ref.shape[1], every_ref.shape[2], every_ref.shape[3]
    branch_all = every_ref.reshape(blocks, tok, model)
    columns = 512
    lead = 256 - heads.wide
    load_w = load_slab(kv_hbm, qo_hbm, w_ref, slab_sem)
    load_out = pltpu.make_async_copy(out_hbm, part_ref, load_sem.at[1])
    load_own = pltpu.make_async_copy(branch_hbm, branch_all.at[place.me], load_sem.at[2])
    load_merged = pltpu.make_async_copy(merged_hbm, merged_ref, load_sem.at[3])
    load_out.start()
    load_own.start()
    for copy in load_w:
        copy.start()
    load_kept = [pltpu.make_async_copy(src, dst, kept_sem.at[i]) for i, (src, dst) in enumerate((
        (qa_hbm, qa_ref), (vt_hbm, vt_ref), (o_hbm, o_ref), (ka_hbm, ka_ref), (kt_hbm, kt_ref), (raw_hbm, raw_ref),
        (inv_hbm, inv_ref)))]
    for copy in load_kept:
        copy.start()
    load_merged.start()
    place.greet_all(4)
    gather = Gather(place, branch_hbm, branch_all, ag_send, ag_recv)
    gather.start()
    line = Line(place)
    ffn = [RowScatter(line, part, recv, ffn_merge.at[i], ffn_merge.at[i], z_send.at[i], z_recv.at[i])
           for i, (part, recv) in enumerate(((gate_grad, gate_recv), (up_grad, up_recv)))]
    for one in ffn:
        one.start_over()
    for one in ffn:
        one.start()
    first = Scatter(place, part_ref, sibling_ref, passing_ref, final_ref, rs_send, rs_recv)
    second = Scatter(place, every_ref, sibling_ref, passing_ref, final_ref, rs2_send, rs2_recv)
    load_out.wait()
    for copy in first.exchange:
        copy.start()

    def ffn_add(i):
        own = (gate_grad, up_grad)[i]

        def work():
            load = pltpu.make_async_copy(own.at[line.c], ffn_own, own_sem.at[0])
            load.start()
            load.wait()

            def add(n, _):
                rows = span(n * 64, 64)
                ffn_merge[i, rows, :] = ffn_merge[i, rows, :] + ffn_own[rows, :]
                return 0

            lax.fori_loop(0, ffn_own.shape[0] // 64, add, 0)

        ffn[i].add(work)

    def tell(n, others):
        for other in others:
            pl.semaphore_signal(ready_sem.at[n], inc=1, device_id=(place.row, other), device_id_type=MESH)

    back = Backward(heads, place.me, table_ref, gq_ref, gk_ref, raw_ref, o_ref, qa_ref, ka_ref, kt_ref, vt_ref, inv_ref,
                    doa_ref, dopad_ref, qpad_ref, va_ref, dq_ref, acc_ref)

    def prepare(b, _):
        back.prepare(b)
        return 0

    for copy in load_kept:
        copy.wait()
    lax.fori_loop(0, blocks, prepare, 0, unroll=2)
    for copy in load_w:
        copy.wait()
    load_own.wait()

    def compute(k):
        m = place.chips[k]

        def gradient(j, _):
            b = 2 * m + j
            dm = dot(branch_all[b], w_ref[:, 384:640])
            back.gradient(b, dm[:, lead:])
            return 0

        lax.fori_loop(0, 2, gradient, 0, unroll=True)
        back.query_block(m)

    gather.own_chip()
    compute(0)
    gather.neighbours()
    first.combine(3)
    first.pass1.start()
    first.pass2.start()
    ffn_add(0)
    gather.chip1()
    compute(1)
    first.combine(1)
    first.first1.start()
    gather.chip2()
    ffn_add(1)
    compute(2)
    first.combine(2)
    first.first2.start()
    gather.diagonal()
    first.combine(0)
    tell(0, (place.sib,))
    gather.chip3()
    compute(3)
    first.finish_two()
    tell(1, place.same[1:3])
    load_merged.wait()
    tile = 256
    count = model // tile

    def x_copy(i, slot):
        return pltpu.make_async_copy(x_hbm.at[:, :, span(i * tile, tile)], xt_ref.at[slot], xt_sem.at[slot])

    x_copy(0, 0).start()

    def out_rows(i, _):
        out = dot_tn(branch_all[:, :, span(i * tile, tile)].reshape(blocks * tok, tile), merged_ref[...])
        gwo_ref[i] = out.astype(BF16)
        return 0

    lax.fori_loop(0, count, out_rows, 0, unroll=4)
    gather.close()
    pad = 512 - heads.qkv

    def finish(b, sums):
        grad, sums = back.finish(b, sums)
        grad = jnp.concatenate([grad, jnp.zeros((pad, tok), F32)], axis=0)
        pg_ref[b] = jnp.transpose(grad).astype(BF16)
        return sums

    zero = jnp.zeros((D, tok), F32)
    sums = lax.fori_loop(0, blocks, finish, (zero, zero), unroll=2)

    def grad_copy(i, slot):
        return pltpu.make_async_copy(wstage_ref.at[slot], grad_hbm.at[i // 2, lax.rem(i, 2)], wstage_sem.at[slot])

    def weight_rows(i, _):
        slot = lax.rem(i, 2)

        @pl.when(i + 1 < count)
        def _():
            x_copy(i + 1, 1 - slot).start()

        @pl.when(i >= 2)
        def _():
            grad_copy(i - 2, slot).wait()

        x_copy(i, slot).wait()
        x = xt_ref[slot].reshape(blocks * tok, tile)
        qkv = dot_tn(x, pg_ref[...].reshape(blocks * tok, 512))
        even = place.core == 0
        cols = span(i * tile, tile)
        kv_own[i // 2, lax.rem(i, 2)] = jnp.where(even, qkv[:, 0:128], qkv[:, 128:256]).astype(BF16)
        merged_ref[cols, 0:128] = jnp.where(even, qkv[:, 128:256], qkv[:, 0:128]).astype(BF16)
        wstage_ref[slot, :, 0:heads.wide] = qkv[:, 256:256 + heads.wide].astype(BF16)
        wstage_ref[slot, :, heads.wide:2 * heads.wide] = gwo_ref[i, :, lead:]
        grad_copy(i, slot).start()
        return 0

    lax.fori_loop(0, count, weight_rows, 0, unroll=2)
    for i in (count - 2, count - 1):
        grad_copy(i, i % 2).wait()

    pair = place.send(merged_ref.at[:, 0:128], kv_in, pair_send, pair_recv, 0, place.sib)
    pair.start()
    attn = RowScatter(line, grad_hbm, qo_recv, amerge_ref, amerge_ref, z_send.at[2], z_recv.at[2])
    attn.start_over()
    attn.start()
    load_passed = pltpu.make_async_copy(grad_hbm.at[line.c], aown_ref, own_sem.at[2])
    load_passed.start()
    pair.wait_recv()

    def add_pair(n, _):
        b, rows = n // 4, span(lax.rem(n, 4) * 64, 64)
        for r in range(4):
            kv_own[r, b, rows, :] = kv_own[r, b, rows, :] + kv_in[span(r * 512 + n * 64, 64), :]
        return 0

    lax.fori_loop(0, 8, add_pair, 0)
    kv_sum = RowScatter(line, kv_own, kv_recv, kmerge_ref, kmerge_ref, z_send.at[3], z_recv.at[3])
    kv_sum.start_over()
    kv_sum.start()

    def attn_work():
        def add(n, _):
            b, rows = n // 4, span(lax.rem(n, 4) * 64, 64)
            amerge_ref[b, rows, :] = amerge_ref[b, rows, :] + aown_ref[b, rows, :]
            return 0

        lax.fori_loop(0, 8, add, 0)

    def kv_work():
        def add(n, _):
            b, rows = n // 4, span(lax.rem(n, 4) * 64, 64)
            kmerge_ref[b, rows, :] = kmerge_ref[b, rows, :] + kv_own[line.c, b, rows, :]
            return 0

        lax.fori_loop(0, 8, add, 0)

    def project(k):
        m = place.chips[k]

        def model_tile(n, _):
            cols = span(n * 512, 512)
            out = dot_nt(pg_ref[pl.ds(2 * m, 2)].reshape(2 * tok, 512), w_ref[cols, 0:512])
            every_ref[k, :, :, cols] = out.astype(BF16).reshape(2, tok, 512)
            return 0

        lax.fori_loop(0, model // 512, model_tile, 0, unroll=True)
        if k == 3:
            pl.semaphore_wait(ready_sem.at[0], 1)
        second.exchange[k].start()

    project(3)
    project(1)
    second.combine(3)
    pl.semaphore_wait(ready_sem.at[1], 2)
    second.pass1.start()
    second.pass2.start()
    project(2)
    second.combine(1)
    load_passed.wait()
    attn.add(attn_work)
    project(0)
    kv_sum.add(kv_work)
    second.combine(2)

    head_gains = jnp.sum(jnp.transpose(jnp.concatenate(sums, axis=0)), axis=0, keepdims=True)
    row8 = lax.broadcasted_iota(jnp.int32, (8, 128), 0)
    for r in range(4):
        for n in range(PLANE):
            start = (r * PLANE + n) * D
            piece = jnp.concatenate([gain_grad_ref[:, start:start + D], jnp.zeros((1, 128 - D), F32)], axis=1)
            small_ref[r, n] = jnp.where(row8 == 0, piece, jnp.where(row8 == 1, head_gains, 0.0))
    small_sends = []
    for j in range(1, 4):
        other = lax.rem(place.row + j, 4)
        small_sends.append(line.send(small_ref.at[other], small_row.at[place.row], s_send, j, s_recv, j, other))
    for copy in small_sends:
        copy.start()
    small_row[place.row] = small_ref[place.row]

    def take(out_ref, scatter):
        def one(i, _):
            rows = span(i * 32, 32)
            out_ref[rows, :] = scatter.total(rows)
            return 0

        lax.fori_loop(0, tok // 32, one, 0)

    first.arrive()
    take(outsum_ref, first)
    tell(2, place.same[1:3])
    first.close()
    pl.semaphore_wait(ready_sem.at[2], 2)
    second.first1.start()
    second.first2.start()
    second.combine(0)
    def fetch(n, qo, kv, sem):
        return [pltpu.make_async_copy(qo, part_ref.at[n, :, :, 128:columns], own_sem.at[sem]),
                pltpu.make_async_copy(kv, part_ref.at[n, :, :, 0:128], own_sem.at[sem + 1])]

    own_term = fetch(0, grad_hbm.at[place.row], kv_own.at[place.row], 4)
    for copy in own_term:
        copy.start()

    def add_blocks(target, source):
        def add(n, _):
            b, rows = n // 4, span(lax.rem(n, 4) * 64, 64)
            part_ref[target, b, rows, 0:columns] = part_ref[target, b, rows, 0:columns] + part_ref[source, b, rows, 0:columns]
            return 0

        lax.fori_loop(0, 8, add, 0)

    second.finish_two()
    for copy in small_sends:
        copy.wait_recv()
    small_mid[...] = (small_row[0] + small_row[1]) + (small_row[2] + small_row[3])
    plane_sends = []
    for j in range(1, PLANE):
        other = lax.rem(place.me + j, PLANE)
        plane_sends.append(place.send(small_mid.at[other], small_last.at[place.me], t_send, t_recv, j, other))
    for copy in plane_sends:
        copy.start()
    small_last[place.me] = small_mid[place.me]
    for copy in plane_sends:
        copy.wait_recv()
    total = small_last[0]
    for n in range(1, PLANE):
        total = total + small_last[n]
    small_out[...] = total
    for copy in own_term:
        copy.wait()
    attn.finish()
    kv_sum.finish()

    def fold(slots):
        loads = []
        for slot in slots:
            loads += fetch(slot + 1, qo_recv.at[slot], kv_recv.at[slot], 6 + 2 * slot)
        for copy in loads:
            copy.start()
        for copy in loads:
            copy.wait()
        for slot in slots:
            add_blocks(0, slot + 1)

    @pl.when(line.middle)
    def _():
        fold((0, 1, 2))

    @pl.when(jnp.logical_not(line.middle))
    def _():
        fold((0, 2))

    def piece(n):
        return part_ref.at[0, n // 4, span(lax.rem(n, 4) * 64, 64), 0:columns]

    keep = pltpu.make_async_copy(piece(place.me), pieces_ref.at[place.me], own_sem.at[1])
    keep.start()
    for j in range(1, PLANE):
        other = lax.rem(place.me + j, PLANE)
        copy = place.send(piece(other), pieces_ref.at[place.me], p_send, p_recv, j, other)
        copy.start()
        plane_sends.append(copy)
    second.arrive()
    take(ysum_ref, second)
    for one in ffn:
        one.finish()
        one.close()
    for copy in plane_sends[PLANE - 1:]:
        copy.wait_recv()
    keep.wait()
    unscaled, out_t = attention_sums(heads, lambda s: pieces_ref[s].astype(F32), True)
    grad_gain_ref[...] = jnp.broadcast_to(jnp.sum(unscaled * qkv_ref[...].astype(F32), axis=1, keepdims=True), grad_gain_ref.shape)
    grad_qkv_ref[...] = unscaled * gain_ref[...]
    grad_out_ref[...] = jnp.transpose(out_t)
    for copy in plane_sends + small_sends + [pair]:
        copy.wait_send()
    attn.close()
    kv_sum.close()
    second.close()


def backward_phase(heads, branch, out_part, x_all, kv, qo, weight_grads, table, gq, gk, gain_grad, w_qkv, gain_attn, kept):
    blocks, tok, model = x_all.shape
    length = blocks * tok
    depth = w_qkv.shape[0]
    dma = pltpu.SemaphoreType.DMA
    raw, merged, *rest = kept
    return pl.pallas_call(
        functools.partial(backward_kernel, heads),
        out_shape=(
            jax.ShapeDtypeStruct((tok, model), F32),
            jax.ShapeDtypeStruct((tok, model), F32),
            jax.ShapeDtypeStruct(w_qkv.shape, F32),
            jax.ShapeDtypeStruct((QUERY_HEADS * D, depth), F32),
            jax.ShapeDtypeStruct((depth, 128), F32),
            jax.ShapeDtypeStruct((8, 128), F32),
            jax.ShapeDtypeStruct((4, 2, 256, 384), BF16),
            *(jax.ShapeDtypeStruct((3,) + grad.shape[1:], BF16) for grad in weight_grads),
            jax.ShapeDtypeStruct((3, 2, 256, 384), BF16),
            jax.ShapeDtypeStruct((3, 2, 256, 128), BF16),
        ),
        in_specs=[ANY_SPEC] * 8 + [VMEM_SPEC] * 6 + [ANY_SPEC] * (1 + len(rest)),
        out_specs=(VMEM_SPEC,) * 6 + (ANY_SPEC,) * 5,
        scratch_shapes=[
            *(pltpu.VMEM(array.shape, array.dtype) for array in (raw, *rest)),
            dma((7,)),
            pltpu.VMEM((4, 2, tok, model), BF16),
            pltpu.VMEM((model, heads.columns), BF16),
            pltpu.VMEM((blocks, tok, 512), BF16),
            pltpu.VMEM(merged.shape, BF16),
            pltpu.VMEM((2, blocks, tok, 256), BF16),
            pltpu.VMEM((2, 256, 384), BF16),
            pltpu.VMEM((model // 256, 256, 256), BF16),
            *backward_scratch(heads, length),
            *scatter_scratch(tok, model),
            dma((SCATTER_SLOTS,)), dma((SCATTER_SLOTS,)),
            dma((GATHER_SLOTS,)), dma((GATHER_SLOTS,)), dma((4,)), dma((2,)), dma((2,)),
            pltpu.SemaphoreType.REGULAR((3,)),
            pltpu.VMEM((2,) + weight_grads[0].shape[1:], BF16),
            pltpu.VMEM(weight_grads[0].shape[1:], BF16),
            dma((4, ROW_SLOTS)), dma((4, ROW_SLOTS)), dma((12,)),
            pltpu.VMEM((4, PLANE, 8, 128), F32),
            pltpu.VMEM((4, PLANE, 8, 128), F32),
            pltpu.VMEM((PLANE, 8, 128), F32),
            pltpu.VMEM((PLANE, 8, 128), F32),
            pltpu.VMEM((PLANE, depth, 512), BF16),
            pltpu.VMEM((2, 256, 384), BF16),
            pltpu.VMEM((2, 256, 384), BF16),
            pltpu.VMEM((4, 2, 256, 128), BF16),
            pltpu.VMEM((model, 128), BF16),
            pltpu.VMEM((2, 256, 128), BF16),
            dma((3,)), dma((1,)), dma((1,)),
            dma((4,)), dma((4,)), dma((PLANE,)), dma((PLANE,)), dma((PLANE,)), dma((PLANE,)),
        ],
        compiler_params=pltpu.CompilerParams(collective_id=3, has_side_effects=True, vmem_limit_bytes=63 * 1024 * 1024),
        cost_estimate=pl.CostEstimate(flops=60 << 30, bytes_accessed=64 << 20, transcendentals=0),
    )(branch, out_part, x_all, kv, qo, *weight_grads, merged, table, gq, gk, gain_grad, w_qkv, gain_attn, raw, *rest)


def norm_back(grad_normed, values_in, inv_rms, gain):
    scaled = grad_normed * gain
    gain_grad = jnp.sum(grad_normed * values_in * inv_rms, axis=0)
    input_grad = inv_rms * scaled - values_in * inv_rms**3 * jnp.mean(scaled * values_in, axis=-1, keepdims=True)
    return input_grad, gain_grad


def start_wide(x, table, pieces, gain):
    return (
        lax.all_gather(x, "seq", axis=0, tiled=False),
        lax.all_gather(table, "seq", axis=0, tiled=False),
        lax.all_gather(lax.all_to_all(pieces, "seq", 0, 0, tiled=False), "rows", axis=0, tiled=False),
        lax.all_gather(lax.all_gather(gain, "seq", axis=0, tiled=False), "rows", axis=0, tiled=False),
    )


def scatter_rows(part, tok):
    return lax.psum_scatter(part.reshape(-1, part.shape[-1]), "seq", scatter_dimension=0, tiled=True).astype(F32)


def attention_wide(heads, x_all, g, w, table, gq, gk):
    blocks, tok, model = x_all.shape
    proj = dot(x_all.reshape(blocks * tok, model), w[:, :heads.qkv])
    kept = pl.pallas_call(
        functools.partial(local_forward_kernel, heads),
        out_shape=kept_shapes(heads, blocks * tok, 0),
        compiler_params=pltpu.CompilerParams(vmem_limit_bytes=VMEM_LIMIT),
    )(proj, table, gq, gk)
    total = scatter_rows(dot_nt(kept[1], w[:, heads.qkv:]).astype(BF16), tok)
    own = lax.dynamic_index_in_dim(x_all, lax.axis_index("seq"), 0, keepdims=False)
    return (own.astype(F32) + total, lax.all_gather(g, "seq", axis=0, tiled=False)) + tuple(kept)


def feed_forward_wide(res, gain, g_blocks, gate_slab, up_slab, down_slab):
    blocks, tok, model = g_blocks.shape
    inv = norm_inverse(res)
    two_all = lax.all_gather((res * inv * gain).astype(BF16), "seq", axis=0, tiled=True)
    g_all = g_blocks.reshape(blocks * tok, model)
    gate_act = dot(two_all, gate_slab)
    up_act = dot(two_all, up_slab)
    s = jax.nn.sigmoid(gate_act)
    hidden = (gate_act * s * up_act).astype(BF16)
    hidden_grad = dot_nt(g_all, down_slab)
    gate_grad = (hidden_grad * up_act * s * (1.0 + gate_act * (1.0 - s))).astype(BF16)
    up_grad = (hidden_grad * gate_act * s).astype(BF16)
    two_grad = scatter_rows((dot_nt(gate_grad, gate_slab) + dot_nt(up_grad, up_slab)).astype(BF16), tok)
    branch_part = dot(hidden, down_slab).astype(BF16).reshape(blocks, tok, model)
    norm_grad, gain_grad = norm_back(two_grad, res, inv, gain)
    g = lax.dynamic_index_in_dim(g_blocks, lax.axis_index("seq"), 0, keepdims=False)
    residual_grad = g.astype(F32) + norm_grad
    return (branch_part, residual_grad, residual_grad.astype(BF16), gain_grad[None],
            dot_tn(two_all, gate_grad).astype(BF16), dot_tn(two_all, up_grad).astype(BF16),
            dot_tn(hidden, g_all).astype(BF16))


def backward_wide(heads, branch, out_part, x_all, w, table, gq, gk, kept):
    blocks, tok, model = x_all.shape
    length = blocks * tok
    raw, merged, *rest = kept
    out_sum = scatter_rows(out_part, tok)
    branch_all = lax.all_gather(branch, "seq", axis=0, tiled=True)
    pg, gains = pl.pallas_call(
        functools.partial(local_backward_kernel, heads),
        out_shape=(jax.ShapeDtypeStruct((length, heads.qkv), BF16), jax.ShapeDtypeStruct((2 * D, 128), F32)),
        scratch_shapes=backward_scratch(heads, length),
        compiler_params=pltpu.CompilerParams(vmem_limit_bytes=VMEM_LIMIT),
    )(dot(branch_all, w[:, heads.qkv:]), table, gq, gk, raw, *rest)
    y_sum = scatter_rows(dot_nt(pg, w[:, :heads.qkv]).astype(BF16), tok)
    grad = jnp.concatenate([dot_tn(x_all.reshape(length, model), pg), dot_tn(branch_all, merged)], axis=1)
    return y_sum, out_sum, grad.astype(BF16), gains


def rotary_table(x, positions, segments):
    inverse = jnp.exp(-math.log(THETA) * jnp.arange(HALF, dtype=F32) * 2.0 / D)
    angles = inverse[:, None] * positions.astype(F32)[None, :]
    hot = jnp.arange(SEGMENT_KINDS, dtype=jnp.int32)[:, None] == segments[None, :]
    root = jnp.pad(norm_inverse(x).T, ((0, 7), (0, 0)))
    return jnp.concatenate([jnp.cos(angles), jnp.sin(angles), hot.astype(F32), root], axis=0)


def attention_pieces(heads, w_qkv, w_out, split):
    depth = w_qkv.shape[0]
    qw, kw = QUERY_HEADS * D, KEY_VALUE_HEADS * D
    out_t = w_out.T

    def columns(array, start, first, count, most):
        parts = []
        for i in range(count):
            n = first + i
            parts.append(array[:, start + n * D:start + (n + 1) * D] if n < most else jnp.zeros((depth, D), BF16))
        return parts

    pairs, others = [], []
    for s in range(heads.seq):
        q, k = s * heads.queries, heads.first(s)
        parts = []
        for n in ([k + s % 2] if split else range(k, k + heads.pairs)):
            parts += columns(w_qkv, qw, n, 1, KEY_VALUE_HEADS) + columns(w_qkv, qw + kw, n, 1, KEY_VALUE_HEADS)
        pairs.append(jnp.concatenate(parts, axis=1))
        others.append(jnp.concatenate(columns(w_qkv, 0, q, heads.queries, QUERY_HEADS)
                                      + columns(out_t, 0, q, heads.queries, QUERY_HEADS), axis=1))
    pairs, others = jnp.stack(pairs), jnp.stack(others)
    return (pairs, others) if split else jnp.concatenate([pairs, others], axis=2)


def attention_sums(heads, piece, split):
    pieces = [piece(s) for s in range(heads.seq)]
    held = 1 if split else heads.pairs
    first = [heads.first(s) + (s % 2 if split else 0) for s in range(heads.seq)]
    lead = 2 * held * D
    cut = lambda s, start, n: pieces[s][:, start + n * D:start + (n + 1) * D]
    queries = [cut(n // heads.queries, lead, n % heads.queries) for n in range(QUERY_HEADS)]
    outs = [cut(n // heads.queries, lead + heads.wide, n % heads.queries) for n in range(QUERY_HEADS)]

    def pairs(value):
        found = []
        for n in range(KEY_VALUE_HEADS):
            terms = [cut(s, value * D, 2 * (n - first[s])) for s in range(heads.seq)
                     if s * heads.queries < QUERY_HEADS and 0 <= n - first[s] < held]
            found.append(functools.reduce(jnp.add, terms))
        return found

    qkv = jnp.concatenate(queries + pairs(0) + pairs(1), axis=1)
    return qkv, jnp.concatenate(outs, axis=1)


def body(tokens, segments, positions, cotangent, gain_attn, w_qkv, gain_q, gain_k, w_out, gain_ffn, w_gate, w_up, w_down):
    seq = lax.axis_size("seq")
    rows = lax.axis_size("rows")
    heads = Heads(seq)
    depth = w_qkv.shape[0]
    tok, model = tokens.shape[1:]
    plane = seq == PLANE and rows == 4
    row = lax.axis_index("rows")

    gq = gain_q.astype(F32)[:, None]
    gk = gain_k.astype(F32)[:, None]
    x = tokens[0].astype(F32)
    scaled = (w_qkv.astype(F32) * gain_attn.astype(F32)[:, None]).astype(BF16)
    pieces = attention_pieces(heads, scaled, w_out, plane)
    gain = jnp.pad(gain_ffn.astype(F32)[None], ((0, 7), (0, 128 - depth)))
    table = rotary_table(x, positions[0], segments[0])
    if plane:
        x_all, table, kv, qo, gains = start_phase(rows, tokens[0], table, *pieces, gain)
        kv, qo = kv.reshape(2, model, -1), qo.reshape(model, -1)
    else:
        x_all, table, w, gains = start_wide(tokens[0], table, pieces, gain)
        w = w.reshape(model, heads.columns)
    gain_two = gains[:, :, 0, :depth].reshape(1, model)
    inv = norm_inverse(x)

    if plane:
        residual, two, g_all, gate, up, *kept = attention_phase(
            heads, x_all, cotangent[0], kv, qo, (w_gate, w_up), table, gq, gk, gain_two)
        out_part, residual_grad, branch, gain_two_grad, *weight_grads, gate_own, up_own, down_own, down_recv = feed_forward(
            residual, gain_two, two, cotangent[0], g_all, (w_gate, gate, w_up, up, w_down))
        weight_grads = [grad.reshape((4,) + w_gate.shape) for grad in weight_grads]
        y_sum, out_sum, grad_qkv, grad_out, grad_gain_attn, small, _, gate_recv, up_recv, *_ = backward_phase(
            heads, branch, out_part, x_all, kv, qo, weight_grads, table, gq, gk, gain_two_grad, w_qkv,
            gain_attn.astype(F32)[:, None], kept)
        grad_gain_attn = grad_gain_attn[:, 0]
        middle = (row + 1) // 2 == 1

        def row_total(own, recv):
            return own.astype(F32) + recv[0].astype(F32) + recv[2].astype(F32) + jnp.where(middle, recv[1].astype(F32), 0.0)

        grad_gate, grad_up, grad_down = (
            row_total(own, recv) for own, recv in ((gate_own, gate_recv), (up_own, up_recv), (down_own, down_recv)))
        grad_gain_ffn, head_gains = small[0, :depth], small[1]
    else:
        gate_slab = lax.all_gather(w_gate, "rows", axis=0, tiled=True)
        up_slab = lax.all_gather(w_up, "rows", axis=0, tiled=True)
        down_slab = lax.all_gather(w_down, "rows", axis=1, tiled=True)
        residual, g_all, *kept = attention_wide(heads, x_all, cotangent[0], w, table, gq, gk)
        out_part, residual_grad, branch, gain_two_grad, gate_wgrad, up_wgrad, down_wgrad = feed_forward_wide(
            residual, gain_two, g_all, gate_slab, up_slab, down_slab)
        grad_gate = lax.psum_scatter(gate_wgrad, "rows", scatter_dimension=0, tiled=True).astype(F32)
        grad_up = lax.psum_scatter(up_wgrad, "rows", scatter_dimension=0, tiled=True).astype(F32)
        grad_down = lax.psum_scatter(down_wgrad, "rows", scatter_dimension=1, tiled=True).astype(F32)
        y_sum, out_sum, attn_grad, head_gains = backward_wide(heads, branch, out_part, x_all, w, table, gq, gk, kept)
        attn_grad = lax.psum_scatter(attn_grad, "rows", scatter_dimension=0, tiled=True)
        attn_grad = lax.all_to_all(attn_grad.reshape(seq, depth, heads.columns), "seq", 0, 0, tiled=False)
        small = lax.psum(jnp.concatenate([gain_two_grad[0], head_gains[:, 0]]), ("rows", "seq"))
        grad_gain_ffn = lax.dynamic_slice_in_dim(small, (row * seq + lax.axis_index("seq")) * depth, depth)
        head_gains = small[model:]
        attn_grad = attn_grad.astype(F32)
        unscaled, grad_out = attention_sums(heads, lambda s: attn_grad[s], False)
        grad_out = grad_out.T
        grad_gain_attn = jnp.sum(unscaled * w_qkv.astype(F32), axis=1)
        grad_qkv = unscaled * gain_attn.astype(F32)[:, None]

    layer_out = (residual + out_sum).astype(BF16)
    grad_tokens = residual_grad + y_sum - x * (inv * inv * jnp.mean(y_sum * x, axis=-1, keepdims=True))
    return (
        layer_out[None],
        grad_tokens[None],
        grad_gain_attn,
        grad_qkv,
        head_gains[:D],
        head_gains[D:],
        grad_out,
        grad_gain_ffn,
        grad_gate,
        grad_up,
        grad_down,
    )


def solution(mesh):
    both = ("rows", "seq")
    return jax.shard_map(
        body,
        mesh=mesh,
        in_specs=(
            P("rows", "seq", None), P("rows", "seq"), P("rows", "seq"), P("rows", "seq", None),
            P(both), P(both, None), P(), P(), P(None, both), P(both),
            P("rows", "seq"), P("rows", "seq"), P("seq", "rows"),
        ),
        out_specs=(
            P("rows", "seq", None), P("rows", "seq", None), P(both), P(both, None), P(), P(),
            P(None, both), P(both), P("rows", "seq"), P("rows", "seq"), P("seq", "rows"),
        ),
        check_vma=False,
    )
```

```python
import functools
import math

import jax
import jax.numpy as jnp
from jax import lax
from jax.experimental import pallas as pl
from jax.experimental.pallas import tpu as pltpu
from jax.sharding import PartitionSpec as P

QUERY_HEADS = 24
KEY_VALUE_HEADS = 6
GROUP = QUERY_HEADS // KEY_VALUE_HEADS
D = 64
HALF = D // 2
EPSILON = 1e-06
THETA = 10000.0
PENALTY = -10000.0
SEGMENT_KINDS = 8
TABLE_ROWS = 80
BLOCK = 512
PLANE = 8
F32 = jnp.float32
BF16 = jnp.bfloat16
VMEM_LIMIT = 60 * 1024 * 1024
MESH = pl.DeviceIdType.MESH
ANY_SPEC = pl.BlockSpec(memory_space=pl.ANY)
VMEM_SPEC = pl.BlockSpec(memory_space=pltpu.VMEM)


def dot(a, b):
    return jnp.dot(a, b, preferred_element_type=F32)


def dot_nt(a, b):
    return lax.dot_general(a, b, (((1,), (1,)), ((), ())), preferred_element_type=F32)


def dot_tn(a, b):
    return lax.dot_general(a, b, (((0,), (0,)), ((), ())), preferred_element_type=F32)


def norm_inverse(x):
    return lax.rsqrt(jnp.mean(x * x, axis=-1, keepdims=True) + EPSILON)


def split3(x):
    high = x.astype(BF16).astype(F32)
    mid = (x - high).astype(BF16).astype(F32)
    return high, mid, x - high - mid


def column(ref):
    row = ref[...].astype(F32)
    return jnp.transpose(jnp.broadcast_to(row, (128, row.shape[1])))[:, 0:1]


def gain_row(ref):
    return jnp.concatenate([ref[r, n, 0:1, 0:D] for r in range(ref.shape[0]) for n in range(ref.shape[1])], axis=1)


def span(start, size):
    return pl.ds(pl.multiple_of(start, size), size)


class Heads:
    def __init__(self, seq):
        self.seq = seq
        self.queries = -(-QUERY_HEADS // seq)
        last = [min((s + 1) * self.queries, QUERY_HEADS) - 1 for s in range(seq)]
        self.pairs = max(last[s] // GROUP - self.first(s) + 1 for s in range(seq) if last[s] >= s * self.queries)
        self.wide = self.queries * D
        self.narrow = self.pairs * D
        self.qkv = self.wide + 2 * self.narrow
        self.columns = self.qkv + self.wide

    def first(self, s):
        return (s // 2 * 2 * self.queries) // GROUP

    def slot(self, s, h):
        return (s * self.queries + h) // GROUP - self.first(s)


class Place:
    def __init__(self):
        self.row = lax.axis_index("rows")
        self.me = lax.axis_index("seq")
        self.core = lax.rem(self.me, 2)
        self.chip = self.me // 2
        self.sib = self.me + 1 - 2 * self.core
        chip = self.chip
        self.chips = (chip, chip + 1 - 2 * lax.rem(chip, 2), lax.rem(chip + 2, 4), 3 - chip)
        self.same = tuple(2 * q + self.core for q in self.chips)

    def greet(self, rows=1):
        barrier = pltpu.get_barrier_semaphore()
        for other in (self.sib, self.same[1], self.same[2]):
            pl.semaphore_signal(barrier, inc=1, device_id=(self.row, other), device_id_type=MESH)
        for j in range(1, rows):
            other = lax.rem(self.row + j, rows)
            pl.semaphore_signal(barrier, inc=1, device_id=(other, self.me), device_id_type=MESH)
        pl.semaphore_wait(barrier, 3 + rows - 1)

    def greet_all(self, rows):
        barrier = pltpu.get_barrier_semaphore()
        for j in range(1, PLANE):
            other = lax.rem(self.me + j, PLANE)
            pl.semaphore_signal(barrier, inc=1, device_id=(self.row, other), device_id_type=MESH)
        for j in range(1, rows):
            other = lax.rem(self.row + j, rows)
            pl.semaphore_signal(barrier, inc=1, device_id=(other, self.me), device_id_type=MESH)
        pl.semaphore_wait(barrier, PLANE - 1 + rows - 1)

    def send(self, src, dst, send_sem, recv_sem, slot, target):
        return pltpu.make_async_remote_copy(
            src_ref=src, dst_ref=dst, send_sem=send_sem.at[slot], recv_sem=recv_sem.at[slot],
            device_id=(self.row, target), device_id_type=MESH)


class Line:
    def __init__(self, place):
        self.place = place
        row = place.row
        self.a = row + 1 - 2 * lax.rem(row, 2)
        self.b = 3 - row
        self.c = lax.rem(row + 2, 4)
        self.middle = (row + 1) // 2 == 1

    def send(self, src, dst, send_sem, send_slot, recv_sem, recv_slot, target):
        return pltpu.make_async_remote_copy(
            src_ref=src, dst_ref=dst, send_sem=send_sem.at[send_slot], recv_sem=recv_sem.at[recv_slot],
            device_id=(target, self.place.me), device_id_type=MESH)


ROW_SLOTS = 4


class RowGather:
    def __init__(self, line, own, at, send_sem, recv_sem):
        self.line = line
        mine, passed = at(line.place.row), at(line.c)
        self.to_a = line.send(own, mine, send_sem, 0, recv_sem, 0, line.a)
        self.to_c = line.send(own, mine, send_sem, 1, recv_sem, 1, line.c)
        self.to_b = line.send(own, mine, send_sem, 2, recv_sem, 2, line.b)
        self.on = line.send(passed, passed, send_sem, 3, recv_sem, 2, line.a)

    def start(self):
        self.to_c.start()
        self.to_a.start()

        @pl.when(self.line.middle)
        def _():
            self.to_b.start()

    def forward(self):
        self.to_c.wait_recv()

        @pl.when(self.line.middle)
        def _():
            self.on.start()

    def finish(self):
        self.to_a.wait_recv()
        self.to_b.wait_recv()

    def close(self):
        self.to_a.wait_send()
        self.to_c.wait_send()

        @pl.when(self.line.middle)
        def _():
            self.to_b.wait_send()
            self.on.wait_send()


class RowScatter:
    def __init__(self, line, part, recv, merge, total, send_sem, recv_sem):
        self.line, self.total = line, total
        self.to_a = line.send(part.at[line.a], recv.at[0], send_sem, 0, recv_sem, 0, line.a)
        self.to_b = line.send(part.at[line.b], recv.at[1], send_sem, 1, recv_sem, 1, line.b)
        self.to_c = line.send(part.at[line.c], recv.at[2], send_sem, 2, recv_sem, 2, line.c)
        self.added = line.send(total, recv.at[2], send_sem, 2, recv_sem, 2, line.c)
        self.over = line.send(part.at[line.b], merge, send_sem, 3, recv_sem, 3, line.a)

    def start_over(self):
        @pl.when(jnp.logical_not(self.line.middle))
        def _():
            self.over.start()

    def start(self):
        @pl.when(jnp.logical_not(self.line.middle))
        def _():
            self.to_c.start()

        @pl.when(self.line.middle)
        def _():
            self.to_b.start()

        self.to_a.start()

    def add(self, work):
        @pl.when(self.line.middle)
        def _():
            self.over.wait_recv()
            work()
            self.added.start()

    def finish(self):
        self.to_a.wait_recv()
        self.to_c.wait_recv()

        @pl.when(self.line.middle)
        def _():
            self.to_b.wait_recv()

    def close(self):
        self.to_a.wait_send()
        self.to_c.wait_send()

        @pl.when(self.line.middle)
        def _():
            self.to_b.wait_send()

        @pl.when(jnp.logical_not(self.line.middle))
        def _():
            self.over.wait_send()


GATHER_SLOTS = 10


class Gather:
    def __init__(self, place, own, every, send_sem, recv_sem):
        half = every.shape[1] // 2
        low, high, whole = slice(0, half), slice(half, 2 * half), slice(0, 2 * half)

        def send(part, b, slot, target, src=None):
            src = every.at[b, part] if src is None else src.at[part]
            return place.send(src, every.at[b, part], send_sem, recv_sem, slot, target)

        me, (_, s1, s2, s3), sib = place.me, place.same, place.sib
        self.copies = (
            send(whole, me, 0, sib, own),
            send(low, me, 1, s1, own), send(high, me, 2, s1, own),
            send(high, me, 3, s2, own), send(low, me, 4, s2, own),
            send(low, s1, 5, s2), send(high, s2, 6, s1),
            send(whole, s1, 7, sib), send(whole, s2, 8, sib), send(whole, s3, 9, sib),
        )

    def start(self):
        for slot in (1, 3, 2, 4, 0):
            self.copies[slot].start()

    def own_chip(self):
        self.copies[0].wait_recv()

    def neighbours(self):
        c = self.copies
        c[1].wait_recv()
        c[5].start()
        c[3].wait_recv()
        c[6].start()
        c[2].wait_recv()
        c[7].start()
        c[4].wait_recv()
        c[8].start()

    def chip1(self):
        self.copies[7].wait_recv()

    def chip2(self):
        self.copies[8].wait_recv()

    def diagonal(self):
        c = self.copies
        c[5].wait_recv()
        c[6].wait_recv()
        c[9].start()

    def chip3(self):
        self.copies[9].wait_recv()

    def close(self):
        for copy in self.copies:
            copy.wait_send()


SCATTER_SLOTS = 10


class Scatter:
    def __init__(self, place, part, sibling, passing, final, send_sem, recv_sem):
        self.place, self.part, self.sibling, self.passing, self.final = place, part, sibling, passing, final
        half = part.shape[2] // 2
        self.half = half
        core, other = place.core, 1 - place.core
        _, s1, s2, _ = place.same
        send = lambda src, dst, slot, target: place.send(src, dst, send_sem, recv_sem, slot, target)
        low, high = slice(0, half), slice(half, 2 * half)
        self.exchange = tuple(send(part.at[k, other], sibling.at[k], k, place.sib) for k in range(4))
        self.pass1 = send(part.at[3, core, low], passing.at[0], 4, s1)
        self.pass2 = send(part.at[3, core, high], passing.at[1], 5, s2)
        self.first1 = send(part.at[1, core, low], final.at[0, low], 6, s1)
        self.second1 = send(part.at[1, core, high], final.at[0, high], 7, s1)
        self.first2 = send(part.at[2, core, high], final.at[1, high], 8, s2)
        self.second2 = send(part.at[2, core, low], final.at[1, low], 9, s2)

    def add(self, k, start, size, term, offset):
        core, step = self.place.core, 64

        def one(i, _):
            rows = pl.ds(pl.multiple_of(start + i * step, step), step)
            from_rows = pl.ds(pl.multiple_of(offset + i * step, step), step)
            self.part[k, core, rows, :] = self.part[k, core, rows, :] + term[from_rows, :]
            return 0

        lax.fori_loop(0, size // step, one, 0)

    def combine(self, k):
        self.exchange[k].wait_recv()
        self.add(k, 0, 2 * self.half, self.sibling.at[k], 0)

    def finish_two(self):
        self.pass1.wait_recv()
        self.add(2, 0, self.half, self.passing.at[0], 0)
        self.second2.start()
        self.pass2.wait_recv()
        self.add(1, self.half, self.half, self.passing.at[1], 0)
        self.second1.start()

    def arrive(self):
        for copy in (self.first1, self.second1, self.first2, self.second2):
            copy.wait_recv()

    def total(self, rows):
        return (self.part[0, self.place.core, rows, :].astype(F32) + self.final[0, rows, :].astype(F32)
                + self.final[1, rows, :].astype(F32))

    def close(self):
        for copy in self.exchange + (self.pass1, self.pass2, self.first1, self.second1, self.first2, self.second2):
            copy.wait_send()


def scatter_scratch(tok, width):
    return [
        pltpu.VMEM((4, 2, tok, width), BF16),
        pltpu.VMEM((4, tok, width), BF16),
        pltpu.VMEM((2, tok // 2, width), BF16),
        pltpu.VMEM((2, tok, width), BF16),
        pltpu.SemaphoreType.DMA((SCATTER_SLOTS,)),
        pltpu.SemaphoreType.DMA((SCATTER_SLOTS,)),
    ]


def start_kernel(x_ref, table_ref, kv_ref, qo_ref, gain_in, x_all, table_all, kv_all, qo_all, gain_all,
                 x_send, x_recv, t_send, t_recv, k_send, k_recv, p_send, p_recv, g_send, g_recv, z_send, z_recv,
                 w_send, w_recv, pair_send, pair_recv, local_sem, gain_ref):
    place = Place()
    gain = jnp.concatenate([gain_in[...].astype(F32), jnp.zeros((1, 128 - gain_in.shape[1]), F32)], axis=1)
    gain_ref[...] = jnp.broadcast_to(gain, gain_ref.shape)
    rows = qo_all.shape[0]
    me, row, core = place.me, place.row, place.core
    local = [pltpu.make_async_copy(src, dst, local_sem.at[i]) for i, (src, dst) in enumerate((
        (kv_ref.at[me], kv_all.at[core, row, me]), (qo_ref.at[me], qo_all.at[row, me]), (gain_ref, gain_all.at[row, me]),
        (x_ref, x_all.at[me]), (table_ref, table_all.at[me])))]
    for copy in local:
        copy.start()
    place.greet_all(rows)
    exchange, rest = [], []
    for j in range(1, PLANE):
        other = lax.rem(me + j, PLANE)
        exchange.append(place.send(kv_ref.at[other], kv_all.at[lax.rem(other, 2), row, me], k_send, k_recv, j, other))
        rest.append(place.send(qo_ref.at[other], qo_all.at[row, me], p_send, p_recv, j, other))
        rest.append(place.send(gain_ref, gain_all.at[row, me], g_send, g_recv, j, other))
    for copy in exchange + rest:
        copy.start()
    gathers = (Gather(place, x_ref, x_all, x_send, x_recv), Gather(place, table_ref, table_all, t_send, t_recv))
    gathers[1].start()
    gathers[0].start()
    for copy in local[:3]:
        copy.wait()
    line = Line(place)
    weights = [RowGather(line, at(row), at, w_send.at[i], w_recv.at[i])
               for i, at in enumerate((lambda r: kv_all.at[core, r], lambda r: qo_all.at[r]))]
    for copy in exchange:
        copy.wait_recv()
    weights[0].start()
    for copy in rest:
        copy.wait_recv()
    weights[1].start()
    along = []
    for j in range(1, rows):
        other = lax.rem(row + j, rows)
        along.append(line.send(gain_all.at[row], gain_all.at[row], z_send, j, z_recv, j, other))
    for copy in along:
        copy.start()
    for gather in gathers[::-1]:
        gather.own_chip()
    weights[0].forward()
    for gather in gathers[::-1]:
        gather.neighbours()
    weights[0].finish()
    pair = place.send(kv_all.at[core], kv_all.at[core], pair_send, pair_recv, 0, place.sib)
    pair.start()
    weights[1].forward()
    for name in ("chip1", "chip2", "diagonal", "chip3"):
        for gather in gathers[::-1]:
            getattr(gather, name)()
    for copy in local[3:]:
        copy.wait()
    for copy in along:
        copy.wait_recv()
    for copy in exchange + rest + along:
        copy.wait_send()
    for gather in gathers:
        gather.close()
    weights[1].finish()
    pair.wait_recv()
    pair.wait_send()
    for one in weights:
        one.close()


def start_phase(rows, x, table, kv, qo, gain):
    tok, model = x.shape
    dma = pltpu.SemaphoreType.DMA
    return pl.pallas_call(
        start_kernel,
        out_shape=(
            jax.ShapeDtypeStruct((PLANE, tok, model), BF16),
            jax.ShapeDtypeStruct((PLANE,) + table.shape, F32),
            jax.ShapeDtypeStruct((2, rows) + kv.shape, BF16),
            jax.ShapeDtypeStruct((rows,) + qo.shape, BF16),
            jax.ShapeDtypeStruct((rows, PLANE, 8, 128), F32),
        ),
        in_specs=[VMEM_SPEC] * 5,
        out_specs=(ANY_SPEC,) * 5,
        scratch_shapes=[dma((GATHER_SLOTS,))] * 4 + [dma((PLANE,))] * 6 + [dma((rows,))] * 2
        + [dma((2, ROW_SLOTS))] * 2 + [dma((1,))] * 2 + [dma((5,)), pltpu.VMEM((8, 128), F32)],
        compiler_params=pltpu.CompilerParams(collective_id=0, has_side_effects=True),
        cost_estimate=pl.CostEstimate(flops=0, bytes_accessed=160 << 20, transcendentals=0),
    )(x, table, kv, qo, gain)


def load_slab(kv_hbm, qo_hbm, w_ref, sem):
    parts = ((kv_hbm.at[0], 0, 128), (kv_hbm.at[1], 128, 256), (qo_hbm, 256, 640))
    return [pltpu.make_async_copy(src, w_ref.at[:, a:b], sem.at[i]) for i, (src, a, b) in enumerate(parts)]


class Forward:
    def __init__(self, heads, me, table, gq, gk, raw, merged, o, qa, ka, kt, vt, inv):
        self.heads, self.table, self.gq, self.gk = heads, table, column(gq), column(gk)
        self.raw, self.merged, self.o, self.qa, self.ka, self.kt, self.vt, self.inv = raw, merged, o, qa, ka, kt, vt, inv
        self.slots = [heads.slot(me, h) for h in range(heads.queries)]

    def prepare(self, b, projected):
        heads = self.heads
        tok = self.table.shape[2]
        lanes = span(b * tok, tok)
        cos = self.table[b, 0:HALF, :]
        sin = self.table[b, HALF:D, :]
        hot = self.table[b, D:D + 8, :]
        row = lax.broadcasted_iota(jnp.int32, (16, tok), 0)
        one_row = jnp.where(row == 0, 1.0, 0.0).astype(F32)
        penalty = jnp.concatenate([(1.0 - hot) * PENALTY, jnp.zeros((8, tok), F32)], axis=0).astype(BF16)
        lead = 2 * heads.narrow
        self.raw[0:heads.wide, lanes] = projected[lead:lead + heads.wide]

        def rotated(raw, gain):
            inv = lax.rsqrt(jnp.mean(raw * raw, axis=0, keepdims=True) + EPSILON)
            n = raw * inv * gain
            a, c = n[:HALF], n[HALF:]
            return inv, jnp.concatenate([a * cos - c * sin, c * cos + a * sin], axis=0)

        for h in range(heads.queries):
            inv, q = rotated(projected[lead + h * D:lead + (h + 1) * D], self.gq)
            self.inv[h:h + 1, lanes] = inv
            self.qa[h, :, lanes] = jnp.concatenate([(q * (D ** -0.5)).astype(BF16), penalty], axis=0)
        for g in range(heads.pairs):
            start = 2 * g * D
            self.raw[heads.wide + g * D:heads.wide + (g + 1) * D, lanes] = projected[start:start + D]
            inv, k = rotated(projected[start:start + D], self.gk)
            self.inv[heads.queries + g:heads.queries + g + 1, lanes] = inv
            self.kt[g, :, lanes] = k.astype(BF16)
            full = jnp.concatenate([k, hot, jnp.ones((8, tok), F32), jnp.zeros((48, tok), F32)], axis=0)
            self.ka[g, lanes, :] = jnp.transpose(full).astype(BF16)
            start += D
            self.vt[g, :, lanes] = jnp.concatenate([projected[start:start + D], one_row], axis=0).astype(BF16)

    def query_block(self, i):
        heads = self.heads
        cols = span(i * BLOCK, BLOCK)
        causal = (lax.broadcasted_iota(jnp.int32, (BLOCK, BLOCK), 0)
                  <= lax.broadcasted_iota(jnp.int32, (BLOCK, BLOCK), 1))

        def step(j, accs, diagonal):
            rows = span(j * BLOCK, BLOCK)
            new = []
            for h in range(heads.queries):
                slot = self.slots[h]
                p = jnp.exp(dot(self.ka[slot, rows, 0:80], self.qa[h, :, cols]))
                if diagonal:
                    p = jnp.where(causal, p, 0.0)
                new.append(accs[h] + dot(self.vt[slot, :, rows], p.astype(BF16)))
            return tuple(new)

        accs = tuple(jnp.zeros((80, BLOCK), F32) for _ in range(heads.queries))
        accs = lax.fori_loop(0, i, lambda j, c: step(j, c, False), accs)
        accs = step(i, accs, True)
        row = lax.broadcasted_iota(jnp.int32, (16, BLOCK), 0)
        lead = self.merged.shape[1] - heads.wide
        outs = [jnp.zeros((lead, BLOCK), F32)] if lead else []
        for h in range(heads.queries):
            total = accs[h][D:D + 1]
            o = accs[h][:D] * (1.0 / total)
            self.o[h, :, cols] = o
            outs.append(o)
            pieces = split3(-jnp.log(total))
            old = self.qa[h, 64:80, cols].astype(F32)
            extra = jnp.where(row == 8, pieces[0],
                              jnp.where(row == 9, pieces[1], jnp.where(row == 10, pieces[2], old)))
            self.qa[h, 64:80, cols] = extra.astype(BF16)
        merged = jnp.transpose(jnp.concatenate(outs, axis=0)).astype(BF16)
        self.merged[cols, :] = merged
        return merged


class Backward:
    def __init__(self, heads, me, table, gq, gk, raw, o, qa, ka, kt, vt, inv, doa, dopad, qpad, va, dq, acc):
        self.heads, self.table, self.gq, self.gk = heads, table, column(gq), column(gk)
        self.raw, self.o, self.qa, self.ka, self.kt, self.vt, self.inv = raw, o, qa, ka, kt, vt, inv
        self.doa, self.dopad, self.qpad, self.va, self.dq, self.acc = doa, dopad, qpad, va, dq, acc
        self.slots = [heads.slot(me, h) for h in range(heads.queries)]

    def prepare(self, b):
        heads = self.heads
        tok = self.table.shape[2]
        lanes = span(b * tok, tok)
        for h in range(heads.queries):
            q = jnp.concatenate([jnp.zeros((D, tok), F32), self.qa[h, 0:D, lanes].astype(F32)], axis=0)
            self.qpad[h, lanes, :] = jnp.transpose(q).astype(BF16)
            self.acc[h, lanes, :] = jnp.zeros((tok, 2 * D), F32)
        for g in range(heads.pairs):
            v = jnp.concatenate([self.vt[g, 0:D, lanes].astype(F32), jnp.ones((D, tok), F32)], axis=0)
            self.va[g, lanes, :] = jnp.transpose(v).astype(BF16)

    def gradient(self, b, dm):
        heads = self.heads
        tok = self.table.shape[2]
        lanes = span(b * tok, tok)
        row = lax.broadcasted_iota(jnp.int32, (16, tok), 0)
        dmt = jnp.transpose(dm.astype(BF16).astype(F32))
        for h in range(heads.queries):
            do = dmt[h * D:(h + 1) * D]
            delta = jnp.sum(do * self.o[h, :, lanes], axis=0, keepdims=True)
            pieces = split3(-delta)
            extra = jnp.where(row == 0, pieces[0],
                              jnp.where(row == 1, pieces[1], jnp.where(row == 2, pieces[2], 0.0)))
            self.doa[h, :, lanes] = jnp.concatenate([do, extra], axis=0).astype(BF16)
            both = jnp.concatenate([do, jnp.zeros((D, tok), F32)], axis=0)
            self.dopad[h, lanes, :] = jnp.transpose(both).astype(BF16)

    def query_block(self, i):
        heads = self.heads
        cols = span(i * BLOCK, BLOCK)
        causal = (lax.broadcasted_iota(jnp.int32, (BLOCK, BLOCK), 0)
                  <= lax.broadcasted_iota(jnp.int32, (BLOCK, BLOCK), 1))

        def step(j, accs, diagonal):
            rows = span(j * BLOCK, BLOCK)
            new = []
            for h in range(heads.queries):
                slot = self.slots[h]
                p = jnp.exp(dot(self.ka[slot, rows, 0:80], self.qa[h, :, cols]))
                if diagonal:
                    p = jnp.where(causal, p, 0.0)
                dp = dot(self.va[slot, rows, 0:80], self.doa[h, :, cols])
                ds = (p * dp).astype(BF16)
                self.acc[h, rows, :] += dot(p.astype(BF16), self.dopad[h, cols, :]) + dot(ds, self.qpad[h, cols, :])
                new.append(accs[h] + dot(self.kt[slot, :, rows], ds))
            return tuple(new)

        accs = tuple(jnp.zeros((D, BLOCK), F32) for _ in range(heads.queries))
        accs = lax.fori_loop(0, i, lambda j, c: step(j, c, False), accs)
        accs = step(i, accs, True)
        for h in range(heads.queries):
            self.dq[h, :, cols] = accs[h]

    def finish(self, b, sums):
        heads = self.heads
        tok = self.table.shape[2]
        lanes = span(b * tok, tok)
        cos = self.table[b, 0:HALF, :]
        sin = self.table[b, HALF:D, :]
        scale = self.table[b, 72:73, :]

        def back(grad, raw, inv, gain):
            a, c = grad[:HALF], grad[HALF:]
            n = jnp.concatenate([a * cos + c * sin, c * cos - a * sin], axis=0)
            v = n * gain
            out = inv * v - raw * (inv * inv * inv) * jnp.mean(v * raw, axis=0, keepdims=True)
            return out * scale, n * raw * inv

        sum_q, sum_k = sums
        pairs = [jnp.zeros((2 * D, tok), F32) for _ in range(heads.pairs)]
        out = []
        for h in range(heads.queries):
            raw = self.raw[h * D:(h + 1) * D, lanes]
            grad, part = back(self.dq[h, :, lanes] * (D ** -0.5), raw, self.inv[h:h + 1, lanes], self.gq)
            out.append(grad)
            sum_q = sum_q + part
            both = jnp.transpose(self.acc[h, lanes, :])
            for g in range(heads.pairs):
                pairs[g] = pairs[g] + jnp.where(self.slots[h] == g, both, 0.0)
        both_out = []
        for g in range(heads.pairs):
            start = heads.wide + g * D
            raw = self.raw[start:start + D, lanes]
            inv = self.inv[heads.queries + g:heads.queries + g + 1, lanes]
            grad, part = back(pairs[g][D:], raw, inv, self.gk)
            both_out += [grad, pairs[g][:D] * scale]
            sum_k = sum_k + part
        return jnp.concatenate(both_out + out, axis=0), (sum_q, sum_k)


def kept_shapes(heads, length, lead):
    return (
        jax.ShapeDtypeStruct((heads.wide + heads.narrow, length), F32),
        jax.ShapeDtypeStruct((length, lead + heads.wide), BF16),
        jax.ShapeDtypeStruct((heads.queries, D, length), F32),
        jax.ShapeDtypeStruct((heads.queries, 80, length), BF16),
        jax.ShapeDtypeStruct((heads.pairs, length, 128), BF16),
        jax.ShapeDtypeStruct((heads.pairs, D, length), BF16),
        jax.ShapeDtypeStruct((heads.pairs, 80, length), BF16),
        jax.ShapeDtypeStruct((8, length), F32),
    )


def backward_scratch(heads, length):
    return [
        pltpu.VMEM((heads.queries, 80, length), BF16),
        pltpu.VMEM((heads.queries, length, 2 * D), BF16),
        pltpu.VMEM((heads.queries, length, 2 * D), BF16),
        pltpu.VMEM((heads.pairs, length, 2 * D), BF16),
        pltpu.VMEM((heads.queries, D, length), F32),
        pltpu.VMEM((heads.queries, length, 2 * D), F32),
    ]


def local_forward_kernel(heads, proj_ref, table_ref, gq_ref, gk_ref, *kept):
    forward = Forward(heads, lax.axis_index("seq"), table_ref, gq_ref, gk_ref, *kept)
    blocks, _, tok = table_ref.shape

    def prepare(b, _):
        rows = span(b * tok, tok)
        forward.prepare(b, jnp.transpose(proj_ref[rows, :]) * table_ref[b, 72:73, :])
        return 0

    def query_block(i, _):
        forward.query_block(i)
        return 0

    lax.fori_loop(0, blocks, prepare, 0)
    lax.fori_loop(0, blocks * tok // BLOCK, query_block, 0)


def local_backward_kernel(heads, dm_ref, table_ref, gq_ref, gk_ref, raw_ref, o_ref, qa_ref, ka_ref, kt_ref, vt_ref, inv_ref,
                          pg_ref, gains_ref, *scratch):
    backward = Backward(heads, lax.axis_index("seq"), table_ref, gq_ref, gk_ref, raw_ref, o_ref, qa_ref, ka_ref, kt_ref,
                        vt_ref, inv_ref, *scratch)
    blocks, _, tok = table_ref.shape

    def prepare(b, _):
        backward.prepare(b)
        backward.gradient(b, dm_ref[span(b * tok, tok), :])
        return 0

    def query_block(i, _):
        backward.query_block(i)
        return 0

    def finish(b, sums):
        grad, sums = backward.finish(b, sums)
        pg_ref[span(b * tok, tok), :] = jnp.transpose(grad).astype(BF16)
        return sums

    lax.fori_loop(0, blocks, prepare, 0)
    lax.fori_loop(0, blocks * tok // BLOCK, query_block, 0)
    zero = jnp.zeros((D, tok), F32)
    sum_q, sum_k = lax.fori_loop(0, blocks, finish, (zero, zero))
    gains_ref[0:D, :] = jnp.broadcast_to(jnp.sum(sum_q, axis=1, keepdims=True), (D, 128))
    gains_ref[D:2 * D, :] = jnp.broadcast_to(jnp.sum(sum_k, axis=1, keepdims=True), (D, 128))


def attention_kernel(heads, x_hbm, g_hbm, kv_hbm, qo_hbm, gate_hbm, up_hbm, table_ref, gq_ref, gk_ref, gain_ref,
                     res_ref, two_ref, g_all, gate_all, up_all, raw_hbm, merged_hbm, o_hbm, qa_hbm, ka_hbm, kt_hbm, vt_hbm, inv_hbm,
                     raw_ref, merged_ref, o_ref, qa_ref, ka_ref, kt_ref, vt_ref, inv_ref, kept_sem, x_ref, w_ref, part_ref, sibling_ref, passing_ref, final_ref, rs_send, rs_recv,
                     ag_send, ag_recv, load_sem, slab_sem, z_send, z_recv):
    place = Place()
    blocks, tok, model = x_ref.shape
    slabs = ((gate_hbm, gate_all), (up_hbm, up_all))
    load_w = load_slab(kv_hbm, qo_hbm, w_ref, slab_sem)
    for copy in load_w:
        copy.start()
    loads = [pltpu.make_async_copy(x_hbm.at[b], x_ref.at[b], load_sem.at[b]) for b in range(blocks)]
    for copy in loads:
        copy.start()
    place.greet(4)
    gather = Gather(place, g_hbm, g_all, ag_send, ag_recv)
    scatter = Scatter(place, part_ref, sibling_ref, passing_ref, final_ref, rs_send, rs_recv)
    line = Line(place)
    weights = [RowGather(line, own, lambda r, every=every: every.at[r], z_send.at[i], z_recv.at[i])
               for i, (own, every) in enumerate(slabs)]
    for one in weights:
        one.start()
    gather.start()
    forward = Forward(heads, place.me, table_ref, gq_ref, gk_ref, raw_ref, merged_ref, o_ref, qa_ref, ka_ref, kt_ref,
                      vt_ref, inv_ref)
    for copy in load_w + loads:
        copy.wait()

    def prepare(b, _):
        proj = dot(x_ref[b], w_ref[:, 0:512])
        forward.prepare(b, jnp.transpose(proj) * table_ref[b, 72:73, :])
        return 0

    lax.fori_loop(0, blocks, prepare, 0, unroll=2)
    tile = 512

    def compute(k):
        merged = forward.query_block(place.chips[k])

        def model_tile(n, _):
            cols = span(n * tile, tile)
            out = dot_nt(merged_ref[span(place.chips[k] * BLOCK, BLOCK), :], w_ref[cols, 384:640])
            part_ref[k, :, :, cols] = out.astype(BF16).reshape(2, tok, tile)
            return 0

        lax.fori_loop(0, model // tile, model_tile, 0, unroll=True)
        scatter.exchange[k].start()

    compute(3)
    gather.own_chip()
    gather.neighbours()
    scatter.combine(3)
    scatter.pass1.start()
    scatter.pass2.start()
    compute(1)
    scatter.combine(1)
    scatter.first1.start()
    gather.chip1()
    gather.chip2()
    weights[0].forward()
    compute(2)
    scatter.combine(2)
    scatter.first2.start()
    gather.diagonal()
    compute(0)
    keep = [pltpu.make_async_copy(src, dst, kept_sem.at[i]) for i, (src, dst) in enumerate((
        (raw_ref, raw_hbm), (merged_ref, merged_hbm), (o_ref, o_hbm), (qa_ref, qa_hbm), (ka_ref, ka_hbm),
        (kt_ref, kt_hbm), (vt_ref, vt_hbm), (inv_ref, inv_hbm)))]
    for copy in keep:
        copy.start()
    scatter.combine(0)
    weights[1].forward()
    scatter.finish_two()
    gather.chip3()
    gain = gain_row(gain_ref)
    scatter.arrive()

    def finish(i, _):
        rows = span(i * 32, 32)
        res = x_ref[place.me, rows, :].astype(F32) + scatter.total(rows)
        res_ref[rows, :] = res
        two_ref[rows, :] = (res * norm_inverse(res) * gain).astype(BF16)
        return 0

    lax.fori_loop(0, tok // 32, finish, 0)
    for one in weights:
        one.finish()
        one.close()
    for copy in keep:
        copy.wait()
    gather.close()
    scatter.close()


def attention_phase(heads, x_all, g, kv, qo, slabs, table, gq, gk, gain):
    blocks, tok, model = x_all.shape
    dma = pltpu.SemaphoreType.DMA
    lead = 256 - heads.wide
    kept = kept_shapes(heads, blocks * tok, lead)
    return pl.pallas_call(
        functools.partial(attention_kernel, heads),
        out_shape=(jax.ShapeDtypeStruct((tok, model), F32), jax.ShapeDtypeStruct((tok, model), BF16),
                   jax.ShapeDtypeStruct((blocks, tok, model), BF16))
        + tuple(jax.ShapeDtypeStruct((4,) + slab.shape, BF16) for slab in slabs) + kept,
        in_specs=[ANY_SPEC] * 6 + [VMEM_SPEC] * 4,
        out_specs=(VMEM_SPEC, VMEM_SPEC) + (ANY_SPEC,) * (3 + len(kept)),
        scratch_shapes=[
            *(pltpu.VMEM(array.shape, array.dtype) for array in kept),
            dma((len(kept),)),
            pltpu.VMEM((blocks, tok, model), BF16),
            pltpu.VMEM((model, heads.columns), BF16),
            *scatter_scratch(tok, model),
            dma((GATHER_SLOTS,)), dma((GATHER_SLOTS,)), dma((blocks,)), dma((3,)),
            dma((2, ROW_SLOTS)), dma((2, ROW_SLOTS)),
        ],
        compiler_params=pltpu.CompilerParams(collective_id=1, has_side_effects=True, vmem_limit_bytes=VMEM_LIMIT),
        cost_estimate=pl.CostEstimate(flops=40 << 30, bytes_accessed=64 << 20, transcendentals=0),
    )(x_all, g, kv, qo, *slabs, table, gq, gk, gain)


def ffn_kernel(res_ref, gain_ref, two_hbm, g_own, g_hbm, gate_own, gate_hbm, up_own, up_hbm, down_hbm,
               out_hbm, rgrad_ref, branch_ref, gain_grad_ref, gate_grad_hbm, up_grad_hbm,
               gate_grad_own, up_grad_own, down_own, down_recv,
               two_ref, g_ref, weight_ref, down_ref, hid_ref, gu_ref, stage_ref, wstage_ref, dsum_ref, dgrad_ref, merge_ref,
               part_ref, sibling_ref, passing_ref, final_ref, rs_send, rs_recv,
               ag_send, ag_recv, load_sem, g_sem, stage_sem, wstage_sem, own_sem, za_send, za_recv, zr_send, zr_recv):
    place = Place()
    blocks, tok, model = g_ref.shape
    ff = weight_ref.shape[1] // 2
    share = model // 4
    tile = 256
    def down_at(r):
        return down_ref.at[:, span(r * share, share)]

    loads, g_loads = [], []
    for i, (own, every) in enumerate(((gate_own, gate_hbm), (up_own, up_hbm))):
        for j in range(4):
            r = lax.rem(place.row + j, 4)
            loads.append(pltpu.make_async_copy(
                every.at[r] if j else own, weight_ref.at[span(r * share, share), i * ff:(i + 1) * ff], load_sem.at[4 * i + j]))
    for j in range(blocks):
        b = lax.rem(place.me + j, blocks)
        g_loads.append(pltpu.make_async_copy(g_hbm.at[b] if j else g_own, g_ref.at[b], g_sem.at[j]))
    own_loads = [pltpu.make_async_copy(two_hbm, two_ref.at[place.me], load_sem.at[8]),
                 pltpu.make_async_copy(down_hbm, down_at(place.row), load_sem.at[9])]
    for copy in own_loads + loads + g_loads:
        copy.start()
    place.greet(4)
    line = Line(place)
    gather = Gather(place, two_hbm, two_ref, ag_send, ag_recv)
    scatter = Scatter(place, part_ref, sibling_ref, passing_ref, final_ref, rs_send, rs_recv)
    downs = RowGather(line, down_hbm, down_at, za_send, za_recv)
    down_sum = RowScatter(line, dgrad_ref, down_recv, merge_ref, merge_ref, zr_send, zr_recv)
    gather.start()
    downs.start()
    for copy in loads + own_loads:
        copy.wait()

    def forward(k):
        pair = pl.ds(2 * place.chips[k], 2)

        def hidden_tile(h, _):
            cols, cols2 = span(h * tile, tile), span(ff + h * tile, tile)
            x = two_ref[pair].reshape(2 * tok, model)
            gate = dot(x, weight_ref[:, cols])
            up = dot(x, weight_ref[:, cols2])
            s = 1.0 / (1.0 + jnp.exp(-gate))
            act = gate * s
            hid_ref[pair, :, cols] = (act * up).astype(BF16).reshape(2, tok, tile)
            gu_ref[pair, :, cols] = (up * s * (1.0 + gate * (1.0 - s))).astype(BF16).reshape(2, tok, tile)
            gu_ref[pair, :, cols2] = act.astype(BF16).reshape(2, tok, tile)
            return 0

        lax.fori_loop(0, ff // tile, hidden_tile, 0, unroll=True)

    def backward(k):
        pair = pl.ds(2 * place.chips[k], 2)

        def hidden_tile(h, _):
            cols, cols2 = span(h * tile, tile), span(ff + h * tile, tile)
            back = dot_nt(g_ref[pair].reshape(2 * tok, model), down_ref[cols, :])
            for where in (cols, cols2):
                factor = gu_ref[pair, :, where].reshape(2 * tok, tile).astype(F32)
                gu_ref[pair, :, where] = (back * factor).astype(BF16).reshape(2, tok, tile)
            return 0

        lax.fori_loop(0, ff // tile, hidden_tile, 0, unroll=True)

        def model_tile(n, _):
            cols = span(n * tile, tile)
            back = dot_nt(gu_ref[pair].reshape(2 * tok, 2 * ff), weight_ref[cols, :])
            part_ref[k, :, :, cols] = back.astype(BF16).reshape(2, tok, tile)
            return 0

        lax.fori_loop(0, model // tile, model_tile, 0, unroll=True)
        scatter.exchange[k].start()

    def stage_copy(n):
        slot = lax.rem(n, 2)
        return pltpu.make_async_copy(stage_ref.at[slot], out_hbm.at[n // 4, :, :, span(lax.rem(n, 4) * share, share)],
                                     stage_sem.at[slot])

    def out_tile(n, _):
        @pl.when(n >= 2)
        def _():
            stage_copy(n - 2).wait()

        k, r = n // 4, lax.rem(n, 4)
        chip = place.chip
        m = jnp.where(k == 0, chip, jnp.where(k == 1, place.chips[1], jnp.where(k == 2, place.chips[2], place.chips[3])))
        out = dot(hid_ref[pl.ds(2 * m, 2)].reshape(2 * tok, ff), down_ref[:, span(r * share, share)])
        stage_ref[lax.rem(n, 2)] = out.astype(BF16).reshape(2, tok, share)
        stage_copy(n).start()
        return 0

    def down_grad(k):
        pair = pl.ds(2 * place.chips[k], 2)

        def down_rows(n, _):
            rows, r = span(lax.rem(n, ff // tile) * tile, tile), n // (ff // tile)
            h = hid_ref[pair, :, rows].reshape(2 * tok, tile)
            g = g_ref[pair, :, span(r * share, share)].reshape(2 * tok, share)
            term = dot_tn(h, g)
            if k:
                term = dsum_ref[r, rows, :] + term
            if k < 3:
                dsum_ref[r, rows, :] = term
            else:
                dgrad_ref[r, rows, :] = term.astype(BF16)
            return 0

        lax.fori_loop(0, 4 * (ff // tile), down_rows, 0, unroll=4)

    def wstage_copies(i, slot):
        return (pltpu.make_async_copy(wstage_ref.at[slot, :, 0:ff], gate_grad_hbm.at[i], wstage_sem.at[slot, 0]),
                pltpu.make_async_copy(wstage_ref.at[slot, :, ff:2 * ff], up_grad_hbm.at[i], wstage_sem.at[slot, 1]))

    def own_copies(half, slot):
        rows = span(half * tile, tile)
        return (pltpu.make_async_copy(wstage_ref.at[slot, :, 0:ff], gate_grad_own.at[rows], own_sem.at[0]),
                pltpu.make_async_copy(wstage_ref.at[slot, :, ff:2 * ff], up_grad_own.at[rows], own_sem.at[1]))

    def gate_up_rows(i, _):
        cols = span(i * tile, tile)
        slot = lax.rem(i, 2)

        @pl.when(i >= 2)
        def _():
            for copy in wstage_copies(i - 2, slot):
                copy.wait()

        x = two_ref[:, :, cols].reshape(blocks * tok, tile)
        wstage_ref[slot] = dot_tn(x, gu_ref[...].reshape(blocks * tok, 2 * ff)).astype(BF16)
        for copy in wstage_copies(i, slot):
            copy.start()

        @pl.when(i // 2 == place.row)
        def _():
            for copy in own_copies(lax.rem(i, 2), slot):
                copy.start()

        out_tile(2 * i, 0)
        out_tile(2 * i + 1, 0)

        @pl.when(i // 2 == place.row)
        def _():
            for copy in own_copies(lax.rem(i, 2), slot):
                copy.wait()

        return 0

    gather.own_chip()
    forward(0)
    for copy in g_loads:
        copy.wait()
    down_grad(0)
    gather.neighbours()
    downs.forward()
    gather.chip1()
    forward(1)
    down_grad(1)
    gather.chip2()
    forward(2)
    down_grad(2)
    gather.diagonal()
    gather.chip3()
    forward(3)
    downs.finish()
    backward(3)
    down_grad(3)
    down_sum.start_over()
    down_sum.start()
    own_down = pltpu.make_async_copy(dgrad_ref.at[place.row], down_own, load_sem.at[10])
    own_down.start()
    scatter.combine(3)
    scatter.pass1.start()
    scatter.pass2.start()
    backward(1)
    backward(2)
    scatter.combine(1)
    scatter.first1.start()
    scatter.combine(2)
    scatter.first2.start()
    backward(0)
    scatter.finish_two()
    scatter.combine(0)
    count = model // tile
    lax.fori_loop(0, count // 2, gate_up_rows, 0)

    def merge():
        def add(n, _):
            rows = span(n * 64, 64)
            merge_ref[rows, :] = (merge_ref[rows, :].astype(F32) + dgrad_ref[line.c, rows, :].astype(F32)).astype(BF16)
            return 0

        lax.fori_loop(0, ff // 64, add, 0)

    down_sum.add(merge)
    lax.fori_loop(count // 2, count, gate_up_rows, 0)
    gain = gain_row(gain_ref)
    scatter.arrive()

    def finish(i, sums):
        rows = span(i * 32, 32)
        res = res_ref[rows, :]
        inv = norm_inverse(res)
        grad = scatter.total(rows)
        v = grad * gain
        mean = jnp.mean(v * res, axis=-1, keepdims=True)
        out = g_ref[place.me, rows, :].astype(F32) + inv * v - res * (inv * inv * inv * mean)
        rgrad_ref[rows, :] = out
        branch_ref[rows, :] = out.astype(BF16)
        return sums + jnp.sum(grad * res * inv, axis=0, keepdims=True)

    gain_grad_ref[...] = lax.fori_loop(0, tok // 32, finish, jnp.zeros((1, model), F32), unroll=2)
    for i in (count - 2, count - 1):
        for copy in wstage_copies(i, i % 2):
            copy.wait()
    for n in (14, 15):
        stage_copy(n).wait()
    own_down.wait()
    down_sum.finish()
    down_sum.close()
    downs.close()
    gather.close()
    scatter.close()


def feed_forward(res, gain, two, g, g_all, slabs):
    tok, model = res.shape
    ff = slabs[0].shape[1]
    blocks = g_all.shape[0]
    dma = pltpu.SemaphoreType.DMA
    return pl.pallas_call(
        ffn_kernel,
        out_shape=(
            jax.ShapeDtypeStruct((4, 2, tok, model), BF16),
            jax.ShapeDtypeStruct((tok, model), F32),
            jax.ShapeDtypeStruct((tok, model), BF16),
            jax.ShapeDtypeStruct((1, model), F32),
            jax.ShapeDtypeStruct((model // 256, 256, ff), BF16),
            jax.ShapeDtypeStruct((model // 256, 256, ff), BF16),
            jax.ShapeDtypeStruct((model // 4, ff), BF16),
            jax.ShapeDtypeStruct((model // 4, ff), BF16),
            jax.ShapeDtypeStruct((ff, model // 4), BF16),
            jax.ShapeDtypeStruct((3, ff, model // 4), BF16),
        ),
        in_specs=[VMEM_SPEC, VMEM_SPEC] + [ANY_SPEC] * 8,
        out_specs=(ANY_SPEC, VMEM_SPEC, VMEM_SPEC, VMEM_SPEC) + (ANY_SPEC,) * 6,
        scratch_shapes=[
            pltpu.VMEM((blocks, tok, model), BF16),
            pltpu.VMEM((blocks, tok, model), BF16),
            pltpu.VMEM((model, 2 * ff), BF16),
            pltpu.VMEM((ff, model), BF16),
            pltpu.VMEM((blocks, tok, ff), BF16),
            pltpu.VMEM((blocks, tok, 2 * ff), BF16),
            pltpu.VMEM((2, 2, tok, model // 4), BF16),
            pltpu.VMEM((2, 256, 2 * ff), BF16),
            pltpu.VMEM((4, ff, model // 4), F32),
            pltpu.VMEM((4, ff, model // 4), BF16),
            pltpu.VMEM((ff, model // 4), BF16),
            *scatter_scratch(tok, model),
            dma((GATHER_SLOTS,)), dma((GATHER_SLOTS,)), dma((11,)), dma((blocks,)), dma((2,)), dma((2, 2)), dma((2,)),
            dma((ROW_SLOTS,)), dma((ROW_SLOTS,)), dma((ROW_SLOTS,)), dma((ROW_SLOTS,)),
        ],
        compiler_params=pltpu.CompilerParams(collective_id=2, has_side_effects=True, vmem_limit_bytes=62 * 1024 * 1024),
        cost_estimate=pl.CostEstimate(flops=18 * blocks * tok * model * ff, bytes_accessed=64 << 20, transcendentals=0),
    )(res, gain, two, g, g_all, *slabs)


def backward_kernel(heads, branch_hbm, out_hbm, x_hbm, kv_hbm, qo_hbm, gate_grad, up_grad, merged_hbm,
                    table_ref, gq_ref, gk_ref, gain_grad_ref, qkv_ref, gain_ref,
                    raw_hbm, o_hbm, qa_hbm, ka_hbm, kt_hbm, vt_hbm, inv_hbm,
                    ysum_hbm, outsum_hbm, grad_qkv_ref, grad_out_ref, grad_gain_ref, small_out,
                    grad_hbm, gate_recv, up_recv, qo_recv, kv_recv,
                    raw_ref, o_ref, qa_ref, ka_ref, kt_ref, vt_ref, inv_ref, kept_sem,
                    every_ref, w_ref, pg_ref, merged_ref, xt_ref, wstage_ref, gwo_ref,
                    doa_ref, dopad_ref, qpad_ref, va_ref, dq_ref, acc_ref,
                    part_ref, sibling_ref, passing_ref, final_ref, rs_send, rs_recv, rs2_send, rs2_recv,
                    ag_send, ag_recv, load_sem, xt_sem, wstage_sem, ready_sem,
                    ffn_merge, ffn_own, z_send, z_recv, own_sem, small_ref, small_row, small_mid, small_last, pieces_ref, amerge_ref, aown_ref,
                    kv_own, kv_in, kmerge_ref, ysum_ref, outsum_ref, sum_sem, slab_sem, pair_send, pair_recv,
                    s_send, s_recv, t_send, t_recv, p_send, p_recv):
    place = Place()
    blocks, tok, model = every_ref.shape[0] * every_ref.shape[1], every_ref.shape[2], every_ref.shape[3]
    branch_all = every_ref.reshape(blocks, tok, model)
    columns = 512
    lead = 256 - heads.wide
    load_w = load_slab(kv_hbm, qo_hbm, w_ref, slab_sem)
    load_out = pltpu.make_async_copy(out_hbm, part_ref, load_sem.at[1])
    load_own = pltpu.make_async_copy(branch_hbm, branch_all.at[place.me], load_sem.at[2])
    load_merged = pltpu.make_async_copy(merged_hbm, merged_ref, load_sem.at[3])
    load_out.start()
    load_own.start()
    for copy in load_w:
        copy.start()
    load_kept = [pltpu.make_async_copy(src, dst, kept_sem.at[i]) for i, (src, dst) in enumerate((
        (qa_hbm, qa_ref), (vt_hbm, vt_ref), (o_hbm, o_ref), (ka_hbm, ka_ref), (kt_hbm, kt_ref), (raw_hbm, raw_ref),
        (inv_hbm, inv_ref)))]
    for copy in load_kept:
        copy.start()
    load_merged.start()
    place.greet_all(4)
    gather = Gather(place, branch_hbm, branch_all, ag_send, ag_recv)
    gather.start()
    line = Line(place)
    ffn = [RowScatter(line, part, recv, ffn_merge.at[i], ffn_merge.at[i], z_send.at[i], z_recv.at[i])
           for i, (part, recv) in enumerate(((gate_grad, gate_recv), (up_grad, up_recv)))]
    for one in ffn:
        one.start_over()
    for one in ffn:
        one.start()
    first = Scatter(place, part_ref, sibling_ref, passing_ref, final_ref, rs_send, rs_recv)
    second = Scatter(place, every_ref, sibling_ref, passing_ref, final_ref, rs2_send, rs2_recv)
    load_out.wait()
    for copy in first.exchange:
        copy.start()

    def ffn_add(i):
        own = (gate_grad, up_grad)[i]

        def work():
            load = pltpu.make_async_copy(own.at[line.c], ffn_own, own_sem.at[0])
            load.start()
            load.wait()

            def add(n, _):
                rows = span(n * 64, 64)
                ffn_merge[i, rows, :] = ffn_merge[i, rows, :] + ffn_own[rows, :]
                return 0

            lax.fori_loop(0, ffn_own.shape[0] // 64, add, 0)

        ffn[i].add(work)

    def tell(n, others):
        for other in others:
            pl.semaphore_signal(ready_sem.at[n], inc=1, device_id=(place.row, other), device_id_type=MESH)

    back = Backward(heads, place.me, table_ref, gq_ref, gk_ref, raw_ref, o_ref, qa_ref, ka_ref, kt_ref, vt_ref, inv_ref,
                    doa_ref, dopad_ref, qpad_ref, va_ref, dq_ref, acc_ref)

    def prepare(b, _):
        back.prepare(b)
        return 0

    for copy in load_kept:
        copy.wait()
    lax.fori_loop(0, blocks, prepare, 0, unroll=2)
    for copy in load_w:
        copy.wait()
    load_own.wait()

    def compute(k):
        m = place.chips[k]

        def gradient(j, _):
            b = 2 * m + j
            dm = dot(branch_all[b], w_ref[:, 384:640])
            back.gradient(b, dm[:, lead:])
            return 0

        lax.fori_loop(0, 2, gradient, 0, unroll=True)
        back.query_block(m)

    gather.own_chip()
    compute(0)
    gather.neighbours()
    first.combine(3)
    first.pass1.start()
    first.pass2.start()
    ffn_add(0)
    gather.chip1()
    compute(1)
    first.combine(1)
    first.first1.start()
    gather.chip2()
    ffn_add(1)
    compute(2)
    first.combine(2)
    first.first2.start()
    gather.diagonal()
    first.combine(0)
    tell(0, (place.sib,))
    gather.chip3()
    compute(3)
    first.finish_two()
    tell(1, place.same[1:3])
    load_merged.wait()
    tile = 256
    count = model // tile

    def x_copy(i, slot):
        return pltpu.make_async_copy(x_hbm.at[:, :, span(i * tile, tile)], xt_ref.at[slot], xt_sem.at[slot])

    x_copy(0, 0).start()

    def out_rows(i, _):
        out = dot_tn(branch_all[:, :, span(i * tile, tile)].reshape(blocks * tok, tile), merged_ref[...])
        gwo_ref[i] = out.astype(BF16)
        return 0

    lax.fori_loop(0, count, out_rows, 0, unroll=4)
    gather.close()
    pad = 512 - heads.qkv

    def finish(b, sums):
        grad, sums = back.finish(b, sums)
        grad = jnp.concatenate([grad, jnp.zeros((pad, tok), F32)], axis=0)
        pg_ref[b] = jnp.transpose(grad).astype(BF16)
        return sums

    zero = jnp.zeros((D, tok), F32)
    sums = lax.fori_loop(0, blocks, finish, (zero, zero), unroll=2)

    def grad_copy(i, slot):
        return pltpu.make_async_copy(wstage_ref.at[slot], grad_hbm.at[i // 2, lax.rem(i, 2)], wstage_sem.at[slot])

    def weight_rows(i, _):
        slot = lax.rem(i, 2)

        @pl.when(i + 1 < count)
        def _():
            x_copy(i + 1, 1 - slot).start()

        @pl.when(i >= 2)
        def _():
            grad_copy(i - 2, slot).wait()

        x_copy(i, slot).wait()
        x = xt_ref[slot].reshape(blocks * tok, tile)
        qkv = dot_tn(x, pg_ref[...].reshape(blocks * tok, 512))
        even = place.core == 0
        cols = span(i * tile, tile)
        kv_own[i // 2, lax.rem(i, 2)] = jnp.where(even, qkv[:, 0:128], qkv[:, 128:256]).astype(BF16)
        merged_ref[cols, 0:128] = jnp.where(even, qkv[:, 128:256], qkv[:, 0:128]).astype(BF16)
        wstage_ref[slot, :, 0:heads.wide] = qkv[:, 256:256 + heads.wide].astype(BF16)
        wstage_ref[slot, :, heads.wide:2 * heads.wide] = gwo_ref[i, :, lead:]
        grad_copy(i, slot).start()
        return 0

    lax.fori_loop(0, count, weight_rows, 0, unroll=2)
    for i in (count - 2, count - 1):
        grad_copy(i, i % 2).wait()

    pair = place.send(merged_ref.at[:, 0:128], kv_in, pair_send, pair_recv, 0, place.sib)
    pair.start()
    attn = RowScatter(line, grad_hbm, qo_recv, amerge_ref, amerge_ref, z_send.at[2], z_recv.at[2])
    attn.start_over()
    attn.start()
    load_passed = pltpu.make_async_copy(grad_hbm.at[line.c], aown_ref, own_sem.at[2])
    load_passed.start()
    pair.wait_recv()

    def add_pair(n, _):
        b, rows = n // 4, span(lax.rem(n, 4) * 64, 64)
        for r in range(4):
            kv_own[r, b, rows, :] = kv_own[r, b, rows, :] + kv_in[span(r * 512 + n * 64, 64), :]
        return 0

    lax.fori_loop(0, 8, add_pair, 0)
    kv_sum = RowScatter(line, kv_own, kv_recv, kmerge_ref, kmerge_ref, z_send.at[3], z_recv.at[3])
    kv_sum.start_over()
    kv_sum.start()

    def attn_work():
        def add(n, _):
            b, rows = n // 4, span(lax.rem(n, 4) * 64, 64)
            amerge_ref[b, rows, :] = amerge_ref[b, rows, :] + aown_ref[b, rows, :]
            return 0

        lax.fori_loop(0, 8, add, 0)

    def kv_work():
        def add(n, _):
            b, rows = n // 4, span(lax.rem(n, 4) * 64, 64)
            kmerge_ref[b, rows, :] = kmerge_ref[b, rows, :] + kv_own[line.c, b, rows, :]
            return 0

        lax.fori_loop(0, 8, add, 0)

    def project(k):
        m = place.chips[k]

        def model_tile(n, _):
            cols = span(n * 512, 512)
            out = dot_nt(pg_ref[pl.ds(2 * m, 2)].reshape(2 * tok, 512), w_ref[cols, 0:512])
            every_ref[k, :, :, cols] = out.astype(BF16).reshape(2, tok, 512)
            return 0

        lax.fori_loop(0, model // 512, model_tile, 0, unroll=True)
        if k == 3:
            pl.semaphore_wait(ready_sem.at[0], 1)
        second.exchange[k].start()

    project(3)
    project(1)
    second.combine(3)
    pl.semaphore_wait(ready_sem.at[1], 2)
    second.pass1.start()
    second.pass2.start()
    project(2)
    second.combine(1)
    load_passed.wait()
    attn.add(attn_work)
    project(0)
    kv_sum.add(kv_work)
    second.combine(2)

    head_gains = jnp.sum(jnp.transpose(jnp.concatenate(sums, axis=0)), axis=0, keepdims=True)
    row8 = lax.broadcasted_iota(jnp.int32, (8, 128), 0)
    for r in range(4):
        for n in range(PLANE):
            start = (r * PLANE + n) * D
            piece = jnp.concatenate([gain_grad_ref[:, start:start + D], jnp.zeros((1, 128 - D), F32)], axis=1)
            small_ref[r, n] = jnp.where(row8 == 0, piece, jnp.where(row8 == 1, head_gains, 0.0))
    small_sends = []
    for j in range(1, 4):
        other = lax.rem(place.row + j, 4)
        small_sends.append(line.send(small_ref.at[other], small_row.at[place.row], s_send, j, s_recv, j, other))
    for copy in small_sends:
        copy.start()
    small_row[place.row] = small_ref[place.row]

    def take(out_ref, scatter):
        def one(i, _):
            rows = span(i * 32, 32)
            out_ref[rows, :] = scatter.total(rows)
            return 0

        lax.fori_loop(0, tok // 32, one, 0)

    first.arrive()
    take(outsum_ref, first)
    sums_out = [pltpu.make_async_copy(outsum_ref, outsum_hbm, sum_sem.at[0]),
                pltpu.make_async_copy(ysum_ref, ysum_hbm, sum_sem.at[1])]
    sums_out[0].start()
    tell(2, place.same[1:3])
    first.close()
    pl.semaphore_wait(ready_sem.at[2], 2)
    second.first1.start()
    second.first2.start()
    second.combine(0)
    def fetch(n, qo, kv, sem):
        return [pltpu.make_async_copy(qo, part_ref.at[n, :, :, 128:columns], own_sem.at[sem]),
                pltpu.make_async_copy(kv, part_ref.at[n, :, :, 0:128], own_sem.at[sem + 1])]

    own_term = fetch(0, grad_hbm.at[place.row], kv_own.at[place.row], 4)
    for copy in own_term:
        copy.start()

    second.finish_two()
    for copy in small_sends:
        copy.wait_recv()
    small_mid[...] = (small_row[0] + small_row[1]) + (small_row[2] + small_row[3])
    plane_sends = []
    for j in range(1, PLANE):
        other = lax.rem(place.me + j, PLANE)
        plane_sends.append(place.send(small_mid.at[other], small_last.at[place.me], t_send, t_recv, j, other))
    for copy in plane_sends:
        copy.start()
    small_last[place.me] = small_mid[place.me]
    for copy in plane_sends:
        copy.wait_recv()
    total = small_last[0]
    for n in range(1, PLANE):
        total = total + small_last[n]
    small_out[...] = total
    for copy in own_term:
        copy.wait()
    keeps = []

    def hand_over(index, lanes, total, arrived):
        total.finish()

        def fold(slots):
            loads = [pltpu.make_async_copy(arrived.at[slot], part_ref.at[slot + 1, :, :, lanes], own_sem.at[6 + 2 * slot + index])
                     for slot in slots]
            for copy in loads:
                copy.start()
            for copy in loads:
                copy.wait()

            def add(n, _):
                b, rows = n // 4, span(lax.rem(n, 4) * 64, 64)
                term = part_ref[0, b, rows, lanes]
                for slot in slots:
                    term = term + part_ref[slot + 1, b, rows, lanes]
                part_ref[0, b, rows, lanes] = term
                return 0

            lax.fori_loop(0, 8, add, 0)

        @pl.when(line.middle)
        def _():
            fold((0, 1, 2))

        @pl.when(jnp.logical_not(line.middle))
        def _():
            fold((0, 2))

        def piece(n):
            return part_ref.at[0, n // 4, span(lax.rem(n, 4) * 64, 64), lanes]

        keeps.append(pltpu.make_async_copy(piece(place.me), pieces_ref.at[place.me, :, lanes], own_sem.at[index]))
        keeps[-1].start()
        for j in range(1, PLANE):
            other = lax.rem(place.me + j, PLANE)
            copy = place.send(piece(other), pieces_ref.at[place.me, :, lanes], p_send.at[index], p_recv.at[index], j, other)
            copy.start()
            plane_sends.append(copy)

    hand_over(1, slice(128, columns), attn, qo_recv)
    hand_over(0, slice(0, 128), kv_sum, kv_recv)
    second.arrive()
    take(ysum_ref, second)
    sums_out[1].start()
    for one in ffn:
        one.finish()
        one.close()
    for copy in plane_sends[PLANE - 1:]:
        copy.wait_recv()
    for copy in keeps:
        copy.wait()
    unscaled, out_t = attention_sums(heads, lambda s: pieces_ref[s].astype(F32), True)
    grad_gain_ref[...] = jnp.broadcast_to(jnp.sum(unscaled * qkv_ref[...].astype(F32), axis=1, keepdims=True), grad_gain_ref.shape)
    grad_qkv_ref[...] = unscaled * column(gain_ref)
    grad_out_ref[...] = jnp.transpose(out_t)
    for copy in sums_out:
        copy.wait()
    for copy in plane_sends + small_sends + [pair]:
        copy.wait_send()
    attn.close()
    kv_sum.close()
    second.close()


def backward_phase(heads, branch, out_part, x_all, kv, qo, weight_grads, table, gq, gk, gain_grad, w_qkv, gain_attn, kept):
    blocks, tok, model = x_all.shape
    length = blocks * tok
    depth = w_qkv.shape[0]
    dma = pltpu.SemaphoreType.DMA
    raw, merged, *rest = kept
    return pl.pallas_call(
        functools.partial(backward_kernel, heads),
        out_shape=(
            jax.ShapeDtypeStruct((tok, model), F32),
            jax.ShapeDtypeStruct((tok, model), F32),
            jax.ShapeDtypeStruct(w_qkv.shape, F32),
            jax.ShapeDtypeStruct((QUERY_HEADS * D, depth), F32),
            jax.ShapeDtypeStruct((depth, 128), F32),
            jax.ShapeDtypeStruct((8, 128), F32),
            jax.ShapeDtypeStruct((4, 2, 256, 384), BF16),
            *(jax.ShapeDtypeStruct((3,) + grad.shape[1:], BF16) for grad in weight_grads),
            jax.ShapeDtypeStruct((3, 2, 256, 384), BF16),
            jax.ShapeDtypeStruct((3, 2, 256, 128), BF16),
        ),
        in_specs=[ANY_SPEC] * 8 + [VMEM_SPEC] * 6 + [ANY_SPEC] * (1 + len(rest)),
        out_specs=(ANY_SPEC,) * 2 + (VMEM_SPEC,) * 4 + (ANY_SPEC,) * 5,
        scratch_shapes=[
            *(pltpu.VMEM(array.shape, array.dtype) for array in (raw, *rest)),
            dma((7,)),
            pltpu.VMEM((4, 2, tok, model), BF16),
            pltpu.VMEM((model, heads.columns), BF16),
            pltpu.VMEM((blocks, tok, 512), BF16),
            pltpu.VMEM(merged.shape, BF16),
            pltpu.VMEM((2, blocks, tok, 256), BF16),
            pltpu.VMEM((2, 256, 384), BF16),
            pltpu.VMEM((model // 256, 256, 256), BF16),
            *backward_scratch(heads, length),
            *scatter_scratch(tok, model),
            dma((SCATTER_SLOTS,)), dma((SCATTER_SLOTS,)),
            dma((GATHER_SLOTS,)), dma((GATHER_SLOTS,)), dma((4,)), dma((2,)), dma((2,)),
            pltpu.SemaphoreType.REGULAR((3,)),
            pltpu.VMEM((2,) + weight_grads[0].shape[1:], BF16),
            pltpu.VMEM(weight_grads[0].shape[1:], BF16),
            dma((4, ROW_SLOTS)), dma((4, ROW_SLOTS)), dma((12,)),
            pltpu.VMEM((4, PLANE, 8, 128), F32),
            pltpu.VMEM((4, PLANE, 8, 128), F32),
            pltpu.VMEM((PLANE, 8, 128), F32),
            pltpu.VMEM((PLANE, 8, 128), F32),
            pltpu.VMEM((PLANE, depth, 512), BF16),
            pltpu.VMEM((2, 256, 384), BF16),
            pltpu.VMEM((2, 256, 384), BF16),
            pltpu.VMEM((4, 2, 256, 128), BF16),
            pltpu.VMEM((model, 128), BF16),
            pltpu.VMEM((2, 256, 128), BF16),
            pltpu.VMEM((tok, model), F32),
            pltpu.VMEM((tok, model), F32),
            dma((2,)), dma((3,)), dma((1,)), dma((1,)),
            dma((4,)), dma((4,)), dma((PLANE,)), dma((PLANE,)), dma((2, PLANE)), dma((2, PLANE)),
        ],
        compiler_params=pltpu.CompilerParams(collective_id=3, has_side_effects=True, vmem_limit_bytes=63 * 1024 * 1024),
        cost_estimate=pl.CostEstimate(flops=60 << 30, bytes_accessed=64 << 20, transcendentals=0),
    )(branch, out_part, x_all, kv, qo, *weight_grads, merged, table, gq, gk, gain_grad, w_qkv, gain_attn, raw, *rest)


def norm_back(grad_normed, values_in, inv_rms, gain):
    scaled = grad_normed * gain
    gain_grad = jnp.sum(grad_normed * values_in * inv_rms, axis=0)
    input_grad = inv_rms * scaled - values_in * inv_rms**3 * jnp.mean(scaled * values_in, axis=-1, keepdims=True)
    return input_grad, gain_grad


def start_wide(x, table, pieces, gain):
    return (
        lax.all_gather(x, "seq", axis=0, tiled=False),
        lax.all_gather(table, "seq", axis=0, tiled=False),
        lax.all_gather(lax.all_to_all(pieces, "seq", 0, 0, tiled=False), "rows", axis=0, tiled=False),
        lax.all_gather(lax.all_gather(gain, "seq", axis=0, tiled=False), "rows", axis=0, tiled=False),
    )


def scatter_rows(part, tok):
    return lax.psum_scatter(part.reshape(-1, part.shape[-1]), "seq", scatter_dimension=0, tiled=True).astype(F32)


def attention_wide(heads, x_all, g, w, table, gq, gk):
    blocks, tok, model = x_all.shape
    proj = dot(x_all.reshape(blocks * tok, model), w[:, :heads.qkv])
    kept = pl.pallas_call(
        functools.partial(local_forward_kernel, heads),
        out_shape=kept_shapes(heads, blocks * tok, 0),
        compiler_params=pltpu.CompilerParams(vmem_limit_bytes=VMEM_LIMIT),
    )(proj, table, gq, gk)
    total = scatter_rows(dot_nt(kept[1], w[:, heads.qkv:]).astype(BF16), tok)
    own = lax.dynamic_index_in_dim(x_all, lax.axis_index("seq"), 0, keepdims=False)
    return (own.astype(F32) + total, lax.all_gather(g, "seq", axis=0, tiled=False)) + tuple(kept)


def feed_forward_wide(res, gain, g_blocks, gate_slab, up_slab, down_slab):
    blocks, tok, model = g_blocks.shape
    inv = norm_inverse(res)
    two_all = lax.all_gather((res * inv * gain).astype(BF16), "seq", axis=0, tiled=True)
    g_all = g_blocks.reshape(blocks * tok, model)
    gate_act = dot(two_all, gate_slab)
    up_act = dot(two_all, up_slab)
    s = jax.nn.sigmoid(gate_act)
    hidden = (gate_act * s * up_act).astype(BF16)
    hidden_grad = dot_nt(g_all, down_slab)
    gate_grad = (hidden_grad * up_act * s * (1.0 + gate_act * (1.0 - s))).astype(BF16)
    up_grad = (hidden_grad * gate_act * s).astype(BF16)
    two_grad = scatter_rows((dot_nt(gate_grad, gate_slab) + dot_nt(up_grad, up_slab)).astype(BF16), tok)
    branch_part = dot(hidden, down_slab).astype(BF16).reshape(blocks, tok, model)
    norm_grad, gain_grad = norm_back(two_grad, res, inv, gain)
    g = lax.dynamic_index_in_dim(g_blocks, lax.axis_index("seq"), 0, keepdims=False)
    residual_grad = g.astype(F32) + norm_grad
    return (branch_part, residual_grad, residual_grad.astype(BF16), gain_grad[None],
            dot_tn(two_all, gate_grad).astype(BF16), dot_tn(two_all, up_grad).astype(BF16),
            dot_tn(hidden, g_all).astype(BF16))


def backward_wide(heads, branch, out_part, x_all, w, table, gq, gk, kept):
    blocks, tok, model = x_all.shape
    length = blocks * tok
    raw, merged, *rest = kept
    out_sum = scatter_rows(out_part, tok)
    branch_all = lax.all_gather(branch, "seq", axis=0, tiled=True)
    pg, gains = pl.pallas_call(
        functools.partial(local_backward_kernel, heads),
        out_shape=(jax.ShapeDtypeStruct((length, heads.qkv), BF16), jax.ShapeDtypeStruct((2 * D, 128), F32)),
        scratch_shapes=backward_scratch(heads, length),
        compiler_params=pltpu.CompilerParams(vmem_limit_bytes=VMEM_LIMIT),
    )(dot(branch_all, w[:, heads.qkv:]), table, gq, gk, raw, *rest)
    y_sum = scatter_rows(dot_nt(pg, w[:, :heads.qkv]).astype(BF16), tok)
    grad = jnp.concatenate([dot_tn(x_all.reshape(length, model), pg), dot_tn(branch_all, merged)], axis=1)
    return y_sum, out_sum, grad.astype(BF16), gains


def rotary_table(x, positions, segments):
    inverse = jnp.exp(-math.log(THETA) * jnp.arange(HALF, dtype=F32) * 2.0 / D)
    angles = inverse[:, None] * positions.astype(F32)[None, :]
    hot = jnp.arange(SEGMENT_KINDS, dtype=jnp.int32)[:, None] == segments[None, :]
    root = jnp.pad(norm_inverse(x).T, ((0, 7), (0, 0)))
    return jnp.concatenate([jnp.cos(angles), jnp.sin(angles), hot.astype(F32), root], axis=0)


def attention_pieces(heads, w_qkv, w_out, split):
    depth = w_qkv.shape[0]
    qw, kw = QUERY_HEADS * D, KEY_VALUE_HEADS * D
    out_t = w_out.T

    def columns(array, start, first, count, most):
        parts = []
        for i in range(count):
            n = first + i
            parts.append(array[:, start + n * D:start + (n + 1) * D] if n < most else jnp.zeros((depth, D), BF16))
        return parts

    pairs, others = [], []
    for s in range(heads.seq):
        q, k = s * heads.queries, heads.first(s)
        parts = []
        for n in ([k + s % 2] if split else range(k, k + heads.pairs)):
            parts += columns(w_qkv, qw, n, 1, KEY_VALUE_HEADS) + columns(w_qkv, qw + kw, n, 1, KEY_VALUE_HEADS)
        pairs.append(jnp.concatenate(parts, axis=1))
        others.append(jnp.concatenate(columns(w_qkv, 0, q, heads.queries, QUERY_HEADS)
                                      + columns(out_t, 0, q, heads.queries, QUERY_HEADS), axis=1))
    pairs, others = jnp.stack(pairs), jnp.stack(others)
    return (pairs, others) if split else jnp.concatenate([pairs, others], axis=2)


def attention_sums(heads, piece, split):
    pieces = [piece(s) for s in range(heads.seq)]
    held = 1 if split else heads.pairs
    first = [heads.first(s) + (s % 2 if split else 0) for s in range(heads.seq)]
    lead = 2 * held * D
    cut = lambda s, start, n: pieces[s][:, start + n * D:start + (n + 1) * D]
    queries = [cut(n // heads.queries, lead, n % heads.queries) for n in range(QUERY_HEADS)]
    outs = [cut(n // heads.queries, lead + heads.wide, n % heads.queries) for n in range(QUERY_HEADS)]

    def pairs(value):
        found = []
        for n in range(KEY_VALUE_HEADS):
            terms = [cut(s, value * D, 2 * (n - first[s])) for s in range(heads.seq)
                     if s * heads.queries < QUERY_HEADS and 0 <= n - first[s] < held]
            found.append(functools.reduce(jnp.add, terms))
        return found

    qkv = jnp.concatenate(queries + pairs(0) + pairs(1), axis=1)
    return qkv, jnp.concatenate(outs, axis=1)


def body(tokens, segments, positions, cotangent, gain_attn, w_qkv, gain_q, gain_k, w_out, gain_ffn, w_gate, w_up, w_down):
    seq = lax.axis_size("seq")
    rows = lax.axis_size("rows")
    heads = Heads(seq)
    depth = w_qkv.shape[0]
    tok, model = tokens.shape[1:]
    plane = seq == PLANE and rows == 4
    row = lax.axis_index("rows")

    gq, gk = gain_q[None], gain_k[None]
    x = tokens[0].astype(F32)
    scaled = (w_qkv.astype(F32) * gain_attn.astype(F32)[:, None]).astype(BF16)
    pieces = attention_pieces(heads, scaled, w_out, plane)
    table = rotary_table(x, positions[0], segments[0])
    if plane:
        x_all, table, kv, qo, gains = start_phase(rows, tokens[0], table, *pieces, gain_ffn[None])
        kv, qo = kv.reshape(2, model, -1), qo.reshape(model, -1)
    else:
        gain = jnp.pad(gain_ffn.astype(F32)[None], ((0, 7), (0, 128 - depth)))
        x_all, table, w, gains = start_wide(tokens[0], table, pieces, gain)
        w = w.reshape(model, heads.columns)
        gain_two = gains[:, :, 0, :depth].reshape(1, model)
    inv = norm_inverse(x)

    if plane:
        residual, two, g_all, gate, up, *kept = attention_phase(
            heads, x_all, cotangent[0], kv, qo, (w_gate, w_up), table, gq, gk, gains)
        out_part, residual_grad, branch, gain_two_grad, *weight_grads, gate_own, up_own, down_own, down_recv = feed_forward(
            residual, gains, two, cotangent[0], g_all, (w_gate, gate, w_up, up, w_down))
        weight_grads = [grad.reshape((4,) + w_gate.shape) for grad in weight_grads]
        y_sum, out_sum, grad_qkv, grad_out, grad_gain_attn, small, _, gate_recv, up_recv, *_ = backward_phase(
            heads, branch, out_part, x_all, kv, qo, weight_grads, table, gq, gk, gain_two_grad, w_qkv,
            gain_attn[None], kept)
        grad_gain_attn = grad_gain_attn[:, 0]
        middle = (row + 1) // 2 == 1

        def row_total(own, recv):
            return own.astype(F32) + recv[0].astype(F32) + recv[2].astype(F32) + jnp.where(middle, recv[1].astype(F32), 0.0)

        grad_gate, grad_up, grad_down = (
            row_total(own, recv) for own, recv in ((gate_own, gate_recv), (up_own, up_recv), (down_own, down_recv)))
        grad_gain_ffn, head_gains = small[0, :depth], small[1]
    else:
        gate_slab = lax.all_gather(w_gate, "rows", axis=0, tiled=True)
        up_slab = lax.all_gather(w_up, "rows", axis=0, tiled=True)
        down_slab = lax.all_gather(w_down, "rows", axis=1, tiled=True)
        residual, g_all, *kept = attention_wide(heads, x_all, cotangent[0], w, table, gq, gk)
        out_part, residual_grad, branch, gain_two_grad, gate_wgrad, up_wgrad, down_wgrad = feed_forward_wide(
            residual, gain_two, g_all, gate_slab, up_slab, down_slab)
        grad_gate = lax.psum_scatter(gate_wgrad, "rows", scatter_dimension=0, tiled=True).astype(F32)
        grad_up = lax.psum_scatter(up_wgrad, "rows", scatter_dimension=0, tiled=True).astype(F32)
        grad_down = lax.psum_scatter(down_wgrad, "rows", scatter_dimension=1, tiled=True).astype(F32)
        y_sum, out_sum, attn_grad, head_gains = backward_wide(heads, branch, out_part, x_all, w, table, gq, gk, kept)
        attn_grad = lax.psum_scatter(attn_grad, "rows", scatter_dimension=0, tiled=True)
        attn_grad = lax.all_to_all(attn_grad.reshape(seq, depth, heads.columns), "seq", 0, 0, tiled=False)
        small = lax.psum(jnp.concatenate([gain_two_grad[0], head_gains[:, 0]]), ("rows", "seq"))
        grad_gain_ffn = lax.dynamic_slice_in_dim(small, (row * seq + lax.axis_index("seq")) * depth, depth)
        head_gains = small[model:]
        attn_grad = attn_grad.astype(F32)
        unscaled, grad_out = attention_sums(heads, lambda s: attn_grad[s], False)
        grad_out = grad_out.T
        grad_gain_attn = jnp.sum(unscaled * w_qkv.astype(F32), axis=1)
        grad_qkv = unscaled * gain_attn.astype(F32)[:, None]

    layer_out = (residual + out_sum).astype(BF16)
    grad_tokens = residual_grad + y_sum - x * (inv * inv * jnp.mean(y_sum * x, axis=-1, keepdims=True))
    return (
        layer_out[None],
        grad_tokens[None],
        grad_gain_attn,
        grad_qkv,
        head_gains[:D],
        head_gains[D:],
        grad_out,
        grad_gain_ffn,
        grad_gate,
        grad_up,
        grad_down,
    )


def solution(mesh):
    both = ("rows", "seq")
    return jax.shard_map(
        body,
        mesh=mesh,
        in_specs=(
            P("rows", "seq", None), P("rows", "seq"), P("rows", "seq"), P("rows", "seq", None),
            P(both), P(both, None), P(), P(), P(None, both), P(both),
            P("rows", "seq"), P("rows", "seq"), P("seq", "rows"),
        ),
        out_specs=(
            P("rows", "seq", None), P("rows", "seq", None), P(both), P(both, None), P(), P(),
            P(None, both), P(both), P("rows", "seq"), P("rows", "seq"), P("seq", "rows"),
        ),
        check_vma=False,
    )
```

```python
import functools
import math

import jax
import jax.numpy as jnp
from jax import lax
from jax.experimental import pallas as pl
from jax.experimental.pallas import tpu as pltpu
from jax.sharding import PartitionSpec as P

QUERY_HEADS = 24
KEY_VALUE_HEADS = 6
GROUP = QUERY_HEADS // KEY_VALUE_HEADS
D = 64
HALF = D // 2
EPSILON = 1e-06
THETA = 10000.0
PENALTY = -10000.0
SEGMENT_KINDS = 8
TABLE_ROWS = 80
BLOCK = 512
PLANE = 8
F32 = jnp.float32
BF16 = jnp.bfloat16
VMEM_LIMIT = 60 * 1024 * 1024
MESH = pl.DeviceIdType.MESH
ANY_SPEC = pl.BlockSpec(memory_space=pl.ANY)
VMEM_SPEC = pl.BlockSpec(memory_space=pltpu.VMEM)


def dot(a, b):
    return jnp.dot(a, b, preferred_element_type=F32)


def dot_nt(a, b):
    return lax.dot_general(a, b, (((1,), (1,)), ((), ())), preferred_element_type=F32)


def dot_tn(a, b):
    return lax.dot_general(a, b, (((0,), (0,)), ((), ())), preferred_element_type=F32)


def norm_inverse(x):
    return lax.rsqrt(jnp.mean(x * x, axis=-1, keepdims=True) + EPSILON)


def split3(x):
    high = x.astype(BF16).astype(F32)
    mid = (x - high).astype(BF16).astype(F32)
    return high, mid, x - high - mid


def column(ref):
    row = ref[...].astype(F32)
    return jnp.transpose(jnp.broadcast_to(row, (128, row.shape[1])))[:, 0:1]


def gain_row(ref):
    return jnp.concatenate([ref[r, n, 0:1, 0:D] for r in range(ref.shape[0]) for n in range(ref.shape[1])], axis=1)


def span(start, size):
    return pl.ds(pl.multiple_of(start, size), size)


class Heads:
    def __init__(self, seq):
        self.seq = seq
        self.queries = -(-QUERY_HEADS // seq)
        last = [min((s + 1) * self.queries, QUERY_HEADS) - 1 for s in range(seq)]
        self.pairs = max(last[s] // GROUP - self.first(s) + 1 for s in range(seq) if last[s] >= s * self.queries)
        self.wide = self.queries * D
        self.narrow = self.pairs * D
        self.qkv = self.wide + 2 * self.narrow
        self.columns = self.qkv + self.wide

    def first(self, s):
        return (s // 2 * 2 * self.queries) // GROUP

    def slot(self, s, h):
        return (s * self.queries + h) // GROUP - self.first(s)


class Place:
    def __init__(self):
        self.row = lax.axis_index("rows")
        self.me = lax.axis_index("seq")
        self.core = lax.rem(self.me, 2)
        self.chip = self.me // 2
        self.sib = self.me + 1 - 2 * self.core
        chip = self.chip
        self.chips = (chip, chip + 1 - 2 * lax.rem(chip, 2), lax.rem(chip + 2, 4), 3 - chip)
        self.same = tuple(2 * q + self.core for q in self.chips)

    def greet(self, rows=1):
        barrier = pltpu.get_barrier_semaphore()
        for other in (self.sib, self.same[1], self.same[2]):
            pl.semaphore_signal(barrier, inc=1, device_id=(self.row, other), device_id_type=MESH)
        for j in range(1, rows):
            other = lax.rem(self.row + j, rows)
            pl.semaphore_signal(barrier, inc=1, device_id=(other, self.me), device_id_type=MESH)
        pl.semaphore_wait(barrier, 3 + rows - 1)

    def greet_all(self, rows):
        barrier = pltpu.get_barrier_semaphore()
        for j in range(1, PLANE):
            other = lax.rem(self.me + j, PLANE)
            pl.semaphore_signal(barrier, inc=1, device_id=(self.row, other), device_id_type=MESH)
        for j in range(1, rows):
            other = lax.rem(self.row + j, rows)
            pl.semaphore_signal(barrier, inc=1, device_id=(other, self.me), device_id_type=MESH)
        pl.semaphore_wait(barrier, PLANE - 1 + rows - 1)

    def send(self, src, dst, send_sem, recv_sem, slot, target):
        return pltpu.make_async_remote_copy(
            src_ref=src, dst_ref=dst, send_sem=send_sem.at[slot], recv_sem=recv_sem.at[slot],
            device_id=(self.row, target), device_id_type=MESH)


class Line:
    def __init__(self, place):
        self.place = place
        row = place.row
        self.a = row + 1 - 2 * lax.rem(row, 2)
        self.b = 3 - row
        self.c = lax.rem(row + 2, 4)
        self.middle = (row + 1) // 2 == 1

    def send(self, src, dst, send_sem, send_slot, recv_sem, recv_slot, target):
        return pltpu.make_async_remote_copy(
            src_ref=src, dst_ref=dst, send_sem=send_sem.at[send_slot], recv_sem=recv_sem.at[recv_slot],
            device_id=(target, self.place.me), device_id_type=MESH)


ROW_SLOTS = 4


class RowGather:
    def __init__(self, line, own, at, send_sem, recv_sem):
        self.line = line
        mine, passed = at(line.place.row), at(line.c)
        self.to_a = line.send(own, mine, send_sem, 0, recv_sem, 0, line.a)
        self.to_c = line.send(own, mine, send_sem, 1, recv_sem, 1, line.c)
        self.to_b = line.send(own, mine, send_sem, 2, recv_sem, 2, line.b)
        self.on = line.send(passed, passed, send_sem, 3, recv_sem, 2, line.a)

    def start(self):
        self.to_c.start()
        self.to_a.start()

        @pl.when(self.line.middle)
        def _():
            self.to_b.start()

    def forward(self):
        self.to_c.wait_recv()

        @pl.when(self.line.middle)
        def _():
            self.on.start()

    def finish(self):
        self.to_a.wait_recv()
        self.to_b.wait_recv()

    def close(self):
        self.to_a.wait_send()
        self.to_c.wait_send()

        @pl.when(self.line.middle)
        def _():
            self.to_b.wait_send()
            self.on.wait_send()


class RowScatter:
    def __init__(self, line, part, recv, merge, total, send_sem, recv_sem):
        self.line, self.total = line, total
        self.to_a = line.send(part.at[line.a], recv.at[0], send_sem, 0, recv_sem, 0, line.a)
        self.to_b = line.send(part.at[line.b], recv.at[1], send_sem, 1, recv_sem, 1, line.b)
        self.to_c = line.send(part.at[line.c], recv.at[2], send_sem, 2, recv_sem, 2, line.c)
        self.added = line.send(total, recv.at[2], send_sem, 2, recv_sem, 2, line.c)
        self.over = line.send(part.at[line.b], merge, send_sem, 3, recv_sem, 3, line.a)

    def start_first(self):
        @pl.when(jnp.logical_not(self.line.middle))
        def _():
            self.over.start()

        @pl.when(self.line.middle)
        def _():
            self.to_b.start()
            self.to_a.start()

    def start_far(self):
        @pl.when(jnp.logical_not(self.line.middle))
        def _():
            self.to_c.start()

    def start_near(self):
        @pl.when(jnp.logical_not(self.line.middle))
        def _():
            self.to_a.start()

    def add(self, work):
        @pl.when(self.line.middle)
        def _():
            self.over.wait_recv()
            work()
            self.added.start()

    def finish(self):
        self.to_a.wait_recv()
        self.to_c.wait_recv()

        @pl.when(self.line.middle)
        def _():
            self.to_b.wait_recv()

    def close(self):
        self.to_a.wait_send()
        self.to_c.wait_send()

        @pl.when(self.line.middle)
        def _():
            self.to_b.wait_send()

        @pl.when(jnp.logical_not(self.line.middle))
        def _():
            self.over.wait_send()


GATHER_SLOTS = 10


class Gather:
    def __init__(self, place, own, every, send_sem, recv_sem):
        half = every.shape[1] // 2
        low, high, whole = slice(0, half), slice(half, 2 * half), slice(0, 2 * half)

        def send(part, b, slot, target, src=None):
            src = every.at[b, part] if src is None else src.at[part]
            return place.send(src, every.at[b, part], send_sem, recv_sem, slot, target)

        me, (_, s1, s2, s3), sib = place.me, place.same, place.sib
        self.copies = (
            send(whole, me, 0, sib, own),
            send(low, me, 1, s1, own), send(high, me, 2, s1, own),
            send(high, me, 3, s2, own), send(low, me, 4, s2, own),
            send(low, s1, 5, s2), send(high, s2, 6, s1),
            send(whole, s1, 7, sib), send(whole, s2, 8, sib), send(whole, s3, 9, sib),
        )

    def start(self):
        for slot in (1, 3, 2, 4, 0):
            self.copies[slot].start()

    def own_chip(self):
        self.copies[0].wait_recv()

    def neighbours(self):
        c = self.copies
        c[1].wait_recv()
        c[5].start()
        c[3].wait_recv()
        c[6].start()
        c[2].wait_recv()
        c[7].start()
        c[4].wait_recv()
        c[8].start()

    def chip1(self):
        self.copies[7].wait_recv()

    def chip2(self):
        self.copies[8].wait_recv()

    def diagonal(self):
        c = self.copies
        c[5].wait_recv()
        c[6].wait_recv()
        c[9].start()

    def chip3(self):
        self.copies[9].wait_recv()

    def close(self):
        for copy in self.copies:
            copy.wait_send()


SCATTER_SLOTS = 10


class Scatter:
    def __init__(self, place, part, sibling, passing, final, send_sem, recv_sem):
        self.place, self.part, self.sibling, self.passing, self.final = place, part, sibling, passing, final
        half = part.shape[2] // 2
        self.half = half
        core, other = place.core, 1 - place.core
        _, s1, s2, _ = place.same
        send = lambda src, dst, slot, target: place.send(src, dst, send_sem, recv_sem, slot, target)
        low, high = slice(0, half), slice(half, 2 * half)
        self.exchange = tuple(send(part.at[k, other], sibling.at[k], k, place.sib) for k in range(4))
        self.pass1 = send(part.at[3, core, low], passing.at[0], 4, s1)
        self.pass2 = send(part.at[3, core, high], passing.at[1], 5, s2)
        self.first1 = send(part.at[1, core, low], final.at[0, low], 6, s1)
        self.second1 = send(part.at[1, core, high], final.at[0, high], 7, s1)
        self.first2 = send(part.at[2, core, high], final.at[1, high], 8, s2)
        self.second2 = send(part.at[2, core, low], final.at[1, low], 9, s2)

    def add(self, k, start, size, term, offset):
        core, step = self.place.core, 64

        def one(i, _):
            rows = pl.ds(pl.multiple_of(start + i * step, step), step)
            from_rows = pl.ds(pl.multiple_of(offset + i * step, step), step)
            self.part[k, core, rows, :] = self.part[k, core, rows, :] + term[from_rows, :]
            return 0

        lax.fori_loop(0, size // step, one, 0)

    def combine(self, k):
        self.exchange[k].wait_recv()
        self.add(k, 0, 2 * self.half, self.sibling.at[k], 0)

    def finish_two(self):
        self.pass1.wait_recv()
        self.add(2, 0, self.half, self.passing.at[0], 0)
        self.second2.start()
        self.pass2.wait_recv()
        self.add(1, self.half, self.half, self.passing.at[1], 0)
        self.second1.start()

    def arrive(self):
        for copy in (self.first1, self.second1, self.first2, self.second2):
            copy.wait_recv()

    def total(self, rows):
        return (self.part[0, self.place.core, rows, :].astype(F32) + self.final[0, rows, :].astype(F32)
                + self.final[1, rows, :].astype(F32))

    def close(self):
        for copy in self.exchange + (self.pass1, self.pass2, self.first1, self.second1, self.first2, self.second2):
            copy.wait_send()


def scatter_scratch(tok, width):
    return [
        pltpu.VMEM((4, 2, tok, width), BF16),
        pltpu.VMEM((4, tok, width), BF16),
        pltpu.VMEM((2, tok // 2, width), BF16),
        pltpu.VMEM((2, tok, width), BF16),
        pltpu.SemaphoreType.DMA((SCATTER_SLOTS,)),
        pltpu.SemaphoreType.DMA((SCATTER_SLOTS,)),
    ]


def start_kernel(x_ref, table_ref, kv_ref, qo_ref, gain_in, x_all, table_all, kv_all, qo_all, gain_all,
                 x_send, x_recv, t_send, t_recv, k_send, k_recv, p_send, p_recv, g_send, g_recv, z_send, z_recv,
                 w_send, w_recv, pair_send, pair_recv, local_sem, gain_ref):
    place = Place()
    gain = jnp.concatenate([gain_in[...].astype(F32), jnp.zeros((1, 128 - gain_in.shape[1]), F32)], axis=1)
    gain_ref[...] = jnp.broadcast_to(gain, gain_ref.shape)
    rows = qo_all.shape[0]
    me, row, core = place.me, place.row, place.core
    local = [pltpu.make_async_copy(src, dst, local_sem.at[i]) for i, (src, dst) in enumerate((
        (kv_ref.at[me], kv_all.at[core, row, me]), (qo_ref.at[me], qo_all.at[row, me]), (gain_ref, gain_all.at[row, me]),
        (x_ref, x_all.at[me]), (table_ref, table_all.at[me])))]
    for copy in local:
        copy.start()
    place.greet_all(rows)
    exchange, rest = [], []
    for j in range(1, PLANE):
        other = lax.rem(me + j, PLANE)
        exchange.append(place.send(kv_ref.at[other], kv_all.at[lax.rem(other, 2), row, me], k_send, k_recv, j, other))
        rest.append(place.send(qo_ref.at[other], qo_all.at[row, me], p_send, p_recv, j, other))
        rest.append(place.send(gain_ref, gain_all.at[row, me], g_send, g_recv, j, other))
    for copy in exchange + rest:
        copy.start()
    gathers = (Gather(place, x_ref, x_all, x_send, x_recv), Gather(place, table_ref, table_all, t_send, t_recv))
    gathers[1].start()
    gathers[0].start()
    for copy in local[:3]:
        copy.wait()
    line = Line(place)
    weights = [RowGather(line, at(row), at, w_send.at[i], w_recv.at[i])
               for i, at in enumerate((lambda r: kv_all.at[core, r], lambda r: qo_all.at[r]))]
    for copy in exchange:
        copy.wait_recv()
    weights[0].start()
    for copy in rest:
        copy.wait_recv()
    weights[1].start()
    along = []
    for j in range(1, rows):
        other = lax.rem(row + j, rows)
        along.append(line.send(gain_all.at[row], gain_all.at[row], z_send, j, z_recv, j, other))
    for copy in along:
        copy.start()
    for gather in gathers[::-1]:
        gather.own_chip()
    weights[0].forward()
    for gather in gathers[::-1]:
        gather.neighbours()
    weights[0].finish()
    pair = place.send(kv_all.at[core], kv_all.at[core], pair_send, pair_recv, 0, place.sib)
    pair.start()
    weights[1].forward()
    for name in ("chip1", "chip2", "diagonal", "chip3"):
        for gather in gathers[::-1]:
            getattr(gather, name)()
    for copy in local[3:]:
        copy.wait()
    for copy in along:
        copy.wait_recv()
    for copy in exchange + rest + along:
        copy.wait_send()
    for gather in gathers:
        gather.close()
    weights[1].finish()
    pair.wait_recv()
    pair.wait_send()
    for one in weights:
        one.close()


def start_phase(rows, x, table, kv, qo, gain):
    tok, model = x.shape
    dma = pltpu.SemaphoreType.DMA
    return pl.pallas_call(
        start_kernel,
        out_shape=(
            jax.ShapeDtypeStruct((PLANE, tok, model), BF16),
            jax.ShapeDtypeStruct((PLANE,) + table.shape, F32),
            jax.ShapeDtypeStruct((2, rows) + kv.shape, BF16),
            jax.ShapeDtypeStruct((rows,) + qo.shape, BF16),
            jax.ShapeDtypeStruct((rows, PLANE, 8, 128), F32),
        ),
        in_specs=[VMEM_SPEC] * 5,
        out_specs=(ANY_SPEC,) * 5,
        scratch_shapes=[dma((GATHER_SLOTS,))] * 4 + [dma((PLANE,))] * 6 + [dma((rows,))] * 2
        + [dma((2, ROW_SLOTS))] * 2 + [dma((1,))] * 2 + [dma((5,)), pltpu.VMEM((8, 128), F32)],
        compiler_params=pltpu.CompilerParams(collective_id=0, has_side_effects=True),
        cost_estimate=pl.CostEstimate(flops=0, bytes_accessed=160 << 20, transcendentals=0),
    )(x, table, kv, qo, gain)


def load_slab(kv_hbm, qo_hbm, w_ref, sem):
    parts = ((kv_hbm.at[0], 0, 128), (kv_hbm.at[1], 128, 256), (qo_hbm, 256, 640))
    return [pltpu.make_async_copy(src, w_ref.at[:, a:b], sem.at[i]) for i, (src, a, b) in enumerate(parts)]


class Forward:
    def __init__(self, heads, me, table, gq, gk, raw, merged, o, qa, ka, kt, vt, inv):
        self.heads, self.table, self.gq, self.gk = heads, table, column(gq), column(gk)
        self.raw, self.merged, self.o, self.qa, self.ka, self.kt, self.vt, self.inv = raw, merged, o, qa, ka, kt, vt, inv
        self.slots = [heads.slot(me, h) for h in range(heads.queries)]

    def prepare(self, b, projected):
        heads = self.heads
        tok = self.table.shape[2]
        lanes = span(b * tok, tok)
        cos = self.table[b, 0:HALF, :]
        sin = self.table[b, HALF:D, :]
        hot = self.table[b, D:D + 8, :]
        row = lax.broadcasted_iota(jnp.int32, (16, tok), 0)
        one_row = jnp.where(row == 0, 1.0, 0.0).astype(F32)
        penalty = jnp.concatenate([(1.0 - hot) * PENALTY, jnp.zeros((8, tok), F32)], axis=0).astype(BF16)
        lead = 2 * heads.narrow
        self.raw[0:heads.wide, lanes] = projected[lead:lead + heads.wide]

        def rotated(raw, gain):
            inv = lax.rsqrt(jnp.mean(raw * raw, axis=0, keepdims=True) + EPSILON)
            n = raw * inv * gain
            a, c = n[:HALF], n[HALF:]
            return inv, jnp.concatenate([a * cos - c * sin, c * cos + a * sin], axis=0)

        for h in range(heads.queries):
            inv, q = rotated(projected[lead + h * D:lead + (h + 1) * D], self.gq)
            self.inv[h:h + 1, lanes] = inv
            self.qa[h, :, lanes] = jnp.concatenate([(q * (D ** -0.5)).astype(BF16), penalty], axis=0)
        for g in range(heads.pairs):
            start = 2 * g * D
            self.raw[heads.wide + g * D:heads.wide + (g + 1) * D, lanes] = projected[start:start + D]
            inv, k = rotated(projected[start:start + D], self.gk)
            self.inv[heads.queries + g:heads.queries + g + 1, lanes] = inv
            self.kt[g, :, lanes] = k.astype(BF16)
            full = jnp.concatenate([k, hot, jnp.ones((8, tok), F32), jnp.zeros((48, tok), F32)], axis=0)
            self.ka[g, lanes, :] = jnp.transpose(full).astype(BF16)
            start += D
            self.vt[g, :, lanes] = jnp.concatenate([projected[start:start + D], one_row], axis=0).astype(BF16)

    def query_block(self, i):
        heads = self.heads
        cols = span(i * BLOCK, BLOCK)
        causal = (lax.broadcasted_iota(jnp.int32, (BLOCK, BLOCK), 0)
                  <= lax.broadcasted_iota(jnp.int32, (BLOCK, BLOCK), 1))

        def step(j, accs, diagonal):
            rows = span(j * BLOCK, BLOCK)
            new = []
            for h in range(heads.queries):
                slot = self.slots[h]
                p = jnp.exp(dot(self.ka[slot, rows, 0:80], self.qa[h, :, cols]))
                if diagonal:
                    p = jnp.where(causal, p, 0.0)
                new.append(accs[h] + dot(self.vt[slot, :, rows], p.astype(BF16)))
            return tuple(new)

        accs = tuple(jnp.zeros((80, BLOCK), F32) for _ in range(heads.queries))
        accs = lax.fori_loop(0, i, lambda j, c: step(j, c, False), accs)
        accs = step(i, accs, True)
        row = lax.broadcasted_iota(jnp.int32, (16, BLOCK), 0)
        lead = self.merged.shape[1] - heads.wide
        outs = [jnp.zeros((lead, BLOCK), F32)] if lead else []
        for h in range(heads.queries):
            total = accs[h][D:D + 1]
            o = accs[h][:D] * (1.0 / total)
            self.o[h, :, cols] = o
            outs.append(o)
            pieces = split3(-jnp.log(total))
            old = self.qa[h, 64:80, cols].astype(F32)
            extra = jnp.where(row == 8, pieces[0],
                              jnp.where(row == 9, pieces[1], jnp.where(row == 10, pieces[2], old)))
            self.qa[h, 64:80, cols] = extra.astype(BF16)
        merged = jnp.transpose(jnp.concatenate(outs, axis=0)).astype(BF16)
        self.merged[cols, :] = merged
        return merged


class Backward:
    def __init__(self, heads, me, table, gq, gk, raw, o, qa, ka, kt, vt, inv, doa, dopad, qpad, va, dq, acc):
        self.heads, self.table, self.gq, self.gk = heads, table, column(gq), column(gk)
        self.raw, self.o, self.qa, self.ka, self.kt, self.vt, self.inv = raw, o, qa, ka, kt, vt, inv
        self.doa, self.dopad, self.qpad, self.va, self.dq, self.acc = doa, dopad, qpad, va, dq, acc
        self.slots = [heads.slot(me, h) for h in range(heads.queries)]

    def prepare(self, b):
        heads = self.heads
        tok = self.table.shape[2]
        lanes = span(b * tok, tok)
        for h in range(heads.queries):
            q = jnp.concatenate([jnp.zeros((D, tok), F32), self.qa[h, 0:D, lanes].astype(F32)], axis=0)
            self.qpad[h, lanes, :] = jnp.transpose(q).astype(BF16)
            self.acc[h, lanes, :] = jnp.zeros((tok, 2 * D), F32)
        for g in range(heads.pairs):
            v = jnp.concatenate([self.vt[g, 0:D, lanes].astype(F32), jnp.ones((D, tok), F32)], axis=0)
            self.va[g, lanes, :] = jnp.transpose(v).astype(BF16)

    def gradient(self, b, dm):
        heads = self.heads
        tok = self.table.shape[2]
        lanes = span(b * tok, tok)
        row = lax.broadcasted_iota(jnp.int32, (16, tok), 0)
        dmt = jnp.transpose(dm.astype(BF16).astype(F32))
        for h in range(heads.queries):
            do = dmt[h * D:(h + 1) * D]
            delta = jnp.sum(do * self.o[h, :, lanes], axis=0, keepdims=True)
            pieces = split3(-delta)
            extra = jnp.where(row == 0, pieces[0],
                              jnp.where(row == 1, pieces[1], jnp.where(row == 2, pieces[2], 0.0)))
            self.doa[h, :, lanes] = jnp.concatenate([do, extra], axis=0).astype(BF16)
            both = jnp.concatenate([do, jnp.zeros((D, tok), F32)], axis=0)
            self.dopad[h, lanes, :] = jnp.transpose(both).astype(BF16)

    def query_block(self, i):
        heads = self.heads
        cols = span(i * BLOCK, BLOCK)
        causal = (lax.broadcasted_iota(jnp.int32, (BLOCK, BLOCK), 0)
                  <= lax.broadcasted_iota(jnp.int32, (BLOCK, BLOCK), 1))

        def step(j, accs, diagonal):
            rows = span(j * BLOCK, BLOCK)
            new = []
            for h in range(heads.queries):
                slot = self.slots[h]
                p = jnp.exp(dot(self.ka[slot, rows, 0:80], self.qa[h, :, cols]))
                if diagonal:
                    p = jnp.where(causal, p, 0.0)
                dp = dot(self.va[slot, rows, 0:80], self.doa[h, :, cols])
                ds = (p * dp).astype(BF16)
                self.acc[h, rows, :] += dot(p.astype(BF16), self.dopad[h, cols, :]) + dot(ds, self.qpad[h, cols, :])
                new.append(accs[h] + dot(self.kt[slot, :, rows], ds))
            return tuple(new)

        accs = tuple(jnp.zeros((D, BLOCK), F32) for _ in range(heads.queries))
        accs = lax.fori_loop(0, i, lambda j, c: step(j, c, False), accs)
        accs = step(i, accs, True)
        for h in range(heads.queries):
            self.dq[h, :, cols] = accs[h]

    def finish(self, b, sums):
        heads = self.heads
        tok = self.table.shape[2]
        lanes = span(b * tok, tok)
        cos = self.table[b, 0:HALF, :]
        sin = self.table[b, HALF:D, :]
        scale = self.table[b, 72:73, :]

        def back(grad, raw, inv, gain):
            a, c = grad[:HALF], grad[HALF:]
            n = jnp.concatenate([a * cos + c * sin, c * cos - a * sin], axis=0)
            v = n * gain
            out = inv * v - raw * (inv * inv * inv) * jnp.mean(v * raw, axis=0, keepdims=True)
            return out * scale, n * raw * inv

        sum_q, sum_k = sums
        pairs = [jnp.zeros((2 * D, tok), F32) for _ in range(heads.pairs)]
        out = []
        for h in range(heads.queries):
            raw = self.raw[h * D:(h + 1) * D, lanes]
            grad, part = back(self.dq[h, :, lanes] * (D ** -0.5), raw, self.inv[h:h + 1, lanes], self.gq)
            out.append(grad)
            sum_q = sum_q + part
            both = jnp.transpose(self.acc[h, lanes, :])
            for g in range(heads.pairs):
                pairs[g] = pairs[g] + jnp.where(self.slots[h] == g, both, 0.0)
        both_out = []
        for g in range(heads.pairs):
            start = heads.wide + g * D
            raw = self.raw[start:start + D, lanes]
            inv = self.inv[heads.queries + g:heads.queries + g + 1, lanes]
            grad, part = back(pairs[g][D:], raw, inv, self.gk)
            both_out += [grad, pairs[g][:D] * scale]
            sum_k = sum_k + part
        return jnp.concatenate(both_out + out, axis=0), (sum_q, sum_k)


def kept_shapes(heads, length, lead):
    return (
        jax.ShapeDtypeStruct((heads.wide + heads.narrow, length), F32),
        jax.ShapeDtypeStruct((length, lead + heads.wide), BF16),
        jax.ShapeDtypeStruct((heads.queries, D, length), F32),
        jax.ShapeDtypeStruct((heads.queries, 80, length), BF16),
        jax.ShapeDtypeStruct((heads.pairs, length, 128), BF16),
        jax.ShapeDtypeStruct((heads.pairs, D, length), BF16),
        jax.ShapeDtypeStruct((heads.pairs, 80, length), BF16),
        jax.ShapeDtypeStruct((8, length), F32),
    )


def backward_scratch(heads, length):
    return [
        pltpu.VMEM((heads.queries, 80, length), BF16),
        pltpu.VMEM((heads.queries, length, 2 * D), BF16),
        pltpu.VMEM((heads.queries, length, 2 * D), BF16),
        pltpu.VMEM((heads.pairs, length, 2 * D), BF16),
        pltpu.VMEM((heads.queries, D, length), F32),
        pltpu.VMEM((heads.queries, length, 2 * D), F32),
    ]


def local_forward_kernel(heads, proj_ref, table_ref, gq_ref, gk_ref, *kept):
    forward = Forward(heads, lax.axis_index("seq"), table_ref, gq_ref, gk_ref, *kept)
    blocks, _, tok = table_ref.shape

    def prepare(b, _):
        rows = span(b * tok, tok)
        forward.prepare(b, jnp.transpose(proj_ref[rows, :]) * table_ref[b, 72:73, :])
        return 0

    def query_block(i, _):
        forward.query_block(i)
        return 0

    lax.fori_loop(0, blocks, prepare, 0)
    lax.fori_loop(0, blocks * tok // BLOCK, query_block, 0)


def local_backward_kernel(heads, dm_ref, table_ref, gq_ref, gk_ref, raw_ref, o_ref, qa_ref, ka_ref, kt_ref, vt_ref, inv_ref,
                          pg_ref, gains_ref, *scratch):
    backward = Backward(heads, lax.axis_index("seq"), table_ref, gq_ref, gk_ref, raw_ref, o_ref, qa_ref, ka_ref, kt_ref,
                        vt_ref, inv_ref, *scratch)
    blocks, _, tok = table_ref.shape

    def prepare(b, _):
        backward.prepare(b)
        backward.gradient(b, dm_ref[span(b * tok, tok), :])
        return 0

    def query_block(i, _):
        backward.query_block(i)
        return 0

    def finish(b, sums):
        grad, sums = backward.finish(b, sums)
        pg_ref[span(b * tok, tok), :] = jnp.transpose(grad).astype(BF16)
        return sums

    lax.fori_loop(0, blocks, prepare, 0)
    lax.fori_loop(0, blocks * tok // BLOCK, query_block, 0)
    zero = jnp.zeros((D, tok), F32)
    sum_q, sum_k = lax.fori_loop(0, blocks, finish, (zero, zero))
    gains_ref[0:D, :] = jnp.broadcast_to(jnp.sum(sum_q, axis=1, keepdims=True), (D, 128))
    gains_ref[D:2 * D, :] = jnp.broadcast_to(jnp.sum(sum_k, axis=1, keepdims=True), (D, 128))


def attention_kernel(heads, x_hbm, g_hbm, kv_hbm, qo_hbm, gate_hbm, up_hbm, table_ref, gq_ref, gk_ref, gain_ref,
                     res_ref, two_ref, g_all, gate_all, up_all, raw_hbm, merged_hbm, o_hbm, qa_hbm, ka_hbm, kt_hbm, vt_hbm, inv_hbm,
                     raw_ref, merged_ref, o_ref, qa_ref, ka_ref, kt_ref, vt_ref, inv_ref, kept_sem, x_ref, w_ref, part_ref, sibling_ref, passing_ref, final_ref, rs_send, rs_recv,
                     ag_send, ag_recv, load_sem, slab_sem, z_send, z_recv):
    place = Place()
    blocks, tok, model = x_ref.shape
    slabs = ((gate_hbm, gate_all), (up_hbm, up_all))
    load_w = load_slab(kv_hbm, qo_hbm, w_ref, slab_sem)
    for copy in load_w:
        copy.start()
    loads = [pltpu.make_async_copy(x_hbm.at[b], x_ref.at[b], load_sem.at[b]) for b in range(blocks)]
    for copy in loads:
        copy.start()
    place.greet(4)
    gather = Gather(place, g_hbm, g_all, ag_send, ag_recv)
    scatter = Scatter(place, part_ref, sibling_ref, passing_ref, final_ref, rs_send, rs_recv)
    line = Line(place)
    weights = [RowGather(line, own, lambda r, every=every: every.at[r], z_send.at[i], z_recv.at[i])
               for i, (own, every) in enumerate(slabs)]
    weights[0].start()
    gather.start()
    forward = Forward(heads, place.me, table_ref, gq_ref, gk_ref, raw_ref, merged_ref, o_ref, qa_ref, ka_ref, kt_ref,
                      vt_ref, inv_ref)
    for copy in load_w + loads:
        copy.wait()

    def prepare(b, _):
        proj = dot(x_ref[b], w_ref[:, 0:512])
        forward.prepare(b, jnp.transpose(proj) * table_ref[b, 72:73, :])
        return 0

    lax.fori_loop(0, blocks, prepare, 0, unroll=2)
    tile = 512

    def compute(k):
        merged = forward.query_block(place.chips[k])

        def model_tile(n, _):
            cols = span(n * tile, tile)
            out = dot_nt(merged_ref[span(place.chips[k] * BLOCK, BLOCK), :], w_ref[cols, 384:640])
            part_ref[k, :, :, cols] = out.astype(BF16).reshape(2, tok, tile)
            return 0

        lax.fori_loop(0, model // tile, model_tile, 0, unroll=True)
        scatter.exchange[k].start()

    compute(3)
    gather.own_chip()
    gather.neighbours()
    weights[1].start()
    scatter.combine(3)
    scatter.pass1.start()
    scatter.pass2.start()
    compute(1)
    scatter.combine(1)
    scatter.first1.start()
    gather.chip1()
    gather.chip2()
    weights[0].forward()
    compute(2)
    scatter.combine(2)
    scatter.first2.start()
    gather.diagonal()
    compute(0)
    keep = [pltpu.make_async_copy(src, dst, kept_sem.at[i]) for i, (src, dst) in enumerate((
        (raw_ref, raw_hbm), (merged_ref, merged_hbm), (o_ref, o_hbm), (qa_ref, qa_hbm), (ka_ref, ka_hbm),
        (kt_ref, kt_hbm), (vt_ref, vt_hbm), (inv_ref, inv_hbm)))]
    for copy in keep:
        copy.start()
    scatter.combine(0)
    scatter.finish_two()
    weights[1].forward()
    gather.chip3()
    gain = gain_row(gain_ref)
    scatter.arrive()

    def finish(i, _):
        rows = span(i * 32, 32)
        res = x_ref[place.me, rows, :].astype(F32) + scatter.total(rows)
        res_ref[rows, :] = res
        two_ref[rows, :] = (res * norm_inverse(res) * gain).astype(BF16)
        return 0

    lax.fori_loop(0, tok // 32, finish, 0)
    for one in weights:
        one.finish()
        one.close()
    for copy in keep:
        copy.wait()
    gather.close()
    scatter.close()


def attention_phase(heads, x_all, g, kv, qo, slabs, table, gq, gk, gain):
    blocks, tok, model = x_all.shape
    dma = pltpu.SemaphoreType.DMA
    lead = 256 - heads.wide
    kept = kept_shapes(heads, blocks * tok, lead)
    return pl.pallas_call(
        functools.partial(attention_kernel, heads),
        out_shape=(jax.ShapeDtypeStruct((tok, model), F32), jax.ShapeDtypeStruct((tok, model), BF16),
                   jax.ShapeDtypeStruct((blocks, tok, model), BF16))
        + tuple(jax.ShapeDtypeStruct((4,) + slab.shape, BF16) for slab in slabs) + kept,
        in_specs=[ANY_SPEC] * 6 + [VMEM_SPEC] * 4,
        out_specs=(VMEM_SPEC, VMEM_SPEC) + (ANY_SPEC,) * (3 + len(kept)),
        scratch_shapes=[
            *(pltpu.VMEM(array.shape, array.dtype) for array in kept),
            dma((len(kept),)),
            pltpu.VMEM((blocks, tok, model), BF16),
            pltpu.VMEM((model, heads.columns), BF16),
            *scatter_scratch(tok, model),
            dma((GATHER_SLOTS,)), dma((GATHER_SLOTS,)), dma((blocks,)), dma((3,)),
            dma((2, ROW_SLOTS)), dma((2, ROW_SLOTS)),
        ],
        compiler_params=pltpu.CompilerParams(collective_id=1, has_side_effects=True, vmem_limit_bytes=VMEM_LIMIT),
        cost_estimate=pl.CostEstimate(flops=40 << 30, bytes_accessed=64 << 20, transcendentals=0),
    )(x_all, g, kv, qo, *slabs, table, gq, gk, gain)


def ffn_kernel(res_ref, gain_ref, two_hbm, g_own, g_hbm, gate_own, gate_hbm, up_own, up_hbm, down_hbm,
               out_hbm, rgrad_ref, branch_ref, gain_grad_ref, gate_grad_hbm, up_grad_hbm,
               gate_grad_own, up_grad_own, down_own, down_recv,
               two_ref, g_ref, weight_ref, down_ref, hid_ref, gu_ref, stage_ref, wstage_ref, dsum_ref, dgrad_ref, merge_ref,
               part_ref, sibling_ref, passing_ref, final_ref, rs_send, rs_recv,
               ag_send, ag_recv, load_sem, g_sem, stage_sem, wstage_sem, own_sem, za_send, za_recv, zr_send, zr_recv):
    place = Place()
    blocks, tok, model = g_ref.shape
    ff = weight_ref.shape[1] // 2
    share = model // 4
    tile = 256
    def down_at(r):
        return down_ref.at[:, span(r * share, share)]

    loads, g_loads = [], []
    for i, (own, every) in enumerate(((gate_own, gate_hbm), (up_own, up_hbm))):
        for j in range(4):
            r = lax.rem(place.row + j, 4)
            loads.append(pltpu.make_async_copy(
                every.at[r] if j else own, weight_ref.at[span(r * share, share), i * ff:(i + 1) * ff], load_sem.at[4 * i + j]))
    for j in range(blocks):
        b = lax.rem(place.me + j, blocks)
        g_loads.append(pltpu.make_async_copy(g_hbm.at[b] if j else g_own, g_ref.at[b], g_sem.at[j]))
    own_loads = [pltpu.make_async_copy(two_hbm, two_ref.at[place.me], load_sem.at[8]),
                 pltpu.make_async_copy(down_hbm, down_at(place.row), load_sem.at[9])]
    for copy in own_loads + loads + g_loads:
        copy.start()
    place.greet(4)
    line = Line(place)
    gather = Gather(place, two_hbm, two_ref, ag_send, ag_recv)
    scatter = Scatter(place, part_ref, sibling_ref, passing_ref, final_ref, rs_send, rs_recv)
    downs = RowGather(line, down_hbm, down_at, za_send, za_recv)
    down_sum = RowScatter(line, dgrad_ref, down_recv, merge_ref, merge_ref, zr_send, zr_recv)
    gather.start()
    downs.start()
    for copy in loads + own_loads:
        copy.wait()

    def forward(k):
        pair = pl.ds(2 * place.chips[k], 2)

        def hidden_tile(h, _):
            cols, cols2 = span(h * tile, tile), span(ff + h * tile, tile)
            x = two_ref[pair].reshape(2 * tok, model)
            gate = dot(x, weight_ref[:, cols])
            up = dot(x, weight_ref[:, cols2])
            s = 1.0 / (1.0 + jnp.exp(-gate))
            act = gate * s
            hid_ref[pair, :, cols] = (act * up).astype(BF16).reshape(2, tok, tile)
            gu_ref[pair, :, cols] = (up * s * (1.0 + gate * (1.0 - s))).astype(BF16).reshape(2, tok, tile)
            gu_ref[pair, :, cols2] = act.astype(BF16).reshape(2, tok, tile)
            return 0

        lax.fori_loop(0, ff // tile, hidden_tile, 0, unroll=True)

    def backward(k):
        pair = pl.ds(2 * place.chips[k], 2)

        def hidden_tile(h, _):
            cols, cols2 = span(h * tile, tile), span(ff + h * tile, tile)
            back = dot_nt(g_ref[pair].reshape(2 * tok, model), down_ref[cols, :])
            for where in (cols, cols2):
                factor = gu_ref[pair, :, where].reshape(2 * tok, tile).astype(F32)
                gu_ref[pair, :, where] = (back * factor).astype(BF16).reshape(2, tok, tile)
            return 0

        lax.fori_loop(0, ff // tile, hidden_tile, 0, unroll=True)

        def model_tile(n, _):
            cols = span(n * tile, tile)
            back = dot_nt(gu_ref[pair].reshape(2 * tok, 2 * ff), weight_ref[cols, :])
            part_ref[k, :, :, cols] = back.astype(BF16).reshape(2, tok, tile)
            return 0

        lax.fori_loop(0, model // tile, model_tile, 0, unroll=True)
        scatter.exchange[k].start()

    def stage_copy(n):
        slot = lax.rem(n, 2)
        return pltpu.make_async_copy(stage_ref.at[slot], out_hbm.at[n // 4, :, :, span(lax.rem(n, 4) * share, share)],
                                     stage_sem.at[slot])

    def out_tile(n, _):
        @pl.when(n >= 2)
        def _():
            stage_copy(n - 2).wait()

        k, r = n // 4, lax.rem(n, 4)
        chip = place.chip
        m = jnp.where(k == 0, chip, jnp.where(k == 1, place.chips[1], jnp.where(k == 2, place.chips[2], place.chips[3])))
        out = dot(hid_ref[pl.ds(2 * m, 2)].reshape(2 * tok, ff), down_ref[:, span(r * share, share)])
        stage_ref[lax.rem(n, 2)] = out.astype(BF16).reshape(2, tok, share)
        stage_copy(n).start()
        return 0

    def down_grad(k):
        pair = pl.ds(2 * place.chips[k], 2)

        def down_rows(n, _):
            rows, r = span(lax.rem(n, ff // tile) * tile, tile), n // (ff // tile)
            h = hid_ref[pair, :, rows].reshape(2 * tok, tile)
            g = g_ref[pair, :, span(r * share, share)].reshape(2 * tok, share)
            term = dot_tn(h, g)
            if k:
                term = dsum_ref[r, rows, :] + term
            if k < 3:
                dsum_ref[r, rows, :] = term
            else:
                dgrad_ref[r, rows, :] = term.astype(BF16)
            return 0

        lax.fori_loop(0, 4 * (ff // tile), down_rows, 0, unroll=4)

    def wstage_copies(i, slot):
        return (pltpu.make_async_copy(wstage_ref.at[slot, :, 0:ff], gate_grad_hbm.at[i], wstage_sem.at[slot, 0]),
                pltpu.make_async_copy(wstage_ref.at[slot, :, ff:2 * ff], up_grad_hbm.at[i], wstage_sem.at[slot, 1]))

    def own_copies(half, slot):
        rows = span(half * tile, tile)
        return (pltpu.make_async_copy(wstage_ref.at[slot, :, 0:ff], gate_grad_own.at[rows], own_sem.at[0]),
                pltpu.make_async_copy(wstage_ref.at[slot, :, ff:2 * ff], up_grad_own.at[rows], own_sem.at[1]))

    def gate_up_rows(i, _):
        cols = span(i * tile, tile)
        slot = lax.rem(i, 2)

        @pl.when(i >= 2)
        def _():
            for copy in wstage_copies(i - 2, slot):
                copy.wait()

        x = two_ref[:, :, cols].reshape(blocks * tok, tile)
        wstage_ref[slot] = dot_tn(x, gu_ref[...].reshape(blocks * tok, 2 * ff)).astype(BF16)
        for copy in wstage_copies(i, slot):
            copy.start()

        @pl.when(i // 2 == place.row)
        def _():
            for copy in own_copies(lax.rem(i, 2), slot):
                copy.start()

        out_tile(2 * i, 0)
        out_tile(2 * i + 1, 0)

        @pl.when(i // 2 == place.row)
        def _():
            for copy in own_copies(lax.rem(i, 2), slot):
                copy.wait()

        return 0

    def merge():
        def add(n, _):
            rows = span(n * 64, 64)
            merge_ref[rows, :] = (merge_ref[rows, :].astype(F32) + dgrad_ref[line.c, rows, :].astype(F32)).astype(BF16)
            return 0

        lax.fori_loop(0, ff // 64, add, 0)

    gather.own_chip()
    forward(0)
    for copy in g_loads:
        copy.wait()
    down_grad(0)
    gather.neighbours()
    downs.forward()
    gather.chip1()
    forward(1)
    down_grad(1)
    gather.chip2()
    forward(2)
    down_grad(2)
    gather.diagonal()
    gather.chip3()
    forward(3)
    downs.finish()
    backward(3)
    down_grad(3)
    down_sum.start_first()
    own_down = pltpu.make_async_copy(dgrad_ref.at[place.row], down_own, load_sem.at[10])
    own_down.start()
    scatter.combine(3)
    scatter.pass1.start()
    scatter.pass2.start()
    backward(1)
    down_sum.start_far()
    backward(2)
    down_sum.start_near()
    scatter.combine(1)
    scatter.first1.start()
    scatter.combine(2)
    scatter.first2.start()
    down_sum.add(merge)
    backward(0)
    scatter.finish_two()
    scatter.combine(0)
    count = model // tile
    lax.fori_loop(0, count // 2, gate_up_rows, 0)

    lax.fori_loop(count // 2, count, gate_up_rows, 0)
    gain = gain_row(gain_ref)
    scatter.arrive()

    def finish(i, sums):
        rows = span(i * 32, 32)
        res = res_ref[rows, :]
        inv = norm_inverse(res)
        grad = scatter.total(rows)
        v = grad * gain
        mean = jnp.mean(v * res, axis=-1, keepdims=True)
        out = g_ref[place.me, rows, :].astype(F32) + inv * v - res * (inv * inv * inv * mean)
        rgrad_ref[rows, :] = out
        branch_ref[rows, :] = out.astype(BF16)
        return sums + jnp.sum(grad * res * inv, axis=0, keepdims=True)

    gain_grad_ref[...] = lax.fori_loop(0, tok // 32, finish, jnp.zeros((1, model), F32), unroll=2)
    for i in (count - 2, count - 1):
        for copy in wstage_copies(i, i % 2):
            copy.wait()
    for n in (14, 15):
        stage_copy(n).wait()
    own_down.wait()
    down_sum.finish()
    down_sum.close()
    downs.close()
    gather.close()
    scatter.close()


def feed_forward(res, gain, two, g, g_all, slabs):
    tok, model = res.shape
    ff = slabs[0].shape[1]
    blocks = g_all.shape[0]
    dma = pltpu.SemaphoreType.DMA
    return pl.pallas_call(
        ffn_kernel,
        out_shape=(
            jax.ShapeDtypeStruct((4, 2, tok, model), BF16),
            jax.ShapeDtypeStruct((tok, model), F32),
            jax.ShapeDtypeStruct((tok, model), BF16),
            jax.ShapeDtypeStruct((1, model), F32),
            jax.ShapeDtypeStruct((model // 256, 256, ff), BF16),
            jax.ShapeDtypeStruct((model // 256, 256, ff), BF16),
            jax.ShapeDtypeStruct((model // 4, ff), BF16),
            jax.ShapeDtypeStruct((model // 4, ff), BF16),
            jax.ShapeDtypeStruct((ff, model // 4), BF16),
            jax.ShapeDtypeStruct((3, ff, model // 4), BF16),
        ),
        in_specs=[VMEM_SPEC, VMEM_SPEC] + [ANY_SPEC] * 8,
        out_specs=(ANY_SPEC, VMEM_SPEC, VMEM_SPEC, VMEM_SPEC) + (ANY_SPEC,) * 6,
        scratch_shapes=[
            pltpu.VMEM((blocks, tok, model), BF16),
            pltpu.VMEM((blocks, tok, model), BF16),
            pltpu.VMEM((model, 2 * ff), BF16),
            pltpu.VMEM((ff, model), BF16),
            pltpu.VMEM((blocks, tok, ff), BF16),
            pltpu.VMEM((blocks, tok, 2 * ff), BF16),
            pltpu.VMEM((2, 2, tok, model // 4), BF16),
            pltpu.VMEM((2, 256, 2 * ff), BF16),
            pltpu.VMEM((4, ff, model // 4), F32),
            pltpu.VMEM((4, ff, model // 4), BF16),
            pltpu.VMEM((ff, model // 4), BF16),
            *scatter_scratch(tok, model),
            dma((GATHER_SLOTS,)), dma((GATHER_SLOTS,)), dma((11,)), dma((blocks,)), dma((2,)), dma((2, 2)), dma((2,)),
            dma((ROW_SLOTS,)), dma((ROW_SLOTS,)), dma((ROW_SLOTS,)), dma((ROW_SLOTS,)),
        ],
        compiler_params=pltpu.CompilerParams(collective_id=2, has_side_effects=True, vmem_limit_bytes=62 * 1024 * 1024),
        cost_estimate=pl.CostEstimate(flops=18 * blocks * tok * model * ff, bytes_accessed=64 << 20, transcendentals=0),
    )(res, gain, two, g, g_all, *slabs)


def backward_kernel(heads, branch_hbm, out_hbm, x_hbm, kv_hbm, qo_hbm, gate_grad, up_grad, merged_hbm,
                    table_ref, gq_ref, gk_ref, gain_grad_ref, qkv_ref, gain_ref,
                    raw_hbm, o_hbm, qa_hbm, ka_hbm, kt_hbm, vt_hbm, inv_hbm,
                    ysum_hbm, outsum_hbm, grad_qkv_ref, grad_out_ref, grad_gain_ref, small_out,
                    grad_hbm, gate_recv, up_recv, qo_recv, kv_recv,
                    raw_ref, o_ref, qa_ref, ka_ref, kt_ref, vt_ref, inv_ref, kept_sem,
                    every_ref, w_ref, pg_ref, merged_ref, xt_ref, wstage_ref, gwo_ref,
                    doa_ref, dopad_ref, qpad_ref, va_ref, dq_ref, acc_ref,
                    part_ref, sibling_ref, passing_ref, final_ref, rs_send, rs_recv, rs2_send, rs2_recv,
                    ag_send, ag_recv, load_sem, xt_sem, wstage_sem, ready_sem,
                    ffn_merge, ffn_own, z_send, z_recv, own_sem, small_ref, small_row, small_mid, small_last, pieces_ref, amerge_ref, aown_ref,
                    kv_own, kv_in, kmerge_ref, ysum_ref, outsum_ref, sum_sem, slab_sem, pair_send, pair_recv,
                    s_send, s_recv, t_send, t_recv, p_send, p_recv):
    place = Place()
    blocks, tok, model = every_ref.shape[0] * every_ref.shape[1], every_ref.shape[2], every_ref.shape[3]
    branch_all = every_ref.reshape(blocks, tok, model)
    columns = 512
    lead = 256 - heads.wide
    load_w = load_slab(kv_hbm, qo_hbm, w_ref, slab_sem)
    load_out = pltpu.make_async_copy(out_hbm, part_ref, load_sem.at[1])
    load_own = pltpu.make_async_copy(branch_hbm, branch_all.at[place.me], load_sem.at[2])
    load_merged = pltpu.make_async_copy(merged_hbm, merged_ref, load_sem.at[3])
    load_out.start()
    load_own.start()
    for copy in load_w:
        copy.start()
    load_kept = [pltpu.make_async_copy(src, dst, kept_sem.at[i]) for i, (src, dst) in enumerate((
        (qa_hbm, qa_ref), (vt_hbm, vt_ref), (o_hbm, o_ref), (ka_hbm, ka_ref), (kt_hbm, kt_ref), (raw_hbm, raw_ref),
        (inv_hbm, inv_ref)))]
    for copy in load_kept:
        copy.start()
    load_merged.start()
    place.greet_all(4)
    gather = Gather(place, branch_hbm, branch_all, ag_send, ag_recv)
    gather.start()
    line = Line(place)
    ffn = [RowScatter(line, part, recv, ffn_merge.at[i], ffn_merge.at[i], z_send.at[i], z_recv.at[i])
           for i, (part, recv) in enumerate(((gate_grad, gate_recv), (up_grad, up_recv)))]
    for one in ffn:
        one.start_first()
    first = Scatter(place, part_ref, sibling_ref, passing_ref, final_ref, rs_send, rs_recv)
    second = Scatter(place, every_ref, sibling_ref, passing_ref, final_ref, rs2_send, rs2_recv)
    load_out.wait()
    for copy in first.exchange:
        copy.start()

    def ffn_add(i):
        own = (gate_grad, up_grad)[i]

        def work():
            load = pltpu.make_async_copy(own.at[line.c], ffn_own, own_sem.at[0])
            load.start()
            load.wait()

            def add(n, _):
                rows = span(n * 64, 64)
                ffn_merge[i, rows, :] = ffn_merge[i, rows, :] + ffn_own[rows, :]
                return 0

            lax.fori_loop(0, ffn_own.shape[0] // 64, add, 0)

        ffn[i].add(work)

    def tell(n, others):
        for other in others:
            pl.semaphore_signal(ready_sem.at[n], inc=1, device_id=(place.row, other), device_id_type=MESH)

    back = Backward(heads, place.me, table_ref, gq_ref, gk_ref, raw_ref, o_ref, qa_ref, ka_ref, kt_ref, vt_ref, inv_ref,
                    doa_ref, dopad_ref, qpad_ref, va_ref, dq_ref, acc_ref)

    def prepare(b, _):
        back.prepare(b)
        return 0

    for copy in load_kept:
        copy.wait()
    lax.fori_loop(0, blocks, prepare, 0, unroll=2)
    for copy in load_w:
        copy.wait()
    load_own.wait()

    def compute(k):
        m = place.chips[k]

        def gradient(j, _):
            b = 2 * m + j
            dm = dot(branch_all[b], w_ref[:, 384:640])
            back.gradient(b, dm[:, lead:])
            return 0

        lax.fori_loop(0, 2, gradient, 0, unroll=True)
        back.query_block(m)

    gather.own_chip()
    compute(0)
    gather.neighbours()
    for one in ffn:
        one.start_far()
    first.combine(3)
    first.pass1.start()
    first.pass2.start()
    gather.chip1()
    ffn_add(0)
    ffn_add(1)
    compute(1)
    for one in ffn:
        one.start_near()
    first.combine(1)
    first.first1.start()
    gather.chip2()
    compute(2)
    first.combine(2)
    first.first2.start()
    gather.diagonal()
    first.combine(0)
    tell(0, (place.sib,))
    gather.chip3()
    compute(3)
    first.finish_two()
    tell(1, place.same[1:3])
    load_merged.wait()
    tile = 256
    count = model // tile

    def x_copy(i, slot):
        return pltpu.make_async_copy(x_hbm.at[:, :, span(i * tile, tile)], xt_ref.at[slot], xt_sem.at[slot])

    x_copy(0, 0).start()

    def out_rows(i, _):
        out = dot_tn(branch_all[:, :, span(i * tile, tile)].reshape(blocks * tok, tile), merged_ref[...])
        gwo_ref[i] = out.astype(BF16)
        return 0

    lax.fori_loop(0, count, out_rows, 0, unroll=4)
    gather.close()
    pad = 512 - heads.qkv

    def finish(b, sums):
        grad, sums = back.finish(b, sums)
        grad = jnp.concatenate([grad, jnp.zeros((pad, tok), F32)], axis=0)
        pg_ref[b] = jnp.transpose(grad).astype(BF16)
        return sums

    zero = jnp.zeros((D, tok), F32)
    sums = lax.fori_loop(0, blocks, finish, (zero, zero), unroll=2)

    def grad_copy(i, slot):
        return pltpu.make_async_copy(wstage_ref.at[slot], grad_hbm.at[i // 2, lax.rem(i, 2)], wstage_sem.at[slot])

    def weight_rows(i, _):
        slot = lax.rem(i, 2)

        @pl.when(i + 1 < count)
        def _():
            x_copy(i + 1, 1 - slot).start()

        @pl.when(i >= 2)
        def _():
            grad_copy(i - 2, slot).wait()

        x_copy(i, slot).wait()
        x = xt_ref[slot].reshape(blocks * tok, tile)
        qkv = dot_tn(x, pg_ref[...].reshape(blocks * tok, 512))
        even = place.core == 0
        cols = span(i * tile, tile)
        kv_own[i // 2, lax.rem(i, 2)] = jnp.where(even, qkv[:, 0:128], qkv[:, 128:256]).astype(BF16)
        merged_ref[cols, 0:128] = jnp.where(even, qkv[:, 128:256], qkv[:, 0:128]).astype(BF16)
        wstage_ref[slot, :, 0:heads.wide] = qkv[:, 256:256 + heads.wide].astype(BF16)
        wstage_ref[slot, :, heads.wide:2 * heads.wide] = gwo_ref[i, :, lead:]
        grad_copy(i, slot).start()
        return 0

    lax.fori_loop(0, count, weight_rows, 0, unroll=2)
    for i in (count - 2, count - 1):
        grad_copy(i, i % 2).wait()

    pair = place.send(merged_ref.at[:, 0:128], kv_in, pair_send, pair_recv, 0, place.sib)
    pair.start()
    attn = RowScatter(line, grad_hbm, qo_recv, amerge_ref, amerge_ref, z_send.at[2], z_recv.at[2])
    attn.start_first()
    load_passed = pltpu.make_async_copy(grad_hbm.at[line.c], aown_ref, own_sem.at[2])
    load_passed.start()
    pair.wait_recv()

    def add_pair(n, _):
        b, rows = n // 4, span(lax.rem(n, 4) * 64, 64)
        for r in range(4):
            kv_own[r, b, rows, :] = kv_own[r, b, rows, :] + kv_in[span(r * 512 + n * 64, 64), :]
        return 0

    lax.fori_loop(0, 8, add_pair, 0)
    kv_sum = RowScatter(line, kv_own, kv_recv, kmerge_ref, kmerge_ref, z_send.at[3], z_recv.at[3])
    kv_sum.start_first()

    def attn_work():
        def add(n, _):
            b, rows = n // 4, span(lax.rem(n, 4) * 64, 64)
            amerge_ref[b, rows, :] = amerge_ref[b, rows, :] + aown_ref[b, rows, :]
            return 0

        lax.fori_loop(0, 8, add, 0)

    def kv_work():
        def add(n, _):
            b, rows = n // 4, span(lax.rem(n, 4) * 64, 64)
            kmerge_ref[b, rows, :] = kmerge_ref[b, rows, :] + kv_own[line.c, b, rows, :]
            return 0

        lax.fori_loop(0, 8, add, 0)

    def project(k):
        m = place.chips[k]

        def model_tile(n, _):
            cols = span(n * 512, 512)
            out = dot_nt(pg_ref[pl.ds(2 * m, 2)].reshape(2 * tok, 512), w_ref[cols, 0:512])
            every_ref[k, :, :, cols] = out.astype(BF16).reshape(2, tok, 512)
            return 0

        lax.fori_loop(0, model // 512, model_tile, 0, unroll=True)
        if k == 3:
            pl.semaphore_wait(ready_sem.at[0], 1)
        second.exchange[k].start()

    project(3)
    attn.start_far()
    kv_sum.start_far()
    project(1)
    second.combine(3)
    pl.semaphore_wait(ready_sem.at[1], 2)
    second.pass1.start()
    second.pass2.start()
    project(2)
    second.combine(1)
    load_passed.wait()
    attn.add(attn_work)
    attn.start_near()
    kv_sum.start_near()
    project(0)
    kv_sum.add(kv_work)
    second.combine(2)

    head_gains = jnp.sum(jnp.transpose(jnp.concatenate(sums, axis=0)), axis=0, keepdims=True)
    row8 = lax.broadcasted_iota(jnp.int32, (8, 128), 0)
    for r in range(4):
        for n in range(PLANE):
            start = (r * PLANE + n) * D
            piece = jnp.concatenate([gain_grad_ref[:, start:start + D], jnp.zeros((1, 128 - D), F32)], axis=1)
            small_ref[r, n] = jnp.where(row8 == 0, piece, jnp.where(row8 == 1, head_gains, 0.0))
    small_sends = []
    for j in range(1, 4):
        other = lax.rem(place.row + j, 4)
        small_sends.append(line.send(small_ref.at[other], small_row.at[place.row], s_send, j, s_recv, j, other))
    for copy in small_sends:
        copy.start()
    small_row[place.row] = small_ref[place.row]

    def take(out_ref, scatter):
        def one(i, _):
            rows = span(i * 32, 32)
            out_ref[rows, :] = scatter.total(rows)
            return 0

        lax.fori_loop(0, tok // 32, one, 0)

    first.arrive()
    take(outsum_ref, first)
    sums_out = [pltpu.make_async_copy(outsum_ref, outsum_hbm, sum_sem.at[0]),
                pltpu.make_async_copy(ysum_ref, ysum_hbm, sum_sem.at[1])]
    sums_out[0].start()
    tell(2, place.same[1:3])
    first.close()
    pl.semaphore_wait(ready_sem.at[2], 2)
    second.first1.start()
    second.first2.start()
    second.combine(0)
    def fetch(n, qo, kv, sem):
        return [pltpu.make_async_copy(qo, part_ref.at[n, :, :, 128:columns], own_sem.at[sem]),
                pltpu.make_async_copy(kv, part_ref.at[n, :, :, 0:128], own_sem.at[sem + 1])]

    own_term = fetch(0, grad_hbm.at[place.row], kv_own.at[place.row], 4)
    for copy in own_term:
        copy.start()

    second.finish_two()
    for copy in small_sends:
        copy.wait_recv()
    small_mid[...] = (small_row[0] + small_row[1]) + (small_row[2] + small_row[3])
    plane_sends = []
    for j in range(1, PLANE):
        other = lax.rem(place.me + j, PLANE)
        plane_sends.append(place.send(small_mid.at[other], small_last.at[place.me], t_send, t_recv, j, other))
    for copy in plane_sends:
        copy.start()
    small_last[place.me] = small_mid[place.me]
    for copy in plane_sends:
        copy.wait_recv()
    total = small_last[0]
    for n in range(1, PLANE):
        total = total + small_last[n]
    small_out[...] = total
    for copy in own_term:
        copy.wait()
    keeps = []

    def hand_over(index, lanes, total, arrived):
        total.finish()

        def fold(slots):
            loads = [pltpu.make_async_copy(arrived.at[slot], part_ref.at[slot + 1, :, :, lanes], own_sem.at[6 + 2 * slot + index])
                     for slot in slots]
            for copy in loads:
                copy.start()
            for copy in loads:
                copy.wait()

            def add(n, _):
                b, rows = n // 4, span(lax.rem(n, 4) * 64, 64)
                term = part_ref[0, b, rows, lanes]
                for slot in slots:
                    term = term + part_ref[slot + 1, b, rows, lanes]
                part_ref[0, b, rows, lanes] = term
                return 0

            lax.fori_loop(0, 8, add, 0)

        @pl.when(line.middle)
        def _():
            fold((0, 1, 2))

        @pl.when(jnp.logical_not(line.middle))
        def _():
            fold((0, 2))

        def piece(n):
            return part_ref.at[0, n // 4, span(lax.rem(n, 4) * 64, 64), lanes]

        keeps.append(pltpu.make_async_copy(piece(place.me), pieces_ref.at[place.me, :, lanes], own_sem.at[index]))
        keeps[-1].start()
        for j in range(1, PLANE):
            other = lax.rem(place.me + j, PLANE)
            copy = place.send(piece(other), pieces_ref.at[place.me, :, lanes], p_send.at[index], p_recv.at[index], j, other)
            copy.start()
            plane_sends.append(copy)

    hand_over(1, slice(128, columns), attn, qo_recv)
    hand_over(0, slice(0, 128), kv_sum, kv_recv)
    second.arrive()
    take(ysum_ref, second)
    sums_out[1].start()
    for one in ffn:
        one.finish()
        one.close()
    for copy in plane_sends[PLANE - 1:]:
        copy.wait_recv()
    for copy in keeps:
        copy.wait()
    unscaled, out_t = attention_sums(heads, lambda s: pieces_ref[s].astype(F32), True)
    grad_gain_ref[...] = jnp.broadcast_to(jnp.sum(unscaled * qkv_ref[...].astype(F32), axis=1, keepdims=True), grad_gain_ref.shape)
    grad_qkv_ref[...] = unscaled * column(gain_ref)
    grad_out_ref[...] = jnp.transpose(out_t)
    for copy in sums_out:
        copy.wait()
    for copy in plane_sends + small_sends + [pair]:
        copy.wait_send()
    attn.close()
    kv_sum.close()
    second.close()


def backward_phase(heads, branch, out_part, x_all, kv, qo, weight_grads, table, gq, gk, gain_grad, w_qkv, gain_attn, kept):
    blocks, tok, model = x_all.shape
    length = blocks * tok
    depth = w_qkv.shape[0]
    dma = pltpu.SemaphoreType.DMA
    raw, merged, *rest = kept
    return pl.pallas_call(
        functools.partial(backward_kernel, heads),
        out_shape=(
            jax.ShapeDtypeStruct((tok, model), F32),
            jax.ShapeDtypeStruct((tok, model), F32),
            jax.ShapeDtypeStruct(w_qkv.shape, F32),
            jax.ShapeDtypeStruct((QUERY_HEADS * D, depth), F32),
            jax.ShapeDtypeStruct((depth, 128), F32),
            jax.ShapeDtypeStruct((8, 128), F32),
            jax.ShapeDtypeStruct((4, 2, 256, 384), BF16),
            *(jax.ShapeDtypeStruct((3,) + grad.shape[1:], BF16) for grad in weight_grads),
            jax.ShapeDtypeStruct((3, 2, 256, 384), BF16),
            jax.ShapeDtypeStruct((3, 2, 256, 128), BF16),
        ),
        in_specs=[ANY_SPEC] * 8 + [VMEM_SPEC] * 6 + [ANY_SPEC] * (1 + len(rest)),
        out_specs=(ANY_SPEC,) * 2 + (VMEM_SPEC,) * 4 + (ANY_SPEC,) * 5,
        scratch_shapes=[
            *(pltpu.VMEM(array.shape, array.dtype) for array in (raw, *rest)),
            dma((7,)),
            pltpu.VMEM((4, 2, tok, model), BF16),
            pltpu.VMEM((model, heads.columns), BF16),
            pltpu.VMEM((blocks, tok, 512), BF16),
            pltpu.VMEM(merged.shape, BF16),
            pltpu.VMEM((2, blocks, tok, 256), BF16),
            pltpu.VMEM((2, 256, 384), BF16),
            pltpu.VMEM((model // 256, 256, 256), BF16),
            *backward_scratch(heads, length),
            *scatter_scratch(tok, model),
            dma((SCATTER_SLOTS,)), dma((SCATTER_SLOTS,)),
            dma((GATHER_SLOTS,)), dma((GATHER_SLOTS,)), dma((4,)), dma((2,)), dma((2,)),
            pltpu.SemaphoreType.REGULAR((3,)),
            pltpu.VMEM((2,) + weight_grads[0].shape[1:], BF16),
            pltpu.VMEM(weight_grads[0].shape[1:], BF16),
            dma((4, ROW_SLOTS)), dma((4, ROW_SLOTS)), dma((12,)),
            pltpu.VMEM((4, PLANE, 8, 128), F32),
            pltpu.VMEM((4, PLANE, 8, 128), F32),
            pltpu.VMEM((PLANE, 8, 128), F32),
            pltpu.VMEM((PLANE, 8, 128), F32),
            pltpu.VMEM((PLANE, depth, 512), BF16),
            pltpu.VMEM((2, 256, 384), BF16),
            pltpu.VMEM((2, 256, 384), BF16),
            pltpu.VMEM((4, 2, 256, 128), BF16),
            pltpu.VMEM((model, 128), BF16),
            pltpu.VMEM((2, 256, 128), BF16),
            pltpu.VMEM((tok, model), F32),
            pltpu.VMEM((tok, model), F32),
            dma((2,)), dma((3,)), dma((1,)), dma((1,)),
            dma((4,)), dma((4,)), dma((PLANE,)), dma((PLANE,)), dma((2, PLANE)), dma((2, PLANE)),
        ],
        compiler_params=pltpu.CompilerParams(collective_id=3, has_side_effects=True, vmem_limit_bytes=63 * 1024 * 1024),
        cost_estimate=pl.CostEstimate(flops=60 << 30, bytes_accessed=64 << 20, transcendentals=0),
    )(branch, out_part, x_all, kv, qo, *weight_grads, merged, table, gq, gk, gain_grad, w_qkv, gain_attn, raw, *rest)


def norm_back(grad_normed, values_in, inv_rms, gain):
    scaled = grad_normed * gain
    gain_grad = jnp.sum(grad_normed * values_in * inv_rms, axis=0)
    input_grad = inv_rms * scaled - values_in * inv_rms**3 * jnp.mean(scaled * values_in, axis=-1, keepdims=True)
    return input_grad, gain_grad


def start_wide(x, table, pieces, gain):
    return (
        lax.all_gather(x, "seq", axis=0, tiled=False),
        lax.all_gather(table, "seq", axis=0, tiled=False),
        lax.all_gather(lax.all_to_all(pieces, "seq", 0, 0, tiled=False), "rows", axis=0, tiled=False),
        lax.all_gather(lax.all_gather(gain, "seq", axis=0, tiled=False), "rows", axis=0, tiled=False),
    )


def scatter_rows(part, tok):
    return lax.psum_scatter(part.reshape(-1, part.shape[-1]), "seq", scatter_dimension=0, tiled=True).astype(F32)


def attention_wide(heads, x_all, g, w, table, gq, gk):
    blocks, tok, model = x_all.shape
    proj = dot(x_all.reshape(blocks * tok, model), w[:, :heads.qkv])
    kept = pl.pallas_call(
        functools.partial(local_forward_kernel, heads),
        out_shape=kept_shapes(heads, blocks * tok, 0),
        compiler_params=pltpu.CompilerParams(vmem_limit_bytes=VMEM_LIMIT),
    )(proj, table, gq, gk)
    total = scatter_rows(dot_nt(kept[1], w[:, heads.qkv:]).astype(BF16), tok)
    own = lax.dynamic_index_in_dim(x_all, lax.axis_index("seq"), 0, keepdims=False)
    return (own.astype(F32) + total, lax.all_gather(g, "seq", axis=0, tiled=False)) + tuple(kept)


def feed_forward_wide(res, gain, g_blocks, gate_slab, up_slab, down_slab):
    blocks, tok, model = g_blocks.shape
    inv = norm_inverse(res)
    two_all = lax.all_gather((res * inv * gain).astype(BF16), "seq", axis=0, tiled=True)
    g_all = g_blocks.reshape(blocks * tok, model)
    gate_act = dot(two_all, gate_slab)
    up_act = dot(two_all, up_slab)
    s = jax.nn.sigmoid(gate_act)
    hidden = (gate_act * s * up_act).astype(BF16)
    hidden_grad = dot_nt(g_all, down_slab)
    gate_grad = (hidden_grad * up_act * s * (1.0 + gate_act * (1.0 - s))).astype(BF16)
    up_grad = (hidden_grad * gate_act * s).astype(BF16)
    two_grad = scatter_rows((dot_nt(gate_grad, gate_slab) + dot_nt(up_grad, up_slab)).astype(BF16), tok)
    branch_part = dot(hidden, down_slab).astype(BF16).reshape(blocks, tok, model)
    norm_grad, gain_grad = norm_back(two_grad, res, inv, gain)
    g = lax.dynamic_index_in_dim(g_blocks, lax.axis_index("seq"), 0, keepdims=False)
    residual_grad = g.astype(F32) + norm_grad
    return (branch_part, residual_grad, residual_grad.astype(BF16), gain_grad[None],
            dot_tn(two_all, gate_grad).astype(BF16), dot_tn(two_all, up_grad).astype(BF16),
            dot_tn(hidden, g_all).astype(BF16))


def backward_wide(heads, branch, out_part, x_all, w, table, gq, gk, kept):
    blocks, tok, model = x_all.shape
    length = blocks * tok
    raw, merged, *rest = kept
    out_sum = scatter_rows(out_part, tok)
    branch_all = lax.all_gather(branch, "seq", axis=0, tiled=True)
    pg, gains = pl.pallas_call(
        functools.partial(local_backward_kernel, heads),
        out_shape=(jax.ShapeDtypeStruct((length, heads.qkv), BF16), jax.ShapeDtypeStruct((2 * D, 128), F32)),
        scratch_shapes=backward_scratch(heads, length),
        compiler_params=pltpu.CompilerParams(vmem_limit_bytes=VMEM_LIMIT),
    )(dot(branch_all, w[:, heads.qkv:]), table, gq, gk, raw, *rest)
    y_sum = scatter_rows(dot_nt(pg, w[:, :heads.qkv]).astype(BF16), tok)
    grad = jnp.concatenate([dot_tn(x_all.reshape(length, model), pg), dot_tn(branch_all, merged)], axis=1)
    return y_sum, out_sum, grad.astype(BF16), gains


def rotary_table(x, positions, segments):
    inverse = jnp.exp(-math.log(THETA) * jnp.arange(HALF, dtype=F32) * 2.0 / D)
    angles = inverse[:, None] * positions.astype(F32)[None, :]
    hot = jnp.arange(SEGMENT_KINDS, dtype=jnp.int32)[:, None] == segments[None, :]
    root = jnp.pad(norm_inverse(x).T, ((0, 7), (0, 0)))
    return jnp.concatenate([jnp.cos(angles), jnp.sin(angles), hot.astype(F32), root], axis=0)


def attention_pieces(heads, w_qkv, w_out, split):
    depth = w_qkv.shape[0]
    qw, kw = QUERY_HEADS * D, KEY_VALUE_HEADS * D
    out_t = w_out.T

    def columns(array, start, first, count, most):
        parts = []
        for i in range(count):
            n = first + i
            parts.append(array[:, start + n * D:start + (n + 1) * D] if n < most else jnp.zeros((depth, D), BF16))
        return parts

    pairs, others = [], []
    for s in range(heads.seq):
        q, k = s * heads.queries, heads.first(s)
        parts = []
        for n in ([k + s % 2] if split else range(k, k + heads.pairs)):
            parts += columns(w_qkv, qw, n, 1, KEY_VALUE_HEADS) + columns(w_qkv, qw + kw, n, 1, KEY_VALUE_HEADS)
        pairs.append(jnp.concatenate(parts, axis=1))
        others.append(jnp.concatenate(columns(w_qkv, 0, q, heads.queries, QUERY_HEADS)
                                      + columns(out_t, 0, q, heads.queries, QUERY_HEADS), axis=1))
    pairs, others = jnp.stack(pairs), jnp.stack(others)
    return (pairs, others) if split else jnp.concatenate([pairs, others], axis=2)


def attention_sums(heads, piece, split):
    pieces = [piece(s) for s in range(heads.seq)]
    held = 1 if split else heads.pairs
    first = [heads.first(s) + (s % 2 if split else 0) for s in range(heads.seq)]
    lead = 2 * held * D
    cut = lambda s, start, n: pieces[s][:, start + n * D:start + (n + 1) * D]
    queries = [cut(n // heads.queries, lead, n % heads.queries) for n in range(QUERY_HEADS)]
    outs = [cut(n // heads.queries, lead + heads.wide, n % heads.queries) for n in range(QUERY_HEADS)]

    def pairs(value):
        found = []
        for n in range(KEY_VALUE_HEADS):
            terms = [cut(s, value * D, 2 * (n - first[s])) for s in range(heads.seq)
                     if s * heads.queries < QUERY_HEADS and 0 <= n - first[s] < held]
            found.append(functools.reduce(jnp.add, terms))
        return found

    qkv = jnp.concatenate(queries + pairs(0) + pairs(1), axis=1)
    return qkv, jnp.concatenate(outs, axis=1)


def body(tokens, segments, positions, cotangent, gain_attn, w_qkv, gain_q, gain_k, w_out, gain_ffn, w_gate, w_up, w_down):
    seq = lax.axis_size("seq")
    rows = lax.axis_size("rows")
    heads = Heads(seq)
    depth = w_qkv.shape[0]
    tok, model = tokens.shape[1:]
    plane = seq == PLANE and rows == 4
    row = lax.axis_index("rows")

    gq, gk = gain_q[None], gain_k[None]
    x = tokens[0].astype(F32)
    scaled = (w_qkv.astype(F32) * gain_attn.astype(F32)[:, None]).astype(BF16)
    pieces = attention_pieces(heads, scaled, w_out, plane)
    table = rotary_table(x, positions[0], segments[0])
    if plane:
        x_all, table, kv, qo, gains = start_phase(rows, tokens[0], table, *pieces, gain_ffn[None])
        kv, qo = kv.reshape(2, model, -1), qo.reshape(model, -1)
    else:
        gain = jnp.pad(gain_ffn.astype(F32)[None], ((0, 7), (0, 128 - depth)))
        x_all, table, w, gains = start_wide(tokens[0], table, pieces, gain)
        w = w.reshape(model, heads.columns)
        gain_two = gains[:, :, 0, :depth].reshape(1, model)
    inv = norm_inverse(x)

    if plane:
        residual, two, g_all, gate, up, *kept = attention_phase(
            heads, x_all, cotangent[0], kv, qo, (w_gate, w_up), table, gq, gk, gains)
        out_part, residual_grad, branch, gain_two_grad, *weight_grads, gate_own, up_own, down_own, down_recv = feed_forward(
            residual, gains, two, cotangent[0], g_all, (w_gate, gate, w_up, up, w_down))
        weight_grads = [grad.reshape((4,) + w_gate.shape) for grad in weight_grads]
        y_sum, out_sum, grad_qkv, grad_out, grad_gain_attn, small, _, gate_recv, up_recv, *_ = backward_phase(
            heads, branch, out_part, x_all, kv, qo, weight_grads, table, gq, gk, gain_two_grad, w_qkv,
            gain_attn[None], kept)
        grad_gain_attn = grad_gain_attn[:, 0]
        middle = (row + 1) // 2 == 1

        def row_total(own, recv):
            return own.astype(F32) + recv[0].astype(F32) + recv[2].astype(F32) + jnp.where(middle, recv[1].astype(F32), 0.0)

        grad_gate, grad_up, grad_down = (
            row_total(own, recv) for own, recv in ((gate_own, gate_recv), (up_own, up_recv), (down_own, down_recv)))
        grad_gain_ffn, head_gains = small[0, :depth], small[1]
    else:
        gate_slab = lax.all_gather(w_gate, "rows", axis=0, tiled=True)
        up_slab = lax.all_gather(w_up, "rows", axis=0, tiled=True)
        down_slab = lax.all_gather(w_down, "rows", axis=1, tiled=True)
        residual, g_all, *kept = attention_wide(heads, x_all, cotangent[0], w, table, gq, gk)
        out_part, residual_grad, branch, gain_two_grad, gate_wgrad, up_wgrad, down_wgrad = feed_forward_wide(
            residual, gain_two, g_all, gate_slab, up_slab, down_slab)
        grad_gate = lax.psum_scatter(gate_wgrad, "rows", scatter_dimension=0, tiled=True).astype(F32)
        grad_up = lax.psum_scatter(up_wgrad, "rows", scatter_dimension=0, tiled=True).astype(F32)
        grad_down = lax.psum_scatter(down_wgrad, "rows", scatter_dimension=1, tiled=True).astype(F32)
        y_sum, out_sum, attn_grad, head_gains = backward_wide(heads, branch, out_part, x_all, w, table, gq, gk, kept)
        attn_grad = lax.psum_scatter(attn_grad, "rows", scatter_dimension=0, tiled=True)
        attn_grad = lax.all_to_all(attn_grad.reshape(seq, depth, heads.columns), "seq", 0, 0, tiled=False)
        small = lax.psum(jnp.concatenate([gain_two_grad[0], head_gains[:, 0]]), ("rows", "seq"))
        grad_gain_ffn = lax.dynamic_slice_in_dim(small, (row * seq + lax.axis_index("seq")) * depth, depth)
        head_gains = small[model:]
        attn_grad = attn_grad.astype(F32)
        unscaled, grad_out = attention_sums(heads, lambda s: attn_grad[s], False)
        grad_out = grad_out.T
        grad_gain_attn = jnp.sum(unscaled * w_qkv.astype(F32), axis=1)
        grad_qkv = unscaled * gain_attn.astype(F32)[:, None]

    layer_out = (residual + out_sum).astype(BF16)
    grad_tokens = residual_grad + y_sum - x * (inv * inv * jnp.mean(y_sum * x, axis=-1, keepdims=True))
    return (
        layer_out[None],
        grad_tokens[None],
        grad_gain_attn,
        grad_qkv,
        head_gains[:D],
        head_gains[D:],
        grad_out,
        grad_gain_ffn,
        grad_gate,
        grad_up,
        grad_down,
    )


def solution(mesh):
    both = ("rows", "seq")
    return jax.shard_map(
        body,
        mesh=mesh,
        in_specs=(
            P("rows", "seq", None), P("rows", "seq"), P("rows", "seq"), P("rows", "seq", None),
            P(both), P(both, None), P(), P(), P(None, both), P(both),
            P("rows", "seq"), P("rows", "seq"), P("seq", "rows"),
        ),
        out_specs=(
            P("rows", "seq", None), P("rows", "seq", None), P(both), P(both, None), P(), P(),
            P(None, both), P(both), P("rows", "seq"), P("rows", "seq"), P("seq", "rows"),
        ),
        check_vma=False,
    )
```

```python
import functools
import math

import jax
import jax.numpy as jnp
from jax import lax
from jax.experimental import pallas as pl
from jax.experimental.pallas import tpu as pltpu
from jax.sharding import PartitionSpec as P

QUERY_HEADS = 24
KEY_VALUE_HEADS = 6
GROUP = QUERY_HEADS // KEY_VALUE_HEADS
D = 64
HALF = D // 2
EPSILON = 1e-06
THETA = 10000.0
PENALTY = -10000.0
SEGMENT_KINDS = 8
TABLE_ROWS = 80
BLOCK = 512
PLANE = 8
F32 = jnp.float32
BF16 = jnp.bfloat16
VMEM_LIMIT = 60 * 1024 * 1024
MESH = pl.DeviceIdType.MESH
ANY_SPEC = pl.BlockSpec(memory_space=pl.ANY)
VMEM_SPEC = pl.BlockSpec(memory_space=pltpu.VMEM)


def dot(a, b):
    return jnp.dot(a, b, preferred_element_type=F32)


def dot_nt(a, b):
    return lax.dot_general(a, b, (((1,), (1,)), ((), ())), preferred_element_type=F32)


def dot_tn(a, b):
    return lax.dot_general(a, b, (((0,), (0,)), ((), ())), preferred_element_type=F32)


def norm_inverse(x):
    return lax.rsqrt(jnp.mean(x * x, axis=-1, keepdims=True) + EPSILON)


def split3(x):
    high = x.astype(BF16).astype(F32)
    mid = (x - high).astype(BF16).astype(F32)
    return high, mid, x - high - mid


def column(ref):
    row = ref[...].astype(F32)
    return jnp.transpose(jnp.broadcast_to(row, (128, row.shape[1])))[:, 0:1]


def gain_row(ref):
    return jnp.concatenate([ref[r, n, 0:1, 0:D] for r in range(ref.shape[0]) for n in range(ref.shape[1])], axis=1)


def span(start, size):
    return pl.ds(pl.multiple_of(start, size), size)


class Heads:
    def __init__(self, seq):
        self.seq = seq
        self.queries = -(-QUERY_HEADS // seq)
        last = [min((s + 1) * self.queries, QUERY_HEADS) - 1 for s in range(seq)]
        self.pairs = max(last[s] // GROUP - self.first(s) + 1 for s in range(seq) if last[s] >= s * self.queries)
        self.wide = self.queries * D
        self.narrow = self.pairs * D
        self.qkv = self.wide + 2 * self.narrow
        self.columns = self.qkv + self.wide

    def first(self, s):
        return (s // 2 * 2 * self.queries) // GROUP

    def slot(self, s, h):
        return (s * self.queries + h) // GROUP - self.first(s)


class Place:
    def __init__(self):
        self.row = lax.axis_index("rows")
        self.me = lax.axis_index("seq")
        self.core = lax.rem(self.me, 2)
        self.chip = self.me // 2
        self.sib = self.me + 1 - 2 * self.core
        chip = self.chip
        self.chips = (chip, chip + 1 - 2 * lax.rem(chip, 2), lax.rem(chip + 2, 4), 3 - chip)
        self.same = tuple(2 * q + self.core for q in self.chips)

    def greet(self, rows=1):
        barrier = pltpu.get_barrier_semaphore()
        for other in (self.sib, self.same[1], self.same[2]):
            pl.semaphore_signal(barrier, inc=1, device_id=(self.row, other), device_id_type=MESH)
        for j in range(1, rows):
            other = lax.rem(self.row + j, rows)
            pl.semaphore_signal(barrier, inc=1, device_id=(other, self.me), device_id_type=MESH)
        pl.semaphore_wait(barrier, 3 + rows - 1)

    def greet_all(self, rows):
        barrier = pltpu.get_barrier_semaphore()
        for j in range(1, PLANE):
            other = lax.rem(self.me + j, PLANE)
            pl.semaphore_signal(barrier, inc=1, device_id=(self.row, other), device_id_type=MESH)
        for j in range(1, rows):
            other = lax.rem(self.row + j, rows)
            pl.semaphore_signal(barrier, inc=1, device_id=(other, self.me), device_id_type=MESH)
        pl.semaphore_wait(barrier, PLANE - 1 + rows - 1)

    def send(self, src, dst, send_sem, recv_sem, slot, target):
        return pltpu.make_async_remote_copy(
            src_ref=src, dst_ref=dst, send_sem=send_sem.at[slot], recv_sem=recv_sem.at[slot],
            device_id=(self.row, target), device_id_type=MESH)


class Line:
    def __init__(self, place):
        self.place = place
        row = place.row
        self.a = row + 1 - 2 * lax.rem(row, 2)
        self.b = 3 - row
        self.c = lax.rem(row + 2, 4)
        self.middle = (row + 1) // 2 == 1

    def send(self, src, dst, send_sem, send_slot, recv_sem, recv_slot, target):
        return pltpu.make_async_remote_copy(
            src_ref=src, dst_ref=dst, send_sem=send_sem.at[send_slot], recv_sem=recv_sem.at[recv_slot],
            device_id=(target, self.place.me), device_id_type=MESH)


ROW_SLOTS = 4


class RowGather:
    def __init__(self, line, own, at, send_sem, recv_sem):
        self.line = line
        mine, passed = at(line.place.row), at(line.c)
        self.to_a = line.send(own, mine, send_sem, 0, recv_sem, 0, line.a)
        self.to_c = line.send(own, mine, send_sem, 1, recv_sem, 1, line.c)
        self.to_b = line.send(own, mine, send_sem, 2, recv_sem, 2, line.b)
        self.on = line.send(passed, passed, send_sem, 3, recv_sem, 2, line.a)

    def start(self):
        self.to_c.start()
        self.to_a.start()

        @pl.when(self.line.middle)
        def _():
            self.to_b.start()

    def forward(self):
        self.to_c.wait_recv()

        @pl.when(self.line.middle)
        def _():
            self.on.start()

    def finish(self):
        self.to_a.wait_recv()
        self.to_b.wait_recv()

    def close(self):
        self.to_a.wait_send()
        self.to_c.wait_send()

        @pl.when(self.line.middle)
        def _():
            self.to_b.wait_send()
            self.on.wait_send()


class RowScatter:
    def __init__(self, line, part, recv, merge, total, send_sem, recv_sem):
        self.line, self.total = line, total
        self.to_a = line.send(part.at[line.a], recv.at[0], send_sem, 0, recv_sem, 0, line.a)
        self.to_b = line.send(part.at[line.b], recv.at[1], send_sem, 1, recv_sem, 1, line.b)
        self.to_c = line.send(part.at[line.c], recv.at[2], send_sem, 2, recv_sem, 2, line.c)
        self.added = line.send(total, recv.at[2], send_sem, 2, recv_sem, 2, line.c)
        self.over = line.send(part.at[line.b], merge, send_sem, 3, recv_sem, 3, line.a)

    def start_first(self):
        @pl.when(jnp.logical_not(self.line.middle))
        def _():
            self.over.start()

        @pl.when(self.line.middle)
        def _():
            self.to_b.start()
            self.to_a.start()

    def start_far(self):
        @pl.when(jnp.logical_not(self.line.middle))
        def _():
            self.to_c.start()

    def start_near(self):
        @pl.when(jnp.logical_not(self.line.middle))
        def _():
            self.to_a.start()

    def add(self, work):
        @pl.when(self.line.middle)
        def _():
            self.over.wait_recv()
            work()
            self.added.start()

    def finish(self):
        self.to_a.wait_recv()
        self.to_c.wait_recv()

        @pl.when(self.line.middle)
        def _():
            self.to_b.wait_recv()

    def close(self):
        self.to_a.wait_send()
        self.to_c.wait_send()

        @pl.when(self.line.middle)
        def _():
            self.to_b.wait_send()

        @pl.when(jnp.logical_not(self.line.middle))
        def _():
            self.over.wait_send()


GATHER_SLOTS = 10


class Gather:
    def __init__(self, place, own, every, send_sem, recv_sem):
        half = every.shape[1] // 2
        low, high, whole = slice(0, half), slice(half, 2 * half), slice(0, 2 * half)

        def send(part, b, slot, target, src=None):
            src = every.at[b, part] if src is None else src.at[part]
            return place.send(src, every.at[b, part], send_sem, recv_sem, slot, target)

        me, (_, s1, s2, s3), sib = place.me, place.same, place.sib
        self.copies = (
            send(whole, me, 0, sib, own),
            send(low, me, 1, s1, own), send(high, me, 2, s1, own),
            send(high, me, 3, s2, own), send(low, me, 4, s2, own),
            send(low, s1, 5, s2), send(high, s2, 6, s1),
            send(whole, s1, 7, sib), send(whole, s2, 8, sib), send(whole, s3, 9, sib),
        )

    def start(self):
        for slot in (1, 3, 2, 4, 0):
            self.copies[slot].start()

    def own_chip(self):
        self.copies[0].wait_recv()

    def neighbours(self):
        c = self.copies
        c[1].wait_recv()
        c[5].start()
        c[3].wait_recv()
        c[6].start()
        c[2].wait_recv()
        c[7].start()
        c[4].wait_recv()
        c[8].start()

    def chip1(self):
        self.copies[7].wait_recv()

    def chip2(self):
        self.copies[8].wait_recv()

    def diagonal(self):
        c = self.copies
        c[5].wait_recv()
        c[6].wait_recv()
        c[9].start()

    def chip3(self):
        self.copies[9].wait_recv()

    def close(self):
        for copy in self.copies:
            copy.wait_send()


SCATTER_SLOTS = 10


class Scatter:
    def __init__(self, place, part, sibling, passing, final, send_sem, recv_sem):
        self.place, self.part, self.sibling, self.passing, self.final = place, part, sibling, passing, final
        half = part.shape[2] // 2
        self.half = half
        core, other = place.core, 1 - place.core
        _, s1, s2, _ = place.same
        send = lambda src, dst, slot, target: place.send(src, dst, send_sem, recv_sem, slot, target)
        low, high = slice(0, half), slice(half, 2 * half)
        self.exchange = tuple(send(part.at[k, other], sibling.at[k], k, place.sib) for k in range(4))
        self.pass1 = send(part.at[3, core, low], passing.at[0], 4, s1)
        self.pass2 = send(part.at[3, core, high], passing.at[1], 5, s2)
        self.first1 = send(part.at[1, core, low], final.at[0, low], 6, s1)
        self.second1 = send(part.at[1, core, high], final.at[0, high], 7, s1)
        self.first2 = send(part.at[2, core, high], final.at[1, high], 8, s2)
        self.second2 = send(part.at[2, core, low], final.at[1, low], 9, s2)

    def add(self, k, start, size, term, offset):
        core, step = self.place.core, 64

        def one(i, _):
            rows = pl.ds(pl.multiple_of(start + i * step, step), step)
            from_rows = pl.ds(pl.multiple_of(offset + i * step, step), step)
            self.part[k, core, rows, :] = self.part[k, core, rows, :] + term[from_rows, :]
            return 0

        lax.fori_loop(0, size // step, one, 0)

    def combine(self, k):
        self.exchange[k].wait_recv()
        self.add(k, 0, 2 * self.half, self.sibling.at[k], 0)

    def finish_two(self):
        self.pass1.wait_recv()
        self.add(2, 0, self.half, self.passing.at[0], 0)
        self.second2.start()
        self.pass2.wait_recv()
        self.add(1, self.half, self.half, self.passing.at[1], 0)
        self.second1.start()

    def arrive(self):
        for copy in (self.first1, self.second1, self.first2, self.second2):
            copy.wait_recv()

    def total(self, rows):
        return (self.part[0, self.place.core, rows, :].astype(F32) + self.final[0, rows, :].astype(F32)
                + self.final[1, rows, :].astype(F32))

    def close(self):
        for copy in self.exchange + (self.pass1, self.pass2, self.first1, self.second1, self.first2, self.second2):
            copy.wait_send()


def scatter_scratch(tok, width):
    return [
        pltpu.VMEM((4, 2, tok, width), BF16),
        pltpu.VMEM((4, tok, width), BF16),
        pltpu.VMEM((2, tok // 2, width), BF16),
        pltpu.VMEM((2, tok, width), BF16),
        pltpu.SemaphoreType.DMA((SCATTER_SLOTS,)),
        pltpu.SemaphoreType.DMA((SCATTER_SLOTS,)),
    ]


def start_kernel(x_ref, table_ref, kv_ref, qo_ref, gain_in, x_all, table_all, kv_all, qo_all, gain_all,
                 x_send, x_recv, t_send, t_recv, k_send, k_recv, p_send, p_recv, g_send, g_recv, z_send, z_recv,
                 w_send, w_recv, pair_send, pair_recv, local_sem, gain_ref):
    place = Place()
    gain = jnp.concatenate([gain_in[...].astype(F32), jnp.zeros((1, 128 - gain_in.shape[1]), F32)], axis=1)
    gain_ref[...] = jnp.broadcast_to(gain, gain_ref.shape)
    rows = qo_all.shape[0]
    me, row, core = place.me, place.row, place.core
    local = [pltpu.make_async_copy(src, dst, local_sem.at[i]) for i, (src, dst) in enumerate((
        (kv_ref.at[me], kv_all.at[core, row, me]), (qo_ref.at[me], qo_all.at[row, me]), (gain_ref, gain_all.at[row, me]),
        (x_ref, x_all.at[me]), (table_ref, table_all.at[me])))]
    for copy in local:
        copy.start()
    place.greet_all(rows)
    exchange, rest = [], []
    for j in range(1, PLANE):
        other = lax.rem(me + j, PLANE)
        exchange.append(place.send(kv_ref.at[other], kv_all.at[lax.rem(other, 2), row, me], k_send, k_recv, j, other))
        rest.append(place.send(qo_ref.at[other], qo_all.at[row, me], p_send, p_recv, j, other))
        rest.append(place.send(gain_ref, gain_all.at[row, me], g_send, g_recv, j, other))
    for copy in exchange + rest:
        copy.start()
    gathers = (Gather(place, x_ref, x_all, x_send, x_recv), Gather(place, table_ref, table_all, t_send, t_recv))
    gathers[1].start()
    gathers[0].start()
    for copy in local[:3]:
        copy.wait()
    line = Line(place)
    weights = [RowGather(line, at(row), at, w_send.at[i], w_recv.at[i])
               for i, at in enumerate((lambda r: kv_all.at[core, r], lambda r: qo_all.at[r]))]
    for copy in exchange:
        copy.wait_recv()
    weights[0].start()
    for copy in rest:
        copy.wait_recv()
    weights[1].start()
    along = []
    for j in range(1, rows):
        other = lax.rem(row + j, rows)
        along.append(line.send(gain_all.at[row], gain_all.at[row], z_send, j, z_recv, j, other))
    for copy in along:
        copy.start()
    for gather in gathers[::-1]:
        gather.own_chip()
    weights[0].forward()
    for gather in gathers[::-1]:
        gather.neighbours()
    weights[0].finish()
    pair = place.send(kv_all.at[core], kv_all.at[core], pair_send, pair_recv, 0, place.sib)
    pair.start()
    weights[1].forward()
    for name in ("chip1", "chip2", "diagonal", "chip3"):
        for gather in gathers[::-1]:
            getattr(gather, name)()
    for copy in local[3:]:
        copy.wait()
    for copy in along:
        copy.wait_recv()
    for copy in exchange + rest + along:
        copy.wait_send()
    for gather in gathers:
        gather.close()
    weights[1].finish()
    pair.wait_recv()
    pair.wait_send()
    for one in weights:
        one.close()


def start_phase(rows, x, table, kv, qo, gain):
    tok, model = x.shape
    dma = pltpu.SemaphoreType.DMA
    return pl.pallas_call(
        start_kernel,
        out_shape=(
            jax.ShapeDtypeStruct((PLANE, tok, model), BF16),
            jax.ShapeDtypeStruct((PLANE,) + table.shape, F32),
            jax.ShapeDtypeStruct((2, rows) + kv.shape, BF16),
            jax.ShapeDtypeStruct((rows,) + qo.shape, BF16),
            jax.ShapeDtypeStruct((rows, PLANE, 8, 128), F32),
        ),
        in_specs=[VMEM_SPEC] * 5,
        out_specs=(ANY_SPEC,) * 5,
        scratch_shapes=[dma((GATHER_SLOTS,))] * 4 + [dma((PLANE,))] * 6 + [dma((rows,))] * 2
        + [dma((2, ROW_SLOTS))] * 2 + [dma((1,))] * 2 + [dma((5,)), pltpu.VMEM((8, 128), F32)],
        compiler_params=pltpu.CompilerParams(collective_id=0, has_side_effects=True),
        cost_estimate=pl.CostEstimate(flops=0, bytes_accessed=160 << 20, transcendentals=0),
    )(x, table, kv, qo, gain)


def load_slab(kv_hbm, qo_hbm, w_ref, sem):
    parts = ((kv_hbm.at[0], 0, 128), (kv_hbm.at[1], 128, 256), (qo_hbm, 256, 640))
    return [pltpu.make_async_copy(src, w_ref.at[:, a:b], sem.at[i]) for i, (src, a, b) in enumerate(parts)]


class Forward:
    def __init__(self, heads, me, table, gq, gk, raw, merged, o, qa, ka, kt, vt, inv):
        self.heads, self.table, self.gq, self.gk = heads, table, column(gq), column(gk)
        self.raw, self.merged, self.o, self.qa, self.ka, self.kt, self.vt, self.inv = raw, merged, o, qa, ka, kt, vt, inv
        self.slots = [heads.slot(me, h) for h in range(heads.queries)]

    def prepare(self, b, projected):
        heads = self.heads
        tok = self.table.shape[2]
        lanes = span(b * tok, tok)
        cos = self.table[b, 0:HALF, :]
        sin = self.table[b, HALF:D, :]
        hot = self.table[b, D:D + 8, :]
        row = lax.broadcasted_iota(jnp.int32, (16, tok), 0)
        one_row = jnp.where(row == 0, 1.0, 0.0).astype(F32)
        penalty = jnp.concatenate([(1.0 - hot) * PENALTY, jnp.zeros((8, tok), F32)], axis=0).astype(BF16)
        lead = 2 * heads.narrow
        self.raw[0:heads.wide, lanes] = projected[lead:lead + heads.wide]

        def rotated(raw, gain):
            inv = lax.rsqrt(jnp.mean(raw * raw, axis=0, keepdims=True) + EPSILON)
            n = raw * inv * gain
            a, c = n[:HALF], n[HALF:]
            return inv, jnp.concatenate([a * cos - c * sin, c * cos + a * sin], axis=0)

        for h in range(heads.queries):
            inv, q = rotated(projected[lead + h * D:lead + (h + 1) * D], self.gq)
            self.inv[h:h + 1, lanes] = inv
            self.qa[h, :, lanes] = jnp.concatenate([(q * (D ** -0.5)).astype(BF16), penalty], axis=0)
        for g in range(heads.pairs):
            start = 2 * g * D
            self.raw[heads.wide + g * D:heads.wide + (g + 1) * D, lanes] = projected[start:start + D]
            inv, k = rotated(projected[start:start + D], self.gk)
            self.inv[heads.queries + g:heads.queries + g + 1, lanes] = inv
            self.kt[g, :, lanes] = k.astype(BF16)
            full = jnp.concatenate([k, hot, jnp.ones((8, tok), F32), jnp.zeros((48, tok), F32)], axis=0)
            self.ka[g, lanes, :] = jnp.transpose(full).astype(BF16)
            start += D
            self.vt[g, :, lanes] = jnp.concatenate([projected[start:start + D], one_row], axis=0).astype(BF16)

    def query_block(self, i):
        heads = self.heads
        cols = span(i * BLOCK, BLOCK)
        causal = (lax.broadcasted_iota(jnp.int32, (BLOCK, BLOCK), 0)
                  <= lax.broadcasted_iota(jnp.int32, (BLOCK, BLOCK), 1))

        def step(j, accs, diagonal):
            rows = span(j * BLOCK, BLOCK)
            new = []
            for h in range(heads.queries):
                slot = self.slots[h]
                p = jnp.exp(dot(self.ka[slot, rows, 0:80], self.qa[h, :, cols]))
                if diagonal:
                    p = jnp.where(causal, p, 0.0)
                new.append(accs[h] + dot(self.vt[slot, :, rows], p.astype(BF16)))
            return tuple(new)

        accs = tuple(jnp.zeros((80, BLOCK), F32) for _ in range(heads.queries))
        accs = lax.fori_loop(0, i, lambda j, c: step(j, c, False), accs)
        accs = step(i, accs, True)
        row = lax.broadcasted_iota(jnp.int32, (16, BLOCK), 0)
        lead = self.merged.shape[1] - heads.wide
        outs = [jnp.zeros((lead, BLOCK), F32)] if lead else []
        for h in range(heads.queries):
            total = accs[h][D:D + 1]
            o = accs[h][:D] * (1.0 / total)
            self.o[h, :, cols] = o
            outs.append(o)
            pieces = split3(-jnp.log(total))
            old = self.qa[h, 64:80, cols].astype(F32)
            extra = jnp.where(row == 8, pieces[0],
                              jnp.where(row == 9, pieces[1], jnp.where(row == 10, pieces[2], old)))
            self.qa[h, 64:80, cols] = extra.astype(BF16)
        merged = jnp.transpose(jnp.concatenate(outs, axis=0)).astype(BF16)
        self.merged[cols, :] = merged
        return merged


class Backward:
    def __init__(self, heads, me, table, gq, gk, raw, o, qa, ka, kt, vt, inv, doa, dopad, qpad, va, dq, acc):
        self.heads, self.table, self.gq, self.gk = heads, table, column(gq), column(gk)
        self.raw, self.o, self.qa, self.ka, self.kt, self.vt, self.inv = raw, o, qa, ka, kt, vt, inv
        self.doa, self.dopad, self.qpad, self.va, self.dq, self.acc = doa, dopad, qpad, va, dq, acc
        self.slots = [heads.slot(me, h) for h in range(heads.queries)]

    def prepare(self, b):
        heads = self.heads
        tok = self.table.shape[2]
        lanes = span(b * tok, tok)
        for h in range(heads.queries):
            q = jnp.concatenate([jnp.zeros((D, tok), F32), self.qa[h, 0:D, lanes].astype(F32)], axis=0)
            self.qpad[h, lanes, :] = jnp.transpose(q).astype(BF16)
            self.acc[h, lanes, :] = jnp.zeros((tok, 2 * D), F32)
        for g in range(heads.pairs):
            v = jnp.concatenate([self.vt[g, 0:D, lanes].astype(F32), jnp.ones((D, tok), F32)], axis=0)
            self.va[g, lanes, :] = jnp.transpose(v).astype(BF16)

    def gradient(self, b, dm):
        heads = self.heads
        tok = self.table.shape[2]
        lanes = span(b * tok, tok)
        row = lax.broadcasted_iota(jnp.int32, (16, tok), 0)
        dmt = jnp.transpose(dm.astype(BF16).astype(F32))
        for h in range(heads.queries):
            do = dmt[h * D:(h + 1) * D]
            delta = jnp.sum(do * self.o[h, :, lanes], axis=0, keepdims=True)
            pieces = split3(-delta)
            extra = jnp.where(row == 0, pieces[0],
                              jnp.where(row == 1, pieces[1], jnp.where(row == 2, pieces[2], 0.0)))
            self.doa[h, :, lanes] = jnp.concatenate([do, extra], axis=0).astype(BF16)
            both = jnp.concatenate([do, jnp.zeros((D, tok), F32)], axis=0)
            self.dopad[h, lanes, :] = jnp.transpose(both).astype(BF16)

    def query_block(self, i):
        heads = self.heads
        cols = span(i * BLOCK, BLOCK)
        causal = (lax.broadcasted_iota(jnp.int32, (BLOCK, BLOCK), 0)
                  <= lax.broadcasted_iota(jnp.int32, (BLOCK, BLOCK), 1))

        def step(j, accs, diagonal):
            rows = span(j * BLOCK, BLOCK)
            new = []
            for h in range(heads.queries):
                slot = self.slots[h]
                p = jnp.exp(dot(self.ka[slot, rows, 0:80], self.qa[h, :, cols]))
                if diagonal:
                    p = jnp.where(causal, p, 0.0)
                dp = dot(self.va[slot, rows, 0:80], self.doa[h, :, cols])
                ds = (p * dp).astype(BF16)
                self.acc[h, rows, :] += dot(p.astype(BF16), self.dopad[h, cols, :]) + dot(ds, self.qpad[h, cols, :])
                new.append(accs[h] + dot(self.kt[slot, :, rows], ds))
            return tuple(new)

        accs = tuple(jnp.zeros((D, BLOCK), F32) for _ in range(heads.queries))
        accs = lax.fori_loop(0, i, lambda j, c: step(j, c, False), accs)
        accs = step(i, accs, True)
        for h in range(heads.queries):
            self.dq[h, :, cols] = accs[h]

    def finish(self, b, sums):
        heads = self.heads
        tok = self.table.shape[2]
        lanes = span(b * tok, tok)
        cos = self.table[b, 0:HALF, :]
        sin = self.table[b, HALF:D, :]
        scale = self.table[b, 72:73, :]

        def back(grad, raw, inv, gain):
            a, c = grad[:HALF], grad[HALF:]
            n = jnp.concatenate([a * cos + c * sin, c * cos - a * sin], axis=0)
            v = n * gain
            out = inv * v - raw * (inv * inv * inv) * jnp.mean(v * raw, axis=0, keepdims=True)
            return out * scale, n * raw * inv

        sum_q, sum_k = sums
        pairs = [jnp.zeros((2 * D, tok), F32) for _ in range(heads.pairs)]
        out = []
        for h in range(heads.queries):
            raw = self.raw[h * D:(h + 1) * D, lanes]
            grad, part = back(self.dq[h, :, lanes] * (D ** -0.5), raw, self.inv[h:h + 1, lanes], self.gq)
            out.append(grad)
            sum_q = sum_q + part
            both = jnp.transpose(self.acc[h, lanes, :])
            for g in range(heads.pairs):
                pairs[g] = pairs[g] + jnp.where(self.slots[h] == g, both, 0.0)
        both_out = []
        for g in range(heads.pairs):
            start = heads.wide + g * D
            raw = self.raw[start:start + D, lanes]
            inv = self.inv[heads.queries + g:heads.queries + g + 1, lanes]
            grad, part = back(pairs[g][D:], raw, inv, self.gk)
            both_out += [grad, pairs[g][:D] * scale]
            sum_k = sum_k + part
        return jnp.concatenate(both_out + out, axis=0), (sum_q, sum_k)


def kept_shapes(heads, length, lead):
    return (
        jax.ShapeDtypeStruct((heads.wide + heads.narrow, length), F32),
        jax.ShapeDtypeStruct((length, lead + heads.wide), BF16),
        jax.ShapeDtypeStruct((heads.queries, D, length), F32),
        jax.ShapeDtypeStruct((heads.queries, 80, length), BF16),
        jax.ShapeDtypeStruct((heads.pairs, length, 128), BF16),
        jax.ShapeDtypeStruct((heads.pairs, D, length), BF16),
        jax.ShapeDtypeStruct((heads.pairs, 80, length), BF16),
        jax.ShapeDtypeStruct((8, length), F32),
    )


def backward_scratch(heads, length):
    return [
        pltpu.VMEM((heads.queries, 80, length), BF16),
        pltpu.VMEM((heads.queries, length, 2 * D), BF16),
        pltpu.VMEM((heads.queries, length, 2 * D), BF16),
        pltpu.VMEM((heads.pairs, length, 2 * D), BF16),
        pltpu.VMEM((heads.queries, D, length), F32),
        pltpu.VMEM((heads.queries, length, 2 * D), F32),
    ]


def local_forward_kernel(heads, proj_ref, table_ref, gq_ref, gk_ref, *kept):
    forward = Forward(heads, lax.axis_index("seq"), table_ref, gq_ref, gk_ref, *kept)
    blocks, _, tok = table_ref.shape

    def prepare(b, _):
        rows = span(b * tok, tok)
        forward.prepare(b, jnp.transpose(proj_ref[rows, :]) * table_ref[b, 72:73, :])
        return 0

    def query_block(i, _):
        forward.query_block(i)
        return 0

    lax.fori_loop(0, blocks, prepare, 0)
    lax.fori_loop(0, blocks * tok // BLOCK, query_block, 0)


def local_backward_kernel(heads, dm_ref, table_ref, gq_ref, gk_ref, raw_ref, o_ref, qa_ref, ka_ref, kt_ref, vt_ref, inv_ref,
                          pg_ref, gains_ref, *scratch):
    backward = Backward(heads, lax.axis_index("seq"), table_ref, gq_ref, gk_ref, raw_ref, o_ref, qa_ref, ka_ref, kt_ref,
                        vt_ref, inv_ref, *scratch)
    blocks, _, tok = table_ref.shape

    def prepare(b, _):
        backward.prepare(b)
        backward.gradient(b, dm_ref[span(b * tok, tok), :])
        return 0

    def query_block(i, _):
        backward.query_block(i)
        return 0

    def finish(b, sums):
        grad, sums = backward.finish(b, sums)
        pg_ref[span(b * tok, tok), :] = jnp.transpose(grad).astype(BF16)
        return sums

    lax.fori_loop(0, blocks, prepare, 0)
    lax.fori_loop(0, blocks * tok // BLOCK, query_block, 0)
    zero = jnp.zeros((D, tok), F32)
    sum_q, sum_k = lax.fori_loop(0, blocks, finish, (zero, zero))
    gains_ref[0:D, :] = jnp.broadcast_to(jnp.sum(sum_q, axis=1, keepdims=True), (D, 128))
    gains_ref[D:2 * D, :] = jnp.broadcast_to(jnp.sum(sum_k, axis=1, keepdims=True), (D, 128))


def attention_kernel(heads, x_hbm, g_hbm, kv_hbm, qo_hbm, gate_hbm, up_hbm, table_ref, gq_ref, gk_ref, gain_ref,
                     res_ref, two_ref, g_all, gate_all, up_all, raw_hbm, merged_hbm, o_hbm, qa_hbm, ka_hbm, kt_hbm, vt_hbm, inv_hbm,
                     raw_ref, merged_ref, o_ref, qa_ref, ka_ref, kt_ref, vt_ref, inv_ref, kept_sem, x_ref, w_ref, part_ref, sibling_ref, passing_ref, final_ref, rs_send, rs_recv,
                     ag_send, ag_recv, load_sem, slab_sem, z_send, z_recv):
    place = Place()
    blocks, tok, model = x_ref.shape
    slabs = ((gate_hbm, gate_all), (up_hbm, up_all))
    load_w = load_slab(kv_hbm, qo_hbm, w_ref, slab_sem)
    for copy in load_w:
        copy.start()
    loads = [pltpu.make_async_copy(x_hbm.at[b], x_ref.at[b], load_sem.at[b]) for b in range(blocks)]
    for copy in loads:
        copy.start()
    place.greet(4)
    gather = Gather(place, g_hbm, g_all, ag_send, ag_recv)
    scatter = Scatter(place, part_ref, sibling_ref, passing_ref, final_ref, rs_send, rs_recv)
    line = Line(place)
    weights = [RowGather(line, own, lambda r, every=every: every.at[r], z_send.at[i], z_recv.at[i])
               for i, (own, every) in enumerate(slabs)]
    weights[0].start()
    gather.start()
    forward = Forward(heads, place.me, table_ref, gq_ref, gk_ref, raw_ref, merged_ref, o_ref, qa_ref, ka_ref, kt_ref,
                      vt_ref, inv_ref)
    for copy in load_w + loads:
        copy.wait()

    def prepare(b, _):
        proj = dot(x_ref[b], w_ref[:, 0:512])
        forward.prepare(b, jnp.transpose(proj) * table_ref[b, 72:73, :])
        return 0

    lax.fori_loop(0, blocks, prepare, 0, unroll=2)
    tile = 512

    def compute(k):
        merged = forward.query_block(place.chips[k])

        def model_tile(n, _):
            cols = span(n * tile, tile)
            out = dot_nt(merged_ref[span(place.chips[k] * BLOCK, BLOCK), :], w_ref[cols, 384:640])
            part_ref[k, :, :, cols] = out.astype(BF16).reshape(2, tok, tile)
            return 0

        lax.fori_loop(0, model // tile, model_tile, 0, unroll=True)
        scatter.exchange[k].start()

    compute(3)
    gather.own_chip()
    gather.neighbours()
    weights[1].start()
    scatter.combine(3)
    scatter.pass1.start()
    scatter.pass2.start()
    compute(1)
    scatter.combine(1)
    scatter.first1.start()
    gather.chip1()
    gather.chip2()
    weights[0].forward()
    compute(2)
    scatter.combine(2)
    scatter.first2.start()
    gather.diagonal()
    compute(0)
    keep = [pltpu.make_async_copy(src, dst, kept_sem.at[i]) for i, (src, dst) in enumerate((
        (raw_ref, raw_hbm), (merged_ref, merged_hbm), (o_ref, o_hbm), (qa_ref, qa_hbm), (ka_ref, ka_hbm),
        (kt_ref, kt_hbm), (vt_ref, vt_hbm), (inv_ref, inv_hbm)))]
    for copy in keep:
        copy.start()
    scatter.combine(0)
    scatter.finish_two()
    weights[1].forward()
    gather.chip3()
    gain = gain_row(gain_ref)
    scatter.arrive()

    def finish(i, _):
        rows = span(i * 32, 32)
        res = x_ref[place.me, rows, :].astype(F32) + scatter.total(rows)
        res_ref[rows, :] = res
        two_ref[rows, :] = (res * norm_inverse(res) * gain).astype(BF16)
        return 0

    lax.fori_loop(0, tok // 32, finish, 0)
    for one in weights:
        one.finish()
        one.close()
    for copy in keep:
        copy.wait()
    gather.close()
    scatter.close()


def attention_phase(heads, x_all, g, kv, qo, slabs, table, gq, gk, gain):
    blocks, tok, model = x_all.shape
    dma = pltpu.SemaphoreType.DMA
    lead = 256 - heads.wide
    kept = kept_shapes(heads, blocks * tok, lead)
    return pl.pallas_call(
        functools.partial(attention_kernel, heads),
        out_shape=(jax.ShapeDtypeStruct((tok, model), F32), jax.ShapeDtypeStruct((tok, model), BF16),
                   jax.ShapeDtypeStruct((blocks, tok, model), BF16))
        + tuple(jax.ShapeDtypeStruct((4,) + slab.shape, BF16) for slab in slabs) + kept,
        in_specs=[ANY_SPEC] * 6 + [VMEM_SPEC] * 4,
        out_specs=(VMEM_SPEC, VMEM_SPEC) + (ANY_SPEC,) * (3 + len(kept)),
        scratch_shapes=[
            *(pltpu.VMEM(array.shape, array.dtype) for array in kept),
            dma((len(kept),)),
            pltpu.VMEM((blocks, tok, model), BF16),
            pltpu.VMEM((model, heads.columns), BF16),
            *scatter_scratch(tok, model),
            dma((GATHER_SLOTS,)), dma((GATHER_SLOTS,)), dma((blocks,)), dma((3,)),
            dma((2, ROW_SLOTS)), dma((2, ROW_SLOTS)),
        ],
        compiler_params=pltpu.CompilerParams(collective_id=1, has_side_effects=True, vmem_limit_bytes=VMEM_LIMIT),
        cost_estimate=pl.CostEstimate(flops=40 << 30, bytes_accessed=64 << 20, transcendentals=0),
    )(x_all, g, kv, qo, *slabs, table, gq, gk, gain)


def ffn_kernel(res_ref, gain_ref, two_hbm, g_own, g_hbm, gate_own, gate_hbm, up_own, up_hbm, down_hbm,
               out_hbm, rgrad_ref, branch_ref, gain_grad_ref, gate_grad_hbm, up_grad_hbm,
               gate_grad_own, up_grad_own, down_own, down_recv,
               two_ref, g_ref, weight_ref, down_ref, hid_ref, gu_ref, stage_ref, wstage_ref, dsum_ref, dgrad_ref, merge_ref,
               part_ref, sibling_ref, passing_ref, final_ref, rs_send, rs_recv,
               ag_send, ag_recv, load_sem, g_sem, stage_sem, wstage_sem, own_sem, za_send, za_recv, zr_send, zr_recv):
    place = Place()
    blocks, tok, model = g_ref.shape
    ff = weight_ref.shape[1] // 2
    share = model // 4
    tile = 256
    def down_at(r):
        return down_ref.at[:, span(r * share, share)]

    loads, g_loads = [], []
    for i, (own, every) in enumerate(((gate_own, gate_hbm), (up_own, up_hbm))):
        for j in range(4):
            r = lax.rem(place.row + j, 4)
            loads.append(pltpu.make_async_copy(
                every.at[r] if j else own, weight_ref.at[span(r * share, share), i * ff:(i + 1) * ff], load_sem.at[4 * i + j]))
    for j in range(blocks):
        b = lax.rem(place.me + j, blocks)
        g_loads.append(pltpu.make_async_copy(g_hbm.at[b] if j else g_own, g_ref.at[b], g_sem.at[j]))
    own_loads = [pltpu.make_async_copy(two_hbm, two_ref.at[place.me], load_sem.at[8]),
                 pltpu.make_async_copy(down_hbm, down_at(place.row), load_sem.at[9])]
    for copy in own_loads + loads + g_loads:
        copy.start()
    place.greet(4)
    line = Line(place)
    gather = Gather(place, two_hbm, two_ref, ag_send, ag_recv)
    scatter = Scatter(place, part_ref, sibling_ref, passing_ref, final_ref, rs_send, rs_recv)
    downs = RowGather(line, down_hbm, down_at, za_send, za_recv)
    down_sum = RowScatter(line, dgrad_ref, down_recv, merge_ref, merge_ref, zr_send, zr_recv)
    gather.start()
    downs.start()
    for copy in loads + own_loads:
        copy.wait()

    def forward(k):
        pair = pl.ds(2 * place.chips[k], 2)

        def hidden_tile(h, _):
            cols, cols2 = span(h * tile, tile), span(ff + h * tile, tile)
            x = two_ref[pair].reshape(2 * tok, model)
            gate = dot(x, weight_ref[:, cols])
            up = dot(x, weight_ref[:, cols2])
            s = 1.0 / (1.0 + jnp.exp(-gate))
            act = gate * s
            hid_ref[pair, :, cols] = (act * up).astype(BF16).reshape(2, tok, tile)
            gu_ref[pair, :, cols] = (up * s * (1.0 + gate * (1.0 - s))).astype(BF16).reshape(2, tok, tile)
            gu_ref[pair, :, cols2] = act.astype(BF16).reshape(2, tok, tile)
            return 0

        lax.fori_loop(0, ff // tile, hidden_tile, 0, unroll=True)

    def backward(k):
        pair = pl.ds(2 * place.chips[k], 2)

        def hidden_tile(h, _):
            cols, cols2 = span(h * tile, tile), span(ff + h * tile, tile)
            back = dot_nt(g_ref[pair].reshape(2 * tok, model), down_ref[cols, :])
            for where in (cols, cols2):
                factor = gu_ref[pair, :, where].reshape(2 * tok, tile).astype(F32)
                gu_ref[pair, :, where] = (back * factor).astype(BF16).reshape(2, tok, tile)
            return 0

        lax.fori_loop(0, ff // tile, hidden_tile, 0, unroll=True)

        def model_tile(n, _):
            cols = span(n * tile, tile)
            back = dot_nt(gu_ref[pair].reshape(2 * tok, 2 * ff), weight_ref[cols, :])
            part_ref[k, :, :, cols] = back.astype(BF16).reshape(2, tok, tile)
            return 0

        lax.fori_loop(0, model // tile, model_tile, 0, unroll=True)
        scatter.exchange[k].start()

    def stage_copy(n):
        slot = lax.rem(n, 2)
        return pltpu.make_async_copy(stage_ref.at[slot], out_hbm.at[n // 4, :, :, span(lax.rem(n, 4) * share, share)],
                                     stage_sem.at[slot])

    def out_tile(n, _):
        @pl.when(n >= 2)
        def _():
            stage_copy(n - 2).wait()

        k, r = n // 4, lax.rem(n, 4)
        chip = place.chip
        m = jnp.where(k == 0, chip, jnp.where(k == 1, place.chips[1], jnp.where(k == 2, place.chips[2], place.chips[3])))
        out = dot(hid_ref[pl.ds(2 * m, 2)].reshape(2 * tok, ff), down_ref[:, span(r * share, share)])
        stage_ref[lax.rem(n, 2)] = out.astype(BF16).reshape(2, tok, share)
        stage_copy(n).start()
        return 0

    def down_grad(k):
        pair = pl.ds(2 * place.chips[k], 2)

        def down_rows(n, _):
            rows, r = span(lax.rem(n, ff // tile) * tile, tile), n // (ff // tile)
            h = hid_ref[pair, :, rows].reshape(2 * tok, tile)
            g = g_ref[pair, :, span(r * share, share)].reshape(2 * tok, share)
            term = dot_tn(h, g)
            if k:
                term = dsum_ref[r, rows, :] + term
            if k < 3:
                dsum_ref[r, rows, :] = term
            else:
                dgrad_ref[r, rows, :] = term.astype(BF16)
            return 0

        lax.fori_loop(0, 4 * (ff // tile), down_rows, 0, unroll=4)

    def wstage_copies(i, slot):
        return (pltpu.make_async_copy(wstage_ref.at[slot, :, 0:ff], gate_grad_hbm.at[i], wstage_sem.at[slot, 0]),
                pltpu.make_async_copy(wstage_ref.at[slot, :, ff:2 * ff], up_grad_hbm.at[i], wstage_sem.at[slot, 1]))

    def own_copies(half, slot):
        rows = span(half * tile, tile)
        return (pltpu.make_async_copy(wstage_ref.at[slot, :, 0:ff], gate_grad_own.at[rows], own_sem.at[0]),
                pltpu.make_async_copy(wstage_ref.at[slot, :, ff:2 * ff], up_grad_own.at[rows], own_sem.at[1]))

    def gate_up_rows(i, _):
        cols = span(i * tile, tile)
        slot = lax.rem(i, 2)

        @pl.when(i >= 2)
        def _():
            for copy in wstage_copies(i - 2, slot):
                copy.wait()

        x = two_ref[:, :, cols].reshape(blocks * tok, tile)
        wstage_ref[slot] = dot_tn(x, gu_ref[...].reshape(blocks * tok, 2 * ff)).astype(BF16)
        for copy in wstage_copies(i, slot):
            copy.start()

        @pl.when(i // 2 == place.row)
        def _():
            for copy in own_copies(lax.rem(i, 2), slot):
                copy.start()

        out_tile(2 * i, 0)
        out_tile(2 * i + 1, 0)

        @pl.when(i // 2 == place.row)
        def _():
            for copy in own_copies(lax.rem(i, 2), slot):
                copy.wait()

        return 0

    def merge():
        def add(n, _):
            rows = span(n * 64, 64)
            merge_ref[rows, :] = (merge_ref[rows, :].astype(F32) + dgrad_ref[line.c, rows, :].astype(F32)).astype(BF16)
            return 0

        lax.fori_loop(0, ff // 64, add, 0)

    gather.own_chip()
    forward(0)
    for copy in g_loads:
        copy.wait()
    down_grad(0)
    gather.neighbours()
    downs.forward()
    gather.chip1()
    forward(1)
    down_grad(1)
    gather.chip2()
    forward(2)
    down_grad(2)
    gather.diagonal()
    gather.chip3()
    forward(3)
    downs.finish()
    backward(3)
    down_grad(3)
    down_sum.start_first()
    own_down = pltpu.make_async_copy(dgrad_ref.at[place.row], down_own, load_sem.at[10])
    own_down.start()
    scatter.combine(3)
    scatter.pass1.start()
    scatter.pass2.start()
    backward(1)
    down_sum.start_far()
    backward(2)
    down_sum.start_near()
    scatter.combine(1)
    scatter.first1.start()
    scatter.combine(2)
    scatter.first2.start()
    down_sum.add(merge)
    backward(0)
    scatter.finish_two()
    scatter.combine(0)
    count = model // tile
    lax.fori_loop(0, count // 2, gate_up_rows, 0)

    lax.fori_loop(count // 2, count, gate_up_rows, 0)
    gain = gain_row(gain_ref)
    scatter.arrive()

    def finish(i, sums):
        rows = span(i * 32, 32)
        res = res_ref[rows, :]
        inv = norm_inverse(res)
        grad = scatter.total(rows)
        v = grad * gain
        mean = jnp.mean(v * res, axis=-1, keepdims=True)
        out = g_ref[place.me, rows, :].astype(F32) + inv * v - res * (inv * inv * inv * mean)
        rgrad_ref[rows, :] = out
        branch_ref[rows, :] = out.astype(BF16)
        return sums + jnp.sum(grad * res * inv, axis=0, keepdims=True)

    gain_grad_ref[...] = lax.fori_loop(0, tok // 32, finish, jnp.zeros((1, model), F32), unroll=2)
    for i in (count - 2, count - 1):
        for copy in wstage_copies(i, i % 2):
            copy.wait()
    for n in (14, 15):
        stage_copy(n).wait()
    own_down.wait()
    down_sum.finish()
    down_sum.close()
    downs.close()
    gather.close()
    scatter.close()


def feed_forward(res, gain, two, g, g_all, slabs):
    tok, model = res.shape
    ff = slabs[0].shape[1]
    blocks = g_all.shape[0]
    dma = pltpu.SemaphoreType.DMA
    return pl.pallas_call(
        ffn_kernel,
        out_shape=(
            jax.ShapeDtypeStruct((4, 2, tok, model), BF16),
            jax.ShapeDtypeStruct((tok, model), F32),
            jax.ShapeDtypeStruct((tok, model), BF16),
            jax.ShapeDtypeStruct((1, model), F32),
            jax.ShapeDtypeStruct((model // 256, 256, ff), BF16),
            jax.ShapeDtypeStruct((model // 256, 256, ff), BF16),
            jax.ShapeDtypeStruct((model // 4, ff), BF16),
            jax.ShapeDtypeStruct((model // 4, ff), BF16),
            jax.ShapeDtypeStruct((ff, model // 4), BF16),
            jax.ShapeDtypeStruct((3, ff, model // 4), BF16),
        ),
        in_specs=[VMEM_SPEC, VMEM_SPEC] + [ANY_SPEC] * 8,
        out_specs=(ANY_SPEC, VMEM_SPEC, VMEM_SPEC, VMEM_SPEC) + (ANY_SPEC,) * 6,
        scratch_shapes=[
            pltpu.VMEM((blocks, tok, model), BF16),
            pltpu.VMEM((blocks, tok, model), BF16),
            pltpu.VMEM((model, 2 * ff), BF16),
            pltpu.VMEM((ff, model), BF16),
            pltpu.VMEM((blocks, tok, ff), BF16),
            pltpu.VMEM((blocks, tok, 2 * ff), BF16),
            pltpu.VMEM((2, 2, tok, model // 4), BF16),
            pltpu.VMEM((2, 256, 2 * ff), BF16),
            pltpu.VMEM((4, ff, model // 4), F32),
            pltpu.VMEM((4, ff, model // 4), BF16),
            pltpu.VMEM((ff, model // 4), BF16),
            *scatter_scratch(tok, model),
            dma((GATHER_SLOTS,)), dma((GATHER_SLOTS,)), dma((11,)), dma((blocks,)), dma((2,)), dma((2, 2)), dma((2,)),
            dma((ROW_SLOTS,)), dma((ROW_SLOTS,)), dma((ROW_SLOTS,)), dma((ROW_SLOTS,)),
        ],
        compiler_params=pltpu.CompilerParams(collective_id=2, has_side_effects=True, vmem_limit_bytes=62 * 1024 * 1024),
        cost_estimate=pl.CostEstimate(flops=18 * blocks * tok * model * ff, bytes_accessed=64 << 20, transcendentals=0),
    )(res, gain, two, g, g_all, *slabs)


def backward_kernel(heads, branch_hbm, out_hbm, x_hbm, kv_hbm, qo_hbm, gate_grad, up_grad, merged_hbm,
                    table_ref, gq_ref, gk_ref, gain_grad_ref, qkv_ref, gain_ref,
                    raw_hbm, o_hbm, qa_hbm, ka_hbm, kt_hbm, vt_hbm, inv_hbm,
                    ysum_hbm, outsum_hbm, grad_qkv_ref, grad_out_ref, grad_gain_ref, small_out,
                    grad_hbm, gate_recv, up_recv, qo_recv, kv_recv,
                    raw_ref, o_ref, qa_ref, ka_ref, kt_ref, vt_ref, inv_ref, kept_sem,
                    every_ref, w_ref, pg_ref, merged_ref, xt_ref, wstage_ref, gwo_ref,
                    doa_ref, dopad_ref, qpad_ref, va_ref, dq_ref, acc_ref,
                    part_ref, sibling_ref, passing_ref, final_ref, rs_send, rs_recv, rs2_send, rs2_recv,
                    ag_send, ag_recv, load_sem, xt_sem, wstage_sem, ready_sem,
                    ffn_merge, ffn_own, z_send, z_recv, own_sem, small_ref, small_row, small_mid, small_last, pieces_ref, amerge_ref, aown_ref,
                    kv_own, kv_in, kmerge_ref, ysum_ref, outsum_ref, sum_sem, slab_sem, pair_send, pair_recv,
                    s_send, s_recv, t_send, t_recv, p_send, p_recv):
    place = Place()
    blocks, tok, model = every_ref.shape[0] * every_ref.shape[1], every_ref.shape[2], every_ref.shape[3]
    branch_all = every_ref.reshape(blocks, tok, model)
    columns = 512
    lead = 256 - heads.wide
    load_w = load_slab(kv_hbm, qo_hbm, w_ref, slab_sem)
    load_out = pltpu.make_async_copy(out_hbm, part_ref, load_sem.at[1])
    load_own = pltpu.make_async_copy(branch_hbm, branch_all.at[place.me], load_sem.at[2])
    load_merged = pltpu.make_async_copy(merged_hbm, merged_ref, load_sem.at[3])
    load_out.start()
    load_own.start()
    for copy in load_w:
        copy.start()
    load_kept = [pltpu.make_async_copy(src, dst, kept_sem.at[i]) for i, (src, dst) in enumerate((
        (qa_hbm, qa_ref), (vt_hbm, vt_ref), (o_hbm, o_ref), (ka_hbm, ka_ref), (kt_hbm, kt_ref), (raw_hbm, raw_ref),
        (inv_hbm, inv_ref)))]
    for copy in load_kept:
        copy.start()
    load_merged.start()
    place.greet_all(4)
    gather = Gather(place, branch_hbm, branch_all, ag_send, ag_recv)
    gather.start()
    line = Line(place)
    ffn = [RowScatter(line, part, recv, ffn_merge.at[i], ffn_merge.at[i], z_send.at[i], z_recv.at[i])
           for i, (part, recv) in enumerate(((gate_grad, gate_recv), (up_grad, up_recv)))]
    for one in ffn:
        one.start_first()
    first = Scatter(place, part_ref, sibling_ref, passing_ref, final_ref, rs_send, rs_recv)
    second = Scatter(place, every_ref, sibling_ref, passing_ref, final_ref, rs2_send, rs2_recv)
    load_out.wait()
    for copy in first.exchange:
        copy.start()

    def ffn_add(i):
        own = (gate_grad, up_grad)[i]

        def work():
            load = pltpu.make_async_copy(own.at[line.c], ffn_own, own_sem.at[0])
            load.start()
            load.wait()

            def add(n, _):
                rows = span(n * 64, 64)
                ffn_merge[i, rows, :] = ffn_merge[i, rows, :] + ffn_own[rows, :]
                return 0

            lax.fori_loop(0, ffn_own.shape[0] // 64, add, 0)

        ffn[i].add(work)

    def tell(n, others):
        for other in others:
            pl.semaphore_signal(ready_sem.at[n], inc=1, device_id=(place.row, other), device_id_type=MESH)

    back = Backward(heads, place.me, table_ref, gq_ref, gk_ref, raw_ref, o_ref, qa_ref, ka_ref, kt_ref, vt_ref, inv_ref,
                    doa_ref, dopad_ref, qpad_ref, va_ref, dq_ref, acc_ref)

    def prepare(b, _):
        back.prepare(b)
        return 0

    for copy in load_kept:
        copy.wait()
    lax.fori_loop(0, blocks, prepare, 0, unroll=2)
    for copy in load_w:
        copy.wait()
    load_own.wait()

    def compute(k):
        m = place.chips[k]

        def gradient(j, _):
            b = 2 * m + j
            dm = dot(branch_all[b], w_ref[:, 384:640])
            back.gradient(b, dm[:, lead:])
            return 0

        lax.fori_loop(0, 2, gradient, 0, unroll=True)
        back.query_block(m)

    gather.own_chip()
    compute(0)
    gather.neighbours()
    for one in ffn:
        one.start_far()
    first.combine(3)
    first.pass1.start()
    first.pass2.start()
    gather.chip1()
    ffn_add(0)
    ffn_add(1)
    compute(1)
    for one in ffn:
        one.start_near()
    first.combine(1)
    first.first1.start()
    gather.chip2()
    compute(2)
    first.combine(2)
    first.first2.start()
    gather.diagonal()
    first.combine(0)
    tell(0, (place.sib,))
    gather.chip3()
    compute(3)
    first.finish_two()
    tell(1, place.same[1:3])
    load_merged.wait()
    tile = 256
    count = model // tile

    def x_copy(i, slot):
        return pltpu.make_async_copy(x_hbm.at[:, :, span(i * tile, tile)], xt_ref.at[slot], xt_sem.at[slot])

    x_copy(0, 0).start()

    def out_rows(i, _):
        out = dot_tn(branch_all[:, :, span(i * tile, tile)].reshape(blocks * tok, tile), merged_ref[...])
        gwo_ref[i] = out.astype(BF16)
        return 0

    lax.fori_loop(0, count, out_rows, 0, unroll=4)
    gather.close()
    pad = 512 - heads.qkv

    def finish(b, sums):
        grad, sums = back.finish(b, sums)
        grad = jnp.concatenate([grad, jnp.zeros((pad, tok), F32)], axis=0)
        pg_ref[b] = jnp.transpose(grad).astype(BF16)
        return sums

    zero = jnp.zeros((D, tok), F32)
    sums = lax.fori_loop(0, blocks, finish, (zero, zero), unroll=2)

    def grad_copy(i, slot):
        return pltpu.make_async_copy(wstage_ref.at[slot], grad_hbm.at[i // 2, lax.rem(i, 2)], wstage_sem.at[slot])

    def weight_rows(i, _):
        slot = lax.rem(i, 2)

        @pl.when(i + 1 < count)
        def _():
            x_copy(i + 1, 1 - slot).start()

        @pl.when(i >= 2)
        def _():
            grad_copy(i - 2, slot).wait()

        x_copy(i, slot).wait()
        x = xt_ref[slot].reshape(blocks * tok, tile)
        qkv = dot_tn(x, pg_ref[...].reshape(blocks * tok, 512))
        even = place.core == 0
        cols = span(i * tile, tile)
        kv_own[i // 2, lax.rem(i, 2)] = jnp.where(even, qkv[:, 0:128], qkv[:, 128:256]).astype(BF16)
        merged_ref[cols, 0:128] = jnp.where(even, qkv[:, 128:256], qkv[:, 0:128]).astype(BF16)
        wstage_ref[slot, :, 0:heads.wide] = qkv[:, 256:256 + heads.wide].astype(BF16)
        wstage_ref[slot, :, heads.wide:2 * heads.wide] = gwo_ref[i, :, lead:]
        grad_copy(i, slot).start()
        return 0

    lax.fori_loop(0, count, weight_rows, 0, unroll=2)
    for i in (count - 2, count - 1):
        grad_copy(i, i % 2).wait()

    pair = place.send(merged_ref.at[:, 0:128], kv_in, pair_send, pair_recv, 0, place.sib)
    pair.start()
    attn = RowScatter(line, grad_hbm, qo_recv, amerge_ref, amerge_ref, z_send.at[2], z_recv.at[2])
    attn.start_first()
    load_passed = pltpu.make_async_copy(grad_hbm.at[line.c], aown_ref, own_sem.at[2])
    load_passed.start()
    pair.wait_recv()

    def add_pair(n, _):
        b, rows = n // 4, span(lax.rem(n, 4) * 64, 64)
        for r in range(4):
            kv_own[r, b, rows, :] = kv_own[r, b, rows, :] + kv_in[span(r * 512 + n * 64, 64), :]
        return 0

    lax.fori_loop(0, 8, add_pair, 0)
    kv_sum = RowScatter(line, kv_own, kv_recv, kmerge_ref, kmerge_ref, z_send.at[3], z_recv.at[3])
    kv_sum.start_first()

    def attn_work():
        def add(n, _):
            b, rows = n // 4, span(lax.rem(n, 4) * 64, 64)
            amerge_ref[b, rows, :] = amerge_ref[b, rows, :] + aown_ref[b, rows, :]
            return 0

        lax.fori_loop(0, 8, add, 0)

    def kv_work():
        def add(n, _):
            b, rows = n // 4, span(lax.rem(n, 4) * 64, 64)
            kmerge_ref[b, rows, :] = kmerge_ref[b, rows, :] + kv_own[line.c, b, rows, :]
            return 0

        lax.fori_loop(0, 8, add, 0)

    def project(k):
        m = place.chips[k]

        def model_tile(n, _):
            cols = span(n * 512, 512)
            out = dot_nt(pg_ref[pl.ds(2 * m, 2)].reshape(2 * tok, 512), w_ref[cols, 0:512])
            every_ref[k, :, :, cols] = out.astype(BF16).reshape(2, tok, 512)
            return 0

        lax.fori_loop(0, model // 512, model_tile, 0, unroll=True)
        if k == 3:
            pl.semaphore_wait(ready_sem.at[0], 1)
        second.exchange[k].start()

    project(3)
    attn.start_far()
    kv_sum.start_far()
    project(1)
    second.combine(3)
    pl.semaphore_wait(ready_sem.at[1], 2)
    second.pass1.start()
    second.pass2.start()
    project(2)
    second.combine(1)
    load_passed.wait()
    attn.add(attn_work)
    attn.start_near()
    kv_sum.start_near()
    project(0)
    kv_sum.add(kv_work)
    second.combine(2)

    head_gains = jnp.sum(jnp.transpose(jnp.concatenate(sums, axis=0)), axis=0, keepdims=True)
    row8 = lax.broadcasted_iota(jnp.int32, (8, 128), 0)
    for r in range(4):
        for n in range(PLANE):
            start = (r * PLANE + n) * D
            piece = jnp.concatenate([gain_grad_ref[:, start:start + D], jnp.zeros((1, 128 - D), F32)], axis=1)
            small_ref[r, n] = jnp.where(row8 == 0, piece, jnp.where(row8 == 1, head_gains, 0.0))
    small_sends = []
    for j in range(1, 4):
        other = lax.rem(place.row + j, 4)
        small_sends.append(line.send(small_ref.at[other], small_row.at[place.row], s_send, j, s_recv, j, other))
    for copy in small_sends:
        copy.start()
    small_row[place.row] = small_ref[place.row]

    def take(out_ref, scatter):
        def one(i, _):
            rows = span(i * 32, 32)
            out_ref[rows, :] = scatter.total(rows)
            return 0

        lax.fori_loop(0, tok // 32, one, 0)

    first.arrive()
    take(outsum_ref, first)
    sums_out = [pltpu.make_async_copy(outsum_ref, outsum_hbm, sum_sem.at[0]),
                pltpu.make_async_copy(ysum_ref, ysum_hbm, sum_sem.at[1])]
    sums_out[0].start()
    tell(2, place.same[1:3])
    first.close()
    pl.semaphore_wait(ready_sem.at[2], 2)
    second.first1.start()
    second.first2.start()
    second.combine(0)
    def fetch(n, qo, kv, sem):
        return [pltpu.make_async_copy(qo, part_ref.at[n, :, :, 128:columns], own_sem.at[sem]),
                pltpu.make_async_copy(kv, part_ref.at[n, :, :, 0:128], own_sem.at[sem + 1])]

    own_term = fetch(0, grad_hbm.at[place.row], kv_own.at[place.row], 4)
    for copy in own_term:
        copy.start()

    second.finish_two()
    for copy in small_sends:
        copy.wait_recv()
    small_mid[...] = (small_row[0] + small_row[1]) + (small_row[2] + small_row[3])
    plane_sends = []
    for j in range(1, PLANE):
        other = lax.rem(place.me + j, PLANE)
        plane_sends.append(place.send(small_mid.at[other], small_last.at[place.me], t_send, t_recv, j, other))
    for copy in plane_sends:
        copy.start()
    small_last[place.me] = small_mid[place.me]
    for copy in plane_sends:
        copy.wait_recv()
    total = small_last[0]
    for n in range(1, PLANE):
        total = total + small_last[n]
    small_out[...] = total
    for copy in own_term:
        copy.wait()
    keeps = []

    def hand_over(index, lanes, total, arrived):
        total.finish()

        def fold(slots):
            loads = [pltpu.make_async_copy(arrived.at[slot], part_ref.at[slot + 1, :, :, lanes], own_sem.at[6 + 2 * slot + index])
                     for slot in slots]
            for copy in loads:
                copy.start()
            for copy in loads:
                copy.wait()

            def add(n, _):
                b, rows = n // 4, span(lax.rem(n, 4) * 64, 64)
                term = part_ref[0, b, rows, lanes]
                for slot in slots:
                    term = term + part_ref[slot + 1, b, rows, lanes]
                part_ref[0, b, rows, lanes] = term
                return 0

            lax.fori_loop(0, 8, add, 0)

        @pl.when(line.middle)
        def _():
            fold((0, 1, 2))

        @pl.when(jnp.logical_not(line.middle))
        def _():
            fold((0, 2))

        def piece(n):
            return part_ref.at[0, n // 4, span(lax.rem(n, 4) * 64, 64), lanes]

        keeps.append(pltpu.make_async_copy(piece(place.me), pieces_ref.at[place.me, :, lanes], own_sem.at[index]))
        keeps[-1].start()
        for j in range(1, PLANE):
            other = lax.rem(place.me + j, PLANE)
            copy = place.send(piece(other), pieces_ref.at[place.me, :, lanes], p_send.at[index], p_recv.at[index], j, other)
            copy.start()
            plane_sends.append(copy)

    hand_over(1, slice(128, columns), attn, qo_recv)
    hand_over(0, slice(0, 128), kv_sum, kv_recv)
    second.arrive()
    take(ysum_ref, second)
    sums_out[1].start()
    for one in ffn:
        one.finish()
        one.close()
    for copy in plane_sends[PLANE - 1:]:
        copy.wait_recv()
    for copy in keeps:
        copy.wait()
    unscaled, out_t = attention_sums(heads, lambda s: pieces_ref[s].astype(F32), True)
    gain_sums = jnp.sum(unscaled * qkv_ref[...].astype(F32), axis=1, keepdims=True)
    grad_gain_ref[...] = jnp.transpose(jnp.broadcast_to(gain_sums, (gain_sums.shape[0], 128)))[0:8]
    grad_qkv_ref[...] = unscaled * column(gain_ref)
    grad_out_ref[...] = jnp.transpose(out_t)
    for copy in sums_out:
        copy.wait()
    for copy in plane_sends + small_sends + [pair]:
        copy.wait_send()
    attn.close()
    kv_sum.close()
    second.close()


def backward_phase(heads, branch, out_part, x_all, kv, qo, weight_grads, table, gq, gk, gain_grad, w_qkv, gain_attn, kept):
    blocks, tok, model = x_all.shape
    length = blocks * tok
    depth = w_qkv.shape[0]
    dma = pltpu.SemaphoreType.DMA
    raw, merged, *rest = kept
    return pl.pallas_call(
        functools.partial(backward_kernel, heads),
        out_shape=(
            jax.ShapeDtypeStruct((tok, model), F32),
            jax.ShapeDtypeStruct((tok, model), F32),
            jax.ShapeDtypeStruct(w_qkv.shape, F32),
            jax.ShapeDtypeStruct((QUERY_HEADS * D, depth), F32),
            jax.ShapeDtypeStruct((8, depth), F32),
            jax.ShapeDtypeStruct((8, 128), F32),
            jax.ShapeDtypeStruct((4, 2, 256, 384), BF16),
            *(jax.ShapeDtypeStruct((3,) + grad.shape[1:], BF16) for grad in weight_grads),
            jax.ShapeDtypeStruct((3, 2, 256, 384), BF16),
            jax.ShapeDtypeStruct((3, 2, 256, 128), BF16),
        ),
        in_specs=[ANY_SPEC] * 8 + [VMEM_SPEC] * 6 + [ANY_SPEC] * (1 + len(rest)),
        out_specs=(ANY_SPEC,) * 2 + (VMEM_SPEC,) * 4 + (ANY_SPEC,) * 5,
        scratch_shapes=[
            *(pltpu.VMEM(array.shape, array.dtype) for array in (raw, *rest)),
            dma((7,)),
            pltpu.VMEM((4, 2, tok, model), BF16),
            pltpu.VMEM((model, heads.columns), BF16),
            pltpu.VMEM((blocks, tok, 512), BF16),
            pltpu.VMEM(merged.shape, BF16),
            pltpu.VMEM((2, blocks, tok, 256), BF16),
            pltpu.VMEM((2, 256, 384), BF16),
            pltpu.VMEM((model // 256, 256, 256), BF16),
            *backward_scratch(heads, length),
            *scatter_scratch(tok, model),
            dma((SCATTER_SLOTS,)), dma((SCATTER_SLOTS,)),
            dma((GATHER_SLOTS,)), dma((GATHER_SLOTS,)), dma((4,)), dma((2,)), dma((2,)),
            pltpu.SemaphoreType.REGULAR((3,)),
            pltpu.VMEM((2,) + weight_grads[0].shape[1:], BF16),
            pltpu.VMEM(weight_grads[0].shape[1:], BF16),
            dma((4, ROW_SLOTS)), dma((4, ROW_SLOTS)), dma((12,)),
            pltpu.VMEM((4, PLANE, 8, 128), F32),
            pltpu.VMEM((4, PLANE, 8, 128), F32),
            pltpu.VMEM((PLANE, 8, 128), F32),
            pltpu.VMEM((PLANE, 8, 128), F32),
            pltpu.VMEM((PLANE, depth, 512), BF16),
            pltpu.VMEM((2, 256, 384), BF16),
            pltpu.VMEM((2, 256, 384), BF16),
            pltpu.VMEM((4, 2, 256, 128), BF16),
            pltpu.VMEM((model, 128), BF16),
            pltpu.VMEM((2, 256, 128), BF16),
            pltpu.VMEM((tok, model), F32),
            pltpu.VMEM((tok, model), F32),
            dma((2,)), dma((3,)), dma((1,)), dma((1,)),
            dma((4,)), dma((4,)), dma((PLANE,)), dma((PLANE,)), dma((2, PLANE)), dma((2, PLANE)),
        ],
        compiler_params=pltpu.CompilerParams(collective_id=3, has_side_effects=True, vmem_limit_bytes=63 * 1024 * 1024),
        cost_estimate=pl.CostEstimate(flops=60 << 30, bytes_accessed=64 << 20, transcendentals=0),
    )(branch, out_part, x_all, kv, qo, *weight_grads, merged, table, gq, gk, gain_grad, w_qkv, gain_attn, raw, *rest)


def norm_back(grad_normed, values_in, inv_rms, gain):
    scaled = grad_normed * gain
    gain_grad = jnp.sum(grad_normed * values_in * inv_rms, axis=0)
    input_grad = inv_rms * scaled - values_in * inv_rms**3 * jnp.mean(scaled * values_in, axis=-1, keepdims=True)
    return input_grad, gain_grad


def start_wide(x, table, pieces, gain):
    return (
        lax.all_gather(x, "seq", axis=0, tiled=False),
        lax.all_gather(table, "seq", axis=0, tiled=False),
        lax.all_gather(lax.all_to_all(pieces, "seq", 0, 0, tiled=False), "rows", axis=0, tiled=False),
        lax.all_gather(lax.all_gather(gain, "seq", axis=0, tiled=False), "rows", axis=0, tiled=False),
    )


def scatter_rows(part, tok):
    return lax.psum_scatter(part.reshape(-1, part.shape[-1]), "seq", scatter_dimension=0, tiled=True).astype(F32)


def attention_wide(heads, x_all, g, w, table, gq, gk):
    blocks, tok, model = x_all.shape
    proj = dot(x_all.reshape(blocks * tok, model), w[:, :heads.qkv])
    kept = pl.pallas_call(
        functools.partial(local_forward_kernel, heads),
        out_shape=kept_shapes(heads, blocks * tok, 0),
        compiler_params=pltpu.CompilerParams(vmem_limit_bytes=VMEM_LIMIT),
    )(proj, table, gq, gk)
    total = scatter_rows(dot_nt(kept[1], w[:, heads.qkv:]).astype(BF16), tok)
    own = lax.dynamic_index_in_dim(x_all, lax.axis_index("seq"), 0, keepdims=False)
    return (own.astype(F32) + total, lax.all_gather(g, "seq", axis=0, tiled=False)) + tuple(kept)


def feed_forward_wide(res, gain, g_blocks, gate_slab, up_slab, down_slab):
    blocks, tok, model = g_blocks.shape
    inv = norm_inverse(res)
    two_all = lax.all_gather((res * inv * gain).astype(BF16), "seq", axis=0, tiled=True)
    g_all = g_blocks.reshape(blocks * tok, model)
    gate_act = dot(two_all, gate_slab)
    up_act = dot(two_all, up_slab)
    s = jax.nn.sigmoid(gate_act)
    hidden = (gate_act * s * up_act).astype(BF16)
    hidden_grad = dot_nt(g_all, down_slab)
    gate_grad = (hidden_grad * up_act * s * (1.0 + gate_act * (1.0 - s))).astype(BF16)
    up_grad = (hidden_grad * gate_act * s).astype(BF16)
    two_grad = scatter_rows((dot_nt(gate_grad, gate_slab) + dot_nt(up_grad, up_slab)).astype(BF16), tok)
    branch_part = dot(hidden, down_slab).astype(BF16).reshape(blocks, tok, model)
    norm_grad, gain_grad = norm_back(two_grad, res, inv, gain)
    g = lax.dynamic_index_in_dim(g_blocks, lax.axis_index("seq"), 0, keepdims=False)
    residual_grad = g.astype(F32) + norm_grad
    return (branch_part, residual_grad, residual_grad.astype(BF16), gain_grad[None],
            dot_tn(two_all, gate_grad).astype(BF16), dot_tn(two_all, up_grad).astype(BF16),
            dot_tn(hidden, g_all).astype(BF16))


def backward_wide(heads, branch, out_part, x_all, w, table, gq, gk, kept):
    blocks, tok, model = x_all.shape
    length = blocks * tok
    raw, merged, *rest = kept
    out_sum = scatter_rows(out_part, tok)
    branch_all = lax.all_gather(branch, "seq", axis=0, tiled=True)
    pg, gains = pl.pallas_call(
        functools.partial(local_backward_kernel, heads),
        out_shape=(jax.ShapeDtypeStruct((length, heads.qkv), BF16), jax.ShapeDtypeStruct((2 * D, 128), F32)),
        scratch_shapes=backward_scratch(heads, length),
        compiler_params=pltpu.CompilerParams(vmem_limit_bytes=VMEM_LIMIT),
    )(dot(branch_all, w[:, heads.qkv:]), table, gq, gk, raw, *rest)
    y_sum = scatter_rows(dot_nt(pg, w[:, :heads.qkv]).astype(BF16), tok)
    grad = jnp.concatenate([dot_tn(x_all.reshape(length, model), pg), dot_tn(branch_all, merged)], axis=1)
    return y_sum, out_sum, grad.astype(BF16), gains


def rotary_table(x, positions, segments):
    inverse = jnp.exp(-math.log(THETA) * jnp.arange(HALF, dtype=F32) * 2.0 / D)
    angles = inverse[:, None] * positions.astype(F32)[None, :]
    hot = jnp.arange(SEGMENT_KINDS, dtype=jnp.int32)[:, None] == segments[None, :]
    root = jnp.pad(norm_inverse(x).T, ((0, 7), (0, 0)))
    return jnp.concatenate([jnp.cos(angles), jnp.sin(angles), hot.astype(F32), root], axis=0)


def attention_pieces(heads, w_qkv, w_out, split):
    depth = w_qkv.shape[0]
    qw, kw = QUERY_HEADS * D, KEY_VALUE_HEADS * D
    out_t = w_out.T

    def columns(array, start, first, count, most):
        parts = []
        for i in range(count):
            n = first + i
            parts.append(array[:, start + n * D:start + (n + 1) * D] if n < most else jnp.zeros((depth, D), BF16))
        return parts

    pairs, others = [], []
    for s in range(heads.seq):
        q, k = s * heads.queries, heads.first(s)
        parts = []
        for n in ([k + s % 2] if split else range(k, k + heads.pairs)):
            parts += columns(w_qkv, qw, n, 1, KEY_VALUE_HEADS) + columns(w_qkv, qw + kw, n, 1, KEY_VALUE_HEADS)
        pairs.append(jnp.concatenate(parts, axis=1))
        others.append(jnp.concatenate(columns(w_qkv, 0, q, heads.queries, QUERY_HEADS)
                                      + columns(out_t, 0, q, heads.queries, QUERY_HEADS), axis=1))
    pairs, others = jnp.stack(pairs), jnp.stack(others)
    return (pairs, others) if split else jnp.concatenate([pairs, others], axis=2)


def attention_sums(heads, piece, split):
    pieces = [piece(s) for s in range(heads.seq)]
    held = 1 if split else heads.pairs
    first = [heads.first(s) + (s % 2 if split else 0) for s in range(heads.seq)]
    lead = 2 * held * D
    cut = lambda s, start, n: pieces[s][:, start + n * D:start + (n + 1) * D]
    queries = [cut(n // heads.queries, lead, n % heads.queries) for n in range(QUERY_HEADS)]
    outs = [cut(n // heads.queries, lead + heads.wide, n % heads.queries) for n in range(QUERY_HEADS)]

    def pairs(value):
        found = []
        for n in range(KEY_VALUE_HEADS):
            terms = [cut(s, value * D, 2 * (n - first[s])) for s in range(heads.seq)
                     if s * heads.queries < QUERY_HEADS and 0 <= n - first[s] < held]
            found.append(functools.reduce(jnp.add, terms))
        return found

    qkv = jnp.concatenate(queries + pairs(0) + pairs(1), axis=1)
    return qkv, jnp.concatenate(outs, axis=1)


def body(tokens, segments, positions, cotangent, gain_attn, w_qkv, gain_q, gain_k, w_out, gain_ffn, w_gate, w_up, w_down):
    seq = lax.axis_size("seq")
    rows = lax.axis_size("rows")
    heads = Heads(seq)
    depth = w_qkv.shape[0]
    tok, model = tokens.shape[1:]
    plane = seq == PLANE and rows == 4
    row = lax.axis_index("rows")

    gq, gk = gain_q[None], gain_k[None]
    x = tokens[0].astype(F32)
    scaled = (w_qkv.astype(F32) * gain_attn.astype(F32)[:, None]).astype(BF16)
    pieces = attention_pieces(heads, scaled, w_out, plane)
    table = rotary_table(x, positions[0], segments[0])
    if plane:
        x_all, table, kv, qo, gains = start_phase(rows, tokens[0], table, *pieces, gain_ffn[None])
        kv, qo = kv.reshape(2, model, -1), qo.reshape(model, -1)
    else:
        gain = jnp.pad(gain_ffn.astype(F32)[None], ((0, 7), (0, 128 - depth)))
        x_all, table, w, gains = start_wide(tokens[0], table, pieces, gain)
        w = w.reshape(model, heads.columns)
        gain_two = gains[:, :, 0, :depth].reshape(1, model)
    inv = norm_inverse(x)

    if plane:
        residual, two, g_all, gate, up, *kept = attention_phase(
            heads, x_all, cotangent[0], kv, qo, (w_gate, w_up), table, gq, gk, gains)
        out_part, residual_grad, branch, gain_two_grad, *weight_grads, gate_own, up_own, down_own, down_recv = feed_forward(
            residual, gains, two, cotangent[0], g_all, (w_gate, gate, w_up, up, w_down))
        weight_grads = [grad.reshape((4,) + w_gate.shape) for grad in weight_grads]
        y_sum, out_sum, grad_qkv, grad_out, grad_gain_attn, small, _, gate_recv, up_recv, *_ = backward_phase(
            heads, branch, out_part, x_all, kv, qo, weight_grads, table, gq, gk, gain_two_grad, w_qkv,
            gain_attn[None], kept)
        grad_gain_attn = grad_gain_attn[0]
        middle = (row + 1) // 2 == 1

        def row_total(own, recv):
            return own.astype(F32) + recv[0].astype(F32) + recv[2].astype(F32) + jnp.where(middle, recv[1].astype(F32), 0.0)

        grad_gate, grad_up, grad_down = (
            row_total(own, recv) for own, recv in ((gate_own, gate_recv), (up_own, up_recv), (down_own, down_recv)))
        grad_gain_ffn, head_gains = small[0, :depth], small[1]
    else:
        gate_slab = lax.all_gather(w_gate, "rows", axis=0, tiled=True)
        up_slab = lax.all_gather(w_up, "rows", axis=0, tiled=True)
        down_slab = lax.all_gather(w_down, "rows", axis=1, tiled=True)
        residual, g_all, *kept = attention_wide(heads, x_all, cotangent[0], w, table, gq, gk)
        out_part, residual_grad, branch, gain_two_grad, gate_wgrad, up_wgrad, down_wgrad = feed_forward_wide(
            residual, gain_two, g_all, gate_slab, up_slab, down_slab)
        grad_gate = lax.psum_scatter(gate_wgrad, "rows", scatter_dimension=0, tiled=True).astype(F32)
        grad_up = lax.psum_scatter(up_wgrad, "rows", scatter_dimension=0, tiled=True).astype(F32)
        grad_down = lax.psum_scatter(down_wgrad, "rows", scatter_dimension=1, tiled=True).astype(F32)
        y_sum, out_sum, attn_grad, head_gains = backward_wide(heads, branch, out_part, x_all, w, table, gq, gk, kept)
        attn_grad = lax.psum_scatter(attn_grad, "rows", scatter_dimension=0, tiled=True)
        attn_grad = lax.all_to_all(attn_grad.reshape(seq, depth, heads.columns), "seq", 0, 0, tiled=False)
        small = lax.psum(jnp.concatenate([gain_two_grad[0], head_gains[:, 0]]), ("rows", "seq"))
        grad_gain_ffn = lax.dynamic_slice_in_dim(small, (row * seq + lax.axis_index("seq")) * depth, depth)
        head_gains = small[model:]
        attn_grad = attn_grad.astype(F32)
        unscaled, grad_out = attention_sums(heads, lambda s: attn_grad[s], False)
        grad_out = grad_out.T
        grad_gain_attn = jnp.sum(unscaled * w_qkv.astype(F32), axis=1)
        grad_qkv = unscaled * gain_attn.astype(F32)[:, None]

    layer_out = (residual + out_sum).astype(BF16)
    grad_tokens = residual_grad + y_sum - x * (inv * inv * jnp.mean(y_sum * x, axis=-1, keepdims=True))
    return (
        layer_out[None],
        grad_tokens[None],
        grad_gain_attn,
        grad_qkv,
        head_gains[:D],
        head_gains[D:],
        grad_out,
        grad_gain_ffn,
        grad_gate,
        grad_up,
        grad_down,
    )


def solution(mesh):
    both = ("rows", "seq")
    return jax.shard_map(
        body,
        mesh=mesh,
        in_specs=(
            P("rows", "seq", None), P("rows", "seq"), P("rows", "seq"), P("rows", "seq", None),
            P(both), P(both, None), P(), P(), P(None, both), P(both),
            P("rows", "seq"), P("rows", "seq"), P("seq", "rows"),
        ),
        out_specs=(
            P("rows", "seq", None), P("rows", "seq", None), P(both), P(both, None), P(), P(),
            P(None, both), P(both), P("rows", "seq"), P("rows", "seq"), P("seq", "rows"),
        ),
        check_vma=False,
    )
```
